32 devices in a mesh: ctx: 16 (over z, y, core), wa: 2 (over x).
Axes of the slice: x: 2, y: 2, z: 4, core: 2. Of those that a mesh axis runs over, the one named last changes fastest.
Arguments:
- layer_input: bfloat16 [2, 2048, 1536], P('wa', 'ctx'), may hold values from -6 to 6
- seq_ids: int32 [2, 2048], P('wa'), may hold values from 0 to 2, as said below
- routes: int32 [2, 2048, 4], P('wa', 'ctx'), may hold values from 0 to 7, all different within a row; in each aligned block of 128 rows (0 to 127, 128 to 255, ..., all dimensions but the last counted through in order) at most 128 rows name the same one
- gain_attn: bfloat16 [1536], P('wa'), may hold values from 0.5 to 1.5
- w_query: bfloat16 [1536, 1536], P('wa'), may hold values from -0.15625 to 0.15625
- w_keyval: bfloat16 [1536, 512], P('wa'), may hold values from -0.15625 to 0.15625
- w_out_attn: bfloat16 [1536, 1536], P('wa'), may hold values from -1.75 to 1.75
- gain_ffn: bfloat16 [1536], P('wa'), may hold values from 0.5 to 1.5
- router: bfloat16 [1536, 8], P('wa'), may hold values from -0.078125 to 0.078125
- w_in: bfloat16 [16, 2, 1536, 384], P('ctx', None, None, 'wa'), may hold values from -0.15625 to 0.15625
- w_out: bfloat16 [16, 384, 1536], P('ctx', 'wa'), may hold values from -0.21875 to 0.21875
- d_out: bfloat16 [2, 2048, 1536], P('wa', 'ctx'), may hold values from -6 to 6
Outputs:
- output: bfloat16 [2, 2048, 1536], P('wa', 'ctx')
- d_layer_input: bfloat16 [2, 2048, 1536], P('wa', 'ctx')
- d_gain_attn: float32 [1536], P('wa')
- d_w_query: float32 [1536, 1536], P('wa')
- d_w_keyval: float32 [1536, 512], P('wa')
- d_w_out_attn: float32 [1536, 1536], P('wa')
- d_gain_ffn: float32 [1536], P('wa')
- d_router: float32 [1536, 8], P('wa')
- d_w_in: float32 [16, 2, 1536, 384], P('ctx', None, None, 'wa')
- d_w_out: float32 [16, 384, 1536], P('ctx', 'wa')
The draws below stay inside these ranges and needn't reach their ends.
Inputs may be any that keep to these rules, and one draw needn't show every extreme that they name: `seq_ids`: in each row, id 0 covers a first run of 1 to 127 positions, id 2 a last run of 1 to 127 positions, and id 1 all positions between them. `routes`: each token names 4 different experts. Within the 128 tokens of one device no expert is named by more than 128 tokens, a bound that some block reaches.
All inputs are finite; a program needn't handle non-finite values.
Results may differ from the reference program's by a relative error of at most 0.018.
Values may be sent and summed in bfloat16 or wider, within the bound.
A program may use at most 192 MiB of HBM per device.

```python
import math
import jax
import jax.numpy as jnp
import numpy as np
from jax import lax

D = 1536
HEADS = 12
KV_HEADS = 2
HEAD_DIM = 128
FF = 768
TOP = 4
BLOCK = 256
TOK_DEV = 128
LEN = 2048
SEQS = 2
EXPERTS = 8
HALF_FF = 384
CAP = 128
N_CTX = 16


def draw_seq_ids(key, part):
    key = jax.random.fold_in(key, 7)
    first_key, last_key = jax.random.split(key)
    opening = jax.random.randint(first_key, (SEQS, 1), 1, TOK_DEV)
    closing = jax.random.randint(last_key, (SEQS, 1), 1, TOK_DEV)
    positions = jnp.arange(LEN, dtype=jnp.int32)[None, :]
    return (positions >= opening).astype(jnp.int32) + (positions >= LEN - closing).astype(jnp.int32)


def shard_levels(own_key, dims, shards, least, top_value):
    def one(position, parts):
        steps = jax.random.uniform(jax.random.fold_in(jax.random.fold_in(own_key, 6), position), (parts,), jnp.float32, least / len(shards), top_value / len(shards))
        return jnp.repeat(jnp.exp(steps), dims[position] // parts).reshape((-1,) + (1,) * (len(dims) - position - 1))

    level = one(*shards[0])
    for cut in shards[1:]:
        level = level * one(*cut)
    return level


def assign_block(own_key, own, number, rows, number_of, top, limit, skew):
    order = jax.random.permutation(own_key, number_of)
    crowded, common = load_shares(number_of, rows * top, limit, skew, True), load_shares(number_of, rows * top, limit, skew, False)
    places = jnp.arange(number_of)

    def named(sizes, offset_by):
        used = int((sizes > 0).sum())
        fixed = max(1, used // 4)
        passed = fixed + (places - fixed + offset_by * (used - fixed)) % max(1, number_of - fixed)
        return jnp.zeros((number_of,), jnp.int32).at[order[jnp.where(places < fixed, places, passed)]].set(jnp.asarray(sizes, jnp.int32))

    sizes = jnp.where(number % 4 == 0, named(crowded, number // 4), named(common, number - number // 4 - 1))
    mixed = jax.random.permutation(jax.random.fold_in(own, 3), number_of)
    donor, sink = mixed[0:number_of // 2 * 2:2], mixed[1:number_of // 2 * 2:2]
    slack = jnp.minimum(sizes[donor] - 1, limit - sizes[sink]) // 2
    slack = jnp.where((donor == order[0]) | (sink == order[0]) | (sizes[sink] == 0), 0, jnp.maximum(slack, 0))
    passed = jax.random.randint(jax.random.fold_in(own, 4), (number_of // 2,), 0, 1 << 20) % (slack + 1)
    sizes = sizes.at[donor].add(-passed).at[sink].add(passed)
    labels = jnp.searchsorted(jnp.cumsum(sizes), jnp.arange(rows * top), side="right").astype(jnp.int32)
    table = labels.reshape(top, rows).T
    table = table[jax.random.permutation(jax.random.fold_in(own, 1), rows)]
    offset_by = jax.random.randint(jax.random.fold_in(own, 2), (rows, 1), 0, top)
    return jnp.take_along_axis(table, (jnp.arange(top)[None, :] + offset_by) % top, axis=1)


def load_shares(number_of, total, limit, lean, full):
    loads = [(1 << 20) // math.isqrt(standing ** lean) + 1 for standing in range(1, number_of + 1)]
    largest = limit if full else min(limit, max(-(-total // number_of), total * loads[0] // sum(loads)))
    least = 1 if total - largest >= number_of - 1 else 0
    given, rest = [largest] + [least] * (number_of - 1), total - largest - least * (number_of - 1)
    while rest > 0:
        movable = [i for i in range(1, number_of) if given[i] < largest] or [i for i in range(1, number_of) if given[i] < limit]
        mass, remaining = sum([loads[i] for i in movable]), rest
        for i in movable:
            more = min(limit - given[i], max(1, remaining * loads[i] // mass), rest)
            given[i] = given[i] + more
            rest = rest - more
    return np.array(given)


def noise(stream_key, shape, width, bound, shards=(), kind=jnp.bfloat16):
    loudness = shard_levels(stream_key, shape, shards, -0.22, 0.18) if shards else 1.0
    drawn = jax.random.normal(stream_key, shape, jnp.float32) * width * loudness
    return jnp.minimum(jnp.maximum(drawn, -bound), bound).astype(kind)


def setup_inputs(seed: int = 0) -> dict:
    key_of = jax.random.split(jax.random.key(seed), 13)
    layer_input = noise(key_of[0], (SEQS, LEN, D), 1.0, 6.0, ((0, 2), (1, 16)))
    seq_ids = draw_seq_ids(jax.random.fold_in(key_of[12], 71), 0)
    routes_keys = jax.random.split(jax.random.fold_in(key_of[2], 1), SEQS * LEN // TOK_DEV)
    routes_turns = jax.random.permutation(jax.random.fold_in(key_of[2], 3), SEQS * LEN // TOK_DEV)
    routes = jax.vmap(lambda own, number: assign_block(jax.random.fold_in(key_of[2], 2), own, number, TOK_DEV, EXPERTS, TOP, CAP, 1))(routes_keys, routes_turns).reshape((SEQS, LEN, TOP))
    gain_attn = jnp.clip(1.0 + 0.1 * jax.random.normal(key_of[3], (D,), jnp.float32), 0.5, 1.5).astype(jnp.bfloat16)
    w_query = noise(key_of[4], (D, HEADS * HEAD_DIM), D ** -0.5, 0.15625, ((0, 2),))
    w_keyval = noise(key_of[5], (D, 2 * KV_HEADS * HEAD_DIM), D ** -0.5, 0.15625, ((0, 2),))
    w_out_attn = noise(key_of[6], (HEADS * HEAD_DIM, D), (max(1, HEADS * HEAD_DIM * 16 // (TOK_DEV * N_CTX))) ** -0.5, 1.75, ((0, 2),))
    gain_ffn = jnp.clip(1.0 + 0.1 * jax.random.normal(key_of[7], (D,), jnp.float32), 0.5, 1.5).astype(jnp.bfloat16)
    router = noise(key_of[8], (D, EXPERTS), (4 * D) ** -0.5, 0.078125, ((0, 2),))
    w_in = noise(key_of[9], (2 * EXPERTS, 2, D, HALF_FF), D ** -0.5, 0.15625, ((0, 16), (3, 2)))
    w_out = noise(key_of[10], (2 * EXPERTS, HALF_FF, D), FF ** -0.5, 0.21875, ((0, 16), (1, 2)))
    d_out = noise(key_of[11], (SEQS, LEN, D), 1.0, 6.0, ((0, 2), (1, 16)))
    return dict(layer_input=layer_input, seq_ids=seq_ids, routes=routes, gain_attn=gain_attn, w_query=w_query, w_keyval=w_keyval, w_out_attn=w_out_attn, gain_ffn=gain_ffn, router=router, w_in=w_in, w_out=w_out, d_out=d_out)


EPSILON = 1e-06
THETA = 1000000.0
NEGATIVE = -1e+30
FULL_PRECISION = lax.Precision.HIGHEST

@jax.custom_vjp
def low(v):
    return lax.optimization_barrier(v.astype(jnp.bfloat16)).astype(jnp.float32)

@jax.custom_vjp
def reduced_backward(v):
    return v

def low_keep(v):
    return (low(v), None)

def low_pass(kept, grad):
    return (grad,)

def back_keep(v):
    return (v, None)

def back_low(kept, grad):
    return (low(grad),)
low.defvjp(low_keep, low_pass)
reduced_backward.defvjp(back_keep, back_low)

def rms_scale(values, gain_vec):
    return values * lax.rsqrt(lax.optimization_barrier(jnp.mean(values * values, axis=-1, keepdims=True)) + EPSILON) * gain_vec

def rotate(values, angles):
    half_dim = values.shape[-1] // 2
    cosine = jnp.cos(angles)
    sine_part = jnp.sin(angles)
    first_half = values[..., :half_dim]
    second = values[..., half_dim:]
    return jnp.concatenate([first_half * cosine - second * sine_part, second * cosine + first_half * sine_part], axis=-1)

def angle_table(positions):
    half_dim = HEAD_DIM // 2
    frequency = THETA ** (-2.0 * jnp.arange(half_dim, dtype=jnp.float32) / HEAD_DIM)
    return (positions.astype(jnp.float32)[:, None] * frequency[None, :])[:, None, :]

def gated(stacked):
    return jax.nn.gelu(stacked[..., 0, :], approximate=True) * stacked[..., 1, :]

def slot_table(routes):
    seqs = routes.shape[0]
    group_rows = seqs * N_CTX * CAP
    per_device = routes.reshape(seqs, N_CTX, TOK_DEV * TOP)
    expert_hits = (per_device[..., None] == jnp.arange(EXPERTS, dtype=jnp.int32)).astype(jnp.int32)
    ranks = lax.optimization_barrier(jnp.sum(expert_hits * (jnp.cumsum(expert_hits, axis=2) - expert_hits), axis=-1))
    sources = jnp.arange(seqs, dtype=jnp.int32)[:, None, None] * N_CTX + jnp.arange(N_CTX, dtype=jnp.int32)[None, :, None]
    first_slots = 2 * per_device * group_rows + sources * CAP + ranks
    second_slots = first_slots + group_rows
    total = seqs * N_CTX * TOK_DEV * TOP
    return (first_slots.reshape(total).astype(jnp.int32), second_slots.reshape(total).astype(jnp.int32))

def attend_row(query, keys, values, docs):
    length = query.shape[0]
    block_rows = min(length, 512)
    group = HEADS // KV_HEADS
    key_blocks = jnp.arange(length, dtype=jnp.int32) // BLOCK

    def one_block(block_index):
        first_row = block_index * block_rows
        query_part = lax.dynamic_slice_in_dim(query, first_row, block_rows, 0).reshape(block_rows, KV_HEADS, group, HEAD_DIM)
        scores = reduced_backward(jnp.einsum('bhgd,khd->hgbk', query_part, keys, precision=FULL_PRECISION) * HEAD_DIM ** (-0.5))
        query_docs = lax.dynamic_slice_in_dim(docs, first_row, block_rows, 0)
        query_blocks = (first_row + jnp.arange(block_rows, dtype=jnp.int32)) // BLOCK
        allowed = (query_docs[:, None] == docs[None, :]) & (key_blocks[None, :] <= query_blocks[:, None])
        masked = jnp.where(allowed, scores, NEGATIVE)
        largest = lax.optimization_barrier(jnp.max(masked, axis=-1, keepdims=True))
        weights = jnp.where(allowed, jnp.exp(masked - largest), 0.0)
        probs = low(weights / lax.optimization_barrier(jnp.sum(weights, axis=-1, keepdims=True)))
        attention_mixture = jnp.einsum('hgbk,khd->bhgd', probs, values, precision=FULL_PRECISION)
        return attention_mixture.reshape(block_rows, HEADS * HEAD_DIM)
    mixed_all = lax.map(jax.checkpoint(one_block), jnp.arange(length // block_rows, dtype=jnp.int32))
    return mixed_all.reshape(length, HEADS * HEAD_DIM)

def reference(layer_input, seq_ids, routes, gain_attn, w_query, w_keyval, w_out_attn, gain_ffn, router, w_in, w_out, d_out):
    seqs = layer_input.shape[0]
    length = layer_input.shape[1]
    group_rows = seqs * N_CTX * CAP
    slot_first, slot_second = slot_table(routes)
    pair_token = jnp.arange(seqs * length * TOP, dtype=jnp.int32) // TOP
    token_of_slot = jnp.full((N_CTX * group_rows,), seqs * length, jnp.int32).at[slot_first].set(pair_token).at[slot_second].set(pair_token)
    angles = angle_table(jnp.arange(length, dtype=jnp.int32))
    kv_width = KV_HEADS * HEAD_DIM

    def forward(input_widened, gain_one, query_matrix, keyvalue_matrix, attention_matrix, gain_two, router_matrix, in_weight, out_weight):
        hidden_first_norm = low(rms_scale(input_widened, gain_one))
        query_projected = reduced_backward(jnp.einsum('ryw,wt->ryt', hidden_first_norm, query_matrix, precision=FULL_PRECISION))
        keyvalue_projected = jnp.einsum('ryw,wt->ryt', hidden_first_norm, keyvalue_matrix, precision=FULL_PRECISION)
        key_pre = reduced_backward(keyvalue_projected[..., :kv_width])
        value_all = reduced_backward(low(keyvalue_projected[..., kv_width:])).reshape(seqs, length, KV_HEADS, HEAD_DIM)
        query_all = low(rotate(query_projected.reshape(seqs, length, HEADS, HEAD_DIM), angles))
        key_all = low(rotate(key_pre.reshape(seqs, length, KV_HEADS, HEAD_DIM), angles))
        attention_mixture = jnp.stack([attend_row(query_all[row_index], key_all[row_index], value_all[row_index], seq_ids[row_index]) for row_index in range(seqs)])
        attention_mixture = reduced_backward(low(attention_mixture))
        middle_activation = input_widened + reduced_backward(jnp.einsum('kza,ac->kzc', attention_mixture, attention_matrix, precision=FULL_PRECISION))
        hidden_second_norm = low(rms_scale(middle_activation, gain_two))
        router_logits = reduced_backward(jnp.einsum('ryw,wt->ryt', hidden_second_norm, router_matrix, precision=FULL_PRECISION))
        gates = jax.nn.softmax(jnp.take_along_axis(router_logits, routes, axis=-1), axis=-1)
        padded = jnp.concatenate([hidden_second_norm.reshape(seqs * length, D), jnp.zeros((1, D), hidden_second_norm.dtype)], axis=0)
        rows = reduced_backward(padded[token_of_slot]).reshape(N_CTX, group_rows, D)
        stacked = reduced_backward(jnp.einsum('emd,egdf->emgf', rows, in_weight, precision=FULL_PRECISION))
        hidden = low(gated(stacked))
        result = reduced_backward(low(jnp.einsum('emf,efd->emd', hidden, out_weight, precision=FULL_PRECISION)))
        result_flat = result.reshape(N_CTX * group_rows, D)
        pair_rows = (result_flat[slot_first] + result_flat[slot_second]).reshape(seqs, length, TOP, D)
        return middle_activation + lax.optimization_barrier(jnp.sum(gates[..., None] * pair_rows, axis=2))
    output, pull_back = jax.vjp(forward, layer_input.astype(jnp.float32), gain_attn.astype(jnp.float32), w_query.astype(jnp.float32), w_keyval.astype(jnp.float32), w_out_attn.astype(jnp.float32), gain_ffn.astype(jnp.float32), router.astype(jnp.float32), w_in.astype(jnp.float32), w_out.astype(jnp.float32))
    grads = pull_back(d_out.astype(jnp.float32))
    return (output.astype(jnp.bfloat16), grads[0].astype(jnp.bfloat16), grads[1], grads[2], grads[3], grads[4], grads[5], grads[6], grads[7], grads[8])
```

```python
import functools
import math

import jax
import jax.numpy as jnp
from jax import lax
from jax.experimental import pallas as pl
from jax.experimental.pallas import tpu as pltpu
from jax.sharding import PartitionSpec as P

D = 1536
HEADS = 12
KV_HEADS = 2
HEAD_DIM = 128
TOP = 4
BLOCK = 256


EPSILON = 1e-06
THETA = 1000000.0
NEGATIVE = -1e30


def rms_scale(values, gain_vec):
    return (
        values * lax.rsqrt(jnp.mean(values * values, axis=-1, keepdims=True) + EPSILON) * gain_vec
    )


def rotate(values, angles):
    half_dim = values.shape[-1] // 2
    cosine = jnp.cos(angles)
    sine_part = jnp.sin(angles)
    first_half = values[..., :half_dim]
    second = values[..., half_dim:]
    return jnp.concatenate(
        [first_half * cosine - second * sine_part, second * cosine + first_half * sine_part],
        axis=-1,
    )


def angle_table(positions):
    half_dim = HEAD_DIM // 2
    frequency = THETA ** (-2.0 * jnp.arange(half_dim, dtype=jnp.float32) / HEAD_DIM)
    return (positions.astype(jnp.float32)[:, None] * frequency[None, :])[:, None, :]


def gated(stacked):
    return jax.nn.gelu(stacked[..., 0, :], approximate=True) * stacked[..., 1, :]


def over_keys(key_rows, running, advance):
    key_count = key_rows.shape[0]
    key_width = math.gcd(key_count, 512)

    def one_turn(state_now, block_index):
        key_offset = block_index * key_width
        key_part = lax.dynamic_slice_in_dim(key_rows, key_offset, key_width, 0)
        return (advance(state_now, key_part, key_offset), None)

    running, unused = lax.scan(
        one_turn, running, jnp.arange(key_count // key_width, dtype=jnp.int32)
    )
    return running


def routed_body(
    layer_input,
    seq_ids,
    routes,
    gain_attn,
    w_query,
    w_keyval,
    w_out_attn,
    gain_ffn,
    router,
    w_in,
    w_out,
    d_out,
):
    ctx_count = lax.axis_size("ctx")
    ctx_index = lax.axis_index("ctx")
    tokens = layer_input.shape[1]
    length = tokens * ctx_count
    experts_all = ctx_count // 2
    capacity = 2 * tokens * TOP // experts_all
    group = HEADS // KV_HEADS
    kv_width = KV_HEADS * HEAD_DIM
    row_count = group * tokens
    scale = HEAD_DIM ** (-0.5)
    gain_one, query_matrix, keyvalue_matrix, attention_matrix = (
        lax.all_gather(gain_attn, "wa", axis=0, tiled=True),
        lax.all_gather(w_query, "wa", axis=0, tiled=True),
        lax.all_gather(w_keyval, "wa", axis=0, tiled=True),
        lax.all_gather(w_out_attn, "wa", axis=0, tiled=True),
    )
    residual = layer_input[0].astype(jnp.float32)
    normed_one, norm_one_back = jax.vjp(rms_scale, residual, gain_one.astype(jnp.float32))
    hidden_first_norm = normed_one.astype(jnp.bfloat16)
    positions = ctx_index * tokens + jnp.arange(tokens, dtype=jnp.int32)
    angles = angle_table(positions)
    query_projected = jnp.dot(
        hidden_first_norm, query_matrix, preferred_element_type=jnp.float32
    ).reshape(tokens, HEADS, HEAD_DIM)
    keyvalue_projected = jnp.dot(
        hidden_first_norm, keyvalue_matrix, preferred_element_type=jnp.float32
    )
    key_pre = keyvalue_projected[:, :kv_width].reshape(tokens, KV_HEADS, HEAD_DIM)
    query_low = rotate(query_projected, angles).astype(jnp.bfloat16)
    key_low = rotate(key_pre, angles).astype(jnp.bfloat16)
    value_low = keyvalue_projected[:, kv_width:].astype(jnp.bfloat16)
    keyval_send = jnp.concatenate([key_low.reshape(tokens, kv_width), value_low], axis=1)
    query_rows = (
        query_low.reshape(tokens, KV_HEADS, group, HEAD_DIM)
        .transpose(1, 2, 0, 3)
        .reshape(KV_HEADS, row_count, HEAD_DIM)
    )
    doc_row = seq_ids[0]
    query_docs = lax.dynamic_slice_in_dim(doc_row, ctx_index * tokens, tokens, 0)
    query_blocks = positions // BLOCK

    def block_scores(key_part, first_key):
        key_count = key_part.shape[0]
        split_part = key_part.reshape(key_count, 2, KV_HEADS, HEAD_DIM)
        keys_here = split_part[:, 0]
        values_here = split_part[:, 1]
        scores = (
            jnp.einsum("hrd,nhd->hrn", query_rows, keys_here, preferred_element_type=jnp.float32)
            * scale
        )
        key_docs = lax.dynamic_slice_in_dim(doc_row, first_key, key_count, 0)
        key_blocks = (first_key + jnp.arange(key_count, dtype=jnp.int32)) // BLOCK
        allowed = (query_docs[:, None] == key_docs[None, :]) & (
            key_blocks[None, :] <= query_blocks[:, None]
        )
        allowed = jnp.broadcast_to(allowed[None], (group, tokens, key_count)).reshape(
            1, row_count, key_count
        )
        return (jnp.where(allowed, scores, NEGATIVE), allowed, keys_here, values_here)

    def probs_of(masked, allowed, largest, totals):
        return jnp.where(allowed, jnp.exp(masked - largest[..., None]) / totals[..., None], 0.0)

    def stats_step(running, key_part, first_key):
        largest, totals = running
        masked, allowed, keys_here, values_here = block_scores(key_part, first_key)
        new_largest = jnp.maximum(largest, jnp.max(masked, axis=-1))
        weights = jnp.where(allowed, jnp.exp(masked - new_largest[..., None]), 0.0)
        return (new_largest, totals * jnp.exp(largest - new_largest) + jnp.sum(weights, axis=-1))

    start_stats = (
        jnp.full((KV_HEADS, row_count), NEGATIVE, jnp.float32),
        jnp.zeros((KV_HEADS, row_count), jnp.float32),
    )
    largest, totals = over_keys(
        lax.all_gather(keyval_send, "ctx", axis=0, tiled=True), start_stats, stats_step
    )

    def values_step(running, key_part, first_key):
        masked, allowed, keys_here, values_here = block_scores(key_part, first_key)
        probs_low = probs_of(masked, allowed, largest, totals).astype(jnp.bfloat16)
        return running + jnp.einsum(
            "hrn,nhd->hrd", probs_low, values_here, preferred_element_type=jnp.float32
        )

    start_values = jnp.zeros((KV_HEADS, row_count, HEAD_DIM), jnp.float32)
    mixed_rows = over_keys(
        lax.all_gather(keyval_send, "ctx", axis=0, tiled=True), start_values, values_step
    )
    mixed_low = (
        mixed_rows.reshape(KV_HEADS, group, tokens, HEAD_DIM)
        .transpose(2, 0, 1, 3)
        .reshape(tokens, HEADS * HEAD_DIM)
        .astype(jnp.bfloat16)
    )
    middle_activation = residual + jnp.dot(
        mixed_low, attention_matrix, preferred_element_type=jnp.float32
    )
    gain_two, router_full, w_in_full, w_out_full = (
        lax.all_gather(gain_ffn, "wa", axis=0, tiled=True),
        lax.all_gather(router, "wa", axis=0, tiled=True),
        lax.all_gather(w_in, "wa", axis=3, tiled=True),
        lax.all_gather(w_out, "wa", axis=1, tiled=True),
    )
    in_half = w_in_full[0]
    out_half = w_out_full[0]
    normed_two, norm_two_back = jax.vjp(rms_scale, middle_activation, gain_two.astype(jnp.float32))
    hidden_second_norm = normed_two.astype(jnp.bfloat16)
    router_logits = jnp.dot(hidden_second_norm, router_full, preferred_element_type=jnp.float32)
    route_ids = routes[0]

    def gate_values(logit_rows):
        return jax.nn.softmax(jnp.take_along_axis(logit_rows, route_ids, axis=-1), axis=-1)

    gates, gate_back = jax.vjp(gate_values, router_logits)
    flat_ids = route_ids.reshape(tokens * TOP)
    expert_hits = (flat_ids[:, None] == jnp.arange(experts_all, dtype=jnp.int32)[None, :]).astype(
        jnp.int32
    )
    ranks = jnp.sum(expert_hits * (jnp.cumsum(expert_hits, axis=0) - expert_hits), axis=1)
    slot_first = 2 * flat_ids * capacity + ranks
    slot_second = slot_first + capacity
    slot_total = ctx_count * capacity
    slot_numbers = jnp.arange(slot_total, dtype=jnp.int32)[:, None]
    placed = (
        (slot_first[None, :] == slot_numbers) | (slot_second[None, :] == slot_numbers)
    ).astype(jnp.bfloat16)
    dispatch = jnp.sum(placed.reshape(slot_total, tokens, TOP), axis=2)
    send_rows = (
        jnp.dot(dispatch, hidden_second_norm, preferred_element_type=jnp.float32)
        .astype(jnp.bfloat16)
        .reshape(ctx_count, capacity, D)
    )
    arrived = lax.all_to_all(send_rows, "ctx", split_axis=0, concat_axis=0, tiled=True)
    stacked = jnp.einsum("ncd,gdf->ncgf", arrived, in_half, preferred_element_type=jnp.float32)
    hidden_low = gated(stacked).astype(jnp.bfloat16)
    result = jnp.einsum(
        "ncf,fd->ncd", hidden_low, out_half, preferred_element_type=jnp.float32
    ).astype(jnp.bfloat16)
    returned_rows = lax.all_to_all(result, "ctx", split_axis=0, concat_axis=0, tiled=True)
    returned_flat = returned_rows.reshape(slot_total, D)
    pair_rows = (
        returned_flat[slot_first].astype(jnp.float32)
        + returned_flat[slot_second].astype(jnp.float32)
    ).reshape(tokens, TOP, D)
    output = (middle_activation + jnp.sum(gates[:, :, None] * pair_rows, axis=1)).astype(
        jnp.bfloat16
    )
    grad_out = d_out[0].astype(jnp.float32)
    grad_gates = jnp.sum(pair_rows * grad_out[:, None, :], axis=-1)
    (grad_logits,) = gate_back(grad_gates)
    grad_logits_low = grad_logits.astype(jnp.bfloat16)
    gate_slots = jnp.dot(
        placed.astype(jnp.float32), gates.reshape(tokens * TOP), precision=lax.Precision.HIGHEST
    )
    routed_grad = jnp.dot(dispatch, d_out[0], preferred_element_type=jnp.float32)
    grad_send_rows = (
        (gate_slots[:, None] * routed_grad).astype(jnp.bfloat16).reshape(ctx_count, capacity, D)
    )
    grad_arrived = lax.all_to_all(grad_send_rows, "ctx", split_axis=0, concat_axis=0, tiled=True)
    grad_hidden = jnp.einsum(
        "ncd,fd->ncf", grad_arrived, out_half, preferred_element_type=jnp.float32
    )
    hidden_again, gated_back = jax.vjp(gated, stacked)
    (grad_stacked,) = gated_back(grad_hidden)
    grad_stacked_low = grad_stacked.astype(jnp.bfloat16)
    grad_rows = jnp.einsum(
        "ncgf,gdf->ncd", grad_stacked_low, in_half, preferred_element_type=jnp.float32
    ).astype(jnp.bfloat16)
    grad_returned = lax.all_to_all(grad_rows, "ctx", split_axis=0, concat_axis=0, tiled=True)
    grad_w_in = jnp.einsum(
        "ncd,ncgf->gdf", arrived, grad_stacked_low, preferred_element_type=jnp.float32
    )[None]
    grad_w_out = jnp.einsum(
        "ncf,ncd->fd",
        hidden_again.astype(jnp.bfloat16),
        grad_arrived,
        preferred_element_type=jnp.float32,
    )[None]
    grad_hidden_two = jnp.einsum(
        "st,sd->td",
        dispatch,
        grad_returned.reshape(slot_total, D),
        preferred_element_type=jnp.float32,
    )
    grad_hidden_two = grad_hidden_two + jnp.dot(
        grad_logits_low, router_full.T, preferred_element_type=jnp.float32
    )
    grad_router = jnp.dot(hidden_second_norm.T, grad_logits_low, preferred_element_type=jnp.float32)
    grad_middle_norm, grad_gain_two = norm_two_back(grad_hidden_two)
    grad_middle = grad_out + grad_middle_norm
    grad_middle_low = grad_middle.astype(jnp.bfloat16)
    grad_attn_weight = jnp.dot(mixed_low.T, grad_middle_low, preferred_element_type=jnp.float32)
    grad_mixed = jnp.dot(
        grad_middle_low, attention_matrix.T, preferred_element_type=jnp.float32
    ).astype(jnp.bfloat16)
    grad_rows_out = (
        grad_mixed.reshape(tokens, KV_HEADS, group, HEAD_DIM)
        .transpose(1, 2, 0, 3)
        .reshape(KV_HEADS, row_count, HEAD_DIM)
    )
    delta = jnp.sum(grad_rows_out.astype(jnp.float32) * mixed_rows, axis=-1)

    def score_grads(key_part, first_key):
        masked, allowed, keys_here, values_here = block_scores(key_part, first_key)
        probs = probs_of(masked, allowed, largest, totals)
        grad_probs = jnp.einsum(
            "hrd,nhd->hrn", grad_rows_out, values_here, preferred_element_type=jnp.float32
        )
        grad_scores = (probs * (grad_probs - delta[..., None])).astype(jnp.bfloat16)
        return (grad_scores, probs.astype(jnp.bfloat16), keys_here)

    def key_terms(grad_scores, probs_low, key_count):
        grad_keys = (
            jnp.einsum("hrn,hrd->nhd", grad_scores, query_rows, preferred_element_type=jnp.float32)
            * scale
        )
        grad_values = jnp.einsum(
            "hrn,hrd->nhd", probs_low, grad_rows_out, preferred_element_type=jnp.float32
        )
        return jnp.concatenate(
            [grad_keys.reshape(key_count, kv_width), grad_values.reshape(key_count, kv_width)],
            axis=1,
        )

    start_query = jnp.zeros((KV_HEADS, row_count, HEAD_DIM), jnp.float32)

    def back_step(running, key_part, first_key):
        grad_query_rows, grad_keyvals = running
        grad_scores, probs_low, keys_here = score_grads(key_part, first_key)
        grad_query_rows = (
            grad_query_rows
            + jnp.einsum("hrn,nhd->hrd", grad_scores, keys_here, preferred_element_type=jnp.float32)
            * scale
        )
        fresh = key_terms(grad_scores, probs_low, key_part.shape[0])
        return (grad_query_rows, lax.dynamic_update_slice_in_dim(grad_keyvals, fresh, first_key, 0))

    start_back = (start_query, jnp.zeros((length, 2 * kv_width), jnp.float32))
    grad_query_rows, grad_keyvals = over_keys(
        lax.all_gather(keyval_send, "ctx", axis=0, tiled=True), start_back, back_step
    )
    grad_keyval_mine = lax.psum_scatter(grad_keyvals, "ctx", scatter_dimension=0, tiled=True)
    grad_query = grad_query_rows.reshape(KV_HEADS, group, tokens, HEAD_DIM).transpose(2, 0, 1, 3)
    grad_query_pre = (
        rotate(grad_query.reshape(tokens, HEADS, HEAD_DIM), -angles)
        .reshape(tokens, HEADS * HEAD_DIM)
        .astype(jnp.bfloat16)
    )
    grad_key_pre = rotate(
        grad_keyval_mine[:, :kv_width].reshape(tokens, KV_HEADS, HEAD_DIM), -angles
    ).reshape(tokens, kv_width)
    grad_keyval_pre = jnp.concatenate(
        [grad_key_pre, grad_keyval_mine[:, kv_width:]], axis=1
    ).astype(jnp.bfloat16)
    grad_hidden_one = jnp.dot(
        grad_query_pre, query_matrix.T, preferred_element_type=jnp.float32
    ) + jnp.dot(grad_keyval_pre, keyvalue_matrix.T, preferred_element_type=jnp.float32)
    grad_query_weight = jnp.dot(
        hidden_first_norm.T, grad_query_pre, preferred_element_type=jnp.float32
    )
    grad_keyval_weight = jnp.dot(
        hidden_first_norm.T, grad_keyval_pre, preferred_element_type=jnp.float32
    )
    grad_residual_norm, grad_gain_one = norm_one_back(grad_hidden_one)
    grad_input = (grad_middle + grad_residual_norm).astype(jnp.bfloat16)
    shares = (
        lax.psum_scatter(
            grad_gain_one.astype(jnp.bfloat16), "wa", scatter_dimension=0, tiled=True
        ).astype(jnp.float32),
        lax.psum_scatter(
            grad_query_weight.astype(jnp.bfloat16), "wa", scatter_dimension=0, tiled=True
        ).astype(jnp.float32),
        lax.psum_scatter(
            grad_keyval_weight.astype(jnp.bfloat16), "wa", scatter_dimension=0, tiled=True
        ).astype(jnp.float32),
        lax.psum_scatter(
            grad_attn_weight.astype(jnp.bfloat16), "wa", scatter_dimension=0, tiled=True
        ).astype(jnp.float32),
        lax.psum_scatter(
            grad_gain_two.astype(jnp.bfloat16), "wa", scatter_dimension=0, tiled=True
        ).astype(jnp.float32),
        lax.psum_scatter(
            grad_router.astype(jnp.bfloat16), "wa", scatter_dimension=0, tiled=True
        ).astype(jnp.float32),
        lax.psum_scatter(
            grad_w_in.astype(jnp.bfloat16), "wa", scatter_dimension=3, tiled=True
        ).astype(jnp.float32),
        lax.psum_scatter(
            grad_w_out.astype(jnp.bfloat16), "wa", scatter_dimension=1, tiled=True
        ).astype(jnp.float32),
    )
    summed = lax.psum((shares[0], shares[1], shares[2], shares[3], shares[4], shares[5]), "ctx")
    return (
        output[None],
        grad_input[None],
        summed[0],
        summed[1],
        summed[2],
        summed[3],
        summed[4],
        summed[5],
        shares[6],
        shares[7],
    )


MESH = pl.DeviceIdType.MESH
VMEM_LIMIT = 60 * 1024 * 1024


def chip_place():
    count = lax.axis_size("ctx")
    me = lax.axis_index("ctx")
    return me // 4, lax.rem(me // 2, 2), lax.rem(me, 2), count // 4


def ctx_of(z, y, c):
    return (z * 2 + y) * 2 + c


def greet():
    z, y, c, depth = chip_place()
    barrier = pltpu.get_barrier_semaphore()

    def signal(device):
        pl.semaphore_signal(barrier, 1, device_id={"ctx": device}, device_id_type=MESH)

    signal(ctx_of(z, y, 1 - c))
    signal(ctx_of(z, 1 - y, c))
    pl.when(z > 0)(lambda: signal(ctx_of(z - 1, y, c)))
    pl.when(z < depth - 1)(lambda: signal(ctx_of(z + 1, y, c)))
    pl.semaphore_wait(barrier, 2 + (z > 0).astype(jnp.int32) + (z < depth - 1).astype(jnp.int32))


def gather_steps(out, z_sems, y_sems, c_sems):
    z, y, c, depth = chip_place()
    other_y, other_c = 1 - y, 1 - c
    me = ctx_of(z, y, c)

    def copy(slot, sems, at, target):
        return pltpu.make_async_remote_copy(
            src_ref=out.at[slot],
            dst_ref=out.at[slot],
            send_sem=sems.at[(0,) + at],
            recv_sem=sems.at[(1,) + at],
            device_id={"ctx": target},
            device_id_type=MESH,
        )

    up, down = ctx_of(jnp.minimum(z + 1, depth - 1), y, c), ctx_of(jnp.maximum(z - 1, 0), y, c)

    def send_up(of_z):
        return copy(ctx_of(of_z, y, c), z_sems, (0, of_z), up)

    def send_down(of_z):
        return copy(ctx_of(of_z, y, c), z_sems, (1, of_z), down)

    def send_y(of_z):
        return copy(ctx_of(of_z, y, c), y_sems, (of_z,), ctx_of(z, other_y, c))

    def take_y(of_z):
        return copy(ctx_of(of_z, other_y, c), y_sems, (of_z,), ctx_of(z, other_y, c))

    def send_c(of_z, of_y):
        return copy(ctx_of(of_z, of_y, c), c_sems, (of_z * 2 + of_y,), ctx_of(z, y, other_c))

    def take_c(of_z, of_y):
        return copy(ctx_of(of_z, of_y, other_c), c_sems, (of_z * 2 + of_y,), ctx_of(z, y, other_c))

    pl.when(z < depth - 1)(lambda: send_up(z).start())
    pl.when(z > 0)(lambda: send_down(z).start())
    send_y(z).start()
    send_c(z, y).start()
    for step in range(1, depth):

        def from_below(of_z=z - step):
            send_up(of_z).wait_recv()
            pl.when(z < depth - 1)(lambda: send_up(of_z).start())
            send_y(of_z).start()
            send_c(of_z, y).start()

        def from_above(of_z=z + step):
            send_down(of_z).wait_recv()
            pl.when(z > 0)(lambda: send_down(of_z).start())
            send_y(of_z).start()
            send_c(of_z, y).start()

        pl.when(z - step >= 0)(from_below)
        pl.when(z + step < depth)(from_above)

    def across(of_z):
        take_y(of_z).wait_recv()
        send_c(of_z, other_y).start()

    across(z)
    for step in range(1, depth):
        pl.when(z - step >= 0)(lambda: across(z - step))
        pl.when(z + step < depth)(lambda: across(z + step))
    for of_z in range(depth):
        pl.when((z < depth - 1) & (of_z <= z))(lambda: send_up(of_z).wait_send())
        pl.when((z > 0) & (of_z >= z))(lambda: send_down(of_z).wait_send())
        send_y(of_z).wait_send()
        for of_y in range(2):
            send_c(of_z, of_y).wait_send()
            take_c(of_z, of_y).wait_recv()
    return me


def gather_sems(depth):
    return [
        pltpu.SemaphoreType.DMA((2, 2, depth)),
        pltpu.SemaphoreType.DMA((2, depth)),
        pltpu.SemaphoreType.DMA((2, 2 * depth)),
    ]


def add_into(target, terms, rows):
    @pl.loop(0, rows // 16)
    def _(turn):
        at = pl.ds(pl.multiple_of(turn * 16, 16), 16)
        total = terms[0][at, :].astype(jnp.float32)
        for term in terms[1:]:
            total = total + term[at, :].astype(jnp.float32)
        target[at, :] = total.astype(target.dtype)


def scatter_steps(part, result, from_core, sums, from_y, from_z, c_sems, y_sems, z_sems):
    z, y, c, depth = chip_place()
    rows = part.shape[1]
    other_y, other_c = 1 - y, 1 - c

    def copy(source, target_ref, sems, at, target):
        return pltpu.make_async_remote_copy(
            src_ref=source,
            dst_ref=target_ref,
            send_sem=sems.at[(0,) + at],
            recv_sem=sems.at[(1,) + at],
            device_id={"ctx": target},
            device_id_type=MESH,
        )

    def core_copy(chip):
        return copy(
            part.at[chip * 2 + other_c], from_core.at[chip], c_sems, (chip,), ctx_of(z, y, other_c)
        )

    def y_copy(of_z):
        return copy(
            sums.at[of_z * 2 + other_y], from_y.at[of_z], y_sems, (of_z,), ctx_of(z, other_y, c)
        )

    def z_copy(way, of_z):
        target = jnp.minimum(z + 1, depth - 1) if way == 0 else jnp.maximum(z - 1, 0)
        return copy(
            sums.at[of_z * 2 + y],
            from_z.at[way, of_z],
            z_sems,
            (way, of_z),
            ctx_of(target, y, c),
        )

    def in_order(act):
        for step in range(depth - 1, 0, -1):
            pl.when(z + step < depth)(functools.partial(act, z + step))
            pl.when(z - step >= 0)(functools.partial(act, z - step))
        act(z)

    def send_cores(of_z):
        core_copy(of_z * 2 + other_y).start()
        core_copy(of_z * 2 + y).start()

    in_order(send_cores)

    def add_cores(of_z):
        for of_y in (other_y, y):
            chip = of_z * 2 + of_y
            core_copy(chip).wait_recv()
            add_into(sums.at[chip], (part.at[chip * 2 + c], from_core.at[chip]), rows)
            if of_y is other_y:
                y_copy(of_z).start()

    in_order(add_cores)

    def add_y(of_z):
        y_copy(of_z).wait_recv()
        own = sums.at[of_z * 2 + y]

        def upward():
            z_copy(0, of_z).wait_recv()
            add_into(own, (own, from_y.at[of_z], from_z.at[0, of_z]), rows)

        def downward():
            z_copy(1, of_z).wait_recv()
            add_into(own, (own, from_y.at[of_z], from_z.at[1, of_z]), rows)

        inner = ((of_z > z) & (z > 0)) | ((of_z < z) & (z < depth - 1))
        pl.when((of_z > z) & (z > 0))(upward)
        pl.when((of_z < z) & (z < depth - 1))(downward)
        pl.when(jnp.logical_not(inner))(lambda: add_into(own, (own, from_y.at[of_z]), rows))
        pl.when(of_z > z)(lambda: z_copy(0, of_z).start())
        pl.when(of_z < z)(lambda: z_copy(1, of_z).start())

    in_order(add_y)
    own = sums.at[z * 2 + y]
    pl.when(z > 0)(lambda: z_copy(0, z).wait_recv())
    pl.when(z < depth - 1)(lambda: z_copy(1, z).wait_recv())

    @pl.when((z > 0) & (z < depth - 1))
    def _():
        add_into(result, (own, from_z.at[0, z], from_z.at[1, z]), rows)

    pl.when(z == 0)(lambda: add_into(result, (own, from_z.at[1, z]), rows))
    pl.when(z == depth - 1)(lambda: add_into(result, (own, from_z.at[0, z]), rows))
    for of_z in range(depth):
        y_copy(of_z).wait_send()
        core_copy(of_z * 2).wait_send()
        core_copy(of_z * 2 + 1).wait_send()
        pl.when(of_z > z)(lambda: z_copy(0, of_z).wait_send())
        pl.when(of_z < z)(lambda: z_copy(1, of_z).wait_send())


def scatter_scratch(depth, rows, columns):
    return [
        pltpu.VMEM((2 * depth, rows, columns), jnp.bfloat16),
        pltpu.VMEM((2 * depth, rows, columns), jnp.bfloat16),
        pltpu.VMEM((depth, rows, columns), jnp.bfloat16),
        pltpu.VMEM((2, depth, rows, columns), jnp.bfloat16),
        pltpu.SemaphoreType.DMA((2, 2 * depth)),
        pltpu.SemaphoreType.DMA((2, depth)),
        pltpu.SemaphoreType.DMA((2, 2, depth)),
    ]


def in_vmem(kernel, out, scratch, number, name, *operands):
    return pl.pallas_call(
        kernel,
        out_shape=out,
        in_specs=[pl.BlockSpec(memory_space=pltpu.VMEM)] * len(operands),
        out_specs=jax.tree.map(lambda _: pl.BlockSpec(memory_space=pltpu.VMEM), out),
        scratch_shapes=scratch,
        compiler_params=pltpu.CompilerParams(
            collective_id=number,
            has_side_effects=number is not None,
            vmem_limit_bytes=VMEM_LIMIT,
        ),
        name=name,
    )(*operands)


def gather_ctx(block, number, name):
    count = lax.axis_size("ctx")

    def kernel(block_ref, out, *sems):
        out[lax.axis_index("ctx")] = block_ref[...]
        greet()
        gather_steps(out, *sems)

    out = jax.ShapeDtypeStruct((count,) + block.shape, block.dtype)
    return in_vmem(kernel, out, gather_sems(count // 4), number, name, block)


def scatter_ctx(parts, number, name):
    count, rows, columns = parts.shape

    def kernel(part, result, *scratch):
        greet()
        scatter_steps(part, result, *scratch)

    out = jax.ShapeDtypeStruct((rows, columns), jnp.float32)
    return in_vmem(kernel, out, scatter_scratch(count // 4, rows, columns), number, name, parts)


def sum_ctx(parts, number, name):
    count, rows, columns = parts.shape
    depth = count // 4

    def kernel(part, out, *scratch):
        greet()
        scatter_steps(part, out.at[lax.axis_index("ctx")], *scratch[:7])
        gather_steps(out, *scratch[7:])

    out = jax.ShapeDtypeStruct(parts.shape, jnp.bfloat16)
    scratch = scatter_scratch(depth, rows, columns) + gather_sems(depth)
    return in_vmem(kernel, out, scratch, number, name, parts)


def rows_by_rows(left, right):
    return lax.dot_general(
        left, right, (((1,), (1,)), ((), ())), preferred_element_type=jnp.float32
    )


def columns_by_columns(left, right):
    return lax.dot_general(
        left, right, (((0,), (0,)), ((), ())), preferred_element_type=jnp.float32
    )


def allowed_bias(doc_row, doc_column, tokens):
    keys = doc_row.shape[1]
    query_block = lax.axis_index("ctx") * tokens // BLOCK
    key_block = lax.broadcasted_iota(jnp.int32, (tokens, keys), 1) // BLOCK
    allowed = (doc_row == doc_column) & (key_block <= query_block)
    return jnp.where(allowed, 0.0, NEGATIVE)


def attend_kernel(query, keyval, doc_row, doc_column, mixed, level, stacked, bias):
    tokens = query.shape[0]
    bias[...] = allowed_bias(doc_row[...], doc_column[...], tokens)
    for head in range(HEADS):
        stacked[head * tokens : (head + 1) * tokens, :] = query[:, head * 128 : (head + 1) * 128]

    @pl.loop(0, HEADS // 2)
    def _(pair):
        rows = pl.ds(pl.multiple_of(pair * 2 * tokens, 128), 2 * tokens)
        kind = pair // (HEADS // KV_HEADS // 2)
        keys = keyval[:, pl.ds(pl.multiple_of(kind * 128, 128), 128)]
        vals = keyval[:, pl.ds(pl.multiple_of(kind * 128 + 256, 128), 128)]
        scores = rows_by_rows(stacked[rows, :], keys) * HEAD_DIM**-0.5
        scores = (scores.reshape(2, tokens, -1) + bias[...][None]).reshape(scores.shape)
        top = jnp.max(scores, axis=-1, keepdims=True)
        weights = jnp.exp(scores - top)
        total = jnp.sum(weights, axis=-1, keepdims=True)
        probs = (weights / total).astype(jnp.bfloat16)
        mixture = jnp.dot(probs, vals, preferred_element_type=jnp.float32)
        for half in range(2):
            columns = pl.ds(pl.multiple_of((pair * 2 + half) * 128, 128), 128)
            mixed[:, columns] = mixture[half * tokens : (half + 1) * tokens]
        level[rows, :] = top + jnp.log(total)


def attend(query, keyval, doc_row, doc_column):
    tokens, keys = query.shape[0], keyval.shape[0]
    out = (
        jax.ShapeDtypeStruct(query.shape, jnp.float32),
        jax.ShapeDtypeStruct((HEADS * tokens, 1), jnp.float32),
    )
    scratch = [
        pltpu.VMEM((HEADS * tokens, HEAD_DIM), jnp.bfloat16),
        pltpu.VMEM((tokens, keys), jnp.float32),
    ]
    return in_vmem(
        attend_kernel, out, scratch, None, "attend", query, keyval, doc_row, doc_column
    )


def attend_back_kernel(
    query, keyval, doc_row, doc_column, level, mixed, grad_mixed,
    grad_query, grad_keyval, stacked, grads, bias, delta, total,
):
    tokens = query.shape[0]
    bias[...] = allowed_bias(doc_row[...], doc_column[...], tokens)
    total[...] = jnp.zeros_like(total)
    for head in range(HEADS):
        rows, columns = slice(head * tokens, (head + 1) * tokens), slice(head * 128, head * 128 + 128)
        stacked[rows, :] = query[:, columns]
        grads[rows, :] = grad_mixed[:, columns]
        delta[rows, :] = jnp.sum(
            grad_mixed[:, columns].astype(jnp.float32) * mixed[:, columns], axis=-1, keepdims=True
        )

    @pl.loop(0, HEADS // 2)
    def _(pair):
        rows = pl.ds(pl.multiple_of(pair * 2 * tokens, 128), 2 * tokens)
        kind = pair // (HEADS // KV_HEADS // 2)
        key_columns = pl.ds(pl.multiple_of(kind * 128, 128), 128)
        val_columns = pl.ds(pl.multiple_of(kind * 128 + 256, 128), 128)
        keys, vals = keyval[:, key_columns], keyval[:, val_columns]
        own, grad = stacked[rows, :], grads[rows, :]
        scores = rows_by_rows(own, keys) * HEAD_DIM**-0.5
        scores = (scores.reshape(2, tokens, -1) + bias[...][None]).reshape(scores.shape)
        probs = jnp.exp(scores - level[rows, :])
        grad_probs = rows_by_rows(grad, vals)
        grad_scores = (probs * (grad_probs - delta[rows, :])).astype(jnp.bfloat16)
        own_grad = jnp.dot(grad_scores, keys, preferred_element_type=jnp.float32)
        for half in range(2):
            columns = pl.ds(pl.multiple_of((pair * 2 + half) * 128, 128), 128)
            grad_query[:, columns] = own_grad[half * tokens : (half + 1) * tokens] * HEAD_DIM**-0.5
        total[:, key_columns] += columns_by_columns(grad_scores, own) * HEAD_DIM**-0.5
        total[:, val_columns] += columns_by_columns(probs.astype(jnp.bfloat16), grad)

    grad_keyval[...] = total[...].astype(jnp.bfloat16)


def attend_back(query, keyval, doc_row, doc_column, level, mixed, grad_mixed):
    tokens, keys = query.shape[0], keyval.shape[0]
    out = (
        jax.ShapeDtypeStruct(query.shape, jnp.float32),
        jax.ShapeDtypeStruct(keyval.shape, jnp.bfloat16),
    )
    scratch = [
        pltpu.VMEM((HEADS * tokens, HEAD_DIM), jnp.bfloat16),
        pltpu.VMEM((HEADS * tokens, HEAD_DIM), jnp.bfloat16),
        pltpu.VMEM((tokens, keys), jnp.float32),
        pltpu.VMEM((HEADS * tokens, 1), jnp.float32),
        pltpu.VMEM(keyval.shape, jnp.float32),
    ]
    return in_vmem(
        attend_back_kernel, out, scratch, None, "attend_back",
        query, keyval, doc_row, doc_column, level, mixed, grad_mixed,
    )


def rms_back(values, gain_vec, grad):
    scale = lax.rsqrt(jnp.mean(values * values, axis=-1, keepdims=True) + EPSILON)
    through = jnp.mean(gain_vec * grad * values, axis=-1, keepdims=True)
    back = scale * gain_vec * grad - values * scale**3 * through
    return back, jnp.sum(grad * values * scale, axis=0)


def swap_wa(values):
    return jax.tree.map(lambda v: lax.ppermute(v, "wa", ((0, 1), (1, 0))), values)


def gathered_body(
    layer_input, seq_ids, routes, gain_attn, w_query, w_keyval, w_out_attn, gain_ffn, router,
    w_in, w_out, d_out,
):
    count, me, side = lax.axis_size("ctx"), lax.axis_index("ctx"), lax.axis_index("wa")
    tokens = layer_input.shape[1]
    length = tokens * count
    experts = router.shape[1]
    kv_width = KV_HEADS * HEAD_DIM
    half = D // 2

    def gathered(values, axis):
        return lax.all_gather(values, "wa", axis=axis, tiled=True)

    def other_half(values):
        return lax.dynamic_slice_in_dim(values, (1 - side) * half, half, 1)

    def own_half(values):
        return lax.dynamic_slice_in_dim(values, side * half, half, 1)

    d_out_all = gather_ctx(d_out[0], 0, "gather_d_out").reshape(length, D)
    query_matrix, keyval_matrix = gathered(w_query, 0), gathered(w_keyval, 0)
    attention_matrix = gathered(w_out_attn, 0)
    gain_one = gathered(gain_attn, 0).astype(jnp.float32)
    gain_two = gathered(gain_ffn, 0).astype(jnp.float32)
    router_full = gathered(router, 0)
    in_half, out_half = gathered(w_in, 3)[0], gathered(w_out, 1)[0]
    in_matrix = in_half.transpose(1, 0, 2).reshape(D, -1)

    residual = layer_input[0].astype(jnp.float32)
    hidden_one = rms_scale(residual, gain_one).astype(jnp.bfloat16)
    hidden_one_there = swap_wa(other_half(hidden_one))
    positions = me * tokens + jnp.arange(tokens, dtype=jnp.int32)
    angles = angle_table(positions)
    query_pre = jnp.dot(hidden_one, query_matrix, preferred_element_type=jnp.float32)
    keyval_pre = jnp.dot(hidden_one, keyval_matrix, preferred_element_type=jnp.float32)
    query = rotate(query_pre.reshape(tokens, HEADS, HEAD_DIM), angles).astype(jnp.bfloat16)
    query = query.reshape(tokens, D)
    keys = rotate(keyval_pre[:, :kv_width].reshape(tokens, KV_HEADS, HEAD_DIM), angles)
    keyval = jnp.concatenate([keys.reshape(tokens, kv_width), keyval_pre[:, kv_width:]], axis=1)
    keyval_all = gather_ctx(keyval.astype(jnp.bfloat16), 1, "gather_kv").reshape(length, -1)
    doc_column = lax.dynamic_slice_in_dim(seq_ids[0], me * tokens, tokens, 0)[:, None]
    mixed, level = attend(query, keyval_all, seq_ids, doc_column)
    mixed_low = mixed.astype(jnp.bfloat16)
    mixed_there = swap_wa(other_half(mixed_low))
    middle = residual + jnp.dot(mixed_low, attention_matrix, preferred_element_type=jnp.float32)

    hidden_two = rms_scale(middle, gain_two).astype(jnp.bfloat16)
    logits = jnp.dot(hidden_two, router_full, preferred_element_type=jnp.float32)
    numbers = jnp.arange(experts, dtype=jnp.int32)
    chosen = jnp.any(routes[0][:, :, None] == numbers[None, None, :], axis=1)
    masked = jnp.where(chosen, logits, NEGATIVE)
    weights = jnp.exp(masked - jnp.max(masked, axis=1, keepdims=True))
    gates = weights / jnp.sum(weights, axis=1, keepdims=True)
    gates_high = gates.astype(jnp.bfloat16)
    gates_low = (gates - gates_high.astype(jnp.float32)).astype(jnp.bfloat16)
    spare = jnp.zeros((tokens, 128 - 2 * experts), jnp.bfloat16)
    send = jnp.concatenate([hidden_two, gates_high, gates_low, spare], axis=1)
    hidden_all = gather_ctx(send, 2, "gather_hidden").reshape(length, -1)

    rows = hidden_all[:, :D]
    expert = me // 2
    lane = jnp.arange(128, dtype=jnp.int32)[None, :]
    gate = jnp.sum(
        jnp.where(
            (lane == expert) | (lane == expert + experts), hidden_all[:, D:].astype(jnp.float32), 0.0
        ),
        axis=1,
        keepdims=True,
    )
    both = jnp.dot(rows, in_matrix, preferred_element_type=jnp.float32)
    width = both.shape[1] // 2

    def gate_unit(first, second):
        return jax.nn.gelu(first, approximate=True) * second

    hidden, unit_back = jax.vjp(gate_unit, both[:, :width], both[:, width:])
    hidden_gated = (hidden * gate).astype(jnp.bfloat16)
    result = jnp.dot(hidden_gated, out_half, preferred_element_type=jnp.float32)
    grad_hidden = rows_by_rows(d_out_all, out_half)
    grad_gate = jnp.sum(grad_hidden * hidden, axis=1, keepdims=True)
    grad_both = jnp.concatenate(unit_back(grad_hidden * gate), axis=1).astype(jnp.bfloat16)
    grad_rows = rows_by_rows(grad_both, in_matrix)
    gate_columns = jnp.where(lane == expert, grad_gate, 0.0)
    grad_send = jnp.concatenate([grad_rows, gate_columns], axis=1).astype(jnp.bfloat16)
    returned = scatter_ctx(grad_send.reshape(count, tokens, -1), 3, "scatter_grad_rows")
    result_sum = scatter_ctx(
        result.astype(jnp.bfloat16).reshape(count, tokens, D), 4, "scatter_result"
    )
    output = (middle + result_sum).astype(jnp.bfloat16)
    grad_in_matrix = columns_by_columns(rows, grad_both).reshape(D, 2, width).transpose(1, 0, 2)
    grad_out_half = columns_by_columns(hidden_gated, d_out_all)
    grad_w_in = lax.psum_scatter(
        grad_in_matrix[None].astype(jnp.bfloat16), "wa", scatter_dimension=3, tiled=True
    ).astype(jnp.float32)
    grad_w_out = lax.psum_scatter(
        grad_out_half[None].astype(jnp.bfloat16), "wa", scatter_dimension=1, tiled=True
    ).astype(jnp.float32)

    grad_out = d_out[0].astype(jnp.float32)
    grad_gates = returned[:, D : D + experts]
    grad_logits = gates * (grad_gates - jnp.sum(gates * grad_gates, axis=1, keepdims=True))
    grad_logits_low = grad_logits.astype(jnp.bfloat16)
    grad_hidden_two = returned[:, :D] + rows_by_rows(grad_logits_low, router_full)
    grad_router = columns_by_columns(hidden_two, grad_logits_low)
    back_two, grad_gain_two = rms_back(middle, gain_two, grad_hidden_two)
    grad_middle = grad_out + back_two
    grad_middle_low = grad_middle.astype(jnp.bfloat16)
    grad_middle_there = swap_wa(grad_middle_low)
    grad_mixed = rows_by_rows(grad_middle_low, attention_matrix).astype(jnp.bfloat16)
    grad_query, grad_keyval = attend_back(
        query, keyval_all, seq_ids, doc_column, level, mixed, grad_mixed
    )
    grad_query_pre = rotate(grad_query.reshape(tokens, HEADS, HEAD_DIM), -angles)
    grad_query_pre = grad_query_pre.reshape(tokens, D).astype(jnp.bfloat16)
    grad_query_there = swap_wa(grad_query_pre)
    grad_keyval_own = scatter_ctx(grad_keyval.reshape(count, tokens, -1), 5, "scatter_grad_kv")
    grad_keys = rotate(
        grad_keyval_own[:, :kv_width].reshape(tokens, KV_HEADS, HEAD_DIM), -angles
    ).reshape(tokens, kv_width)
    grad_keyval_pre = jnp.concatenate([grad_keys, grad_keyval_own[:, kv_width:]], axis=1)
    grad_keyval_pre = grad_keyval_pre.astype(jnp.bfloat16)
    grad_keyval_there = swap_wa(grad_keyval_pre)
    grad_hidden_one = rows_by_rows(grad_query_pre, query_matrix) + rows_by_rows(
        grad_keyval_pre, keyval_matrix
    )
    back_one, grad_gain_one = rms_back(residual, gain_one, grad_hidden_one)
    grad_input = (grad_middle + back_one).astype(jnp.bfloat16)

    small = jnp.concatenate(
        [grad_router, grad_gain_two[:, None], grad_gain_one[:, None]], axis=1
    )
    small_half = lax.dynamic_slice_in_dim(small, side * half, half, 0)
    small_there = swap_wa(lax.dynamic_slice_in_dim(small, (1 - side) * half, half, 0))
    small_sum = small_half + small_there

    def pair_sum(left, left_there, right, right_there):
        return columns_by_columns(
            jnp.concatenate([own_half(left), left_there]), jnp.concatenate([right, right_there])
        ).astype(jnp.bfloat16)

    shares = jnp.concatenate(
        [
            pair_sum(hidden_one, hidden_one_there, grad_query_pre, grad_query_there),
            pair_sum(hidden_one, hidden_one_there, grad_keyval_pre, grad_keyval_there),
            pair_sum(mixed_low, mixed_there, grad_middle_low, grad_middle_there),
            jnp.pad(small_sum, ((0, 0), (0, 128 - experts - 2))).astype(jnp.bfloat16),
        ],
        axis=1,
    )
    summed = sum_ctx(shares.reshape(count, half // count, -1), 6, "sum_shares")
    summed = summed.reshape(half, -1).astype(jnp.float32)
    first, second, third = D, D + 2 * kv_width, 2 * D + 2 * kv_width
    return (
        output[None],
        grad_input[None],
        summed[:, third + experts + 1],
        summed[:, :first],
        summed[:, first:second],
        summed[:, second:third],
        summed[:, third + experts],
        summed[:, third : third + experts],
        grad_w_in,
        grad_w_out,
    )


def solution(mesh):
    in_specs = (
        P("wa", "ctx", None),
        P("wa", None),
        P("wa", "ctx", None),
        P("wa"),
        P("wa", None),
        P("wa", None),
        P("wa", None),
        P("wa"),
        P("wa", None),
        P("ctx", None, None, "wa"),
        P("ctx", "wa", None),
        P("wa", "ctx", None),
    )
    out_specs = (
        P("wa", "ctx", None),
        P("wa", "ctx", None),
        P("wa"),
        P("wa", None),
        P("wa", None),
        P("wa", None),
        P("wa"),
        P("wa", None),
        P("ctx", None, None, "wa"),
        P("ctx", "wa", None),
    )
    depth = mesh.shape["ctx"]
    body = gathered_body if depth == 16 else routed_body
    return jax.shard_map(body, mesh=mesh, in_specs=in_specs, out_specs=out_specs, check_vma=False)
```

```python
import functools
import math

import jax
import jax.numpy as jnp
from jax import lax
from jax.experimental import pallas as pl
from jax.experimental.pallas import tpu as pltpu
from jax.sharding import PartitionSpec as P

D = 1536
HEADS = 12
KV_HEADS = 2
HEAD_DIM = 128
TOP = 4
BLOCK = 256


EPSILON = 1e-06
THETA = 1000000.0
NEGATIVE = -1e30


def rms_scale(values, gain_vec):
    return (
        values * lax.rsqrt(jnp.mean(values * values, axis=-1, keepdims=True) + EPSILON) * gain_vec
    )


def rotate(values, angles):
    half_dim = values.shape[-1] // 2
    cosine = jnp.cos(angles)
    sine_part = jnp.sin(angles)
    first_half = values[..., :half_dim]
    second = values[..., half_dim:]
    return jnp.concatenate(
        [first_half * cosine - second * sine_part, second * cosine + first_half * sine_part],
        axis=-1,
    )


def angle_table(positions):
    half_dim = HEAD_DIM // 2
    frequency = THETA ** (-2.0 * jnp.arange(half_dim, dtype=jnp.float32) / HEAD_DIM)
    return (positions.astype(jnp.float32)[:, None] * frequency[None, :])[:, None, :]


def gated(stacked):
    return jax.nn.gelu(stacked[..., 0, :], approximate=True) * stacked[..., 1, :]


def over_keys(key_rows, running, advance):
    key_count = key_rows.shape[0]
    key_width = math.gcd(key_count, 512)

    def one_turn(state_now, block_index):
        key_offset = block_index * key_width
        key_part = lax.dynamic_slice_in_dim(key_rows, key_offset, key_width, 0)
        return (advance(state_now, key_part, key_offset), None)

    running, unused = lax.scan(
        one_turn, running, jnp.arange(key_count // key_width, dtype=jnp.int32)
    )
    return running


def routed_body(
    layer_input,
    seq_ids,
    routes,
    gain_attn,
    w_query,
    w_keyval,
    w_out_attn,
    gain_ffn,
    router,
    w_in,
    w_out,
    d_out,
):
    ctx_count = lax.axis_size("ctx")
    ctx_index = lax.axis_index("ctx")
    tokens = layer_input.shape[1]
    length = tokens * ctx_count
    experts_all = ctx_count // 2
    capacity = 2 * tokens * TOP // experts_all
    group = HEADS // KV_HEADS
    kv_width = KV_HEADS * HEAD_DIM
    row_count = group * tokens
    scale = HEAD_DIM ** (-0.5)
    gain_one, query_matrix, keyvalue_matrix, attention_matrix = (
        lax.all_gather(gain_attn, "wa", axis=0, tiled=True),
        lax.all_gather(w_query, "wa", axis=0, tiled=True),
        lax.all_gather(w_keyval, "wa", axis=0, tiled=True),
        lax.all_gather(w_out_attn, "wa", axis=0, tiled=True),
    )
    residual = layer_input[0].astype(jnp.float32)
    normed_one, norm_one_back = jax.vjp(rms_scale, residual, gain_one.astype(jnp.float32))
    hidden_first_norm = normed_one.astype(jnp.bfloat16)
    positions = ctx_index * tokens + jnp.arange(tokens, dtype=jnp.int32)
    angles = angle_table(positions)
    query_projected = jnp.dot(
        hidden_first_norm, query_matrix, preferred_element_type=jnp.float32
    ).reshape(tokens, HEADS, HEAD_DIM)
    keyvalue_projected = jnp.dot(
        hidden_first_norm, keyvalue_matrix, preferred_element_type=jnp.float32
    )
    key_pre = keyvalue_projected[:, :kv_width].reshape(tokens, KV_HEADS, HEAD_DIM)
    query_low = rotate(query_projected, angles).astype(jnp.bfloat16)
    key_low = rotate(key_pre, angles).astype(jnp.bfloat16)
    value_low = keyvalue_projected[:, kv_width:].astype(jnp.bfloat16)
    keyval_send = jnp.concatenate([key_low.reshape(tokens, kv_width), value_low], axis=1)
    query_rows = (
        query_low.reshape(tokens, KV_HEADS, group, HEAD_DIM)
        .transpose(1, 2, 0, 3)
        .reshape(KV_HEADS, row_count, HEAD_DIM)
    )
    doc_row = seq_ids[0]
    query_docs = lax.dynamic_slice_in_dim(doc_row, ctx_index * tokens, tokens, 0)
    query_blocks = positions // BLOCK

    def block_scores(key_part, first_key):
        key_count = key_part.shape[0]
        split_part = key_part.reshape(key_count, 2, KV_HEADS, HEAD_DIM)
        keys_here = split_part[:, 0]
        values_here = split_part[:, 1]
        scores = (
            jnp.einsum("hrd,nhd->hrn", query_rows, keys_here, preferred_element_type=jnp.float32)
            * scale
        )
        key_docs = lax.dynamic_slice_in_dim(doc_row, first_key, key_count, 0)
        key_blocks = (first_key + jnp.arange(key_count, dtype=jnp.int32)) // BLOCK
        allowed = (query_docs[:, None] == key_docs[None, :]) & (
            key_blocks[None, :] <= query_blocks[:, None]
        )
        allowed = jnp.broadcast_to(allowed[None], (group, tokens, key_count)).reshape(
            1, row_count, key_count
        )
        return (jnp.where(allowed, scores, NEGATIVE), allowed, keys_here, values_here)

    def probs_of(masked, allowed, largest, totals):
        return jnp.where(allowed, jnp.exp(masked - largest[..., None]) / totals[..., None], 0.0)

    def stats_step(running, key_part, first_key):
        largest, totals = running
        masked, allowed, keys_here, values_here = block_scores(key_part, first_key)
        new_largest = jnp.maximum(largest, jnp.max(masked, axis=-1))
        weights = jnp.where(allowed, jnp.exp(masked - new_largest[..., None]), 0.0)
        return (new_largest, totals * jnp.exp(largest - new_largest) + jnp.sum(weights, axis=-1))

    start_stats = (
        jnp.full((KV_HEADS, row_count), NEGATIVE, jnp.float32),
        jnp.zeros((KV_HEADS, row_count), jnp.float32),
    )
    largest, totals = over_keys(
        lax.all_gather(keyval_send, "ctx", axis=0, tiled=True), start_stats, stats_step
    )

    def values_step(running, key_part, first_key):
        masked, allowed, keys_here, values_here = block_scores(key_part, first_key)
        probs_low = probs_of(masked, allowed, largest, totals).astype(jnp.bfloat16)
        return running + jnp.einsum(
            "hrn,nhd->hrd", probs_low, values_here, preferred_element_type=jnp.float32
        )

    start_values = jnp.zeros((KV_HEADS, row_count, HEAD_DIM), jnp.float32)
    mixed_rows = over_keys(
        lax.all_gather(keyval_send, "ctx", axis=0, tiled=True), start_values, values_step
    )
    mixed_low = (
        mixed_rows.reshape(KV_HEADS, group, tokens, HEAD_DIM)
        .transpose(2, 0, 1, 3)
        .reshape(tokens, HEADS * HEAD_DIM)
        .astype(jnp.bfloat16)
    )
    middle_activation = residual + jnp.dot(
        mixed_low, attention_matrix, preferred_element_type=jnp.float32
    )
    gain_two, router_full, w_in_full, w_out_full = (
        lax.all_gather(gain_ffn, "wa", axis=0, tiled=True),
        lax.all_gather(router, "wa", axis=0, tiled=True),
        lax.all_gather(w_in, "wa", axis=3, tiled=True),
        lax.all_gather(w_out, "wa", axis=1, tiled=True),
    )
    in_half = w_in_full[0]
    out_half = w_out_full[0]
    normed_two, norm_two_back = jax.vjp(rms_scale, middle_activation, gain_two.astype(jnp.float32))
    hidden_second_norm = normed_two.astype(jnp.bfloat16)
    router_logits = jnp.dot(hidden_second_norm, router_full, preferred_element_type=jnp.float32)
    route_ids = routes[0]

    def gate_values(logit_rows):
        return jax.nn.softmax(jnp.take_along_axis(logit_rows, route_ids, axis=-1), axis=-1)

    gates, gate_back = jax.vjp(gate_values, router_logits)
    flat_ids = route_ids.reshape(tokens * TOP)
    expert_hits = (flat_ids[:, None] == jnp.arange(experts_all, dtype=jnp.int32)[None, :]).astype(
        jnp.int32
    )
    ranks = jnp.sum(expert_hits * (jnp.cumsum(expert_hits, axis=0) - expert_hits), axis=1)
    slot_first = 2 * flat_ids * capacity + ranks
    slot_second = slot_first + capacity
    slot_total = ctx_count * capacity
    slot_numbers = jnp.arange(slot_total, dtype=jnp.int32)[:, None]
    placed = (
        (slot_first[None, :] == slot_numbers) | (slot_second[None, :] == slot_numbers)
    ).astype(jnp.bfloat16)
    dispatch = jnp.sum(placed.reshape(slot_total, tokens, TOP), axis=2)
    send_rows = (
        jnp.dot(dispatch, hidden_second_norm, preferred_element_type=jnp.float32)
        .astype(jnp.bfloat16)
        .reshape(ctx_count, capacity, D)
    )
    arrived = lax.all_to_all(send_rows, "ctx", split_axis=0, concat_axis=0, tiled=True)
    stacked = jnp.einsum("ncd,gdf->ncgf", arrived, in_half, preferred_element_type=jnp.float32)
    hidden_low = gated(stacked).astype(jnp.bfloat16)
    result = jnp.einsum(
        "ncf,fd->ncd", hidden_low, out_half, preferred_element_type=jnp.float32
    ).astype(jnp.bfloat16)
    returned_rows = lax.all_to_all(result, "ctx", split_axis=0, concat_axis=0, tiled=True)
    returned_flat = returned_rows.reshape(slot_total, D)
    pair_rows = (
        returned_flat[slot_first].astype(jnp.float32)
        + returned_flat[slot_second].astype(jnp.float32)
    ).reshape(tokens, TOP, D)
    output = (middle_activation + jnp.sum(gates[:, :, None] * pair_rows, axis=1)).astype(
        jnp.bfloat16
    )
    grad_out = d_out[0].astype(jnp.float32)
    grad_gates = jnp.sum(pair_rows * grad_out[:, None, :], axis=-1)
    (grad_logits,) = gate_back(grad_gates)
    grad_logits_low = grad_logits.astype(jnp.bfloat16)
    gate_slots = jnp.dot(
        placed.astype(jnp.float32), gates.reshape(tokens * TOP), precision=lax.Precision.HIGHEST
    )
    routed_grad = jnp.dot(dispatch, d_out[0], preferred_element_type=jnp.float32)
    grad_send_rows = (
        (gate_slots[:, None] * routed_grad).astype(jnp.bfloat16).reshape(ctx_count, capacity, D)
    )
    grad_arrived = lax.all_to_all(grad_send_rows, "ctx", split_axis=0, concat_axis=0, tiled=True)
    grad_hidden = jnp.einsum(
        "ncd,fd->ncf", grad_arrived, out_half, preferred_element_type=jnp.float32
    )
    hidden_again, gated_back = jax.vjp(gated, stacked)
    (grad_stacked,) = gated_back(grad_hidden)
    grad_stacked_low = grad_stacked.astype(jnp.bfloat16)
    grad_rows = jnp.einsum(
        "ncgf,gdf->ncd", grad_stacked_low, in_half, preferred_element_type=jnp.float32
    ).astype(jnp.bfloat16)
    grad_returned = lax.all_to_all(grad_rows, "ctx", split_axis=0, concat_axis=0, tiled=True)
    grad_w_in = jnp.einsum(
        "ncd,ncgf->gdf", arrived, grad_stacked_low, preferred_element_type=jnp.float32
    )[None]
    grad_w_out = jnp.einsum(
        "ncf,ncd->fd",
        hidden_again.astype(jnp.bfloat16),
        grad_arrived,
        preferred_element_type=jnp.float32,
    )[None]
    grad_hidden_two = jnp.einsum(
        "st,sd->td",
        dispatch,
        grad_returned.reshape(slot_total, D),
        preferred_element_type=jnp.float32,
    )
    grad_hidden_two = grad_hidden_two + jnp.dot(
        grad_logits_low, router_full.T, preferred_element_type=jnp.float32
    )
    grad_router = jnp.dot(hidden_second_norm.T, grad_logits_low, preferred_element_type=jnp.float32)
    grad_middle_norm, grad_gain_two = norm_two_back(grad_hidden_two)
    grad_middle = grad_out + grad_middle_norm
    grad_middle_low = grad_middle.astype(jnp.bfloat16)
    grad_attn_weight = jnp.dot(mixed_low.T, grad_middle_low, preferred_element_type=jnp.float32)
    grad_mixed = jnp.dot(
        grad_middle_low, attention_matrix.T, preferred_element_type=jnp.float32
    ).astype(jnp.bfloat16)
    grad_rows_out = (
        grad_mixed.reshape(tokens, KV_HEADS, group, HEAD_DIM)
        .transpose(1, 2, 0, 3)
        .reshape(KV_HEADS, row_count, HEAD_DIM)
    )
    delta = jnp.sum(grad_rows_out.astype(jnp.float32) * mixed_rows, axis=-1)

    def score_grads(key_part, first_key):
        masked, allowed, keys_here, values_here = block_scores(key_part, first_key)
        probs = probs_of(masked, allowed, largest, totals)
        grad_probs = jnp.einsum(
            "hrd,nhd->hrn", grad_rows_out, values_here, preferred_element_type=jnp.float32
        )
        grad_scores = (probs * (grad_probs - delta[..., None])).astype(jnp.bfloat16)
        return (grad_scores, probs.astype(jnp.bfloat16), keys_here)

    def key_terms(grad_scores, probs_low, key_count):
        grad_keys = (
            jnp.einsum("hrn,hrd->nhd", grad_scores, query_rows, preferred_element_type=jnp.float32)
            * scale
        )
        grad_values = jnp.einsum(
            "hrn,hrd->nhd", probs_low, grad_rows_out, preferred_element_type=jnp.float32
        )
        return jnp.concatenate(
            [grad_keys.reshape(key_count, kv_width), grad_values.reshape(key_count, kv_width)],
            axis=1,
        )

    start_query = jnp.zeros((KV_HEADS, row_count, HEAD_DIM), jnp.float32)

    def back_step(running, key_part, first_key):
        grad_query_rows, grad_keyvals = running
        grad_scores, probs_low, keys_here = score_grads(key_part, first_key)
        grad_query_rows = (
            grad_query_rows
            + jnp.einsum("hrn,nhd->hrd", grad_scores, keys_here, preferred_element_type=jnp.float32)
            * scale
        )
        fresh = key_terms(grad_scores, probs_low, key_part.shape[0])
        return (grad_query_rows, lax.dynamic_update_slice_in_dim(grad_keyvals, fresh, first_key, 0))

    start_back = (start_query, jnp.zeros((length, 2 * kv_width), jnp.float32))
    grad_query_rows, grad_keyvals = over_keys(
        lax.all_gather(keyval_send, "ctx", axis=0, tiled=True), start_back, back_step
    )
    grad_keyval_mine = lax.psum_scatter(grad_keyvals, "ctx", scatter_dimension=0, tiled=True)
    grad_query = grad_query_rows.reshape(KV_HEADS, group, tokens, HEAD_DIM).transpose(2, 0, 1, 3)
    grad_query_pre = (
        rotate(grad_query.reshape(tokens, HEADS, HEAD_DIM), -angles)
        .reshape(tokens, HEADS * HEAD_DIM)
        .astype(jnp.bfloat16)
    )
    grad_key_pre = rotate(
        grad_keyval_mine[:, :kv_width].reshape(tokens, KV_HEADS, HEAD_DIM), -angles
    ).reshape(tokens, kv_width)
    grad_keyval_pre = jnp.concatenate(
        [grad_key_pre, grad_keyval_mine[:, kv_width:]], axis=1
    ).astype(jnp.bfloat16)
    grad_hidden_one = jnp.dot(
        grad_query_pre, query_matrix.T, preferred_element_type=jnp.float32
    ) + jnp.dot(grad_keyval_pre, keyvalue_matrix.T, preferred_element_type=jnp.float32)
    grad_query_weight = jnp.dot(
        hidden_first_norm.T, grad_query_pre, preferred_element_type=jnp.float32
    )
    grad_keyval_weight = jnp.dot(
        hidden_first_norm.T, grad_keyval_pre, preferred_element_type=jnp.float32
    )
    grad_residual_norm, grad_gain_one = norm_one_back(grad_hidden_one)
    grad_input = (grad_middle + grad_residual_norm).astype(jnp.bfloat16)
    shares = (
        lax.psum_scatter(
            grad_gain_one.astype(jnp.bfloat16), "wa", scatter_dimension=0, tiled=True
        ).astype(jnp.float32),
        lax.psum_scatter(
            grad_query_weight.astype(jnp.bfloat16), "wa", scatter_dimension=0, tiled=True
        ).astype(jnp.float32),
        lax.psum_scatter(
            grad_keyval_weight.astype(jnp.bfloat16), "wa", scatter_dimension=0, tiled=True
        ).astype(jnp.float32),
        lax.psum_scatter(
            grad_attn_weight.astype(jnp.bfloat16), "wa", scatter_dimension=0, tiled=True
        ).astype(jnp.float32),
        lax.psum_scatter(
            grad_gain_two.astype(jnp.bfloat16), "wa", scatter_dimension=0, tiled=True
        ).astype(jnp.float32),
        lax.psum_scatter(
            grad_router.astype(jnp.bfloat16), "wa", scatter_dimension=0, tiled=True
        ).astype(jnp.float32),
        lax.psum_scatter(
            grad_w_in.astype(jnp.bfloat16), "wa", scatter_dimension=3, tiled=True
        ).astype(jnp.float32),
        lax.psum_scatter(
            grad_w_out.astype(jnp.bfloat16), "wa", scatter_dimension=1, tiled=True
        ).astype(jnp.float32),
    )
    summed = lax.psum((shares[0], shares[1], shares[2], shares[3], shares[4], shares[5]), "ctx")
    return (
        output[None],
        grad_input[None],
        summed[0],
        summed[1],
        summed[2],
        summed[3],
        summed[4],
        summed[5],
        shares[6],
        shares[7],
    )

MESH = pl.DeviceIdType.MESH
VMEM_LIMIT = 60 * 1024 * 1024


def chip_place():
    count = lax.axis_size("ctx")
    me = lax.axis_index("ctx")
    return me // 4, lax.rem(me // 2, 2), lax.rem(me, 2), count // 4


def ctx_of(z, y, c):
    return (z * 2 + y) * 2 + c


def greet(across_x=False):
    z, y, c, depth = chip_place()
    barrier = pltpu.get_barrier_semaphore()

    def signal(device):
        pl.semaphore_signal(barrier, 1, device_id=device, device_id_type=MESH)

    signal({"ctx": ctx_of(z, y, 1 - c)})
    signal({"ctx": ctx_of(z, 1 - y, c)})
    if across_x:
        signal({"wa": 1 - lax.axis_index("wa")})
    pl.when(z > 0)(lambda: signal({"ctx": ctx_of(z - 1, y, c)}))
    pl.when(z < depth - 1)(lambda: signal({"ctx": ctx_of(z + 1, y, c)}))
    ends = (z > 0).astype(jnp.int32) + (z < depth - 1).astype(jnp.int32)
    pl.semaphore_wait(barrier, (3 if across_x else 2) + ends)


def remote(source, target_ref, sems, at, device):
    return pltpu.make_async_remote_copy(
        src_ref=source,
        dst_ref=target_ref,
        send_sem=sems.at[(0,) + at],
        recv_sem=sems.at[(1,) + at],
        device_id=device,
        device_id_type=MESH,
    )


def each(step, act):
    z, _, _, depth = chip_place()
    if step == 0:
        act(z)
    else:
        pl.when(z + step < depth)(lambda: act(z + step))
        pl.when(z - step >= 0)(lambda: act(z - step))


class Gather:
    def __init__(self, out, rows, sems):
        self.out, self.rows = out, rows
        self.z_sems, self.y_sems, self.c_sems = sems
        self.z, self.y, self.c, self.depth = chip_place()

    @staticmethod
    def sems(depth):
        return [
            pltpu.SemaphoreType.DMA((2, 2, depth)),
            pltpu.SemaphoreType.DMA((2, depth)),
            pltpu.SemaphoreType.DMA((2, 2 * depth)),
        ]

    def slot(self, z, y, c):
        return self.out.at[pl.ds(pl.multiple_of(ctx_of(z, y, c) * self.rows, 16), self.rows)]

    def own(self):
        return self.slot(self.z, self.y, self.c)

    def on_z(self, way, of_z, source=None):
        goal = jnp.minimum(self.z + 1, self.depth - 1) if way == 0 else jnp.maximum(self.z - 1, 0)
        block = self.slot(of_z, self.y, self.c)
        target = {"ctx": ctx_of(goal, self.y, self.c)}
        return remote(block if source is None else source, block, self.z_sems, (way, of_z), target)

    def on_y(self, of_z, mine=True, source=None):
        block = self.slot(of_z, self.y if mine else 1 - self.y, self.c)
        target = {"ctx": ctx_of(self.z, 1 - self.y, self.c)}
        return remote(block if source is None else source, block, self.y_sems, (of_z,), target)

    def on_core(self, of_z, of_y, mine=True, source=None):
        block = self.slot(of_z, of_y, self.c if mine else 1 - self.c)
        target = {"ctx": ctx_of(self.z, self.y, 1 - self.c)}
        at = (of_z * 2 + of_y,)
        return remote(block if source is None else source, block, self.c_sems, at, target)

    def start(self, source=None):
        z, depth = self.z, self.depth
        pl.when(z < depth - 1)(lambda: self.on_z(0, z, source).start())
        pl.when(z > 0)(lambda: self.on_z(1, z, source).start())
        self.on_y(z, source=source).start()
        self.on_core(z, self.y, source=source).start()

    def along_z(self, step):
        z, depth = self.z, self.depth

        def from_side(way, of_z, more):
            self.on_z(way, of_z).wait_recv()
            pl.when(more)(lambda: self.on_z(way, of_z).start())
            self.on_y(of_z).start()
            self.on_core(of_z, self.y).start()

        pl.when(z - step >= 0)(lambda: from_side(0, z - step, z < depth - 1))
        pl.when(z + step < depth)(lambda: from_side(1, z + step, z > 0))

    def along_y(self, step):
        def across(of_z):
            self.on_y(of_z, mine=False).wait_recv()
            self.on_core(of_z, 1 - self.y).start()

        each(step, across)

    def finish(self):
        z, depth = self.z, self.depth
        for of_z in range(depth):
            pl.when((z < depth - 1) & (of_z <= z))(lambda: self.on_z(0, of_z).wait_send())
            pl.when((z > 0) & (of_z >= z))(lambda: self.on_z(1, of_z).wait_send())
            self.on_y(of_z).wait_send()
            for of_y in range(2):
                self.on_core(of_z, of_y).wait_send()
                self.on_core(of_z, of_y, mine=False).wait_recv()

    def run(self, source=None):
        self.start(source)
        self.along_z(1)
        self.along_y(0)
        for step in range(1, self.depth):
            if step + 1 < self.depth:
                self.along_z(step + 1)
            self.along_y(step)
        self.finish()


def add_into(target, terms, rows):
    @pl.loop(0, rows // 16)
    def _(turn):
        at = pl.ds(pl.multiple_of(turn * 16, 16), 16)
        total = terms[0][at, :].astype(jnp.float32)
        for term in terms[1:]:
            total = total + term[at, :].astype(jnp.float32)
        target[at, :] = total.astype(target.dtype)


class Scatter:
    def __init__(self, part, scratch):
        self.part = part
        self.from_core, self.sums, self.from_y, self.from_z = scratch[:4]
        self.c_sems, self.y_sems, self.z_sems = scratch[4:]
        self.rows = self.sums.shape[1]
        self.z, self.y, self.c, self.depth = chip_place()

    @staticmethod
    def scratch(depth, rows, columns):
        return [
            pltpu.VMEM((2 * depth, rows, columns), jnp.bfloat16),
            pltpu.VMEM((2 * depth, rows, columns), jnp.bfloat16),
            pltpu.VMEM((depth, rows, columns), jnp.bfloat16),
            pltpu.VMEM((2, depth, rows, columns), jnp.bfloat16),
            pltpu.SemaphoreType.DMA((2, 2 * depth)),
            pltpu.SemaphoreType.DMA((2, depth)),
            pltpu.SemaphoreType.DMA((2, 2, depth)),
        ]

    def share(self, chip, c):
        return self.part.at[pl.ds(pl.multiple_of((chip * 2 + c) * self.rows, 16), self.rows)]

    def on_core(self, chip):
        target = {"ctx": ctx_of(self.z, self.y, 1 - self.c)}
        return remote(
            self.share(chip, 1 - self.c), self.from_core.at[chip], self.c_sems, (chip,), target
        )

    def on_y(self, of_z):
        target = {"ctx": ctx_of(self.z, 1 - self.y, self.c)}
        source = self.sums.at[of_z * 2 + 1 - self.y]
        return remote(source, self.from_y.at[of_z], self.y_sems, (of_z,), target)

    def on_z(self, way, of_z):
        goal = jnp.minimum(self.z + 1, self.depth - 1) if way == 0 else jnp.maximum(self.z - 1, 0)
        source = self.sums.at[of_z * 2 + self.y]
        target = {"ctx": ctx_of(goal, self.y, self.c)}
        return remote(source, self.from_z.at[way, of_z], self.z_sems, (way, of_z), target)

    def start(self):
        def send(of_z):
            self.on_core(of_z * 2 + 1 - self.y).start()
            self.on_core(of_z * 2 + self.y).start()

        for step in range(self.depth - 1, -1, -1):
            each(step, send)

    def add_cores(self, step):
        def add(of_z):
            for other in (True, False):
                chip = of_z * 2 + (1 - self.y if other else self.y)
                self.on_core(chip).wait_recv()
                terms = (self.share(chip, self.c), self.from_core.at[chip])
                add_into(self.sums.at[chip], terms, self.rows)
                if other:
                    self.on_y(of_z).start()

        each(step, add)

    def add_y(self, step):
        z, depth = self.z, self.depth

        def add(of_z):
            self.on_y(of_z).wait_recv()
            own = self.sums.at[of_z * 2 + self.y]

            def passing(way):
                self.on_z(way, of_z).wait_recv()
                terms = (own, self.from_y.at[of_z], self.from_z.at[way, of_z])
                add_into(own, terms, self.rows)

            upward, downward = (of_z > z) & (z > 0), (of_z < z) & (z < depth - 1)
            pl.when(upward)(lambda: passing(0))
            pl.when(downward)(lambda: passing(1))

            @pl.when(jnp.logical_not(upward | downward))
            def _():
                add_into(own, (own, self.from_y.at[of_z]), self.rows)

            pl.when(of_z > z)(lambda: self.on_z(0, of_z).start())
            pl.when(of_z < z)(lambda: self.on_z(1, of_z).start())

        each(step, add)

    def last(self, result):
        z, depth = self.z, self.depth
        own = self.sums.at[z * 2 + self.y]
        low, high = self.from_z.at[0, z], self.from_z.at[1, z]
        pl.when(z > 0)(lambda: self.on_z(0, z).wait_recv())
        pl.when(z < depth - 1)(lambda: self.on_z(1, z).wait_recv())
        inside = (z > 0) & (z < depth - 1)
        pl.when(inside)(lambda: add_into(result, (own, low, high), self.rows))
        pl.when(z == 0)(lambda: add_into(result, (own, high), self.rows))
        pl.when(z == depth - 1)(lambda: add_into(result, (own, low), self.rows))

    def finish(self):
        for of_z in range(self.depth):
            self.on_y(of_z).wait_send()
            self.on_core(of_z * 2).wait_send()
            self.on_core(of_z * 2 + 1).wait_send()
            pl.when(of_z > self.z)(lambda: self.on_z(0, of_z).wait_send())
            pl.when(of_z < self.z)(lambda: self.on_z(1, of_z).wait_send())

    def run(self, result):
        steps = range(self.depth - 1, -1, -1)
        self.start()
        for step in steps:
            self.add_cores(step)
        for step in steps:
            self.add_y(step)
        self.last(result)
        self.finish()


def call(kernel, out, scratch, number, name, *operands, outside=(), outside_out=()):
    def spec(position, far):
        return pl.BlockSpec(memory_space=pl.ANY if position in far else pltpu.VMEM)

    many = isinstance(out, (tuple, list))
    out_specs = [spec(i, outside_out) for i in range(len(out) if many else 1)]
    return pl.pallas_call(
        kernel,
        out_shape=out,
        in_specs=[spec(i, outside) for i in range(len(operands))],
        out_specs=out_specs if many else out_specs[0],
        scratch_shapes=scratch,
        compiler_params=pltpu.CompilerParams(
            collective_id=number,
            has_side_effects=number is not None,
            vmem_limit_bytes=VMEM_LIMIT,
        ),
        name=name,
    )(*operands)


def gather_ctx(block, number, name):
    count, rows = lax.axis_size("ctx"), block.shape[0]

    def kernel(block_ref, out, *sems):
        gather = Gather(out, rows, sems)
        gather.own()[...] = block_ref[...]
        greet()
        gather.run()

    out = jax.ShapeDtypeStruct((count * rows, block.shape[1]), block.dtype)
    return call(kernel, out, Gather.sems(count // 4), number, name, block)


def scatter_ctx(parts, number, name):
    count = lax.axis_size("ctx")
    rows, columns = parts.shape[0] // count, parts.shape[1]

    def kernel(part, result, *scratch):
        greet()
        Scatter(part, scratch).run(result)

    out = jax.ShapeDtypeStruct((rows, columns), jnp.float32)
    scratch = Scatter.scratch(count // 4, rows, columns)
    return call(kernel, out, scratch, number, name, parts)


class Relay:
    def __init__(self, source, out, sems, parts=1, over_y=False):
        self.source, self.out, self.sems = source, out, sems
        self.z, self.y, self.c, _ = chip_place()
        self.parts, self.over_y = parts, over_y
        self.rows = source.shape[0] // (4 if over_y else 2 * parts)

    @staticmethod
    def semaphores():
        return pltpu.SemaphoreType.DMA((2, 6))

    def block(self, ref, part, y, c):
        place = y * 2 + c if self.over_y else c * self.parts + part
        return ref.at[pl.ds(pl.multiple_of(place * self.rows, 16), self.rows)]

    def on_x(self, part):
        source = self.block(self.source, part, self.y, self.c)
        target = self.block(self.out, part, self.y, self.c)
        return remote(source, target, self.sems, (part,), {"wa": 1 - lax.axis_index("wa")})

    def on_core(self, part, y, c):
        block = self.block(self.out, part, y, c)
        at = (2 + (jnp.where(y == self.y, 0, 1) if self.over_y else part),)
        return remote(block, block, self.sems, at, {"ctx": ctx_of(self.z, self.y, 1 - self.c)})

    def on_y(self, y):
        block = self.block(self.out, 0, y, self.c)
        return remote(block, block, self.sems, (4,), {"ctx": ctx_of(self.z, 1 - self.y, self.c)})

    def start(self):
        for part in range(self.parts):
            self.on_x(part).start()

    def pass_on(self, part=0):
        self.on_x(part).wait_recv()
        if self.over_y:
            self.on_y(self.y).start()
        self.on_core(part, self.y, self.c).start()

    def pass_on_y(self):
        self.on_y(1 - self.y).wait_recv()
        self.on_core(0, 1 - self.y, self.c).start()

    def finish(self):
        for part in range(self.parts):
            self.on_x(part).wait_send()
            self.on_core(part, self.y, self.c).wait_send()
            self.on_core(part, self.y, 1 - self.c).wait_recv()
        if self.over_y:
            self.on_y(self.y).wait_send()
            self.on_core(0, 1 - self.y, self.c).wait_send()
            self.on_core(0, 1 - self.y, 1 - self.c).wait_recv()


def front(d_out, w_query, w_keyval, w_out_attn, small):
    count, rows = lax.axis_size("ctx"), d_out.shape[0]
    depth = count // 4

    def kernel(
        d_out_ref, query_ref, keyval_ref, attn_ref, small_ref,
        d_out_all, query_there, keyval_there, attn_there, small_there, *sems,
    ):
        gather = Gather(d_out_all, rows, sems[:3])
        query_sems, keyval_sems, attn_sems, small_sems, own_sem = sems[3:]
        query = Relay(query_ref, query_there, query_sems, parts=2)
        keyval = Relay(keyval_ref, keyval_there, keyval_sems)
        attn = Relay(attn_ref, attn_there, attn_sems, over_y=True)
        partner = {"wa": 1 - lax.axis_index("wa")}
        swap = remote(small_ref, small_there, small_sems, (0,), partner)
        keep = pltpu.make_async_copy(d_out_ref, gather.own(), own_sem.at[0])
        keep.start()
        greet(across_x=True)
        swap.start()
        attn.start()
        query.start()
        keyval.start()
        gather.start(d_out_ref)
        gather.along_z(1)
        gather.along_y(0)
        gather.along_z(2)
        attn.pass_on()
        gather.along_y(1)
        gather.along_z(3)
        query.pass_on(0)
        gather.along_y(2)
        attn.pass_on_y()
        gather.along_y(3)
        query.pass_on(1)
        keyval.pass_on()
        gather.finish()
        query.finish()
        keyval.finish()
        attn.finish()
        swap.wait()
        keep.wait()

    def like(values):
        return jax.ShapeDtypeStruct(values.shape, values.dtype)

    out = [
        jax.ShapeDtypeStruct((count * rows, d_out.shape[1]), d_out.dtype),
        like(w_query), like(w_keyval), like(w_out_attn), like(small),
    ]
    scratch = Gather.sems(depth) + [Relay.semaphores()] * 3
    scratch += [pltpu.SemaphoreType.DMA((2, 1)), pltpu.SemaphoreType.DMA((1,))]
    every = range(5)
    return call(
        kernel, out, scratch, 0, "front",
        d_out, w_query, w_keyval, w_out_attn, small, outside=every, outside_out=every,
    )


def finish(hidden, hidden_there, mixed, mixed_there, middle, middle_there, query, keyval, small, small_other, expert_in, expert_out):
    count = lax.axis_size("ctx")
    depth, tokens, half = count // 4, hidden.shape[0], hidden.shape[1]
    rows = half // count
    widths = (middle.shape[1], query.shape[1], keyval.shape[1])

    def kernel(*refs):
        (hidden_ref, hidden_there_ref, mixed_ref, mixed_there_ref, middle_ref, middle_there_ref,
         query_ref, keyval_ref, small_ref, small_other_ref, in_ref, out_ref) = refs[:12]
        attn_sum, query_sum, keyval_sum, small_sum, in_there, out_there = refs[12:18]
        (attn_part, query_part, keyval_part, pair, query_there, keyval_there, small_there,
         small_all, x_sems) = refs[18:27]
        scratch = refs[27:]
        scatters, gathers = [], []
        parts, sums = (attn_part, query_part, keyval_part), (attn_sum, query_sum, keyval_sum)
        for part, total in zip(parts, sums):
            scatters.append(Scatter(part, scratch[:7]))
            gathers.append(Gather(total, rows, scratch[7:10]))
            scratch = scratch[10:]
        small_gather = Gather(small_all, small.shape[0], scratch)
        (attn, query_, keyval_), (attn_out, query_out, keyval_out) = scatters, gathers
        partner = {"wa": 1 - lax.axis_index("wa")}
        swaps = [
            remote(source, target, x_sems, (i,), partner)
            for i, (source, target) in enumerate(
                [(small_other_ref, small_there), (query_ref, query_there), (keyval_ref, keyval_there),
                 (in_ref, in_there), (out_ref, out_there)]
            )
        ]
        greet(across_x=True)
        for swap in swaps:
            swap.start()

        def products(left, left_there, right, right_there, part):
            pair[:tokens] = left[...]
            pair[tokens:] = left_there[...]
            width = part.shape[1]

            @pl.loop(0, width // 512)
            def _(turn):
                at = pl.ds(pl.multiple_of(turn * 512, 512), 512)
                both = jnp.concatenate([right[:, at], right_there[:, at]], axis=0)
                part[:, at] = columns_by_columns(pair[...], both).astype(jnp.bfloat16)

        steps = range(depth - 1, -1, -1)
        products(mixed_ref, mixed_there_ref, middle_ref, middle_there_ref, attn_part)
        attn.start()
        for step in steps:
            attn.add_cores(step)
        swaps[0].wait()
        small_gather.own()[...] = (small_ref[...] + small_there[...]).astype(jnp.bfloat16)
        swaps[1].wait()
        products(hidden_ref, hidden_there_ref, query_ref, query_there, query_part)
        query_.start()
        for step in steps:
            query_.add_cores(step)
        swaps[2].wait()
        products(hidden_ref, hidden_there_ref, keyval_ref, keyval_there, keyval_part)
        keyval_.start()
        for step in steps:
            keyval_.add_cores(step)
        for step in steps:
            attn.add_y(step)
        attn.last(attn_out.own())
        attn_out.start()
        small_gather.start()
        for step in steps:
            query_.add_y(step)
        attn_out.along_z(1)
        query_.last(query_out.own())
        query_out.start()
        attn_out.along_z(2)
        attn_out.along_y(0)
        small_gather.along_z(1)
        for step in steps:
            keyval_.add_y(step)
        attn_out.along_z(3)
        attn_out.along_y(1)
        keyval_.last(keyval_out.own())
        keyval_out.start()
        query_out.along_z(1)
        small_gather.along_z(2)
        attn_out.along_y(2)
        query_out.along_z(2)
        small_gather.along_z(3)
        query_out.along_y(0)
        keyval_out.along_z(1)
        query_out.along_z(3)
        attn_out.along_y(3)
        keyval_out.along_z(2)
        query_out.along_y(1)
        keyval_out.along_z(3)
        query_out.along_y(2)
        small_gather.along_y(0)
        keyval_out.along_y(0)
        small_gather.along_y(1)
        query_out.along_y(3)
        keyval_out.along_y(1)
        small_gather.along_y(2)
        keyval_out.along_y(2)
        small_gather.along_y(3)
        keyval_out.along_y(3)
        for one in [small_gather] + gathers + scatters:
            one.finish()
        small_rows = small.shape[0]
        total = small_all[:small_rows].astype(jnp.float32)
        for device in range(1, count):
            rows_of = slice(device * small_rows, (device + 1) * small_rows)
            total = total + small_all[rows_of].astype(jnp.float32)
        small_sum[...] = total
        swaps[3].wait()
        swaps[4].wait()

    out = [jax.ShapeDtypeStruct((half, width), jnp.bfloat16) for width in widths]
    out += [
        jax.ShapeDtypeStruct(small.shape, jnp.float32),
        jax.ShapeDtypeStruct(expert_in.shape, expert_in.dtype),
        jax.ShapeDtypeStruct(expert_out.shape, expert_out.dtype),
    ]
    scratch = [pltpu.VMEM((half, width), jnp.bfloat16) for width in widths]
    scratch += [
        pltpu.VMEM((2 * tokens, half), jnp.bfloat16),
        pltpu.VMEM(query.shape, jnp.bfloat16),
        pltpu.VMEM(keyval.shape, jnp.bfloat16),
        pltpu.VMEM(small.shape, jnp.float32),
        pltpu.VMEM((count * small.shape[0], small.shape[1]), jnp.bfloat16),
        pltpu.SemaphoreType.DMA((2, 5)),
    ]
    for width in widths:
        scratch += Scatter.scratch(depth, rows, width) + Gather.sems(depth)
    scratch += Gather.sems(depth)
    return call(
        kernel, out, scratch, 1, "finish",
        hidden, hidden_there, mixed, mixed_there, middle, middle_there, query, keyval, small,
        small_other, expert_in, expert_out, outside=(10, 11), outside_out=(4, 5),
    )


def rows_by_rows(left, right):
    return lax.dot_general(
        left, right, (((1,), (1,)), ((), ())), preferred_element_type=jnp.float32
    )


def columns_by_columns(left, right):
    return lax.dot_general(
        left, right, (((0,), (0,)), ((), ())), preferred_element_type=jnp.float32
    )


def allowed_bias(doc_row, doc_column, tokens):
    keys = doc_row.shape[1]
    query_block = lax.axis_index("ctx") * tokens // BLOCK
    key_block = lax.broadcasted_iota(jnp.int32, (tokens, keys), 1) // BLOCK
    allowed = (doc_row == doc_column) & (key_block <= query_block)
    return jnp.where(allowed, 0.0, NEGATIVE)


def attend_kernel(query, keyval, doc_row, doc_column, mixed, level, stacked, bias):
    tokens = query.shape[0]
    bias[...] = allowed_bias(doc_row[...], doc_column[...], tokens)
    for head in range(HEADS):
        stacked[head * tokens : (head + 1) * tokens, :] = query[:, head * 128 : (head + 1) * 128]

    @pl.loop(0, HEADS // 2)
    def _(pair):
        rows = pl.ds(pl.multiple_of(pair * 2 * tokens, 128), 2 * tokens)
        kind = pair // (HEADS // KV_HEADS // 2)
        keys = keyval[:, pl.ds(pl.multiple_of(kind * 128, 128), 128)]
        vals = keyval[:, pl.ds(pl.multiple_of(kind * 128 + 256, 128), 128)]
        scores = rows_by_rows(stacked[rows, :], keys) * HEAD_DIM**-0.5
        scores = (scores.reshape(2, tokens, -1) + bias[...][None]).reshape(scores.shape)
        top = jnp.max(scores, axis=-1, keepdims=True)
        weights = jnp.exp(scores - top)
        total = jnp.sum(weights, axis=-1, keepdims=True)
        probs = (weights / total).astype(jnp.bfloat16)
        mixture = jnp.dot(probs, vals, preferred_element_type=jnp.float32)
        for half in range(2):
            columns = pl.ds(pl.multiple_of((pair * 2 + half) * 128, 128), 128)
            mixed[:, columns] = mixture[half * tokens : (half + 1) * tokens]
        level[rows, :] = top + jnp.log(total)


def attend(query, keyval, doc_row, doc_column):
    tokens, keys = query.shape[0], keyval.shape[0]
    out = (
        jax.ShapeDtypeStruct(query.shape, jnp.float32),
        jax.ShapeDtypeStruct((HEADS * tokens, 1), jnp.float32),
    )
    scratch = [
        pltpu.VMEM((HEADS * tokens, HEAD_DIM), jnp.bfloat16),
        pltpu.VMEM((tokens, keys), jnp.float32),
    ]
    return call(
        attend_kernel, out, scratch, None, "attend", query, keyval, doc_row, doc_column
    )


def attend_back_kernel(
    query, keyval, doc_row, doc_column, level, mixed, grad_mixed,
    grad_query, grad_keyval, stacked, grads, bias, delta, total,
):
    tokens = query.shape[0]
    bias[...] = allowed_bias(doc_row[...], doc_column[...], tokens)
    total[...] = jnp.zeros_like(total)
    for head in range(HEADS):
        rows, columns = slice(head * tokens, (head + 1) * tokens), slice(head * 128, head * 128 + 128)
        stacked[rows, :] = query[:, columns]
        grads[rows, :] = grad_mixed[:, columns]
        delta[rows, :] = jnp.sum(
            grad_mixed[:, columns].astype(jnp.float32) * mixed[:, columns], axis=-1, keepdims=True
        )

    @pl.loop(0, HEADS // 2)
    def _(pair):
        rows = pl.ds(pl.multiple_of(pair * 2 * tokens, 128), 2 * tokens)
        kind = pair // (HEADS // KV_HEADS // 2)
        key_columns = pl.ds(pl.multiple_of(kind * 128, 128), 128)
        val_columns = pl.ds(pl.multiple_of(kind * 128 + 256, 128), 128)
        keys, vals = keyval[:, key_columns], keyval[:, val_columns]
        own, grad = stacked[rows, :], grads[rows, :]
        scores = rows_by_rows(own, keys) * HEAD_DIM**-0.5
        scores = (scores.reshape(2, tokens, -1) + bias[...][None]).reshape(scores.shape)
        probs = jnp.exp(scores - level[rows, :])
        grad_probs = rows_by_rows(grad, vals)
        grad_scores = (probs * (grad_probs - delta[rows, :])).astype(jnp.bfloat16)
        own_grad = jnp.dot(grad_scores, keys, preferred_element_type=jnp.float32)
        for half in range(2):
            columns = pl.ds(pl.multiple_of((pair * 2 + half) * 128, 128), 128)
            grad_query[:, columns] = own_grad[half * tokens : (half + 1) * tokens] * HEAD_DIM**-0.5
        total[:, key_columns] += columns_by_columns(grad_scores, own) * HEAD_DIM**-0.5
        total[:, val_columns] += columns_by_columns(probs.astype(jnp.bfloat16), grad)

    grad_keyval[...] = total[...].astype(jnp.bfloat16)


def attend_back(query, keyval, doc_row, doc_column, level, mixed, grad_mixed):
    tokens, keys = query.shape[0], keyval.shape[0]
    out = (
        jax.ShapeDtypeStruct(query.shape, jnp.float32),
        jax.ShapeDtypeStruct(keyval.shape, jnp.bfloat16),
    )
    scratch = [
        pltpu.VMEM((HEADS * tokens, HEAD_DIM), jnp.bfloat16),
        pltpu.VMEM((HEADS * tokens, HEAD_DIM), jnp.bfloat16),
        pltpu.VMEM((tokens, keys), jnp.float32),
        pltpu.VMEM((HEADS * tokens, 1), jnp.float32),
        pltpu.VMEM(keyval.shape, jnp.float32),
    ]
    return call(
        attend_back_kernel, out, scratch, None, "attend_back",
        query, keyval, doc_row, doc_column, level, mixed, grad_mixed,
    )


def rms_back(values, gain_vec, grad):
    scale = lax.rsqrt(jnp.mean(values * values, axis=-1, keepdims=True) + EPSILON)
    through = jnp.mean(gain_vec * grad * values, axis=-1, keepdims=True)
    back = scale * gain_vec * grad - values * scale**3 * through
    return back, jnp.sum(grad * values * scale, axis=0)


def swap_wa(values):
    return jax.tree.map(lambda v: lax.ppermute(v, "wa", ((0, 1), (1, 0))), values)


def gathered_body(
    layer_input, seq_ids, routes, gain_attn, w_query, w_keyval, w_out_attn, gain_ffn, router,
    w_in, w_out, d_out,
):
    me, side = lax.axis_index("ctx"), lax.axis_index("wa")
    tokens = layer_input.shape[1]
    experts = router.shape[1]
    kv_width = KV_HEADS * HEAD_DIM
    half = D // 2
    quarter = w_in.shape[3]

    def halves(values):
        own = lax.dynamic_slice_in_dim(values, side * half, half, values.ndim - 1)
        return own, lax.dynamic_slice_in_dim(values, (1 - side) * half, half, values.ndim - 1)

    def whole(own, there):
        both = jnp.concatenate([own, there], axis=-1), jnp.concatenate([there, own], axis=-1)
        return jnp.where(side == 0, *both)

    small = jnp.concatenate(
        [router.T, gain_attn[None], gain_ffn[None], jnp.zeros((14 - experts, half), jnp.bfloat16)]
    )
    d_out_all, w_query_there, w_keyval_there, w_out_attn_there, small_there = front(
        d_out[0], w_query, w_keyval, w_out_attn, small
    )
    w_in, w_out, small_there = lax.optimization_barrier((w_in, w_out, small_there))
    small = whole(small, small_there).astype(jnp.float32)
    router_rows, gain_one, gain_two = small[:experts], small[experts], small[experts + 1]
    w_in_there, w_out_there = swap_wa((w_in[0], w_out[0]))
    in_matrix = jnp.concatenate([w_in[0, 0], w_in_there[0], w_in[0, 1], w_in_there[1]], axis=1)
    out_matrix = jnp.concatenate([w_out[0], w_out_there], axis=0)

    def onto(values, weight, weight_there):
        own, there = halves(values)
        return jnp.dot(own, weight, preferred_element_type=jnp.float32) + jnp.dot(
            there, weight_there, preferred_element_type=jnp.float32
        )

    residual = layer_input[0].astype(jnp.float32)
    hidden_one = rms_scale(residual, gain_one).astype(jnp.bfloat16)
    hidden_one_own, hidden_one_other = halves(hidden_one)
    hidden_one_there = swap_wa(hidden_one_other)
    positions = me * tokens + jnp.arange(tokens, dtype=jnp.int32)
    angles = angle_table(positions)
    query_pre = onto(hidden_one, w_query, w_query_there)
    keyval_pre = onto(hidden_one, w_keyval, w_keyval_there)
    query = rotate(query_pre.reshape(tokens, HEADS, HEAD_DIM), angles).astype(jnp.bfloat16)
    query = query.reshape(tokens, D)
    keys = rotate(keyval_pre[:, :kv_width].reshape(tokens, KV_HEADS, HEAD_DIM), angles)
    keyval = jnp.concatenate([keys.reshape(tokens, kv_width), keyval_pre[:, kv_width:]], axis=1)
    keyval_all = gather_ctx(keyval.astype(jnp.bfloat16), 2, "gather_kv")
    doc_column = lax.dynamic_slice_in_dim(seq_ids[0], me * tokens, tokens, 0)[:, None]
    mixed, level = attend(query, keyval_all, seq_ids, doc_column)
    mixed_low = mixed.astype(jnp.bfloat16)
    mixed_own, mixed_other = halves(mixed_low)
    mixed_there = swap_wa(mixed_other)
    middle = residual + onto(mixed_low, w_out_attn, w_out_attn_there)

    hidden_two = rms_scale(middle, gain_two).astype(jnp.bfloat16)
    router_low = router_rows.astype(jnp.bfloat16)
    logits = rows_by_rows(hidden_two, router_low)
    numbers = jnp.arange(experts, dtype=jnp.int32)
    chosen = jnp.any(routes[0][:, :, None] == numbers[None, None, :], axis=1)
    masked = jnp.where(chosen, logits, NEGATIVE)
    weights = jnp.exp(masked - jnp.max(masked, axis=1, keepdims=True))
    gates = weights / jnp.sum(weights, axis=1, keepdims=True)
    gates_high = gates.astype(jnp.bfloat16)
    gates_low = (gates - gates_high.astype(jnp.float32)).astype(jnp.bfloat16)
    spare = jnp.zeros((tokens, 128 - 2 * experts), jnp.bfloat16)
    send = jnp.concatenate([hidden_two, gates_high, gates_low, spare], axis=1)
    hidden_all = gather_ctx(send, 3, "gather_hidden")

    rows = hidden_all[:, :D]
    expert = me // 2
    lane = jnp.arange(128, dtype=jnp.int32)[None, :]
    gate = jnp.sum(
        jnp.where(
            (lane == expert) | (lane == expert + experts), hidden_all[:, D:].astype(jnp.float32), 0.0
        ),
        axis=1,
        keepdims=True,
    )
    both = jnp.dot(rows, in_matrix, preferred_element_type=jnp.float32)
    width = 2 * quarter

    def gate_unit(first, second):
        return jax.nn.gelu(first, approximate=True) * second

    hidden, unit_back = jax.vjp(gate_unit, both[:, :width], both[:, width:])
    hidden_gated = (hidden * gate).astype(jnp.bfloat16)
    result = jnp.dot(hidden_gated, out_matrix, preferred_element_type=jnp.float32)
    grad_hidden = rows_by_rows(d_out_all, out_matrix)
    grad_gate = jnp.sum(grad_hidden * hidden, axis=1, keepdims=True)
    grad_both = jnp.concatenate(unit_back(grad_hidden * gate), axis=1).astype(jnp.bfloat16)
    grad_rows = rows_by_rows(grad_both, in_matrix)
    gate_columns = jnp.where(lane == expert, grad_gate, 0.0)
    grad_send = jnp.concatenate([grad_rows, gate_columns], axis=1).astype(jnp.bfloat16)
    returned = scatter_ctx(grad_send, 4, "scatter_grad_rows")
    result_sum = scatter_ctx(result.astype(jnp.bfloat16), 5, "scatter_result")
    output = (middle + result_sum).astype(jnp.bfloat16)
    grad_in_matrix = columns_by_columns(rows, grad_both)
    grad_out_matrix = columns_by_columns(hidden_gated, d_out_all)

    grad_out = d_out[0].astype(jnp.float32)
    grad_gates = returned[:, D : D + experts]
    grad_logits = gates * (grad_gates - jnp.sum(gates * grad_gates, axis=1, keepdims=True))
    grad_logits_low = grad_logits.astype(jnp.bfloat16)
    grad_hidden_two = returned[:, :D] + jnp.dot(
        grad_logits_low, router_low, preferred_element_type=jnp.float32
    )
    grad_router = columns_by_columns(grad_logits_low, hidden_two)
    back_two, grad_gain_two = rms_back(middle, gain_two, grad_hidden_two)
    grad_middle = grad_out + back_two
    grad_middle_low = grad_middle.astype(jnp.bfloat16)
    grad_middle_there = swap_wa(grad_middle_low)
    grad_mixed = whole(
        rows_by_rows(grad_middle_low, w_out_attn), rows_by_rows(grad_middle_low, w_out_attn_there)
    ).astype(jnp.bfloat16)
    grad_query, grad_keyval = attend_back(
        query, keyval_all, seq_ids, doc_column, level, mixed, grad_mixed
    )
    grad_query_pre = rotate(grad_query.reshape(tokens, HEADS, HEAD_DIM), -angles)
    grad_query_pre = grad_query_pre.reshape(tokens, D).astype(jnp.bfloat16)
    grad_keyval_own = scatter_ctx(grad_keyval, 6, "scatter_grad_kv")
    grad_keys = rotate(
        grad_keyval_own[:, :kv_width].reshape(tokens, KV_HEADS, HEAD_DIM), -angles
    ).reshape(tokens, kv_width)
    grad_keyval_pre = jnp.concatenate([grad_keys, grad_keyval_own[:, kv_width:]], axis=1)
    grad_keyval_pre = grad_keyval_pre.astype(jnp.bfloat16)
    grad_hidden_one = whole(
        rows_by_rows(grad_query_pre, w_query) + rows_by_rows(grad_keyval_pre, w_keyval),
        rows_by_rows(grad_query_pre, w_query_there)
        + rows_by_rows(grad_keyval_pre, w_keyval_there),
    )
    back_one, grad_gain_one = rms_back(residual, gain_one, grad_hidden_one)
    grad_input = (grad_middle + back_one).astype(jnp.bfloat16)

    small_grads = jnp.concatenate(
        [
            grad_router,
            grad_gain_one[None],
            grad_gain_two[None],
            jnp.zeros((14 - experts, D), jnp.float32),
        ]
    )
    attn_sum, query_sum, keyval_sum, small_sum, in_there, out_there = finish(
        hidden_one_own, hidden_one_there, mixed_own, mixed_there, grad_middle_low,
        grad_middle_there, grad_query_pre, grad_keyval_pre, *halves(small_grads),
        jnp.concatenate(
            [grad_in_matrix[:, quarter:width], grad_in_matrix[:, width + quarter :]], axis=1
        ).astype(jnp.bfloat16),
        grad_out_matrix[quarter:].astype(jnp.bfloat16),
    )
    grad_w_in = jnp.stack(
        [
            grad_in_matrix[:, :quarter] + in_there[:, :quarter].astype(jnp.float32),
            grad_in_matrix[:, width : width + quarter]
            + in_there[:, quarter:].astype(jnp.float32),
        ]
    )
    grad_w_out = grad_out_matrix[:quarter] + out_there.astype(jnp.float32)
    return (
        output[None],
        grad_input[None],
        small_sum[experts],
        query_sum.astype(jnp.float32),
        keyval_sum.astype(jnp.float32),
        attn_sum.astype(jnp.float32),
        small_sum[experts + 1],
        small_sum[:experts].T,
        grad_w_in[None],
        grad_w_out[None],
    )


def solution(mesh):
    in_specs = (
        P("wa", "ctx", None),
        P("wa", None),
        P("wa", "ctx", None),
        P("wa"),
        P("wa", None),
        P("wa", None),
        P("wa", None),
        P("wa"),
        P("wa", None),
        P("ctx", None, None, "wa"),
        P("ctx", "wa", None),
        P("wa", "ctx", None),
    )
    out_specs = (
        P("wa", "ctx", None),
        P("wa", "ctx", None),
        P("wa"),
        P("wa", None),
        P("wa", None),
        P("wa", None),
        P("wa"),
        P("wa", None),
        P("ctx", None, None, "wa"),
        P("ctx", "wa", None),
    )
    depth = mesh.shape["ctx"]
    body = gathered_body if depth == 16 else routed_body
    return jax.shard_map(body, mesh=mesh, in_specs=in_specs, out_specs=out_specs, check_vma=False)
```

```python
import functools
import math

import jax
import jax.numpy as jnp
from jax import lax
from jax.experimental import pallas as pl
from jax.experimental.pallas import tpu as pltpu
from jax.sharding import PartitionSpec as P

D = 1536
HEADS = 12
KV_HEADS = 2
HEAD_DIM = 128
TOP = 4
BLOCK = 256


EPSILON = 1e-06
THETA = 1000000.0
NEGATIVE = -1e30


def rms_scale(values, gain_vec):
    return (
        values * lax.rsqrt(jnp.mean(values * values, axis=-1, keepdims=True) + EPSILON) * gain_vec
    )


def rotate(values, angles):
    half_dim = values.shape[-1] // 2
    cosine = jnp.cos(angles)
    sine_part = jnp.sin(angles)
    first_half = values[..., :half_dim]
    second = values[..., half_dim:]
    return jnp.concatenate(
        [first_half * cosine - second * sine_part, second * cosine + first_half * sine_part],
        axis=-1,
    )


def angle_table(positions):
    half_dim = HEAD_DIM // 2
    frequency = THETA ** (-2.0 * jnp.arange(half_dim, dtype=jnp.float32) / HEAD_DIM)
    return (positions.astype(jnp.float32)[:, None] * frequency[None, :])[:, None, :]


def gated(stacked):
    return jax.nn.gelu(stacked[..., 0, :], approximate=True) * stacked[..., 1, :]


def over_keys(key_rows, running, advance):
    key_count = key_rows.shape[0]
    key_width = math.gcd(key_count, 512)

    def one_turn(state_now, block_index):
        key_offset = block_index * key_width
        key_part = lax.dynamic_slice_in_dim(key_rows, key_offset, key_width, 0)
        return (advance(state_now, key_part, key_offset), None)

    running, unused = lax.scan(
        one_turn, running, jnp.arange(key_count // key_width, dtype=jnp.int32)
    )
    return running


def routed_body(
    layer_input,
    seq_ids,
    routes,
    gain_attn,
    w_query,
    w_keyval,
    w_out_attn,
    gain_ffn,
    router,
    w_in,
    w_out,
    d_out,
):
    ctx_count = lax.axis_size("ctx")
    ctx_index = lax.axis_index("ctx")
    tokens = layer_input.shape[1]
    length = tokens * ctx_count
    experts_all = ctx_count // 2
    capacity = 2 * tokens * TOP // experts_all
    group = HEADS // KV_HEADS
    kv_width = KV_HEADS * HEAD_DIM
    row_count = group * tokens
    scale = HEAD_DIM ** (-0.5)
    gain_one, query_matrix, keyvalue_matrix, attention_matrix = (
        lax.all_gather(gain_attn, "wa", axis=0, tiled=True),
        lax.all_gather(w_query, "wa", axis=0, tiled=True),
        lax.all_gather(w_keyval, "wa", axis=0, tiled=True),
        lax.all_gather(w_out_attn, "wa", axis=0, tiled=True),
    )
    residual = layer_input[0].astype(jnp.float32)
    normed_one, norm_one_back = jax.vjp(rms_scale, residual, gain_one.astype(jnp.float32))
    hidden_first_norm = normed_one.astype(jnp.bfloat16)
    positions = ctx_index * tokens + jnp.arange(tokens, dtype=jnp.int32)
    angles = angle_table(positions)
    query_projected = jnp.dot(
        hidden_first_norm, query_matrix, preferred_element_type=jnp.float32
    ).reshape(tokens, HEADS, HEAD_DIM)
    keyvalue_projected = jnp.dot(
        hidden_first_norm, keyvalue_matrix, preferred_element_type=jnp.float32
    )
    key_pre = keyvalue_projected[:, :kv_width].reshape(tokens, KV_HEADS, HEAD_DIM)
    query_low = rotate(query_projected, angles).astype(jnp.bfloat16)
    key_low = rotate(key_pre, angles).astype(jnp.bfloat16)
    value_low = keyvalue_projected[:, kv_width:].astype(jnp.bfloat16)
    keyval_send = jnp.concatenate([key_low.reshape(tokens, kv_width), value_low], axis=1)
    query_rows = (
        query_low.reshape(tokens, KV_HEADS, group, HEAD_DIM)
        .transpose(1, 2, 0, 3)
        .reshape(KV_HEADS, row_count, HEAD_DIM)
    )
    doc_row = seq_ids[0]
    query_docs = lax.dynamic_slice_in_dim(doc_row, ctx_index * tokens, tokens, 0)
    query_blocks = positions // BLOCK

    def block_scores(key_part, first_key):
        key_count = key_part.shape[0]
        split_part = key_part.reshape(key_count, 2, KV_HEADS, HEAD_DIM)
        keys_here = split_part[:, 0]
        values_here = split_part[:, 1]
        scores = (
            jnp.einsum("hrd,nhd->hrn", query_rows, keys_here, preferred_element_type=jnp.float32)
            * scale
        )
        key_docs = lax.dynamic_slice_in_dim(doc_row, first_key, key_count, 0)
        key_blocks = (first_key + jnp.arange(key_count, dtype=jnp.int32)) // BLOCK
        allowed = (query_docs[:, None] == key_docs[None, :]) & (
            key_blocks[None, :] <= query_blocks[:, None]
        )
        allowed = jnp.broadcast_to(allowed[None], (group, tokens, key_count)).reshape(
            1, row_count, key_count
        )
        return (jnp.where(allowed, scores, NEGATIVE), allowed, keys_here, values_here)

    def probs_of(masked, allowed, largest, totals):
        return jnp.where(allowed, jnp.exp(masked - largest[..., None]) / totals[..., None], 0.0)

    def stats_step(running, key_part, first_key):
        largest, totals = running
        masked, allowed, keys_here, values_here = block_scores(key_part, first_key)
        new_largest = jnp.maximum(largest, jnp.max(masked, axis=-1))
        weights = jnp.where(allowed, jnp.exp(masked - new_largest[..., None]), 0.0)
        return (new_largest, totals * jnp.exp(largest - new_largest) + jnp.sum(weights, axis=-1))

    start_stats = (
        jnp.full((KV_HEADS, row_count), NEGATIVE, jnp.float32),
        jnp.zeros((KV_HEADS, row_count), jnp.float32),
    )
    largest, totals = over_keys(
        lax.all_gather(keyval_send, "ctx", axis=0, tiled=True), start_stats, stats_step
    )

    def values_step(running, key_part, first_key):
        masked, allowed, keys_here, values_here = block_scores(key_part, first_key)
        probs_low = probs_of(masked, allowed, largest, totals).astype(jnp.bfloat16)
        return running + jnp.einsum(
            "hrn,nhd->hrd", probs_low, values_here, preferred_element_type=jnp.float32
        )

    start_values = jnp.zeros((KV_HEADS, row_count, HEAD_DIM), jnp.float32)
    mixed_rows = over_keys(
        lax.all_gather(keyval_send, "ctx", axis=0, tiled=True), start_values, values_step
    )
    mixed_low = (
        mixed_rows.reshape(KV_HEADS, group, tokens, HEAD_DIM)
        .transpose(2, 0, 1, 3)
        .reshape(tokens, HEADS * HEAD_DIM)
        .astype(jnp.bfloat16)
    )
    middle_activation = residual + jnp.dot(
        mixed_low, attention_matrix, preferred_element_type=jnp.float32
    )
    gain_two, router_full, w_in_full, w_out_full = (
        lax.all_gather(gain_ffn, "wa", axis=0, tiled=True),
        lax.all_gather(router, "wa", axis=0, tiled=True),
        lax.all_gather(w_in, "wa", axis=3, tiled=True),
        lax.all_gather(w_out, "wa", axis=1, tiled=True),
    )
    in_half = w_in_full[0]
    out_half = w_out_full[0]
    normed_two, norm_two_back = jax.vjp(rms_scale, middle_activation, gain_two.astype(jnp.float32))
    hidden_second_norm = normed_two.astype(jnp.bfloat16)
    router_logits = jnp.dot(hidden_second_norm, router_full, preferred_element_type=jnp.float32)
    route_ids = routes[0]

    def gate_values(logit_rows):
        return jax.nn.softmax(jnp.take_along_axis(logit_rows, route_ids, axis=-1), axis=-1)

    gates, gate_back = jax.vjp(gate_values, router_logits)
    flat_ids = route_ids.reshape(tokens * TOP)
    expert_hits = (flat_ids[:, None] == jnp.arange(experts_all, dtype=jnp.int32)[None, :]).astype(
        jnp.int32
    )
    ranks = jnp.sum(expert_hits * (jnp.cumsum(expert_hits, axis=0) - expert_hits), axis=1)
    slot_first = 2 * flat_ids * capacity + ranks
    slot_second = slot_first + capacity
    slot_total = ctx_count * capacity
    slot_numbers = jnp.arange(slot_total, dtype=jnp.int32)[:, None]
    placed = (
        (slot_first[None, :] == slot_numbers) | (slot_second[None, :] == slot_numbers)
    ).astype(jnp.bfloat16)
    dispatch = jnp.sum(placed.reshape(slot_total, tokens, TOP), axis=2)
    send_rows = (
        jnp.dot(dispatch, hidden_second_norm, preferred_element_type=jnp.float32)
        .astype(jnp.bfloat16)
        .reshape(ctx_count, capacity, D)
    )
    arrived = lax.all_to_all(send_rows, "ctx", split_axis=0, concat_axis=0, tiled=True)
    stacked = jnp.einsum("ncd,gdf->ncgf", arrived, in_half, preferred_element_type=jnp.float32)
    hidden_low = gated(stacked).astype(jnp.bfloat16)
    result = jnp.einsum(
        "ncf,fd->ncd", hidden_low, out_half, preferred_element_type=jnp.float32
    ).astype(jnp.bfloat16)
    returned_rows = lax.all_to_all(result, "ctx", split_axis=0, concat_axis=0, tiled=True)
    returned_flat = returned_rows.reshape(slot_total, D)
    pair_rows = (
        returned_flat[slot_first].astype(jnp.float32)
        + returned_flat[slot_second].astype(jnp.float32)
    ).reshape(tokens, TOP, D)
    output = (middle_activation + jnp.sum(gates[:, :, None] * pair_rows, axis=1)).astype(
        jnp.bfloat16
    )
    grad_out = d_out[0].astype(jnp.float32)
    grad_gates = jnp.sum(pair_rows * grad_out[:, None, :], axis=-1)
    (grad_logits,) = gate_back(grad_gates)
    grad_logits_low = grad_logits.astype(jnp.bfloat16)
    gate_slots = jnp.dot(
        placed.astype(jnp.float32), gates.reshape(tokens * TOP), precision=lax.Precision.HIGHEST
    )
    routed_grad = jnp.dot(dispatch, d_out[0], preferred_element_type=jnp.float32)
    grad_send_rows = (
        (gate_slots[:, None] * routed_grad).astype(jnp.bfloat16).reshape(ctx_count, capacity, D)
    )
    grad_arrived = lax.all_to_all(grad_send_rows, "ctx", split_axis=0, concat_axis=0, tiled=True)
    grad_hidden = jnp.einsum(
        "ncd,fd->ncf", grad_arrived, out_half, preferred_element_type=jnp.float32
    )
    hidden_again, gated_back = jax.vjp(gated, stacked)
    (grad_stacked,) = gated_back(grad_hidden)
    grad_stacked_low = grad_stacked.astype(jnp.bfloat16)
    grad_rows = jnp.einsum(
        "ncgf,gdf->ncd", grad_stacked_low, in_half, preferred_element_type=jnp.float32
    ).astype(jnp.bfloat16)
    grad_returned = lax.all_to_all(grad_rows, "ctx", split_axis=0, concat_axis=0, tiled=True)
    grad_w_in = jnp.einsum(
        "ncd,ncgf->gdf", arrived, grad_stacked_low, preferred_element_type=jnp.float32
    )[None]
    grad_w_out = jnp.einsum(
        "ncf,ncd->fd",
        hidden_again.astype(jnp.bfloat16),
        grad_arrived,
        preferred_element_type=jnp.float32,
    )[None]
    grad_hidden_two = jnp.einsum(
        "st,sd->td",
        dispatch,
        grad_returned.reshape(slot_total, D),
        preferred_element_type=jnp.float32,
    )
    grad_hidden_two = grad_hidden_two + jnp.dot(
        grad_logits_low, router_full.T, preferred_element_type=jnp.float32
    )
    grad_router = jnp.dot(hidden_second_norm.T, grad_logits_low, preferred_element_type=jnp.float32)
    grad_middle_norm, grad_gain_two = norm_two_back(grad_hidden_two)
    grad_middle = grad_out + grad_middle_norm
    grad_middle_low = grad_middle.astype(jnp.bfloat16)
    grad_attn_weight = jnp.dot(mixed_low.T, grad_middle_low, preferred_element_type=jnp.float32)
    grad_mixed = jnp.dot(
        grad_middle_low, attention_matrix.T, preferred_element_type=jnp.float32
    ).astype(jnp.bfloat16)
    grad_rows_out = (
        grad_mixed.reshape(tokens, KV_HEADS, group, HEAD_DIM)
        .transpose(1, 2, 0, 3)
        .reshape(KV_HEADS, row_count, HEAD_DIM)
    )
    delta = jnp.sum(grad_rows_out.astype(jnp.float32) * mixed_rows, axis=-1)

    def score_grads(key_part, first_key):
        masked, allowed, keys_here, values_here = block_scores(key_part, first_key)
        probs = probs_of(masked, allowed, largest, totals)
        grad_probs = jnp.einsum(
            "hrd,nhd->hrn", grad_rows_out, values_here, preferred_element_type=jnp.float32
        )
        grad_scores = (probs * (grad_probs - delta[..., None])).astype(jnp.bfloat16)
        return (grad_scores, probs.astype(jnp.bfloat16), keys_here)

    def key_terms(grad_scores, probs_low, key_count):
        grad_keys = (
            jnp.einsum("hrn,hrd->nhd", grad_scores, query_rows, preferred_element_type=jnp.float32)
            * scale
        )
        grad_values = jnp.einsum(
            "hrn,hrd->nhd", probs_low, grad_rows_out, preferred_element_type=jnp.float32
        )
        return jnp.concatenate(
            [grad_keys.reshape(key_count, kv_width), grad_values.reshape(key_count, kv_width)],
            axis=1,
        )

    start_query = jnp.zeros((KV_HEADS, row_count, HEAD_DIM), jnp.float32)

    def back_step(running, key_part, first_key):
        grad_query_rows, grad_keyvals = running
        grad_scores, probs_low, keys_here = score_grads(key_part, first_key)
        grad_query_rows = (
            grad_query_rows
            + jnp.einsum("hrn,nhd->hrd", grad_scores, keys_here, preferred_element_type=jnp.float32)
            * scale
        )
        fresh = key_terms(grad_scores, probs_low, key_part.shape[0])
        return (grad_query_rows, lax.dynamic_update_slice_in_dim(grad_keyvals, fresh, first_key, 0))

    start_back = (start_query, jnp.zeros((length, 2 * kv_width), jnp.float32))
    grad_query_rows, grad_keyvals = over_keys(
        lax.all_gather(keyval_send, "ctx", axis=0, tiled=True), start_back, back_step
    )
    grad_keyval_mine = lax.psum_scatter(grad_keyvals, "ctx", scatter_dimension=0, tiled=True)
    grad_query = grad_query_rows.reshape(KV_HEADS, group, tokens, HEAD_DIM).transpose(2, 0, 1, 3)
    grad_query_pre = (
        rotate(grad_query.reshape(tokens, HEADS, HEAD_DIM), -angles)
        .reshape(tokens, HEADS * HEAD_DIM)
        .astype(jnp.bfloat16)
    )
    grad_key_pre = rotate(
        grad_keyval_mine[:, :kv_width].reshape(tokens, KV_HEADS, HEAD_DIM), -angles
    ).reshape(tokens, kv_width)
    grad_keyval_pre = jnp.concatenate(
        [grad_key_pre, grad_keyval_mine[:, kv_width:]], axis=1
    ).astype(jnp.bfloat16)
    grad_hidden_one = jnp.dot(
        grad_query_pre, query_matrix.T, preferred_element_type=jnp.float32
    ) + jnp.dot(grad_keyval_pre, keyvalue_matrix.T, preferred_element_type=jnp.float32)
    grad_query_weight = jnp.dot(
        hidden_first_norm.T, grad_query_pre, preferred_element_type=jnp.float32
    )
    grad_keyval_weight = jnp.dot(
        hidden_first_norm.T, grad_keyval_pre, preferred_element_type=jnp.float32
    )
    grad_residual_norm, grad_gain_one = norm_one_back(grad_hidden_one)
    grad_input = (grad_middle + grad_residual_norm).astype(jnp.bfloat16)
    shares = (
        lax.psum_scatter(
            grad_gain_one.astype(jnp.bfloat16), "wa", scatter_dimension=0, tiled=True
        ).astype(jnp.float32),
        lax.psum_scatter(
            grad_query_weight.astype(jnp.bfloat16), "wa", scatter_dimension=0, tiled=True
        ).astype(jnp.float32),
        lax.psum_scatter(
            grad_keyval_weight.astype(jnp.bfloat16), "wa", scatter_dimension=0, tiled=True
        ).astype(jnp.float32),
        lax.psum_scatter(
            grad_attn_weight.astype(jnp.bfloat16), "wa", scatter_dimension=0, tiled=True
        ).astype(jnp.float32),
        lax.psum_scatter(
            grad_gain_two.astype(jnp.bfloat16), "wa", scatter_dimension=0, tiled=True
        ).astype(jnp.float32),
        lax.psum_scatter(
            grad_router.astype(jnp.bfloat16), "wa", scatter_dimension=0, tiled=True
        ).astype(jnp.float32),
        lax.psum_scatter(
            grad_w_in.astype(jnp.bfloat16), "wa", scatter_dimension=3, tiled=True
        ).astype(jnp.float32),
        lax.psum_scatter(
            grad_w_out.astype(jnp.bfloat16), "wa", scatter_dimension=1, tiled=True
        ).astype(jnp.float32),
    )
    summed = lax.psum((shares[0], shares[1], shares[2], shares[3], shares[4], shares[5]), "ctx")
    return (
        output[None],
        grad_input[None],
        summed[0],
        summed[1],
        summed[2],
        summed[3],
        summed[4],
        summed[5],
        shares[6],
        shares[7],
    )

MESH = pl.DeviceIdType.MESH
VMEM_LIMIT = 60 * 1024 * 1024


def chip_place():
    count = lax.axis_size("ctx")
    me = lax.axis_index("ctx")
    return me // 4, lax.rem(me // 2, 2), lax.rem(me, 2), count // 4


def ctx_of(z, y, c):
    return (z * 2 + y) * 2 + c


def greet(across_x=False):
    z, y, c, depth = chip_place()
    barrier = pltpu.get_barrier_semaphore()

    def signal(device):
        pl.semaphore_signal(barrier, 1, device_id=device, device_id_type=MESH)

    signal({"ctx": ctx_of(z, y, 1 - c)})
    signal({"ctx": ctx_of(z, 1 - y, c)})
    if across_x:
        signal({"wa": 1 - lax.axis_index("wa")})
    pl.when(z > 0)(lambda: signal({"ctx": ctx_of(z - 1, y, c)}))
    pl.when(z < depth - 1)(lambda: signal({"ctx": ctx_of(z + 1, y, c)}))
    ends = (z > 0).astype(jnp.int32) + (z < depth - 1).astype(jnp.int32)
    pl.semaphore_wait(barrier, (3 if across_x else 2) + ends)


def remote(source, target_ref, sems, at, device):
    return pltpu.make_async_remote_copy(
        src_ref=source,
        dst_ref=target_ref,
        send_sem=sems.at[(0,) + at],
        recv_sem=sems.at[(1,) + at],
        device_id=device,
        device_id_type=MESH,
    )


def each(step, act):
    z, _, _, depth = chip_place()
    if step == 0:
        act(z)
    else:
        pl.when(z + step < depth)(lambda: act(z + step))
        pl.when(z - step >= 0)(lambda: act(z - step))


def nearest(k):
    z, _, _, depth = chip_place()
    low = jnp.minimum(z, depth - 1 - z)
    step = (k + 1) // 2
    place = jnp.where(k > 2 * low, k, jnp.where(lax.rem(k, 2) == 1, low - step, low + step))
    return jnp.where(z == low, place, depth - 1 - place)


class Gather:
    def __init__(self, out, rows, sems):
        self.out, self.rows = out, rows
        self.z_sems, self.y_sems, self.c_sems = sems
        self.z, self.y, self.c, self.depth = chip_place()

    @staticmethod
    def sems(depth):
        return [
            pltpu.SemaphoreType.DMA((2, 2, depth)),
            pltpu.SemaphoreType.DMA((2, depth)),
            pltpu.SemaphoreType.DMA((2, 2 * depth)),
        ]

    def slot(self, z, y, c):
        return self.out.at[pl.ds(pl.multiple_of(ctx_of(z, y, c) * self.rows, 16), self.rows)]

    def own(self):
        return self.slot(self.z, self.y, self.c)

    def on_z(self, way, of_z, source=None):
        goal = jnp.minimum(self.z + 1, self.depth - 1) if way == 0 else jnp.maximum(self.z - 1, 0)
        block = self.slot(of_z, self.y, self.c)
        target = {"ctx": ctx_of(goal, self.y, self.c)}
        return remote(block if source is None else source, block, self.z_sems, (way, of_z), target)

    def on_y(self, of_z, mine=True, source=None):
        block = self.slot(of_z, self.y if mine else 1 - self.y, self.c)
        target = {"ctx": ctx_of(self.z, 1 - self.y, self.c)}
        return remote(block if source is None else source, block, self.y_sems, (of_z,), target)

    def on_core(self, of_z, of_y, mine=True, source=None):
        block = self.slot(of_z, of_y, self.c if mine else 1 - self.c)
        target = {"ctx": ctx_of(self.z, self.y, 1 - self.c)}
        at = (of_z * 2 + of_y,)
        return remote(block if source is None else source, block, self.c_sems, at, target)

    def start(self, source=None):
        z, depth = self.z, self.depth
        pl.when(z < depth - 1)(lambda: self.on_z(0, z, source).start())
        pl.when(z > 0)(lambda: self.on_z(1, z, source).start())
        self.on_y(z, source=source).start()
        self.on_core(z, self.y, source=source).start()

    def along_z(self, step):
        z, depth = self.z, self.depth

        def from_side(way, of_z, more):
            self.on_z(way, of_z).wait_recv()
            pl.when(more)(lambda: self.on_z(way, of_z).start())
            self.on_y(of_z).start()
            self.on_core(of_z, self.y).start()

        pl.when(z - step >= 0)(lambda: from_side(0, z - step, z < depth - 1))
        pl.when(z + step < depth)(lambda: from_side(1, z + step, z > 0))

    def along_y(self, step):
        def across(of_z):
            self.on_y(of_z, mine=False).wait_recv()
            self.on_core(of_z, 1 - self.y).start()

        each(step, across)

    def finish(self):
        z, depth = self.z, self.depth
        for of_z in range(depth):
            pl.when((z < depth - 1) & (of_z <= z))(lambda: self.on_z(0, of_z).wait_send())
            pl.when((z > 0) & (of_z >= z))(lambda: self.on_z(1, of_z).wait_send())
            self.on_y(of_z).wait_send()
            for of_y in range(2):
                self.on_core(of_z, of_y).wait_send()
                self.on_core(of_z, of_y, mine=False).wait_recv()

    def run(self, source=None):
        self.start(source)
        self.along_z(1)
        self.along_y(0)
        for step in range(1, self.depth):
            if step + 1 < self.depth:
                self.along_z(step + 1)
            self.along_y(step)
        self.finish()


def add_into(target, terms, rows):
    some = 32 if rows % 32 == 0 else 48 if rows % 48 == 0 else 16

    @pl.loop(0, rows // some)
    def _(turn):
        at = pl.ds(pl.multiple_of(turn * some, 16), some)
        total = terms[0][at, :].astype(jnp.float32)
        for term in terms[1:]:
            total = total + term[at, :].astype(jnp.float32)
        target[at, :] = total.astype(target.dtype)


class Scatter:
    def __init__(self, part, scratch, sums=None):
        self.part = part
        self.from_core, self.totals, self.from_y, self.from_z = scratch[:4]
        self.sums = self.totals if sums is None else sums
        self.c_sems, self.y_sems, self.z_sems = scratch[4:]
        self.rows = self.totals.shape[1]
        self.z, self.y, self.c, self.depth = chip_place()

    @staticmethod
    def scratch(depth, rows, columns):
        return [
            pltpu.VMEM((2 * depth, rows, columns), jnp.bfloat16),
            pltpu.VMEM((2 * depth, rows, columns), jnp.bfloat16),
            pltpu.VMEM((depth, rows, columns), jnp.bfloat16),
            pltpu.VMEM((depth + 1, rows, columns), jnp.bfloat16),
            pltpu.SemaphoreType.DMA((2, 2 * depth)),
            pltpu.SemaphoreType.DMA((2, depth)),
            pltpu.SemaphoreType.DMA((2, 2, depth)),
        ]

    def split(self):
        return len(self.part.shape) == 3

    def share(self, chip, c):
        return self.part.at[pl.ds(pl.multiple_of((chip * 2 + c) * self.rows, 16), self.rows)]

    def on_core(self, chip):
        target = {"ctx": ctx_of(self.z, self.y, 1 - self.c)}
        source = self.part.at[chip] if self.split() else self.share(chip, 1 - self.c)
        return remote(source, self.from_core.at[chip], self.c_sems, (chip,), target)

    def on_y(self, of_z):
        target = {"ctx": ctx_of(self.z, 1 - self.y, self.c)}
        source = self.sums.at[of_z * 2 + 1 - self.y]
        return remote(source, self.from_y.at[of_z], self.y_sems, (of_z,), target)

    def on_z(self, way, of_z):
        goal = jnp.minimum(self.z + 1, self.depth - 1) if way == 0 else jnp.maximum(self.z - 1, 0)
        place = of_z if way == 0 else jnp.where(of_z == goal, self.depth, of_z)
        source = self.totals.at[of_z * 2 + self.y]
        target = {"ctx": ctx_of(goal, self.y, self.c)}
        return remote(source, self.from_z.at[place], self.z_sems, (way, of_z), target)

    def start(self):
        def send(of_z):
            self.on_core(of_z * 2 + 1 - self.y).start()
            self.on_core(of_z * 2 + self.y).start()

        for step in range(self.depth - 1, -1, -1):
            each(step, send)

    def add_chip(self, of_z, other, send=True):
        chip = of_z * 2 + (1 - self.y if other else self.y)
        self.on_core(chip).wait_recv()
        own = self.sums.at[chip] if self.split() else self.share(chip, self.c)
        add_into(self.sums.at[chip], (own, self.from_core.at[chip]), self.rows)
        if other and send:
            self.on_y(of_z).start()

    def add_cores(self, step):
        def add(of_z):
            self.add_chip(of_z, True)
            self.add_chip(of_z, False)

        each(step, add)

    def add_y_of(self, of_z):
        z, depth = self.z, self.depth
        self.on_y(of_z).wait_recv()
        place = of_z * 2 + self.y
        total, own, other = self.totals.at[place], self.sums.at[place], self.from_y.at[of_z]
        upward, downward = (of_z > z) & (z > 0), (of_z < z) & (z < depth - 1)
        pl.when(upward)(lambda: self.on_z(0, of_z).wait_recv())
        pl.when(downward)(lambda: self.on_z(1, of_z).wait_recv())

        @pl.when(upward | downward)
        def _():
            add_into(total, (own, other, self.from_z.at[of_z]), self.rows)

        @pl.when(jnp.logical_not(upward | downward))
        def _():
            add_into(total, (own, other), self.rows)

        pl.when(of_z > z)(lambda: self.on_z(0, of_z).start())
        pl.when(of_z < z)(lambda: self.on_z(1, of_z).start())

    def add_y(self, step):
        each(step, self.add_y_of)

    def last(self, result):
        z, depth = self.z, self.depth
        own = self.totals.at[z * 2 + self.y]
        low, high = self.from_z.at[z], self.from_z.at[depth]
        pl.when(z > 0)(lambda: self.on_z(0, z).wait_recv())
        pl.when(z < depth - 1)(lambda: self.on_z(1, z).wait_recv())
        inside = (z > 0) & (z < depth - 1)
        pl.when(inside)(lambda: add_into(result, (own, low, high), self.rows))
        pl.when(z == 0)(lambda: add_into(result, (own, high), self.rows))
        pl.when(z == depth - 1)(lambda: add_into(result, (own, low), self.rows))

    def finish(self, cores=True):
        for of_z in range(self.depth):
            self.on_y(of_z).wait_send()
            if cores:
                self.on_core(of_z * 2).wait_send()
                self.on_core(of_z * 2 + 1).wait_send()
            pl.when(of_z > self.z)(lambda: self.on_z(0, of_z).wait_send())
            pl.when(of_z < self.z)(lambda: self.on_z(1, of_z).wait_send())


def call(kernel, out, scratch, number, name, *operands, outside=(), outside_out=()):
    def spec(position, far):
        return pl.BlockSpec(memory_space=pl.ANY if position in far else pltpu.VMEM)

    many = isinstance(out, (tuple, list))
    out_specs = [spec(i, outside_out) for i in range(len(out) if many else 1)]
    return pl.pallas_call(
        kernel,
        out_shape=out,
        in_specs=[spec(i, outside) for i in range(len(operands))],
        out_specs=out_specs if many else out_specs[0],
        scratch_shapes=scratch,
        compiler_params=pltpu.CompilerParams(
            collective_id=number,
            has_side_effects=number is not None,
            vmem_limit_bytes=VMEM_LIMIT,
        ),
        name=name,
    )(*operands)


def gather_ctx(block, number, name):
    count, rows = lax.axis_size("ctx"), block.shape[0]

    def kernel(block_ref, out, *sems):
        gather = Gather(out, rows, sems)
        gather.own()[...] = block_ref[...]
        greet()
        gather.run()

    out = jax.ShapeDtypeStruct((count * rows, block.shape[1]), block.dtype)
    return call(kernel, out, Gather.sems(count // 4), number, name, block)


class Relay:
    def __init__(self, source, out, sems, parts=1, over_y=False):
        self.source, self.out, self.sems = source, out, sems
        self.z, self.y, self.c, _ = chip_place()
        self.parts, self.over_y = parts, over_y
        self.rows = source.shape[0] // (4 if over_y else 2 * parts)

    @staticmethod
    def semaphores():
        return pltpu.SemaphoreType.DMA((2, 6))

    def block(self, ref, part, y, c):
        place = y * 2 + c if self.over_y else c * self.parts + part
        return ref.at[pl.ds(pl.multiple_of(place * self.rows, 16), self.rows)]

    def on_x(self, part):
        source = self.block(self.source, part, self.y, self.c)
        target = self.block(self.out, part, self.y, self.c)
        return remote(source, target, self.sems, (part,), {"wa": 1 - lax.axis_index("wa")})

    def on_core(self, part, y, c):
        block = self.block(self.out, part, y, c)
        at = (2 + (jnp.where(y == self.y, 0, 1) if self.over_y else part),)
        return remote(block, block, self.sems, at, {"ctx": ctx_of(self.z, self.y, 1 - self.c)})

    def on_y(self, y):
        block = self.block(self.out, 0, y, self.c)
        return remote(block, block, self.sems, (4,), {"ctx": ctx_of(self.z, 1 - self.y, self.c)})

    def start(self):
        for part in range(self.parts):
            self.on_x(part).start()

    def pass_on(self, part=0):
        self.on_x(part).wait_recv()
        if self.over_y:
            self.on_y(self.y).start()
        self.on_core(part, self.y, self.c).start()

    def pass_on_y(self):
        self.on_y(1 - self.y).wait_recv()
        self.on_core(0, 1 - self.y, self.c).start()

    def finish(self):
        for part in range(self.parts):
            self.on_x(part).wait_send()
            self.on_core(part, self.y, self.c).wait_send()
            self.on_core(part, self.y, 1 - self.c).wait_recv()
        if self.over_y:
            self.on_y(self.y).wait_send()
            self.on_core(0, 1 - self.y, self.c).wait_send()
            self.on_core(0, 1 - self.y, 1 - self.c).wait_recv()


def front(d_out, w_query, w_keyval, w_out_attn, small):
    count, rows = lax.axis_size("ctx"), d_out.shape[0]
    depth = count // 4

    def kernel(
        d_out_ref, query_ref, keyval_ref, attn_ref, small_ref,
        d_out_all, query_there, keyval_there, attn_there, small_there, *sems,
    ):
        gather = Gather(d_out_all, rows, sems[:3])
        query_sems, keyval_sems, attn_sems, small_sems, own_sem = sems[3:]
        query = Relay(query_ref, query_there, query_sems, parts=2)
        keyval = Relay(keyval_ref, keyval_there, keyval_sems)
        attn = Relay(attn_ref, attn_there, attn_sems, over_y=True)
        partner = {"wa": 1 - lax.axis_index("wa")}
        swap = remote(small_ref, small_there, small_sems, (0,), partner)
        keep = pltpu.make_async_copy(d_out_ref, gather.own(), own_sem.at[0])
        keep.start()
        greet(across_x=True)
        swap.start()
        attn.start()
        query.start()
        keyval.start()
        gather.start(d_out_ref)
        gather.along_z(1)
        gather.along_y(0)
        gather.along_z(2)
        attn.pass_on()
        gather.along_y(1)
        gather.along_z(3)
        query.pass_on(0)
        gather.along_y(2)
        attn.pass_on_y()
        gather.along_y(3)
        query.pass_on(1)
        keyval.pass_on()
        gather.finish()
        query.finish()
        keyval.finish()
        attn.finish()
        swap.wait()
        keep.wait()

    def like(values):
        return jax.ShapeDtypeStruct(values.shape, values.dtype)

    out = [
        jax.ShapeDtypeStruct((count * rows, d_out.shape[1]), d_out.dtype),
        like(w_query), like(w_keyval), like(w_out_attn), like(small),
    ]
    scratch = Gather.sems(depth) + [Relay.semaphores()] * 3
    scratch += [pltpu.SemaphoreType.DMA((2, 1)), pltpu.SemaphoreType.DMA((1,))]
    every = range(5)
    return call(
        kernel, out, scratch, 0, "front",
        d_out, w_query, w_keyval, w_out_attn, small, outside=every, outside_out=every,
    )


def finish(hidden, hidden_there, mixed, mixed_there, middle, middle_there, query, keyval, small, small_other, expert_in, expert_out):
    count = lax.axis_size("ctx")
    depth, tokens, half = count // 4, hidden.shape[0], hidden.shape[1]
    rows = half // count
    widths = (middle.shape[1], query.shape[1], keyval.shape[1])

    def kernel(*refs):
        (hidden_ref, hidden_there_ref, mixed_ref, mixed_there_ref, middle_ref, middle_there_ref,
         query_ref, keyval_ref, small_ref, small_other_ref, in_ref, out_ref) = refs[:12]
        attn_sum, query_sum, keyval_sum, small_sum, in_there, out_there = refs[12:18]
        (attn_part, query_part, keyval_part, pair, query_there, keyval_there, small_there,
         small_all, x_sems) = refs[18:27]
        scratch = refs[27:]
        scatters, gathers = [], []
        parts, sums = (attn_part, query_part, keyval_part), (attn_sum, query_sum, keyval_sum)
        for part, total in zip(parts, sums):
            scatters.append(Scatter(part, scratch[:7]))
            gathers.append(Gather(total, rows, scratch[7:10]))
            scratch = scratch[10:]
        small_gather = Gather(small_all, small.shape[0], scratch)
        (attn, query_, keyval_), (attn_out, query_out, keyval_out) = scatters, gathers
        partner = {"wa": 1 - lax.axis_index("wa")}
        swaps = [
            remote(source, target, x_sems, (i,), partner)
            for i, (source, target) in enumerate(
                [(small_other_ref, small_there), (query_ref, query_there), (keyval_ref, keyval_there),
                 (in_ref, in_there), (out_ref, out_there)]
            )
        ]
        greet(across_x=True)
        for swap in swaps:
            swap.start()

        def products(left, left_there, right, right_there, part):
            pair[:tokens] = left[...]
            pair[tokens:] = left_there[...]
            width = part.shape[1]

            @pl.loop(0, width // 512)
            def _(turn):
                at = pl.ds(pl.multiple_of(turn * 512, 512), 512)
                both = jnp.concatenate([right[:, at], right_there[:, at]], axis=0)
                part[:, at] = columns_by_columns(pair[...], both).astype(jnp.bfloat16)

        steps = range(depth - 1, -1, -1)
        products(mixed_ref, mixed_there_ref, middle_ref, middle_there_ref, attn_part)
        attn.start()
        for step in steps:
            attn.add_cores(step)
        swaps[0].wait()
        small_gather.own()[...] = (small_ref[...] + small_there[...]).astype(jnp.bfloat16)
        swaps[1].wait()
        products(hidden_ref, hidden_there_ref, query_ref, query_there, query_part)
        query_.start()
        for step in steps:
            query_.add_cores(step)
        swaps[2].wait()
        products(hidden_ref, hidden_there_ref, keyval_ref, keyval_there, keyval_part)
        keyval_.start()
        for step in steps:
            keyval_.add_cores(step)
        for step in steps:
            attn.add_y(step)
        attn.last(attn_out.own())
        attn_out.start()
        small_gather.start()
        for step in steps:
            query_.add_y(step)
        attn_out.along_z(1)
        query_.last(query_out.own())
        query_out.start()
        attn_out.along_z(2)
        attn_out.along_y(0)
        small_gather.along_z(1)
        for step in steps:
            keyval_.add_y(step)
        attn_out.along_z(3)
        attn_out.along_y(1)
        keyval_.last(keyval_out.own())
        keyval_out.start()
        query_out.along_z(1)
        small_gather.along_z(2)
        attn_out.along_y(2)
        query_out.along_z(2)
        small_gather.along_z(3)
        query_out.along_y(0)
        keyval_out.along_z(1)
        query_out.along_z(3)
        attn_out.along_y(3)
        keyval_out.along_z(2)
        query_out.along_y(1)
        keyval_out.along_z(3)
        query_out.along_y(2)
        small_gather.along_y(0)
        keyval_out.along_y(0)
        small_gather.along_y(1)
        query_out.along_y(3)
        keyval_out.along_y(1)
        small_gather.along_y(2)
        keyval_out.along_y(2)
        small_gather.along_y(3)
        keyval_out.along_y(3)
        for one in [small_gather] + gathers + scatters:
            one.finish()
        small_rows = small.shape[0]
        total = small_all[:small_rows].astype(jnp.float32)
        for device in range(1, count):
            rows_of = slice(device * small_rows, (device + 1) * small_rows)
            total = total + small_all[rows_of].astype(jnp.float32)
        small_sum[...] = total
        swaps[3].wait()
        swaps[4].wait()

    out = [jax.ShapeDtypeStruct((half, width), jnp.bfloat16) for width in widths]
    out += [
        jax.ShapeDtypeStruct(small.shape, jnp.float32),
        jax.ShapeDtypeStruct(expert_in.shape, expert_in.dtype),
        jax.ShapeDtypeStruct(expert_out.shape, expert_out.dtype),
    ]
    scratch = [pltpu.VMEM((half, width), jnp.bfloat16) for width in widths]
    scratch += [
        pltpu.VMEM((2 * tokens, half), jnp.bfloat16),
        pltpu.VMEM(query.shape, jnp.bfloat16),
        pltpu.VMEM(keyval.shape, jnp.bfloat16),
        pltpu.VMEM(small.shape, jnp.float32),
        pltpu.VMEM((count * small.shape[0], small.shape[1]), jnp.bfloat16),
        pltpu.SemaphoreType.DMA((2, 5)),
    ]
    for width in widths:
        scratch += Scatter.scratch(depth, rows, width) + Gather.sems(depth)
    scratch += Gather.sems(depth)
    return call(
        kernel, out, scratch, 1, "finish",
        hidden, hidden_there, mixed, mixed_there, middle, middle_there, query, keyval, small,
        small_other, expert_in, expert_out, outside=(10, 11), outside_out=(4, 5),
    )


def rows_by_rows(left, right):
    return lax.dot_general(
        left, right, (((1,), (1,)), ((), ())), preferred_element_type=jnp.float32
    )


def columns_by_columns(left, right):
    return lax.dot_general(
        left, right, (((0,), (0,)), ((), ())), preferred_element_type=jnp.float32
    )


def allowed_bias(doc_row, doc_column, tokens):
    keys = doc_row.shape[1]
    query_block = lax.axis_index("ctx") * tokens // BLOCK
    key_block = lax.broadcasted_iota(jnp.int32, (tokens, keys), 1) // BLOCK
    allowed = (doc_row == doc_column) & (key_block <= query_block)
    return jnp.where(allowed, 0.0, NEGATIVE)


def attend_kernel(query, keyval, doc_row, doc_column, mixed, level, stacked, bias):
    tokens = query.shape[0]
    bias[...] = allowed_bias(doc_row[...], doc_column[...], tokens)
    for head in range(HEADS):
        stacked[head * tokens : (head + 1) * tokens, :] = query[:, head * 128 : (head + 1) * 128]

    @pl.loop(0, HEADS // 2)
    def _(pair):
        rows = pl.ds(pl.multiple_of(pair * 2 * tokens, 128), 2 * tokens)
        kind = pair // (HEADS // KV_HEADS // 2)
        keys = keyval[:, pl.ds(pl.multiple_of(kind * 128, 128), 128)]
        vals = keyval[:, pl.ds(pl.multiple_of(kind * 128 + 256, 128), 128)]
        scores = rows_by_rows(stacked[rows, :], keys) * HEAD_DIM**-0.5
        scores = (scores.reshape(2, tokens, -1) + bias[...][None]).reshape(scores.shape)
        top = jnp.max(scores, axis=-1, keepdims=True)
        weights = jnp.exp(scores - top)
        total = jnp.sum(weights, axis=-1, keepdims=True)
        probs = (weights / total).astype(jnp.bfloat16)
        mixture = jnp.dot(probs, vals, preferred_element_type=jnp.float32)
        for half in range(2):
            columns = pl.ds(pl.multiple_of((pair * 2 + half) * 128, 128), 128)
            mixed[:, columns] = mixture[half * tokens : (half + 1) * tokens]
        level[rows, :] = top + jnp.log(total)


def attend(query, keyval, doc_row, doc_column):
    tokens, keys = query.shape[0], keyval.shape[0]
    out = (
        jax.ShapeDtypeStruct(query.shape, jnp.float32),
        jax.ShapeDtypeStruct((HEADS * tokens, 1), jnp.float32),
    )
    scratch = [
        pltpu.VMEM((HEADS * tokens, HEAD_DIM), jnp.bfloat16),
        pltpu.VMEM((tokens, keys), jnp.float32),
    ]
    return call(
        attend_kernel, out, scratch, None, "attend", query, keyval, doc_row, doc_column
    )


def attend_back(query, keyval, doc_row, doc_column, level, mixed, grad_mixed, results):
    count, tokens, keys = lax.axis_size("ctx"), query.shape[0], keyval.shape[0]
    depth = count // 4

    def kernel(
        query_ref, keyval_ref, doc_row_ref, doc_column_ref, level_ref, mixed_ref, grad_mixed_ref,
        results_ref, grad_query, grad_keyval, output,
        stacked, grads, bias, delta, total, part, *scratch,
    ):
        result = Scatter(None, (None,) + tuple(scratch[:3]) + (None,) + tuple(scratch[3:5]), results_ref)
        keyval_sum = Scatter(part, scratch[5:])
        greet()
        for k in (depth - 1, depth - 2):
            result.on_y(nearest(k)).start()
        bias[...] = allowed_bias(doc_row_ref[...], doc_column_ref[...], tokens)
        total[...] = jnp.zeros_like(total)
        for head in range(HEADS):
            rows = slice(head * tokens, (head + 1) * tokens)
            columns = slice(head * 128, head * 128 + 128)
            stacked[rows, :] = query_ref[:, columns]
            grads[rows, :] = grad_mixed_ref[:, columns]
            delta[rows, :] = jnp.sum(
                grad_mixed_ref[:, columns].astype(jnp.float32) * mixed_ref[:, columns],
                axis=-1,
                keepdims=True,
            )

        @pl.loop(0, HEADS // 2)
        def _(pair):
            rows = pl.ds(pl.multiple_of(pair * 2 * tokens, 128), 2 * tokens)
            kind = pair // (HEADS // KV_HEADS // 2)
            key_columns = pl.ds(pl.multiple_of(kind * 128, 128), 128)
            val_columns = pl.ds(pl.multiple_of(kind * 128 + 256, 128), 128)
            key_part, val_part = keyval_ref[:, key_columns], keyval_ref[:, val_columns]
            own, grad = stacked[rows, :], grads[rows, :]
            scores = rows_by_rows(own, key_part) * HEAD_DIM**-0.5
            scores = (scores.reshape(2, tokens, -1) + bias[...][None]).reshape(scores.shape)
            probs = jnp.exp(scores - level_ref[rows, :])
            grad_probs = rows_by_rows(grad, val_part)
            grad_scores = (probs * (grad_probs - delta[rows, :])).astype(jnp.bfloat16)
            own_grad = jnp.dot(grad_scores, key_part, preferred_element_type=jnp.float32)
            for half in range(2):
                columns = pl.ds(pl.multiple_of((pair * 2 + half) * 128, 128), 128)
                grad_query[:, columns] = (
                    own_grad[half * tokens : (half + 1) * tokens] * HEAD_DIM**-0.5
                )
            total[:, key_columns] += columns_by_columns(grad_scores, own) * HEAD_DIM**-0.5
            total[:, val_columns] += columns_by_columns(probs.astype(jnp.bfloat16), grad)
            pl.when(pair == HEADS // 4)(lambda: result.add_y_of(nearest(depth - 1)))

        part[...] = total[...].astype(jnp.bfloat16)
        keyval_sum.start()
        steps = range(depth - 1, -1, -1)
        for step in steps:
            keyval_sum.add_cores(step)
        for k in range(depth - 3, -1, -1):
            result.on_y(nearest(k)).start()
        result.add_y_of(nearest(depth - 2))
        for step in steps:
            keyval_sum.add_y(step)
        keyval_sum.last(grad_keyval)
        for k in range(depth - 3, -1, -1):
            result.add_y_of(nearest(k))
        result.last(output)
        keyval_sum.finish()
        result.finish(cores=False)

    out = [
        jax.ShapeDtypeStruct(query.shape, jnp.float32),
        jax.ShapeDtypeStruct((tokens, keyval.shape[1]), jnp.float32),
        jax.ShapeDtypeStruct(query.shape, jnp.float32),
    ]
    scratch = [
        pltpu.VMEM((HEADS * tokens, HEAD_DIM), jnp.bfloat16),
        pltpu.VMEM((HEADS * tokens, HEAD_DIM), jnp.bfloat16),
        pltpu.VMEM((tokens, keys), jnp.float32),
        pltpu.VMEM((HEADS * tokens, 1), jnp.float32),
        pltpu.VMEM(keyval.shape, jnp.float32),
        pltpu.VMEM(keyval.shape, jnp.bfloat16),
    ]
    wide = Scatter.scratch(depth, tokens, query.shape[1])
    scratch += wide[1:4] + wide[5:] + Scatter.scratch(depth, tokens, keyval.shape[1])
    return call(
        kernel, out, scratch, 4, "attend_back",
        query, keyval, doc_row, doc_column, level, mixed, grad_mixed, results,
    )


def gate_unit(first, second):
    root, cube = math.sqrt(2 / math.pi), 0.044715
    square = first * first
    bend = jnp.tanh(root * first * (1 + cube * square))
    lift = 0.5 * (1 + bend)
    slope = lift + 0.5 * first * (1 - bend * bend) * root * (1 + 3 * cube * square)
    gelu = first * lift
    return gelu * second, slope * second, gelu


def run_experts(send, d_out_all, in_matrix, out_matrix, experts):
    count, tokens = lax.axis_size("ctx"), send.shape[0]
    depth, chips, length = count // 4, count // 2, count * tokens
    wide, features, width = send.shape[1], d_out_all.shape[1], out_matrix.shape[0]

    def kernel(
        send_ref, d_out_ref, in_ref, out_ref, returned, results, grad_in, grad_out,
        hidden_all, grad_both, gated_hidden, other_part, other_result, result_from, result_sems,
        *scratch,
    ):
        gather = Gather(hidden_all, tokens, scratch[:3])
        scatter = Scatter(other_part, scratch[3:])
        z, y, c, _ = chip_place()
        expert = lax.axis_index("ctx") // 2
        lane = lax.broadcasted_iota(jnp.int32, (1, 128), 1)
        gather.own()[...] = send_ref[...]
        greet()
        gather.run()

        def chip_rows(chip):
            return pl.ds(pl.multiple_of(chip * 2 * tokens, 16), 2 * tokens)

        def parted(values):
            low, high = values[:tokens], values[tokens:]
            return jnp.where(c == 0, low, high), jnp.where(c == 0, high, low)

        def backward(chip):
            rows = chip_rows(chip)
            carried = hidden_all[rows, features:].astype(jnp.float32)
            mine = (lane == expert) | (lane == expert + experts)
            gate = jnp.sum(jnp.where(mine, carried, 0.0), axis=1, keepdims=True)
            both = jnp.dot(
                hidden_all[rows, :features], in_ref[...], preferred_element_type=jnp.float32
            )
            hidden, by_first, by_second = gate_unit(both[:, :width], both[:, width:])
            gated_hidden[rows, :] = (hidden * gate).astype(jnp.bfloat16)
            grad_hidden = rows_by_rows(d_out_ref[rows, :], out_ref[...])
            grad_gate = jnp.sum(grad_hidden * hidden, axis=1, keepdims=True)
            grad_hidden = grad_hidden * gate
            grad_both[rows, :width] = (grad_hidden * by_first).astype(jnp.bfloat16)
            grad_both[rows, width:] = (grad_hidden * by_second).astype(jnp.bfloat16)
            own, other = parted(rows_by_rows(grad_both[rows, :], in_ref[...]))
            scatter.sums[chip, :, :features] = own.astype(jnp.bfloat16)
            other_part[chip, :, :features] = other.astype(jnp.bfloat16)
            own, other = parted(jnp.where(lane == expert, grad_gate, 0.0))
            scatter.sums[chip, :, features:] = own.astype(jnp.bfloat16)
            other_part[chip, :, features:] = other.astype(jnp.bfloat16)
            scatter.on_core(chip).start()

        @pl.loop(0, depth)
        def _(turn):
            of_z = nearest(depth - 1 - turn)
            backward(of_z * 2 + 1 - y)
            pl.when(turn > 0)(lambda: scatter.add_chip(nearest(depth - turn), False))
            backward(of_z * 2 + y)
            scatter.add_chip(of_z, True)

        scatter.add_chip(nearest(0), False)

        def result_copy(chip):
            target = {"ctx": ctx_of(z, y, 1 - c)}
            return remote(
                other_result.at[chip], result_from.at[chip], result_sems, (chip,), target
            )

        @pl.loop(0, chips)
        def _(chip):
            result = jnp.dot(
                gated_hidden[chip_rows(chip), :], out_ref[...], preferred_element_type=jnp.float32
            )
            own, other = parted(result)
            results[chip] = own.astype(jnp.bfloat16)
            other_result[chip] = other.astype(jnp.bfloat16)
            result_copy(chip).start()

        scatter.add_y_of(nearest(depth - 1))

        @pl.loop(0, features // 512)
        def _(turn):
            at = pl.ds(pl.multiple_of(turn * 512, 512), 512)
            grad_out[:, at] = columns_by_columns(gated_hidden[...], d_out_ref[:, at])

        scatter.add_y_of(nearest(depth - 2))

        @pl.loop(0, features // 256)
        def _(turn):
            at = pl.ds(pl.multiple_of(turn * 256, 256), 256)
            grad_in[at, :] = columns_by_columns(hidden_all[:, at], grad_both[...])

        for k in range(depth - 3, -1, -1):
            scatter.add_y_of(nearest(k))

        @pl.loop(0, chips)
        def _(chip):
            result_copy(chip).wait_recv()
            add_into(results.at[chip], (results.at[chip], result_from.at[chip]), tokens)

        scatter.last(returned)
        scatter.finish()
        for chip in range(chips):
            result_copy(chip).wait_send()

    block = (chips, tokens, features)
    out = [
        jax.ShapeDtypeStruct((tokens, wide), jnp.float32),
        jax.ShapeDtypeStruct(block, jnp.bfloat16),
        jax.ShapeDtypeStruct(in_matrix.shape, jnp.float32),
        jax.ShapeDtypeStruct(out_matrix.shape, jnp.float32),
    ]
    scratch = [
        pltpu.VMEM((length, wide), jnp.bfloat16),
        pltpu.VMEM((length, 2 * width), jnp.bfloat16),
        pltpu.VMEM((length, width), jnp.bfloat16),
        pltpu.VMEM((chips, tokens, wide), jnp.bfloat16),
        pltpu.VMEM(block, jnp.bfloat16),
        pltpu.VMEM(block, jnp.bfloat16),
        pltpu.SemaphoreType.DMA((2, chips)),
    ]
    scratch += Gather.sems(depth) + Scatter.scratch(depth, tokens, wide)
    return call(
        kernel, out, scratch, 3, "experts", send, d_out_all, in_matrix, out_matrix
    )


def rms_back(values, gain_vec, grad):
    scale = lax.rsqrt(jnp.mean(values * values, axis=-1, keepdims=True) + EPSILON)
    through = jnp.mean(gain_vec * grad * values, axis=-1, keepdims=True)
    back = scale * gain_vec * grad - values * scale**3 * through
    return back, jnp.sum(grad * values * scale, axis=0)


def swap_wa(values):
    return jax.tree.map(lambda v: lax.ppermute(v, "wa", ((0, 1), (1, 0))), values)


def gathered_body(
    layer_input, seq_ids, routes, gain_attn, w_query, w_keyval, w_out_attn, gain_ffn, router,
    w_in, w_out, d_out,
):
    me, side = lax.axis_index("ctx"), lax.axis_index("wa")
    tokens = layer_input.shape[1]
    experts = router.shape[1]
    kv_width = KV_HEADS * HEAD_DIM
    half = D // 2
    quarter = w_in.shape[3]

    def halves(values):
        own = lax.dynamic_slice_in_dim(values, side * half, half, values.ndim - 1)
        return own, lax.dynamic_slice_in_dim(values, (1 - side) * half, half, values.ndim - 1)

    def whole(own, there):
        both = jnp.concatenate([own, there], axis=-1), jnp.concatenate([there, own], axis=-1)
        return jnp.where(side == 0, *both)

    small = jnp.concatenate(
        [router.T, gain_attn[None], gain_ffn[None], jnp.zeros((14 - experts, half), jnp.bfloat16)]
    )
    d_out_all, w_query_there, w_keyval_there, w_out_attn_there, small_there = front(
        d_out[0], w_query, w_keyval, w_out_attn, small
    )
    w_in, w_out, small_there = lax.optimization_barrier((w_in, w_out, small_there))
    small = whole(small, small_there).astype(jnp.float32)
    router_rows, gain_one, gain_two = small[:experts], small[experts], small[experts + 1]
    w_in_there, w_out_there = swap_wa((w_in[0], w_out[0]))
    in_matrix = jnp.concatenate([w_in[0, 0], w_in_there[0], w_in[0, 1], w_in_there[1]], axis=1)
    out_matrix = jnp.concatenate([w_out[0], w_out_there], axis=0)

    def onto(values, weight, weight_there):
        own, there = halves(values)
        return jnp.dot(own, weight, preferred_element_type=jnp.float32) + jnp.dot(
            there, weight_there, preferred_element_type=jnp.float32
        )

    residual = layer_input[0].astype(jnp.float32)
    hidden_one = rms_scale(residual, gain_one).astype(jnp.bfloat16)
    hidden_one_own, hidden_one_other = halves(hidden_one)
    hidden_one_there = swap_wa(hidden_one_other)
    positions = me * tokens + jnp.arange(tokens, dtype=jnp.int32)
    angles = angle_table(positions)
    query_pre = onto(hidden_one, w_query, w_query_there)
    keyval_pre = onto(hidden_one, w_keyval, w_keyval_there)
    query = rotate(query_pre.reshape(tokens, HEADS, HEAD_DIM), angles).astype(jnp.bfloat16)
    query = query.reshape(tokens, D)
    keys = rotate(keyval_pre[:, :kv_width].reshape(tokens, KV_HEADS, HEAD_DIM), angles)
    keyval = jnp.concatenate([keys.reshape(tokens, kv_width), keyval_pre[:, kv_width:]], axis=1)
    keyval_all = gather_ctx(keyval.astype(jnp.bfloat16), 2, "gather_kv")
    doc_column = lax.dynamic_slice_in_dim(seq_ids[0], me * tokens, tokens, 0)[:, None]
    mixed, level = attend(query, keyval_all, seq_ids, doc_column)
    mixed_low = mixed.astype(jnp.bfloat16)
    mixed_own, mixed_other = halves(mixed_low)
    mixed_there = swap_wa(mixed_other)
    middle = residual + onto(mixed_low, w_out_attn, w_out_attn_there)

    hidden_two = rms_scale(middle, gain_two).astype(jnp.bfloat16)
    router_low = router_rows.astype(jnp.bfloat16)
    logits = rows_by_rows(hidden_two, router_low)
    numbers = jnp.arange(experts, dtype=jnp.int32)
    chosen = jnp.any(routes[0][:, :, None] == numbers[None, None, :], axis=1)
    masked = jnp.where(chosen, logits, NEGATIVE)
    weights = jnp.exp(masked - jnp.max(masked, axis=1, keepdims=True))
    gates = weights / jnp.sum(weights, axis=1, keepdims=True)
    gates_high = gates.astype(jnp.bfloat16)
    gates_low = (gates - gates_high.astype(jnp.float32)).astype(jnp.bfloat16)
    spare = jnp.zeros((tokens, 128 - 2 * experts), jnp.bfloat16)
    send = jnp.concatenate([hidden_two, gates_high, gates_low, spare], axis=1)
    width = 2 * quarter
    returned, results, grad_in_matrix, grad_out_matrix = run_experts(
        send, d_out_all, in_matrix, out_matrix, experts
    )

    grad_out = d_out[0].astype(jnp.float32)
    grad_gates = returned[:, D : D + experts]
    grad_logits = gates * (grad_gates - jnp.sum(gates * grad_gates, axis=1, keepdims=True))
    grad_logits_low = grad_logits.astype(jnp.bfloat16)
    grad_hidden_two = returned[:, :D] + jnp.dot(
        grad_logits_low, router_low, preferred_element_type=jnp.float32
    )
    grad_router = columns_by_columns(grad_logits_low, hidden_two)
    back_two, grad_gain_two = rms_back(middle, gain_two, grad_hidden_two)
    grad_middle = grad_out + back_two
    grad_middle_low = grad_middle.astype(jnp.bfloat16)
    grad_middle_there = swap_wa(grad_middle_low)
    grad_mixed = whole(
        rows_by_rows(grad_middle_low, w_out_attn), rows_by_rows(grad_middle_low, w_out_attn_there)
    ).astype(jnp.bfloat16)
    grad_query, grad_keyval_own, result_sum = attend_back(
        query, keyval_all, seq_ids, doc_column, level, mixed, grad_mixed, results
    )
    output = (middle + result_sum).astype(jnp.bfloat16)
    grad_query_pre = rotate(grad_query.reshape(tokens, HEADS, HEAD_DIM), -angles)
    grad_query_pre = grad_query_pre.reshape(tokens, D).astype(jnp.bfloat16)
    grad_keys = rotate(
        grad_keyval_own[:, :kv_width].reshape(tokens, KV_HEADS, HEAD_DIM), -angles
    ).reshape(tokens, kv_width)
    grad_keyval_pre = jnp.concatenate([grad_keys, grad_keyval_own[:, kv_width:]], axis=1)
    grad_keyval_pre = grad_keyval_pre.astype(jnp.bfloat16)
    grad_hidden_one = whole(
        rows_by_rows(grad_query_pre, w_query) + rows_by_rows(grad_keyval_pre, w_keyval),
        rows_by_rows(grad_query_pre, w_query_there)
        + rows_by_rows(grad_keyval_pre, w_keyval_there),
    )
    back_one, grad_gain_one = rms_back(residual, gain_one, grad_hidden_one)
    grad_input = (grad_middle + back_one).astype(jnp.bfloat16)

    small_grads = jnp.concatenate(
        [
            grad_router,
            grad_gain_one[None],
            grad_gain_two[None],
            jnp.zeros((14 - experts, D), jnp.float32),
        ]
    )
    attn_sum, query_sum, keyval_sum, small_sum, in_there, out_there = finish(
        hidden_one_own, hidden_one_there, mixed_own, mixed_there, grad_middle_low,
        grad_middle_there, grad_query_pre, grad_keyval_pre, *halves(small_grads),
        jnp.concatenate(
            [grad_in_matrix[:, quarter:width], grad_in_matrix[:, width + quarter :]], axis=1
        ).astype(jnp.bfloat16),
        grad_out_matrix[quarter:].astype(jnp.bfloat16),
    )
    grad_w_in = jnp.stack(
        [
            grad_in_matrix[:, :quarter] + in_there[:, :quarter].astype(jnp.float32),
            grad_in_matrix[:, width : width + quarter]
            + in_there[:, quarter:].astype(jnp.float32),
        ]
    )
    grad_w_out = grad_out_matrix[:quarter] + out_there.astype(jnp.float32)
    return (
        output[None],
        grad_input[None],
        small_sum[experts],
        query_sum.astype(jnp.float32),
        keyval_sum.astype(jnp.float32),
        attn_sum.astype(jnp.float32),
        small_sum[experts + 1],
        small_sum[:experts].T,
        grad_w_in[None],
        grad_w_out[None],
    )


def solution(mesh):
    in_specs = (
        P("wa", "ctx", None),
        P("wa", None),
        P("wa", "ctx", None),
        P("wa"),
        P("wa", None),
        P("wa", None),
        P("wa", None),
        P("wa"),
        P("wa", None),
        P("ctx", None, None, "wa"),
        P("ctx", "wa", None),
        P("wa", "ctx", None),
    )
    out_specs = (
        P("wa", "ctx", None),
        P("wa", "ctx", None),
        P("wa"),
        P("wa", None),
        P("wa", None),
        P("wa", None),
        P("wa"),
        P("wa", None),
        P("ctx", None, None, "wa"),
        P("ctx", "wa", None),
    )
    depth = mesh.shape["ctx"]
    body = gathered_body if depth == 16 else routed_body
    return jax.shard_map(body, mesh=mesh, in_specs=in_specs, out_specs=out_specs, check_vma=False)
```

```python
import functools
import math

import jax
import jax.numpy as jnp
from jax import lax
from jax.experimental import pallas as pl
from jax.experimental.pallas import tpu as pltpu
from jax.sharding import PartitionSpec as P

D = 1536
HEADS = 12
KV_HEADS = 2
HEAD_DIM = 128
TOP = 4
BLOCK = 256


EPSILON = 1e-06
THETA = 1000000.0
NEGATIVE = -1e30


def rms_scale(values, gain_vec):
    return (
        values * lax.rsqrt(jnp.mean(values * values, axis=-1, keepdims=True) + EPSILON) * gain_vec
    )


def rotate(values, angles):
    half_dim = values.shape[-1] // 2
    cosine = jnp.cos(angles)
    sine_part = jnp.sin(angles)
    first_half = values[..., :half_dim]
    second = values[..., half_dim:]
    return jnp.concatenate(
        [first_half * cosine - second * sine_part, second * cosine + first_half * sine_part],
        axis=-1,
    )


def angle_table(positions):
    half_dim = HEAD_DIM // 2
    frequency = THETA ** (-2.0 * jnp.arange(half_dim, dtype=jnp.float32) / HEAD_DIM)
    return (positions.astype(jnp.float32)[:, None] * frequency[None, :])[:, None, :]


def gated(stacked):
    return jax.nn.gelu(stacked[..., 0, :], approximate=True) * stacked[..., 1, :]


def over_keys(key_rows, running, advance):
    key_count = key_rows.shape[0]
    key_width = math.gcd(key_count, 512)

    def one_turn(state_now, block_index):
        key_offset = block_index * key_width
        key_part = lax.dynamic_slice_in_dim(key_rows, key_offset, key_width, 0)
        return (advance(state_now, key_part, key_offset), None)

    running, unused = lax.scan(
        one_turn, running, jnp.arange(key_count // key_width, dtype=jnp.int32)
    )
    return running


def routed_body(
    layer_input,
    seq_ids,
    routes,
    gain_attn,
    w_query,
    w_keyval,
    w_out_attn,
    gain_ffn,
    router,
    w_in,
    w_out,
    d_out,
):
    ctx_count = lax.axis_size("ctx")
    ctx_index = lax.axis_index("ctx")
    tokens = layer_input.shape[1]
    length = tokens * ctx_count
    experts_all = ctx_count // 2
    capacity = 2 * tokens * TOP // experts_all
    group = HEADS // KV_HEADS
    kv_width = KV_HEADS * HEAD_DIM
    row_count = group * tokens
    scale = HEAD_DIM ** (-0.5)
    gain_one, query_matrix, keyvalue_matrix, attention_matrix = (
        lax.all_gather(gain_attn, "wa", axis=0, tiled=True),
        lax.all_gather(w_query, "wa", axis=0, tiled=True),
        lax.all_gather(w_keyval, "wa", axis=0, tiled=True),
        lax.all_gather(w_out_attn, "wa", axis=0, tiled=True),
    )
    residual = layer_input[0].astype(jnp.float32)
    normed_one, norm_one_back = jax.vjp(rms_scale, residual, gain_one.astype(jnp.float32))
    hidden_first_norm = normed_one.astype(jnp.bfloat16)
    positions = ctx_index * tokens + jnp.arange(tokens, dtype=jnp.int32)
    angles = angle_table(positions)
    query_projected = jnp.dot(
        hidden_first_norm, query_matrix, preferred_element_type=jnp.float32
    ).reshape(tokens, HEADS, HEAD_DIM)
    keyvalue_projected = jnp.dot(
        hidden_first_norm, keyvalue_matrix, preferred_element_type=jnp.float32
    )
    key_pre = keyvalue_projected[:, :kv_width].reshape(tokens, KV_HEADS, HEAD_DIM)
    query_low = rotate(query_projected, angles).astype(jnp.bfloat16)
    key_low = rotate(key_pre, angles).astype(jnp.bfloat16)
    value_low = keyvalue_projected[:, kv_width:].astype(jnp.bfloat16)
    keyval_send = jnp.concatenate([key_low.reshape(tokens, kv_width), value_low], axis=1)
    query_rows = (
        query_low.reshape(tokens, KV_HEADS, group, HEAD_DIM)
        .transpose(1, 2, 0, 3)
        .reshape(KV_HEADS, row_count, HEAD_DIM)
    )
    doc_row = seq_ids[0]
    query_docs = lax.dynamic_slice_in_dim(doc_row, ctx_index * tokens, tokens, 0)
    query_blocks = positions // BLOCK

    def block_scores(key_part, first_key):
        key_count = key_part.shape[0]
        split_part = key_part.reshape(key_count, 2, KV_HEADS, HEAD_DIM)
        keys_here = split_part[:, 0]
        values_here = split_part[:, 1]
        scores = (
            jnp.einsum("hrd,nhd->hrn", query_rows, keys_here, preferred_element_type=jnp.float32)
            * scale
        )
        key_docs = lax.dynamic_slice_in_dim(doc_row, first_key, key_count, 0)
        key_blocks = (first_key + jnp.arange(key_count, dtype=jnp.int32)) // BLOCK
        allowed = (query_docs[:, None] == key_docs[None, :]) & (
            key_blocks[None, :] <= query_blocks[:, None]
        )
        allowed = jnp.broadcast_to(allowed[None], (group, tokens, key_count)).reshape(
            1, row_count, key_count
        )
        return (jnp.where(allowed, scores, NEGATIVE), allowed, keys_here, values_here)

    def probs_of(masked, allowed, largest, totals):
        return jnp.where(allowed, jnp.exp(masked - largest[..., None]) / totals[..., None], 0.0)

    def stats_step(running, key_part, first_key):
        largest, totals = running
        masked, allowed, keys_here, values_here = block_scores(key_part, first_key)
        new_largest = jnp.maximum(largest, jnp.max(masked, axis=-1))
        weights = jnp.where(allowed, jnp.exp(masked - new_largest[..., None]), 0.0)
        return (new_largest, totals * jnp.exp(largest - new_largest) + jnp.sum(weights, axis=-1))

    start_stats = (
        jnp.full((KV_HEADS, row_count), NEGATIVE, jnp.float32),
        jnp.zeros((KV_HEADS, row_count), jnp.float32),
    )
    largest, totals = over_keys(
        lax.all_gather(keyval_send, "ctx", axis=0, tiled=True), start_stats, stats_step
    )

    def values_step(running, key_part, first_key):
        masked, allowed, keys_here, values_here = block_scores(key_part, first_key)
        probs_low = probs_of(masked, allowed, largest, totals).astype(jnp.bfloat16)
        return running + jnp.einsum(
            "hrn,nhd->hrd", probs_low, values_here, preferred_element_type=jnp.float32
        )

    start_values = jnp.zeros((KV_HEADS, row_count, HEAD_DIM), jnp.float32)
    mixed_rows = over_keys(
        lax.all_gather(keyval_send, "ctx", axis=0, tiled=True), start_values, values_step
    )
    mixed_low = (
        mixed_rows.reshape(KV_HEADS, group, tokens, HEAD_DIM)
        .transpose(2, 0, 1, 3)
        .reshape(tokens, HEADS * HEAD_DIM)
        .astype(jnp.bfloat16)
    )
    middle_activation = residual + jnp.dot(
        mixed_low, attention_matrix, preferred_element_type=jnp.float32
    )
    gain_two, router_full, w_in_full, w_out_full = (
        lax.all_gather(gain_ffn, "wa", axis=0, tiled=True),
        lax.all_gather(router, "wa", axis=0, tiled=True),
        lax.all_gather(w_in, "wa", axis=3, tiled=True),
        lax.all_gather(w_out, "wa", axis=1, tiled=True),
    )
    in_half = w_in_full[0]
    out_half = w_out_full[0]
    normed_two, norm_two_back = jax.vjp(rms_scale, middle_activation, gain_two.astype(jnp.float32))
    hidden_second_norm = normed_two.astype(jnp.bfloat16)
    router_logits = jnp.dot(hidden_second_norm, router_full, preferred_element_type=jnp.float32)
    route_ids = routes[0]

    def gate_values(logit_rows):
        return jax.nn.softmax(jnp.take_along_axis(logit_rows, route_ids, axis=-1), axis=-1)

    gates, gate_back = jax.vjp(gate_values, router_logits)
    flat_ids = route_ids.reshape(tokens * TOP)
    expert_hits = (flat_ids[:, None] == jnp.arange(experts_all, dtype=jnp.int32)[None, :]).astype(
        jnp.int32
    )
    ranks = jnp.sum(expert_hits * (jnp.cumsum(expert_hits, axis=0) - expert_hits), axis=1)
    slot_first = 2 * flat_ids * capacity + ranks
    slot_second = slot_first + capacity
    slot_total = ctx_count * capacity
    slot_numbers = jnp.arange(slot_total, dtype=jnp.int32)[:, None]
    placed = (
        (slot_first[None, :] == slot_numbers) | (slot_second[None, :] == slot_numbers)
    ).astype(jnp.bfloat16)
    dispatch = jnp.sum(placed.reshape(slot_total, tokens, TOP), axis=2)
    send_rows = (
        jnp.dot(dispatch, hidden_second_norm, preferred_element_type=jnp.float32)
        .astype(jnp.bfloat16)
        .reshape(ctx_count, capacity, D)
    )
    arrived = lax.all_to_all(send_rows, "ctx", split_axis=0, concat_axis=0, tiled=True)
    stacked = jnp.einsum("ncd,gdf->ncgf", arrived, in_half, preferred_element_type=jnp.float32)
    hidden_low = gated(stacked).astype(jnp.bfloat16)
    result = jnp.einsum(
        "ncf,fd->ncd", hidden_low, out_half, preferred_element_type=jnp.float32
    ).astype(jnp.bfloat16)
    returned_rows = lax.all_to_all(result, "ctx", split_axis=0, concat_axis=0, tiled=True)
    returned_flat = returned_rows.reshape(slot_total, D)
    pair_rows = (
        returned_flat[slot_first].astype(jnp.float32)
        + returned_flat[slot_second].astype(jnp.float32)
    ).reshape(tokens, TOP, D)
    output = (middle_activation + jnp.sum(gates[:, :, None] * pair_rows, axis=1)).astype(
        jnp.bfloat16
    )
    grad_out = d_out[0].astype(jnp.float32)
    grad_gates = jnp.sum(pair_rows * grad_out[:, None, :], axis=-1)
    (grad_logits,) = gate_back(grad_gates)
    grad_logits_low = grad_logits.astype(jnp.bfloat16)
    gate_slots = jnp.dot(
        placed.astype(jnp.float32), gates.reshape(tokens * TOP), precision=lax.Precision.HIGHEST
    )
    routed_grad = jnp.dot(dispatch, d_out[0], preferred_element_type=jnp.float32)
    grad_send_rows = (
        (gate_slots[:, None] * routed_grad).astype(jnp.bfloat16).reshape(ctx_count, capacity, D)
    )
    grad_arrived = lax.all_to_all(grad_send_rows, "ctx", split_axis=0, concat_axis=0, tiled=True)
    grad_hidden = jnp.einsum(
        "ncd,fd->ncf", grad_arrived, out_half, preferred_element_type=jnp.float32
    )
    hidden_again, gated_back = jax.vjp(gated, stacked)
    (grad_stacked,) = gated_back(grad_hidden)
    grad_stacked_low = grad_stacked.astype(jnp.bfloat16)
    grad_rows = jnp.einsum(
        "ncgf,gdf->ncd", grad_stacked_low, in_half, preferred_element_type=jnp.float32
    ).astype(jnp.bfloat16)
    grad_returned = lax.all_to_all(grad_rows, "ctx", split_axis=0, concat_axis=0, tiled=True)
    grad_w_in = jnp.einsum(
        "ncd,ncgf->gdf", arrived, grad_stacked_low, preferred_element_type=jnp.float32
    )[None]
    grad_w_out = jnp.einsum(
        "ncf,ncd->fd",
        hidden_again.astype(jnp.bfloat16),
        grad_arrived,
        preferred_element_type=jnp.float32,
    )[None]
    grad_hidden_two = jnp.einsum(
        "st,sd->td",
        dispatch,
        grad_returned.reshape(slot_total, D),
        preferred_element_type=jnp.float32,
    )
    grad_hidden_two = grad_hidden_two + jnp.dot(
        grad_logits_low, router_full.T, preferred_element_type=jnp.float32
    )
    grad_router = jnp.dot(hidden_second_norm.T, grad_logits_low, preferred_element_type=jnp.float32)
    grad_middle_norm, grad_gain_two = norm_two_back(grad_hidden_two)
    grad_middle = grad_out + grad_middle_norm
    grad_middle_low = grad_middle.astype(jnp.bfloat16)
    grad_attn_weight = jnp.dot(mixed_low.T, grad_middle_low, preferred_element_type=jnp.float32)
    grad_mixed = jnp.dot(
        grad_middle_low, attention_matrix.T, preferred_element_type=jnp.float32
    ).astype(jnp.bfloat16)
    grad_rows_out = (
        grad_mixed.reshape(tokens, KV_HEADS, group, HEAD_DIM)
        .transpose(1, 2, 0, 3)
        .reshape(KV_HEADS, row_count, HEAD_DIM)
    )
    delta = jnp.sum(grad_rows_out.astype(jnp.float32) * mixed_rows, axis=-1)

    def score_grads(key_part, first_key):
        masked, allowed, keys_here, values_here = block_scores(key_part, first_key)
        probs = probs_of(masked, allowed, largest, totals)
        grad_probs = jnp.einsum(
            "hrd,nhd->hrn", grad_rows_out, values_here, preferred_element_type=jnp.float32
        )
        grad_scores = (probs * (grad_probs - delta[..., None])).astype(jnp.bfloat16)
        return (grad_scores, probs.astype(jnp.bfloat16), keys_here)

    def key_terms(grad_scores, probs_low, key_count):
        grad_keys = (
            jnp.einsum("hrn,hrd->nhd", grad_scores, query_rows, preferred_element_type=jnp.float32)
            * scale
        )
        grad_values = jnp.einsum(
            "hrn,hrd->nhd", probs_low, grad_rows_out, preferred_element_type=jnp.float32
        )
        return jnp.concatenate(
            [grad_keys.reshape(key_count, kv_width), grad_values.reshape(key_count, kv_width)],
            axis=1,
        )

    start_query = jnp.zeros((KV_HEADS, row_count, HEAD_DIM), jnp.float32)

    def back_step(running, key_part, first_key):
        grad_query_rows, grad_keyvals = running
        grad_scores, probs_low, keys_here = score_grads(key_part, first_key)
        grad_query_rows = (
            grad_query_rows
            + jnp.einsum("hrn,nhd->hrd", grad_scores, keys_here, preferred_element_type=jnp.float32)
            * scale
        )
        fresh = key_terms(grad_scores, probs_low, key_part.shape[0])
        return (grad_query_rows, lax.dynamic_update_slice_in_dim(grad_keyvals, fresh, first_key, 0))

    start_back = (start_query, jnp.zeros((length, 2 * kv_width), jnp.float32))
    grad_query_rows, grad_keyvals = over_keys(
        lax.all_gather(keyval_send, "ctx", axis=0, tiled=True), start_back, back_step
    )
    grad_keyval_mine = lax.psum_scatter(grad_keyvals, "ctx", scatter_dimension=0, tiled=True)
    grad_query = grad_query_rows.reshape(KV_HEADS, group, tokens, HEAD_DIM).transpose(2, 0, 1, 3)
    grad_query_pre = (
        rotate(grad_query.reshape(tokens, HEADS, HEAD_DIM), -angles)
        .reshape(tokens, HEADS * HEAD_DIM)
        .astype(jnp.bfloat16)
    )
    grad_key_pre = rotate(
        grad_keyval_mine[:, :kv_width].reshape(tokens, KV_HEADS, HEAD_DIM), -angles
    ).reshape(tokens, kv_width)
    grad_keyval_pre = jnp.concatenate(
        [grad_key_pre, grad_keyval_mine[:, kv_width:]], axis=1
    ).astype(jnp.bfloat16)
    grad_hidden_one = jnp.dot(
        grad_query_pre, query_matrix.T, preferred_element_type=jnp.float32
    ) + jnp.dot(grad_keyval_pre, keyvalue_matrix.T, preferred_element_type=jnp.float32)
    grad_query_weight = jnp.dot(
        hidden_first_norm.T, grad_query_pre, preferred_element_type=jnp.float32
    )
    grad_keyval_weight = jnp.dot(
        hidden_first_norm.T, grad_keyval_pre, preferred_element_type=jnp.float32
    )
    grad_residual_norm, grad_gain_one = norm_one_back(grad_hidden_one)
    grad_input = (grad_middle + grad_residual_norm).astype(jnp.bfloat16)
    shares = (
        lax.psum_scatter(
            grad_gain_one.astype(jnp.bfloat16), "wa", scatter_dimension=0, tiled=True
        ).astype(jnp.float32),
        lax.psum_scatter(
            grad_query_weight.astype(jnp.bfloat16), "wa", scatter_dimension=0, tiled=True
        ).astype(jnp.float32),
        lax.psum_scatter(
            grad_keyval_weight.astype(jnp.bfloat16), "wa", scatter_dimension=0, tiled=True
        ).astype(jnp.float32),
        lax.psum_scatter(
            grad_attn_weight.astype(jnp.bfloat16), "wa", scatter_dimension=0, tiled=True
        ).astype(jnp.float32),
        lax.psum_scatter(
            grad_gain_two.astype(jnp.bfloat16), "wa", scatter_dimension=0, tiled=True
        ).astype(jnp.float32),
        lax.psum_scatter(
            grad_router.astype(jnp.bfloat16), "wa", scatter_dimension=0, tiled=True
        ).astype(jnp.float32),
        lax.psum_scatter(
            grad_w_in.astype(jnp.bfloat16), "wa", scatter_dimension=3, tiled=True
        ).astype(jnp.float32),
        lax.psum_scatter(
            grad_w_out.astype(jnp.bfloat16), "wa", scatter_dimension=1, tiled=True
        ).astype(jnp.float32),
    )
    summed = lax.psum((shares[0], shares[1], shares[2], shares[3], shares[4], shares[5]), "ctx")
    return (
        output[None],
        grad_input[None],
        summed[0],
        summed[1],
        summed[2],
        summed[3],
        summed[4],
        summed[5],
        shares[6],
        shares[7],
    )

MESH = pl.DeviceIdType.MESH
VMEM_LIMIT = 60 * 1024 * 1024


def chip_place():
    count = lax.axis_size("ctx")
    me = lax.axis_index("ctx")
    return me // 4, lax.rem(me // 2, 2), lax.rem(me, 2), count // 4


def ctx_of(z, y, c):
    return (z * 2 + y) * 2 + c


def greet(across_x=False):
    z, y, c, depth = chip_place()
    barrier = pltpu.get_barrier_semaphore()

    def signal(device):
        pl.semaphore_signal(barrier, 1, device_id=device, device_id_type=MESH)

    signal({"ctx": ctx_of(z, y, 1 - c)})
    signal({"ctx": ctx_of(z, 1 - y, c)})
    if across_x:
        signal({"wa": 1 - lax.axis_index("wa")})
    pl.when(z > 0)(lambda: signal({"ctx": ctx_of(z - 1, y, c)}))
    pl.when(z < depth - 1)(lambda: signal({"ctx": ctx_of(z + 1, y, c)}))
    ends = (z > 0).astype(jnp.int32) + (z < depth - 1).astype(jnp.int32)
    pl.semaphore_wait(barrier, (3 if across_x else 2) + ends)


def remote(source, target_ref, sems, at, device):
    return pltpu.make_async_remote_copy(
        src_ref=source,
        dst_ref=target_ref,
        send_sem=sems.at[(0,) + at],
        recv_sem=sems.at[(1,) + at],
        device_id=device,
        device_id_type=MESH,
    )


def each(step, act):
    z, _, _, depth = chip_place()
    if step == 0:
        act(z)
    else:
        pl.when(z + step < depth)(lambda: act(z + step))
        pl.when(z - step >= 0)(lambda: act(z - step))


def nearest(k):
    z, _, _, depth = chip_place()
    low = jnp.minimum(z, depth - 1 - z)
    step = (k + 1) // 2
    place = jnp.where(k > 2 * low, k, jnp.where(lax.rem(k, 2) == 1, low - step, low + step))
    return jnp.where(z == low, place, depth - 1 - place)


class Gather:
    def __init__(self, out, rows, sems):
        self.out, self.rows = out, rows
        self.z_sems, self.y_sems, self.c_sems = sems
        self.z, self.y, self.c, self.depth = chip_place()

    @staticmethod
    def sems(depth):
        return [
            pltpu.SemaphoreType.DMA((2, 2, depth)),
            pltpu.SemaphoreType.DMA((2, depth)),
            pltpu.SemaphoreType.DMA((2, 2 * depth)),
        ]

    def slot(self, z, y, c):
        return self.out.at[pl.ds(pl.multiple_of(ctx_of(z, y, c) * self.rows, 16), self.rows)]

    def own(self):
        return self.slot(self.z, self.y, self.c)

    def on_z(self, way, of_z, source=None):
        goal = jnp.minimum(self.z + 1, self.depth - 1) if way == 0 else jnp.maximum(self.z - 1, 0)
        block = self.slot(of_z, self.y, self.c)
        target = {"ctx": ctx_of(goal, self.y, self.c)}
        return remote(block if source is None else source, block, self.z_sems, (way, of_z), target)

    def on_y(self, of_z, mine=True, source=None):
        block = self.slot(of_z, self.y if mine else 1 - self.y, self.c)
        target = {"ctx": ctx_of(self.z, 1 - self.y, self.c)}
        return remote(block if source is None else source, block, self.y_sems, (of_z,), target)

    def on_core(self, of_z, of_y, mine=True, source=None):
        block = self.slot(of_z, of_y, self.c if mine else 1 - self.c)
        target = {"ctx": ctx_of(self.z, self.y, 1 - self.c)}
        at = (of_z * 2 + of_y,)
        return remote(block if source is None else source, block, self.c_sems, at, target)

    def start(self, source=None):
        z, depth = self.z, self.depth
        pl.when(z < depth - 1)(lambda: self.on_z(0, z, source).start())
        pl.when(z > 0)(lambda: self.on_z(1, z, source).start())
        self.on_y(z, source=source).start()
        self.on_core(z, self.y, source=source).start()

    def along_z(self, step):
        z, depth = self.z, self.depth

        def from_side(way, of_z, more):
            self.on_z(way, of_z).wait_recv()
            pl.when(more)(lambda: self.on_z(way, of_z).start())
            self.on_y(of_z).start()
            self.on_core(of_z, self.y).start()

        pl.when(z - step >= 0)(lambda: from_side(0, z - step, z < depth - 1))
        pl.when(z + step < depth)(lambda: from_side(1, z + step, z > 0))

    def along_y(self, step):
        def across(of_z):
            self.on_y(of_z, mine=False).wait_recv()
            self.on_core(of_z, 1 - self.y).start()

        each(step, across)

    def finish(self):
        z, depth = self.z, self.depth
        for of_z in range(depth):
            pl.when((z < depth - 1) & (of_z <= z))(lambda: self.on_z(0, of_z).wait_send())
            pl.when((z > 0) & (of_z >= z))(lambda: self.on_z(1, of_z).wait_send())
            self.on_y(of_z).wait_send()
            for of_y in range(2):
                self.on_core(of_z, of_y).wait_send()
                self.on_core(of_z, of_y, mine=False).wait_recv()

    def run(self):
        self.start()
        self.follow()

    def follow(self):
        self.along_z(1)
        self.along_y(0)
        for step in range(1, self.depth):
            if step + 1 < self.depth:
                self.along_z(step + 1)
            self.along_y(step)
        self.finish()


def add_into(target, terms, rows):
    some = 32 if rows % 32 == 0 else 48 if rows % 48 == 0 else 16

    @pl.loop(0, rows // some)
    def _(turn):
        at = pl.ds(pl.multiple_of(turn * some, 16), some)
        total = terms[0][at, :].astype(jnp.float32)
        for term in terms[1:]:
            total = total + term[at, :].astype(jnp.float32)
        target[at, :] = total.astype(target.dtype)


class Scatter:
    def __init__(self, part, scratch, sums=None):
        self.part = part
        self.from_core, self.totals, self.from_y, self.from_z = scratch[:4]
        self.sums = self.totals if sums is None else sums
        self.c_sems, self.y_sems, self.z_sems = scratch[4:]
        self.rows = self.totals.shape[1]
        self.z, self.y, self.c, self.depth = chip_place()

    @staticmethod
    def scratch(depth, rows, columns):
        return [
            pltpu.VMEM((2 * depth, rows, columns), jnp.bfloat16),
            pltpu.VMEM((2 * depth, rows, columns), jnp.bfloat16),
            pltpu.VMEM((depth, rows, columns), jnp.bfloat16),
            pltpu.VMEM((depth + 1, rows, columns), jnp.bfloat16),
            pltpu.SemaphoreType.DMA((2, 2 * depth)),
            pltpu.SemaphoreType.DMA((2, depth)),
            pltpu.SemaphoreType.DMA((2, 2, depth)),
        ]

    def split(self):
        return len(self.part.shape) == 3

    def share(self, chip, c):
        return self.part.at[pl.ds(pl.multiple_of((chip * 2 + c) * self.rows, 16), self.rows)]

    def on_core(self, chip):
        target = {"ctx": ctx_of(self.z, self.y, 1 - self.c)}
        source = self.part.at[chip] if self.split() else self.share(chip, 1 - self.c)
        return remote(source, self.from_core.at[chip], self.c_sems, (chip,), target)

    def on_y(self, of_z):
        target = {"ctx": ctx_of(self.z, 1 - self.y, self.c)}
        source = self.sums.at[of_z * 2 + 1 - self.y]
        return remote(source, self.from_y.at[of_z], self.y_sems, (of_z,), target)

    def on_z(self, way, of_z):
        goal = jnp.minimum(self.z + 1, self.depth - 1) if way == 0 else jnp.maximum(self.z - 1, 0)
        place = of_z if way == 0 else jnp.where(of_z == goal, self.depth, of_z)
        source = self.totals.at[of_z * 2 + self.y]
        target = {"ctx": ctx_of(goal, self.y, self.c)}
        return remote(source, self.from_z.at[place], self.z_sems, (way, of_z), target)

    def start(self):
        def send(of_z):
            self.on_core(of_z * 2 + 1 - self.y).start()
            self.on_core(of_z * 2 + self.y).start()

        for step in range(self.depth - 1, -1, -1):
            each(step, send)

    def add_chip(self, of_z, other, send=True):
        chip = of_z * 2 + (1 - self.y if other else self.y)
        self.on_core(chip).wait_recv()
        own = self.sums.at[chip] if self.split() else self.share(chip, self.c)
        add_into(self.sums.at[chip], (own, self.from_core.at[chip]), self.rows)
        if other and send:
            self.on_y(of_z).start()

    def add_cores(self, step):
        def add(of_z):
            self.add_chip(of_z, True)
            self.add_chip(of_z, False)

        each(step, add)

    def add_y_of(self, of_z):
        z, depth = self.z, self.depth
        self.on_y(of_z).wait_recv()
        place = of_z * 2 + self.y
        total, own, other = self.totals.at[place], self.sums.at[place], self.from_y.at[of_z]
        upward, downward = (of_z > z) & (z > 0), (of_z < z) & (z < depth - 1)
        pl.when(upward)(lambda: self.on_z(0, of_z).wait_recv())
        pl.when(downward)(lambda: self.on_z(1, of_z).wait_recv())

        @pl.when(upward | downward)
        def _():
            add_into(total, (own, other, self.from_z.at[of_z]), self.rows)

        @pl.when(jnp.logical_not(upward | downward))
        def _():
            add_into(total, (own, other), self.rows)

        pl.when(of_z > z)(lambda: self.on_z(0, of_z).start())
        pl.when(of_z < z)(lambda: self.on_z(1, of_z).start())

    def add_y(self, step):
        each(step, self.add_y_of)

    def last(self, result):
        z, depth = self.z, self.depth
        own = self.totals.at[z * 2 + self.y]
        low, high = self.from_z.at[z], self.from_z.at[depth]
        pl.when(z > 0)(lambda: self.on_z(0, z).wait_recv())
        pl.when(z < depth - 1)(lambda: self.on_z(1, z).wait_recv())
        inside = (z > 0) & (z < depth - 1)
        pl.when(inside)(lambda: add_into(result, (own, low, high), self.rows))
        pl.when(z == 0)(lambda: add_into(result, (own, high), self.rows))
        pl.when(z == depth - 1)(lambda: add_into(result, (own, low), self.rows))

    def finish(self, cores=True):
        for of_z in range(self.depth):
            self.on_y(of_z).wait_send()
            if cores:
                self.on_core(of_z * 2).wait_send()
                self.on_core(of_z * 2 + 1).wait_send()
            pl.when(of_z > self.z)(lambda: self.on_z(0, of_z).wait_send())
            pl.when(of_z < self.z)(lambda: self.on_z(1, of_z).wait_send())


def call(kernel, out, scratch, number, name, *operands, outside=(), outside_out=()):
    def spec(position, far):
        return pl.BlockSpec(memory_space=pl.ANY if position in far else pltpu.VMEM)

    many = isinstance(out, (tuple, list))
    out_specs = [spec(i, outside_out) for i in range(len(out) if many else 1)]
    return pl.pallas_call(
        kernel,
        out_shape=out,
        in_specs=[spec(i, outside) for i in range(len(operands))],
        out_specs=out_specs if many else out_specs[0],
        scratch_shapes=scratch,
        compiler_params=pltpu.CompilerParams(
            collective_id=number,
            has_side_effects=number is not None,
            vmem_limit_bytes=VMEM_LIMIT,
        ),
        name=name,
    )(*operands)


class Relay:
    def __init__(self, source, out, sems, parts=1, over_y=False):
        self.source, self.out, self.sems = source, out, sems
        self.z, self.y, self.c, _ = chip_place()
        self.parts, self.over_y = parts, over_y
        self.rows = source.shape[0] // (4 if over_y else 2 * parts)

    @staticmethod
    def semaphores():
        return pltpu.SemaphoreType.DMA((2, 6))

    def block(self, ref, part, y, c):
        place = y * 2 + c if self.over_y else c * self.parts + part
        return ref.at[pl.ds(pl.multiple_of(place * self.rows, 16), self.rows)]

    def on_x(self, part):
        source = self.block(self.source, part, self.y, self.c)
        target = self.block(self.out, part, self.y, self.c)
        return remote(source, target, self.sems, (part,), {"wa": 1 - lax.axis_index("wa")})

    def on_core(self, part, y, c):
        block = self.block(self.out, part, y, c)
        at = (2 + (jnp.where(y == self.y, 0, 1) if self.over_y else part),)
        return remote(block, block, self.sems, at, {"ctx": ctx_of(self.z, self.y, 1 - self.c)})

    def on_y(self, y):
        block = self.block(self.out, 0, y, self.c)
        return remote(block, block, self.sems, (4,), {"ctx": ctx_of(self.z, 1 - self.y, self.c)})

    def start(self):
        for part in range(self.parts):
            self.on_x(part).start()

    def pass_on(self, part=0):
        self.on_x(part).wait_recv()
        if self.over_y:
            self.on_y(self.y).start()
        self.on_core(part, self.y, self.c).start()

    def pass_on_y(self):
        self.on_y(1 - self.y).wait_recv()
        self.on_core(0, 1 - self.y, self.c).start()

    def finish(self):
        for part in range(self.parts):
            self.on_x(part).wait_send()
            self.on_core(part, self.y, self.c).wait_send()
            self.on_core(part, self.y, 1 - self.c).wait_recv()
        if self.over_y:
            self.on_y(self.y).wait_send()
            self.on_core(0, 1 - self.y, self.c).wait_send()
            self.on_core(0, 1 - self.y, 1 - self.c).wait_recv()


def front(d_out, w_query, w_keyval, w_out_attn, small):
    count, rows = lax.axis_size("ctx"), d_out.shape[0]
    depth = count // 4

    def kernel(
        d_out_ref, query_ref, keyval_ref, attn_ref, small_ref,
        d_out_all, query_there, keyval_there, attn_there, small_there, *sems,
    ):
        gather = Gather(d_out_all, rows, sems[:3])
        query_sems, keyval_sems, attn_sems, small_sems, own_sem = sems[3:]
        query = Relay(query_ref, query_there, query_sems, parts=2)
        keyval = Relay(keyval_ref, keyval_there, keyval_sems)
        attn = Relay(attn_ref, attn_there, attn_sems, over_y=True)
        partner = {"wa": 1 - lax.axis_index("wa")}
        swap = remote(small_ref, small_there, small_sems, (0,), partner)
        keep = pltpu.make_async_copy(d_out_ref, gather.own(), own_sem.at[0])
        keep.start()
        greet(across_x=True)
        swap.start()
        attn.start()
        query.start()
        keyval.start()
        gather.start(d_out_ref)
        gather.along_z(1)
        gather.along_y(0)
        gather.along_z(2)
        attn.pass_on()
        gather.along_y(1)
        gather.along_z(3)
        query.pass_on(0)
        gather.along_y(2)
        attn.pass_on_y()
        gather.along_y(3)
        query.pass_on(1)
        keyval.pass_on()
        gather.finish()
        query.finish()
        keyval.finish()
        attn.finish()
        swap.wait()
        keep.wait()

    def like(values):
        return jax.ShapeDtypeStruct(values.shape, values.dtype)

    out = [
        jax.ShapeDtypeStruct((count * rows, d_out.shape[1]), d_out.dtype),
        like(w_query), like(w_keyval), like(w_out_attn), like(small),
    ]
    scratch = Gather.sems(depth) + [Relay.semaphores()] * 3
    scratch += [pltpu.SemaphoreType.DMA((2, 1)), pltpu.SemaphoreType.DMA((1,))]
    every = range(5)
    return call(
        kernel, out, scratch, 0, "front",
        d_out, w_query, w_keyval, w_out_attn, small, outside=every, outside_out=every,
    )


def rows_by_rows(left, right):
    return lax.dot_general(
        left, right, (((1,), (1,)), ((), ())), preferred_element_type=jnp.float32
    )


def columns_by_columns(left, right):
    return lax.dot_general(
        left, right, (((0,), (0,)), ((), ())), preferred_element_type=jnp.float32
    )


def allowed_bias(doc_row, doc_column, tokens):
    keys = doc_row.shape[1]
    query_block = lax.axis_index("ctx") * tokens // BLOCK
    key_block = lax.broadcasted_iota(jnp.int32, (tokens, keys), 1) // BLOCK
    allowed = (doc_row == doc_column) & (key_block <= query_block)
    return jnp.where(allowed, 0.0, NEGATIVE)


def side_columns(own):
    side = lax.axis_index("wa")
    return pl.ds(pl.multiple_of((side if own else 1 - side) * (D // 2), 128), D // 2)


def turned(values, cosine, sine):
    heads = []
    for head in range(values.shape[1] // HEAD_DIM):
        one = values[:, head * HEAD_DIM : (head + 1) * HEAD_DIM]
        heads.append(one * cosine + pltpu.roll(one, HEAD_DIM // 2, axis=1) * sine)
    return jnp.concatenate(heads, axis=1)


def normed(values, gain_vec):
    return values * lax.rsqrt(jnp.mean(values * values, axis=-1, keepdims=True) + EPSILON) * gain_vec


def fill_small(full, small, small_there):
    full[:, side_columns(True)] = small[...].astype(jnp.float32)
    full[:, side_columns(False)] = small_there[...].astype(jnp.float32)


def router_block(full, experts):
    rows = full[:experts]
    spare = jnp.zeros((128 - 2 * experts, rows.shape[1]), jnp.float32)
    return jnp.concatenate([rows, rows, spare], axis=0).astype(jnp.bfloat16)


def attend(x, small, small_there, matrices, angles, docs, chosen, experts):
    count, tokens, features = lax.axis_size("ctx"), x.shape[0], x.shape[1]
    depth, length = count // 4, count * tokens
    kv_columns, half = matrices[2].shape[1], features // 2

    def kernel(
        x_ref, small_ref, small_there_ref, query_own, query_other, keyval_own, keyval_other,
        attn_own, attn_other, cosine_ref, sine_ref, doc_row, doc_column, chosen_ref,
        query, keyval, level, mixed, hidden_own, hidden_there, mixed_own, mixed_there, middle,
        send, gates_out,
        hidden, mixed_low, full, stacked, bias, x_sems, *sems,
    ):
        gather = Gather(keyval, tokens, sems)
        partner = {"wa": 1 - lax.axis_index("wa")}
        fill_small(full, small_ref, small_there_ref)
        residual = x_ref[...].astype(jnp.float32)
        hidden[...] = normed(residual, full[experts : experts + 1]).astype(jnp.bfloat16)
        hidden_own[...] = hidden[:, side_columns(True)]
        own, other = hidden[:, side_columns(True)], hidden[:, side_columns(False)]
        cosine, sine = cosine_ref[...], sine_ref[...]

        def onto(matrix, matrix_other):
            return jnp.dot(own, matrix[...], preferred_element_type=jnp.float32) + jnp.dot(
                other, matrix_other[...], preferred_element_type=jnp.float32
            )

        pre = onto(keyval_own, keyval_other)
        keys = turned(pre[:, : kv_columns // 2], cosine, sine)
        block = jnp.concatenate([keys, pre[:, kv_columns // 2 :]], axis=1)
        gather.own()[...] = block.astype(jnp.bfloat16)
        greet(across_x=True)
        gather.start()
        swap = remote(hidden.at[:, side_columns(False)], hidden_there, x_sems, (0,), partner)
        swap.start()
        query[...] = turned(onto(query_own, query_other), cosine, sine).astype(jnp.bfloat16)
        bias[...] = allowed_bias(doc_row[...], doc_column[...], tokens)
        for head in range(HEADS):
            rows = slice(head * tokens, (head + 1) * tokens)
            stacked[rows, :] = query[:, head * 128 : (head + 1) * 128]
        gather.follow()

        @pl.loop(0, HEADS // 2)
        def _(pair):
            rows = pl.ds(pl.multiple_of(pair * 2 * tokens, 128), 2 * tokens)
            kind = pair // (HEADS // KV_HEADS // 2)
            key_part = keyval[:, pl.ds(pl.multiple_of(kind * 128, 128), 128)]
            val_part = keyval[:, pl.ds(pl.multiple_of(kind * 128 + 256, 128), 128)]
            scores = rows_by_rows(stacked[rows, :], key_part) * HEAD_DIM**-0.5
            scores = (scores.reshape(2, tokens, -1) + bias[...][None]).reshape(scores.shape)
            top = jnp.max(scores, axis=-1, keepdims=True)
            weights = jnp.exp(scores - top)
            total = jnp.sum(weights, axis=-1, keepdims=True)
            probs = (weights / total).astype(jnp.bfloat16)
            mixture = jnp.dot(probs, val_part, preferred_element_type=jnp.float32)
            for part in range(2):
                columns = pl.ds(pl.multiple_of((pair * 2 + part) * 128, 128), 128)
                mixed[:, columns] = mixture[part * tokens : (part + 1) * tokens]
            level[rows, :] = top + jnp.log(total)

        mixed_low[...] = mixed[...].astype(jnp.bfloat16)
        mixed_own[...] = mixed_low[:, side_columns(True)]
        swap_mixed = remote(
            mixed_low.at[:, side_columns(False)], mixed_there, x_sems, (1,), partner
        )
        swap_mixed.start()
        own, other = mixed_low[:, side_columns(True)], mixed_low[:, side_columns(False)]
        middle[...] = residual + onto(attn_own, attn_other)
        hidden_two = normed(middle[...], full[experts + 1 : experts + 2]).astype(jnp.bfloat16)
        send[:, :features] = hidden_two
        logits = rows_by_rows(hidden_two, router_block(full, experts))
        lane = lax.broadcasted_iota(jnp.int32, logits.shape, 1)
        masked = jnp.where(chosen_ref[...] > 0, logits, NEGATIVE)
        weights = jnp.exp(masked - jnp.max(masked, axis=1, keepdims=True))
        total = jnp.sum(jnp.where(lane < experts, weights, 0.0), axis=1, keepdims=True)
        gates = weights / total
        high = gates.astype(jnp.bfloat16).astype(jnp.float32)
        carried = jnp.where(lane < experts, high, jnp.where(lane < 2 * experts, gates - high, 0.0))
        send[:, features:] = carried.astype(jnp.bfloat16)
        gates_out[...] = jnp.where(lane < experts, gates, 0.0)
        swap.wait()
        swap_mixed.wait()

    def shape(rows, columns, kind=jnp.bfloat16):
        return jax.ShapeDtypeStruct((rows, columns), kind)

    wide = features + 128
    out = [
        shape(tokens, features), shape(length, kv_columns), shape(HEADS * tokens, 1, jnp.float32),
        shape(tokens, features, jnp.float32),
        shape(tokens, half), shape(tokens, half), shape(tokens, half), shape(tokens, half),
        shape(tokens, features, jnp.float32), shape(tokens, wide), shape(tokens, 128, jnp.float32),
    ]
    scratch = [
        pltpu.VMEM((tokens, features), jnp.bfloat16),
        pltpu.VMEM((tokens, features), jnp.bfloat16),
        pltpu.VMEM((small.shape[0], features), jnp.float32),
        pltpu.VMEM((HEADS * tokens, HEAD_DIM), jnp.bfloat16),
        pltpu.VMEM((tokens, length), jnp.float32),
        pltpu.SemaphoreType.DMA((2, 2)),
    ] + Gather.sems(depth)
    return call(
        kernel, out, scratch, 2, "attend",
        x, small, small_there, *matrices, *angles, *docs, chosen,
    )


def norm_back(values, gain_vec, grad):
    scale = lax.rsqrt(jnp.mean(values * values, axis=-1, keepdims=True) + EPSILON)
    through = jnp.mean(gain_vec * grad * values, axis=-1, keepdims=True)
    back = scale * gain_vec * grad - values * (scale * scale * scale * through)
    return back, jnp.sum(grad * values * scale, axis=0, keepdims=True)


def attend_back(
    returned, gates, small, small_there, middle, d_out, send, attn_own, attn_other, query, keyval,
    angles, docs, level, mixed, results, experts,
):
    count, tokens, features = lax.axis_size("ctx"), query.shape[0], query.shape[1]
    depth, length, kv_columns = count // 4, keyval.shape[0], keyval.shape[1]

    def kernel(
        returned_ref, gates_ref, small_ref, small_there_ref, middle_ref, d_out_ref, send_ref,
        attn_own_ref, attn_other_ref, query_ref, keyval_ref, cosine_ref, sine_ref, doc_row,
        doc_column, level_ref, mixed_ref, results_ref,
        output, grad_middle, grad_middle_low, grad_middle_there, grad_query, grad_query_there,
        grad_keyval, grad_keyval_there, small_grads,
        full, grad_mixed, turned_query, own_keyval, result_sum, stacked, grads, bias, delta, total,
        part, x_sems, *scratch,
    ):
        result = Scatter(
            None, (None,) + tuple(scratch[:3]) + (None,) + tuple(scratch[3:5]), results_ref
        )
        keyval_sum = Scatter(part, scratch[5:])
        partner = {"wa": 1 - lax.axis_index("wa")}
        swaps = [
            remote(source, target, x_sems, (i,), partner)
            for i, (source, target) in enumerate(
                [(grad_middle_low, grad_middle_there), (grad_query, grad_query_there),
                 (grad_keyval, grad_keyval_there)]
            )
        ]
        greet(across_x=True)
        for k in (depth - 1, depth - 2):
            result.on_y(nearest(k)).start()
        fill_small(full, small_ref, small_there_ref)
        lane = lax.broadcasted_iota(jnp.int32, (tokens, 128), 1)
        gates = gates_ref[...]
        grad_gates = jnp.where(lane < experts, returned_ref[:, features:], 0.0)
        inner = jnp.sum(gates * grad_gates, axis=1, keepdims=True)
        grad_logits = (gates * (grad_gates - inner)).astype(jnp.bfloat16)
        grad_two = returned_ref[:, :features] + jnp.dot(
            grad_logits, router_block(full, experts), preferred_element_type=jnp.float32
        )
        grad_router = columns_by_columns(grad_logits, send_ref[:, :features])
        back, grad_gain = norm_back(middle_ref[...], full[experts + 1 : experts + 2], grad_two)
        grad_middle[...] = d_out_ref[...].astype(jnp.float32) + back
        grad_middle_low[...] = grad_middle[...].astype(jnp.bfloat16)
        swaps[0].start()
        small_grads[:experts] = grad_router[:experts]
        row = lax.broadcasted_iota(jnp.int32, (small_grads.shape[0] - experts, 1), 0)
        small_grads[experts:] = jnp.where(row == 1, grad_gain, 0.0)
        grad_mixed[:, side_columns(True)] = rows_by_rows(
            grad_middle_low[...], attn_own_ref[...]
        ).astype(jnp.bfloat16)
        grad_mixed[:, side_columns(False)] = rows_by_rows(
            grad_middle_low[...], attn_other_ref[...]
        ).astype(jnp.bfloat16)
        bias[...] = allowed_bias(doc_row[...], doc_column[...], tokens)
        total[...] = jnp.zeros_like(total)
        for head in range(HEADS):
            rows = slice(head * tokens, (head + 1) * tokens)
            columns = slice(head * 128, head * 128 + 128)
            stacked[rows, :] = query_ref[:, columns]
            grads[rows, :] = grad_mixed[:, columns]
            delta[rows, :] = jnp.sum(
                grad_mixed[:, columns].astype(jnp.float32) * mixed_ref[:, columns],
                axis=-1,
                keepdims=True,
            )

        @pl.loop(0, HEADS // 2)
        def _(pair):
            rows = pl.ds(pl.multiple_of(pair * 2 * tokens, 128), 2 * tokens)
            kind = pair // (HEADS // KV_HEADS // 2)
            key_columns = pl.ds(pl.multiple_of(kind * 128, 128), 128)
            val_columns = pl.ds(pl.multiple_of(kind * 128 + 256, 128), 128)
            key_part, val_part = keyval_ref[:, key_columns], keyval_ref[:, val_columns]
            own, grad = stacked[rows, :], grads[rows, :]
            scores = rows_by_rows(own, key_part) * HEAD_DIM**-0.5
            scores = (scores.reshape(2, tokens, -1) + bias[...][None]).reshape(scores.shape)
            probs = jnp.exp(scores - level_ref[rows, :])
            grad_probs = rows_by_rows(grad, val_part)
            grad_scores = (probs * (grad_probs - delta[rows, :])).astype(jnp.bfloat16)
            own_grad = jnp.dot(grad_scores, key_part, preferred_element_type=jnp.float32)
            for half in range(2):
                columns = pl.ds(pl.multiple_of((pair * 2 + half) * 128, 128), 128)
                turned_query[:, columns] = (
                    own_grad[half * tokens : (half + 1) * tokens] * HEAD_DIM**-0.5
                )
            total[:, key_columns] += columns_by_columns(grad_scores, own) * HEAD_DIM**-0.5
            total[:, val_columns] += columns_by_columns(probs.astype(jnp.bfloat16), grad)
            pl.when(pair == HEADS // 4)(lambda: result.add_y_of(nearest(depth - 1)))

        part[...] = total[...].astype(jnp.bfloat16)
        keyval_sum.start()
        cosine, sine = cosine_ref[...], -sine_ref[...]
        grad_query[...] = turned(turned_query[...], cosine, sine).astype(jnp.bfloat16)
        swaps[1].start()
        steps = range(depth - 1, -1, -1)
        for step in steps:
            keyval_sum.add_cores(step)
        for k in range(depth - 3, -1, -1):
            result.on_y(nearest(k)).start()
        result.add_y_of(nearest(depth - 2))
        for step in steps:
            keyval_sum.add_y(step)
        keyval_sum.last(own_keyval)
        keys = turned(own_keyval[:, : kv_columns // 2], cosine, sine)
        grad_keyval[...] = jnp.concatenate(
            [keys, own_keyval[:, kv_columns // 2 :]], axis=1
        ).astype(jnp.bfloat16)
        swaps[2].start()
        for k in range(depth - 3, -1, -1):
            result.add_y_of(nearest(k))
        result.last(result_sum)
        output[...] = (middle_ref[...] + result_sum[...]).astype(jnp.bfloat16)
        keyval_sum.finish()
        result.finish(cores=False)
        for swap in swaps:
            swap.wait()

    def shape(like, kind=jnp.bfloat16):
        return jax.ShapeDtypeStruct(like, kind)

    rows, narrow = (tokens, features), (tokens, kv_columns)
    small_shape = (small.shape[0], features)
    out = [
        shape(rows), shape(rows, jnp.float32), shape(rows), shape(rows), shape(rows), shape(rows),
        shape(narrow), shape(narrow), shape(small_shape, jnp.float32),
    ]
    scratch = [
        pltpu.VMEM(small_shape, jnp.float32),
        pltpu.VMEM(rows, jnp.bfloat16),
        pltpu.VMEM(rows, jnp.float32),
        pltpu.VMEM(narrow, jnp.float32),
        pltpu.VMEM(rows, jnp.float32),
        pltpu.VMEM((HEADS * tokens, HEAD_DIM), jnp.bfloat16),
        pltpu.VMEM((HEADS * tokens, HEAD_DIM), jnp.bfloat16),
        pltpu.VMEM((tokens, length), jnp.float32),
        pltpu.VMEM((HEADS * tokens, 1), jnp.float32),
        pltpu.VMEM(keyval.shape, jnp.float32),
        pltpu.VMEM(keyval.shape, jnp.bfloat16),
        pltpu.SemaphoreType.DMA((2, 3)),
    ]
    wide = Scatter.scratch(depth, tokens, features)
    scratch += wide[1:4] + wide[5:] + Scatter.scratch(depth, tokens, kv_columns)
    return call(
        kernel, out, scratch, 4, "attend_back",
        returned, gates, small, small_there, middle, d_out, send, attn_own, attn_other, query,
        keyval, *angles, *docs, level, mixed, results,
    )


def gate_unit(first, second):
    root, cube = math.sqrt(2 / math.pi), 0.044715
    square = first * first
    bend = jnp.tanh(root * first * (1 + cube * square))
    lift = 0.5 * (1 + bend)
    slope = lift + 0.5 * first * (1 - bend * bend) * root * (1 + 3 * cube * square)
    gelu = first * lift
    return gelu * second, slope * second, gelu


def run_experts(send, d_out_all, in_own, out_own, experts):
    count, tokens = lax.axis_size("ctx"), send.shape[0]
    depth, chips, length = count // 4, count // 2, count * tokens
    wide, features = send.shape[1], d_out_all.shape[1]
    quarter = out_own.shape[0]
    width = 2 * quarter

    def kernel(
        send_ref, d_out_ref, in_own_ref, out_own_ref,
        returned, results, grad_in, grad_in_other, grad_out, grad_out_other,
        hidden_all, grad_both, gated_hidden, other_part, other_result, result_from, result_sems,
        in_ref, out_ref, x_sems, *scratch,
    ):
        gather = Gather(hidden_all, tokens, scratch[:3])
        scatter = Scatter(other_part, scratch[3:])
        z, y, c, _ = chip_place()
        expert = lax.axis_index("ctx") // 2
        lane = lax.broadcasted_iota(jnp.int32, (1, 128), 1)
        gather.own()[...] = send_ref[...]
        partner = {"wa": 1 - lax.axis_index("wa")}
        in_there = gated_hidden.at[pl.ds(0, features)]
        swaps = [
            remote(in_own_ref, in_there, x_sems, (0,), partner),
            remote(out_own_ref, out_ref.at[pl.ds(quarter, quarter)], x_sems, (1,), partner),
        ]
        greet(across_x=True)
        for swap in swaps:
            swap.start()
        out_ref[:quarter] = out_own_ref[...]
        gather.run()
        for swap in swaps:
            swap.wait()

        @pl.loop(0, features // 256)
        def _(turn):
            at = pl.ds(pl.multiple_of(turn * 256, 256), 256)
            own, there = in_own_ref[at, :], gated_hidden[at, :]
            in_ref[at, :] = jnp.concatenate(
                [own[:, :quarter], there[:, :quarter], own[:, quarter:], there[:, quarter:]], axis=1
            )

        def chip_rows(chip):
            return pl.ds(pl.multiple_of(chip * 2 * tokens, 16), 2 * tokens)

        def parted(values):
            low, high = values[:tokens], values[tokens:]
            return jnp.where(c == 0, low, high), jnp.where(c == 0, high, low)

        def backward(chip):
            rows = chip_rows(chip)
            carried = hidden_all[rows, features:].astype(jnp.float32)
            mine = (lane == expert) | (lane == expert + experts)
            gate = jnp.sum(jnp.where(mine, carried, 0.0), axis=1, keepdims=True)
            both = jnp.dot(
                hidden_all[rows, :features], in_ref[...], preferred_element_type=jnp.float32
            )
            hidden, by_first, by_second = gate_unit(both[:, :width], both[:, width:])
            gated_hidden[rows, :] = (hidden * gate).astype(jnp.bfloat16)
            grad_hidden = rows_by_rows(d_out_ref[rows, :], out_ref[...])
            grad_gate = jnp.sum(grad_hidden * hidden, axis=1, keepdims=True)
            grad_hidden = grad_hidden * gate
            grad_both[rows, :width] = (grad_hidden * by_first).astype(jnp.bfloat16)
            grad_both[rows, width:] = (grad_hidden * by_second).astype(jnp.bfloat16)
            own, other = parted(rows_by_rows(grad_both[rows, :], in_ref[...]))
            scatter.sums[chip, :, :features] = own.astype(jnp.bfloat16)
            other_part[chip, :, :features] = other.astype(jnp.bfloat16)
            own, other = parted(jnp.where(lane == expert, grad_gate, 0.0))
            scatter.sums[chip, :, features:] = own.astype(jnp.bfloat16)
            other_part[chip, :, features:] = other.astype(jnp.bfloat16)
            scatter.on_core(chip).start()

        @pl.loop(0, depth)
        def _(turn):
            of_z = nearest(depth - 1 - turn)
            backward(of_z * 2 + 1 - y)
            pl.when(turn > 0)(lambda: scatter.add_chip(nearest(depth - turn), False))
            backward(of_z * 2 + y)
            scatter.add_chip(of_z, True)

        scatter.add_chip(nearest(0), False)

        def result_copy(chip):
            target = {"ctx": ctx_of(z, y, 1 - c)}
            return remote(
                other_result.at[chip], result_from.at[chip], result_sems, (chip,), target
            )

        @pl.loop(0, chips)
        def _(chip):
            result = jnp.dot(
                gated_hidden[chip_rows(chip), :], out_ref[...], preferred_element_type=jnp.float32
            )
            own, other = parted(result)
            results[chip] = own.astype(jnp.bfloat16)
            other_result[chip] = other.astype(jnp.bfloat16)
            result_copy(chip).start()

        scatter.add_y_of(nearest(depth - 1))

        @pl.loop(0, features // 512)
        def _(turn):
            at = pl.ds(pl.multiple_of(turn * 512, 512), 512)
            grad = columns_by_columns(gated_hidden[...], d_out_ref[:, at])
            grad_out[:, at] = grad[:quarter]
            grad_out_other[:, at] = grad[quarter:].astype(jnp.bfloat16)

        scatter.add_y_of(nearest(depth - 2))

        @pl.loop(0, features // 256)
        def _(turn):
            at = pl.ds(pl.multiple_of(turn * 256, 256), 256)
            grad = columns_by_columns(hidden_all[:, at], grad_both[...])
            grad_in[at, :] = jnp.concatenate(
                [grad[:, :quarter], grad[:, width : width + quarter]], axis=1
            )
            grad_in_other[at, :] = jnp.concatenate(
                [grad[:, quarter:width], grad[:, width + quarter :]], axis=1
            ).astype(jnp.bfloat16)

        for k in range(depth - 3, -1, -1):
            scatter.add_y_of(nearest(k))

        @pl.loop(0, chips)
        def _(chip):
            result_copy(chip).wait_recv()
            add_into(results.at[chip], (results.at[chip], result_from.at[chip]), tokens)

        scatter.last(returned)
        scatter.finish()
        for chip in range(chips):
            result_copy(chip).wait_send()

    block = (chips, tokens, features)
    out = [
        jax.ShapeDtypeStruct((tokens, wide), jnp.float32),
        jax.ShapeDtypeStruct(block, jnp.bfloat16),
        jax.ShapeDtypeStruct(in_own.shape, jnp.float32),
        jax.ShapeDtypeStruct(in_own.shape, jnp.bfloat16),
        jax.ShapeDtypeStruct(out_own.shape, jnp.float32),
        jax.ShapeDtypeStruct(out_own.shape, jnp.bfloat16),
    ]
    scratch = [
        pltpu.VMEM((length, wide), jnp.bfloat16),
        pltpu.VMEM((length, 2 * width), jnp.bfloat16),
        pltpu.VMEM((length, width), jnp.bfloat16),
        pltpu.VMEM((chips, tokens, wide), jnp.bfloat16),
        pltpu.VMEM(block, jnp.bfloat16),
        pltpu.VMEM(block, jnp.bfloat16),
        pltpu.SemaphoreType.DMA((2, chips)),
        pltpu.VMEM((features, 2 * width), jnp.bfloat16),
        pltpu.VMEM((width, features), jnp.bfloat16),
        pltpu.SemaphoreType.DMA((2, 2)),
    ]
    scratch += Gather.sems(depth) + Scatter.scratch(depth, tokens, wide)
    return call(kernel, out, scratch, 3, "experts", send, d_out_all, in_own, out_own)


def finish(
    x, grad_middle, small, small_there, small_grads, matrices, hidden, mixed, middle, query, keyval,
    expert_in, expert_out,
):
    count, tokens, half = lax.axis_size("ctx"), x.shape[0], x.shape[1] // 2
    depth, rows = count // 4, half // count
    widths = (middle[0].shape[1], query[0].shape[1], keyval[0].shape[1])
    experts = small.shape[0] // 2

    def kernel(
        x_ref, grad_middle_ref, small_ref, small_there_ref, small_grads_ref,
        query_own, query_other, keyval_own, keyval_other,
        hidden_ref, hidden_there, mixed_ref, mixed_there, middle_ref, middle_there,
        query_ref, query_there, keyval_ref, keyval_there, in_ref, out_ref,
        attn_sum, query_sum, keyval_sum, small_sum, grad_input, in_there, out_there,
        attn_part, query_part, keyval_part, pair, full, grad_one, small_mine, small_came, small_all,
        x_sems, *scratch,
    ):
        scatters, gathers = [], []
        parts, sums = (attn_part, query_part, keyval_part), (attn_sum, query_sum, keyval_sum)
        for part, total in zip(parts, sums):
            scatters.append(Scatter(part, scratch[:7]))
            gathers.append(Gather(total, rows, scratch[7:10]))
            scratch = scratch[10:]
        small_out = Gather(small_all, small_came.shape[0], scratch)
        (attn, query_, keyval_), (attn_out, query_out, keyval_out) = scatters, gathers
        partner = {"wa": 1 - lax.axis_index("wa")}
        swaps = [
            remote(source, target, x_sems, (i,), partner)
            for i, (source, target) in enumerate(
                [(small_mine.at[:, side_columns(False)], small_came), (in_ref, in_there),
                 (out_ref, out_there)]
            )
        ]
        steps = range(depth - 1, -1, -1)

        def products(left, left_there, right, right_there, part):
            pair[:tokens] = left[...]
            pair[tokens:] = left_there[...]

            @pl.loop(0, part.shape[1] // 512)
            def _(turn):
                at = pl.ds(pl.multiple_of(turn * 512, 512), 512)
                both = jnp.concatenate([right[:, at], right_there[:, at]], axis=0)
                part[:, at] = columns_by_columns(pair[...], both).astype(jnp.bfloat16)

        products(mixed_ref, mixed_there, middle_ref, middle_there, attn_part)
        greet(across_x=True)
        attn.start()
        products(hidden_ref, hidden_there, query_ref, query_there, query_part)
        for step in steps:
            attn.add_cores(step)
        query_.start()
        swaps[1].start()
        swaps[2].start()
        products(hidden_ref, hidden_there, keyval_ref, keyval_there, keyval_part)
        keyval_.start()
        for step in steps:
            query_.add_cores(step)
        attn.add_y(depth - 1)
        fill_small(full, small_ref, small_there_ref)
        grad_one[:, side_columns(True)] = rows_by_rows(
            query_ref[...], query_own[...]
        ) + rows_by_rows(keyval_ref[...], keyval_own[...])
        attn.add_y(depth - 2)
        grad_one[:, side_columns(False)] = rows_by_rows(
            query_ref[...], query_other[...]
        ) + rows_by_rows(keyval_ref[...], keyval_other[...])
        back, grad_gain = norm_back(
            x_ref[...].astype(jnp.float32), full[experts : experts + 1], grad_one[...]
        )
        grad_input[...] = (grad_middle_ref[...] + back).astype(jnp.bfloat16)
        row = lax.broadcasted_iota(jnp.int32, (small_mine.shape[0], 1), 0)
        small_mine[...] = jnp.where(row == experts, grad_gain, small_grads_ref[...])
        swaps[0].start()
        for step in range(depth - 3, -1, -1):
            attn.add_y(step)
        for step in steps:
            keyval_.add_cores(step)
        attn.last(attn_out.own())
        attn_out.start()
        swaps[0].wait()
        small_out.own()[...] = (small_mine[:, side_columns(True)] + small_came[...]).astype(
            jnp.bfloat16
        )
        small_out.start()
        for step in steps:
            query_.add_y(step)
        attn_out.along_z(1)
        query_.last(query_out.own())
        query_out.start()
        attn_out.along_z(2)
        attn_out.along_y(0)
        small_out.along_z(1)
        for step in steps:
            keyval_.add_y(step)
        attn_out.along_z(3)
        attn_out.along_y(1)
        keyval_.last(keyval_out.own())
        keyval_out.start()
        query_out.along_z(1)
        small_out.along_z(2)
        attn_out.along_y(2)
        query_out.along_z(2)
        small_out.along_z(3)
        query_out.along_y(0)
        keyval_out.along_z(1)
        query_out.along_z(3)
        attn_out.along_y(3)
        keyval_out.along_z(2)
        query_out.along_y(1)
        keyval_out.along_z(3)
        query_out.along_y(2)
        small_out.along_y(0)
        keyval_out.along_y(0)
        small_out.along_y(1)
        query_out.along_y(3)
        keyval_out.along_y(1)
        small_out.along_y(2)
        keyval_out.along_y(2)
        small_out.along_y(3)
        keyval_out.along_y(3)
        for one in [small_out] + gathers + scatters:
            one.finish()
        small_rows = small_came.shape[0]
        total = small_all[:small_rows].astype(jnp.float32)
        for device in range(1, count):
            rows_of = slice(device * small_rows, (device + 1) * small_rows)
            total = total + small_all[rows_of].astype(jnp.float32)
        small_sum[...] = total
        swaps[1].wait()
        swaps[2].wait()

    small_shape = (small.shape[0], half)
    out = [jax.ShapeDtypeStruct((half, width), jnp.bfloat16) for width in widths]
    out += [
        jax.ShapeDtypeStruct(small_shape, jnp.float32),
        jax.ShapeDtypeStruct(x.shape, jnp.bfloat16),
        jax.ShapeDtypeStruct(expert_in.shape, expert_in.dtype),
        jax.ShapeDtypeStruct(expert_out.shape, expert_out.dtype),
    ]
    scratch = [pltpu.VMEM((half, width), jnp.bfloat16) for width in widths]
    scratch += [
        pltpu.VMEM((2 * tokens, half), jnp.bfloat16),
        pltpu.VMEM(small_grads.shape, jnp.float32),
        pltpu.VMEM(x.shape, jnp.float32),
        pltpu.VMEM(small_grads.shape, jnp.float32),
        pltpu.VMEM(small_shape, jnp.float32),
        pltpu.VMEM((count * small.shape[0], half), jnp.bfloat16),
        pltpu.SemaphoreType.DMA((2, 3)),
    ]
    for width in widths:
        scratch += Scatter.scratch(depth, rows, width) + Gather.sems(depth)
    scratch += Gather.sems(depth)
    return call(
        kernel, out, scratch, 1, "finish",
        x, grad_middle, small, small_there, small_grads, *matrices, *hidden, *mixed, *middle,
        *query, *keyval, expert_in, expert_out, outside=(19, 20), outside_out=(5, 6),
    )


def widen(query, keyval, attn, grad_in, in_there, grad_out, out_there):
    half, quarter, features = query.shape[0], grad_out.shape[0], grad_out.shape[1]
    steps = 4

    def kernel(*refs):
        query_ref, keyval_ref, attn_ref, in_ref, in_there_ref, out_ref, out_there_ref = refs[:7]
        query_out, keyval_out, attn_out, in_out, out_out = refs[7:]
        query_out[...] = query_ref[...].astype(jnp.float32)
        keyval_out[...] = keyval_ref[...].astype(jnp.float32)
        attn_out[...] = attn_ref[...].astype(jnp.float32)
        both = in_ref[...] + in_there_ref[...].astype(jnp.float32)
        in_out[0, 0] = both[:, :quarter]
        in_out[0, 1] = both[:, quarter:]
        out_out[0] = out_ref[...] + out_there_ref[...].astype(jnp.float32)

    def rows(values):
        return pl.BlockSpec((values.shape[0] // steps, values.shape[1]), lambda i: (i, 0))

    operands = (query, keyval, attn, grad_in, in_there, grad_out, out_there)
    return pl.pallas_call(
        kernel,
        grid=(steps,),
        out_shape=[
            jax.ShapeDtypeStruct(query.shape, jnp.float32),
            jax.ShapeDtypeStruct(keyval.shape, jnp.float32),
            jax.ShapeDtypeStruct(attn.shape, jnp.float32),
            jax.ShapeDtypeStruct((1, 2, features, quarter), jnp.float32),
            jax.ShapeDtypeStruct((1, quarter, features), jnp.float32),
        ],
        in_specs=[rows(values) for values in operands],
        out_specs=[
            rows(query), rows(keyval), rows(attn),
            pl.BlockSpec((1, 2, features // steps, quarter), lambda i: (0, 0, i, 0)),
            pl.BlockSpec((1, quarter // steps, features), lambda i: (0, i, 0)),
        ],
        compiler_params=pltpu.CompilerParams(vmem_limit_bytes=VMEM_LIMIT),
        name="widen",
    )(*operands)


def gathered_body(
    layer_input, seq_ids, routes, gain_attn, w_query, w_keyval, w_out_attn, gain_ffn, router,
    w_in, w_out, d_out,
):
    me = lax.axis_index("ctx")
    tokens, experts = layer_input.shape[1], router.shape[1]
    x, grad_out = layer_input[0], d_out[0]
    small = jnp.concatenate(
        [router.T, gain_attn[None], gain_ffn[None], jnp.zeros((experts - 2, D // 2), jnp.bfloat16)]
    )
    turns = angle_table(me * tokens + jnp.arange(tokens, dtype=jnp.int32))[:, 0]
    cosine, sine = jnp.cos(turns), jnp.sin(turns)
    angles = (
        jnp.concatenate([cosine, cosine], axis=1), jnp.concatenate([-sine, sine], axis=1)
    )
    docs = (seq_ids, lax.dynamic_slice_in_dim(seq_ids[0], me * tokens, tokens, 0)[:, None])
    numbers = jnp.arange(128, dtype=jnp.int32)
    named = jnp.any(routes[0][:, :, None] == (numbers % experts)[None, None, :], axis=1)
    chosen = (named & (numbers < 2 * experts)[None, :]).astype(jnp.float32)
    in_own = jnp.concatenate([w_in[0, 0], w_in[0, 1]], axis=1)

    d_out_all, w_query_there, w_keyval_there, w_out_attn_there, small_there = front(
        grad_out, w_query, w_keyval, w_out_attn, small
    )
    projections = (w_query, w_query_there, w_keyval, w_keyval_there)
    (
        query, keyval, level, mixed, hidden_own, hidden_there, mixed_own, mixed_there, middle,
        send, gates,
    ) = attend(
        x, small, small_there, projections + (w_out_attn, w_out_attn_there), angles, docs, chosen,
        experts,
    )
    returned, results, grad_in, grad_in_other, grad_out_matrix, grad_out_other = run_experts(
        send, d_out_all, in_own, w_out[0], experts
    )
    (
        output, grad_middle, middle_low, middle_there, grad_query, query_there, grad_keyval,
        keyval_there, small_grads,
    ) = attend_back(
        returned, gates, small, small_there, middle, grad_out, send, w_out_attn, w_out_attn_there,
        query, keyval, angles, docs, level, mixed, results, experts,
    )
    attn_sum, query_sum, keyval_sum, small_sum, grad_input, in_there, out_there = finish(
        x, grad_middle, small, small_there, small_grads, projections, (hidden_own, hidden_there),
        (mixed_own, mixed_there), (middle_low, middle_there), (grad_query, query_there),
        (grad_keyval, keyval_there), grad_in_other, grad_out_other,
    )
    query_sum, keyval_sum, attn_sum, grad_w_in, grad_w_out = widen(
        query_sum, keyval_sum, attn_sum, grad_in, in_there, grad_out_matrix, out_there
    )
    return (
        output[None],
        grad_input[None],
        small_sum[experts],
        query_sum,
        keyval_sum,
        attn_sum,
        small_sum[experts + 1],
        small_sum[:experts].T,
        grad_w_in,
        grad_w_out,
    )


def solution(mesh):
    in_specs = (
        P("wa", "ctx", None),
        P("wa", None),
        P("wa", "ctx", None),
        P("wa"),
        P("wa", None),
        P("wa", None),
        P("wa", None),
        P("wa"),
        P("wa", None),
        P("ctx", None, None, "wa"),
        P("ctx", "wa", None),
        P("wa", "ctx", None),
    )
    out_specs = (
        P("wa", "ctx", None),
        P("wa", "ctx", None),
        P("wa"),
        P("wa", None),
        P("wa", None),
        P("wa", None),
        P("wa"),
        P("wa", None),
        P("ctx", None, None, "wa"),
        P("ctx", "wa", None),
    )
    depth = mesh.shape["ctx"]
    body = gathered_body if depth == 16 else routed_body
    return jax.shard_map(body, mesh=mesh, in_specs=in_specs, out_specs=out_specs, check_vma=False)
```

```python
import functools
import math

import jax
import jax.numpy as jnp
from jax import lax
from jax.experimental import pallas as pl
from jax.experimental.pallas import tpu as pltpu
from jax.sharding import PartitionSpec as P

D = 1536
HEADS = 12
KV_HEADS = 2
HEAD_DIM = 128
TOP = 4
BLOCK = 256


EPSILON = 1e-06
THETA = 1000000.0
NEGATIVE = -1e30


def rms_scale(values, gain_vec):
    return (
        values * lax.rsqrt(jnp.mean(values * values, axis=-1, keepdims=True) + EPSILON) * gain_vec
    )


def rotate(values, angles):
    half_dim = values.shape[-1] // 2
    cosine = jnp.cos(angles)
    sine_part = jnp.sin(angles)
    first_half = values[..., :half_dim]
    second = values[..., half_dim:]
    return jnp.concatenate(
        [first_half * cosine - second * sine_part, second * cosine + first_half * sine_part],
        axis=-1,
    )


def angle_table(positions):
    half_dim = HEAD_DIM // 2
    frequency = THETA ** (-2.0 * jnp.arange(half_dim, dtype=jnp.float32) / HEAD_DIM)
    return (positions.astype(jnp.float32)[:, None] * frequency[None, :])[:, None, :]


def gated(stacked):
    return jax.nn.gelu(stacked[..., 0, :], approximate=True) * stacked[..., 1, :]


def over_keys(key_rows, running, advance):
    key_count = key_rows.shape[0]
    key_width = math.gcd(key_count, 512)

    def one_turn(state_now, block_index):
        key_offset = block_index * key_width
        key_part = lax.dynamic_slice_in_dim(key_rows, key_offset, key_width, 0)
        return (advance(state_now, key_part, key_offset), None)

    running, unused = lax.scan(
        one_turn, running, jnp.arange(key_count // key_width, dtype=jnp.int32)
    )
    return running


def routed_body(
    layer_input,
    seq_ids,
    routes,
    gain_attn,
    w_query,
    w_keyval,
    w_out_attn,
    gain_ffn,
    router,
    w_in,
    w_out,
    d_out,
):
    ctx_count = lax.axis_size("ctx")
    ctx_index = lax.axis_index("ctx")
    tokens = layer_input.shape[1]
    length = tokens * ctx_count
    experts_all = ctx_count // 2
    capacity = 2 * tokens * TOP // experts_all
    group = HEADS // KV_HEADS
    kv_width = KV_HEADS * HEAD_DIM
    row_count = group * tokens
    scale = HEAD_DIM ** (-0.5)
    gain_one, query_matrix, keyvalue_matrix, attention_matrix = (
        lax.all_gather(gain_attn, "wa", axis=0, tiled=True),
        lax.all_gather(w_query, "wa", axis=0, tiled=True),
        lax.all_gather(w_keyval, "wa", axis=0, tiled=True),
        lax.all_gather(w_out_attn, "wa", axis=0, tiled=True),
    )
    residual = layer_input[0].astype(jnp.float32)
    normed_one, norm_one_back = jax.vjp(rms_scale, residual, gain_one.astype(jnp.float32))
    hidden_first_norm = normed_one.astype(jnp.bfloat16)
    positions = ctx_index * tokens + jnp.arange(tokens, dtype=jnp.int32)
    angles = angle_table(positions)
    query_projected = jnp.dot(
        hidden_first_norm, query_matrix, preferred_element_type=jnp.float32
    ).reshape(tokens, HEADS, HEAD_DIM)
    keyvalue_projected = jnp.dot(
        hidden_first_norm, keyvalue_matrix, preferred_element_type=jnp.float32
    )
    key_pre = keyvalue_projected[:, :kv_width].reshape(tokens, KV_HEADS, HEAD_DIM)
    query_low = rotate(query_projected, angles).astype(jnp.bfloat16)
    key_low = rotate(key_pre, angles).astype(jnp.bfloat16)
    value_low = keyvalue_projected[:, kv_width:].astype(jnp.bfloat16)
    keyval_send = jnp.concatenate([key_low.reshape(tokens, kv_width), value_low], axis=1)
    query_rows = (
        query_low.reshape(tokens, KV_HEADS, group, HEAD_DIM)
        .transpose(1, 2, 0, 3)
        .reshape(KV_HEADS, row_count, HEAD_DIM)
    )
    doc_row = seq_ids[0]
    query_docs = lax.dynamic_slice_in_dim(doc_row, ctx_index * tokens, tokens, 0)
    query_blocks = positions // BLOCK

    def block_scores(key_part, first_key):
        key_count = key_part.shape[0]
        split_part = key_part.reshape(key_count, 2, KV_HEADS, HEAD_DIM)
        keys_here = split_part[:, 0]
        values_here = split_part[:, 1]
        scores = (
            jnp.einsum("hrd,nhd->hrn", query_rows, keys_here, preferred_element_type=jnp.float32)
            * scale
        )
        key_docs = lax.dynamic_slice_in_dim(doc_row, first_key, key_count, 0)
        key_blocks = (first_key + jnp.arange(key_count, dtype=jnp.int32)) // BLOCK
        allowed = (query_docs[:, None] == key_docs[None, :]) & (
            key_blocks[None, :] <= query_blocks[:, None]
        )
        allowed = jnp.broadcast_to(allowed[None], (group, tokens, key_count)).reshape(
            1, row_count, key_count
        )
        return (jnp.where(allowed, scores, NEGATIVE), allowed, keys_here, values_here)

    def probs_of(masked, allowed, largest, totals):
        return jnp.where(allowed, jnp.exp(masked - largest[..., None]) / totals[..., None], 0.0)

    def stats_step(running, key_part, first_key):
        largest, totals = running
        masked, allowed, keys_here, values_here = block_scores(key_part, first_key)
        new_largest = jnp.maximum(largest, jnp.max(masked, axis=-1))
        weights = jnp.where(allowed, jnp.exp(masked - new_largest[..., None]), 0.0)
        return (new_largest, totals * jnp.exp(largest - new_largest) + jnp.sum(weights, axis=-1))

    start_stats = (
        jnp.full((KV_HEADS, row_count), NEGATIVE, jnp.float32),
        jnp.zeros((KV_HEADS, row_count), jnp.float32),
    )
    largest, totals = over_keys(
        lax.all_gather(keyval_send, "ctx", axis=0, tiled=True), start_stats, stats_step
    )

    def values_step(running, key_part, first_key):
        masked, allowed, keys_here, values_here = block_scores(key_part, first_key)
        probs_low = probs_of(masked, allowed, largest, totals).astype(jnp.bfloat16)
        return running + jnp.einsum(
            "hrn,nhd->hrd", probs_low, values_here, preferred_element_type=jnp.float32
        )

    start_values = jnp.zeros((KV_HEADS, row_count, HEAD_DIM), jnp.float32)
    mixed_rows = over_keys(
        lax.all_gather(keyval_send, "ctx", axis=0, tiled=True), start_values, values_step
    )
    mixed_low = (
        mixed_rows.reshape(KV_HEADS, group, tokens, HEAD_DIM)
        .transpose(2, 0, 1, 3)
        .reshape(tokens, HEADS * HEAD_DIM)
        .astype(jnp.bfloat16)
    )
    middle_activation = residual + jnp.dot(
        mixed_low, attention_matrix, preferred_element_type=jnp.float32
    )
    gain_two, router_full, w_in_full, w_out_full = (
        lax.all_gather(gain_ffn, "wa", axis=0, tiled=True),
        lax.all_gather(router, "wa", axis=0, tiled=True),
        lax.all_gather(w_in, "wa", axis=3, tiled=True),
        lax.all_gather(w_out, "wa", axis=1, tiled=True),
    )
    in_half = w_in_full[0]
    out_half = w_out_full[0]
    normed_two, norm_two_back = jax.vjp(rms_scale, middle_activation, gain_two.astype(jnp.float32))
    hidden_second_norm = normed_two.astype(jnp.bfloat16)
    router_logits = jnp.dot(hidden_second_norm, router_full, preferred_element_type=jnp.float32)
    route_ids = routes[0]

    def gate_values(logit_rows):
        return jax.nn.softmax(jnp.take_along_axis(logit_rows, route_ids, axis=-1), axis=-1)

    gates, gate_back = jax.vjp(gate_values, router_logits)
    flat_ids = route_ids.reshape(tokens * TOP)
    expert_hits = (flat_ids[:, None] == jnp.arange(experts_all, dtype=jnp.int32)[None, :]).astype(
        jnp.int32
    )
    ranks = jnp.sum(expert_hits * (jnp.cumsum(expert_hits, axis=0) - expert_hits), axis=1)
    slot_first = 2 * flat_ids * capacity + ranks
    slot_second = slot_first + capacity
    slot_total = ctx_count * capacity
    slot_numbers = jnp.arange(slot_total, dtype=jnp.int32)[:, None]
    placed = (
        (slot_first[None, :] == slot_numbers) | (slot_second[None, :] == slot_numbers)
    ).astype(jnp.bfloat16)
    dispatch = jnp.sum(placed.reshape(slot_total, tokens, TOP), axis=2)
    send_rows = (
        jnp.dot(dispatch, hidden_second_norm, preferred_element_type=jnp.float32)
        .astype(jnp.bfloat16)
        .reshape(ctx_count, capacity, D)
    )
    arrived = lax.all_to_all(send_rows, "ctx", split_axis=0, concat_axis=0, tiled=True)
    stacked = jnp.einsum("ncd,gdf->ncgf", arrived, in_half, preferred_element_type=jnp.float32)
    hidden_low = gated(stacked).astype(jnp.bfloat16)
    result = jnp.einsum(
        "ncf,fd->ncd", hidden_low, out_half, preferred_element_type=jnp.float32
    ).astype(jnp.bfloat16)
    returned_rows = lax.all_to_all(result, "ctx", split_axis=0, concat_axis=0, tiled=True)
    returned_flat = returned_rows.reshape(slot_total, D)
    pair_rows = (
        returned_flat[slot_first].astype(jnp.float32)
        + returned_flat[slot_second].astype(jnp.float32)
    ).reshape(tokens, TOP, D)
    output = (middle_activation + jnp.sum(gates[:, :, None] * pair_rows, axis=1)).astype(
        jnp.bfloat16
    )
    grad_out = d_out[0].astype(jnp.float32)
    grad_gates = jnp.sum(pair_rows * grad_out[:, None, :], axis=-1)
    (grad_logits,) = gate_back(grad_gates)
    grad_logits_low = grad_logits.astype(jnp.bfloat16)
    gate_slots = jnp.dot(
        placed.astype(jnp.float32), gates.reshape(tokens * TOP), precision=lax.Precision.HIGHEST
    )
    routed_grad = jnp.dot(dispatch, d_out[0], preferred_element_type=jnp.float32)
    grad_send_rows = (
        (gate_slots[:, None] * routed_grad).astype(jnp.bfloat16).reshape(ctx_count, capacity, D)
    )
    grad_arrived = lax.all_to_all(grad_send_rows, "ctx", split_axis=0, concat_axis=0, tiled=True)
    grad_hidden = jnp.einsum(
        "ncd,fd->ncf", grad_arrived, out_half, preferred_element_type=jnp.float32
    )
    hidden_again, gated_back = jax.vjp(gated, stacked)
    (grad_stacked,) = gated_back(grad_hidden)
    grad_stacked_low = grad_stacked.astype(jnp.bfloat16)
    grad_rows = jnp.einsum(
        "ncgf,gdf->ncd", grad_stacked_low, in_half, preferred_element_type=jnp.float32
    ).astype(jnp.bfloat16)
    grad_returned = lax.all_to_all(grad_rows, "ctx", split_axis=0, concat_axis=0, tiled=True)
    grad_w_in = jnp.einsum(
        "ncd,ncgf->gdf", arrived, grad_stacked_low, preferred_element_type=jnp.float32
    )[None]
    grad_w_out = jnp.einsum(
        "ncf,ncd->fd",
        hidden_again.astype(jnp.bfloat16),
        grad_arrived,
        preferred_element_type=jnp.float32,
    )[None]
    grad_hidden_two = jnp.einsum(
        "st,sd->td",
        dispatch,
        grad_returned.reshape(slot_total, D),
        preferred_element_type=jnp.float32,
    )
    grad_hidden_two = grad_hidden_two + jnp.dot(
        grad_logits_low, router_full.T, preferred_element_type=jnp.float32
    )
    grad_router = jnp.dot(hidden_second_norm.T, grad_logits_low, preferred_element_type=jnp.float32)
    grad_middle_norm, grad_gain_two = norm_two_back(grad_hidden_two)
    grad_middle = grad_out + grad_middle_norm
    grad_middle_low = grad_middle.astype(jnp.bfloat16)
    grad_attn_weight = jnp.dot(mixed_low.T, grad_middle_low, preferred_element_type=jnp.float32)
    grad_mixed = jnp.dot(
        grad_middle_low, attention_matrix.T, preferred_element_type=jnp.float32
    ).astype(jnp.bfloat16)
    grad_rows_out = (
        grad_mixed.reshape(tokens, KV_HEADS, group, HEAD_DIM)
        .transpose(1, 2, 0, 3)
        .reshape(KV_HEADS, row_count, HEAD_DIM)
    )
    delta = jnp.sum(grad_rows_out.astype(jnp.float32) * mixed_rows, axis=-1)

    def score_grads(key_part, first_key):
        masked, allowed, keys_here, values_here = block_scores(key_part, first_key)
        probs = probs_of(masked, allowed, largest, totals)
        grad_probs = jnp.einsum(
            "hrd,nhd->hrn", grad_rows_out, values_here, preferred_element_type=jnp.float32
        )
        grad_scores = (probs * (grad_probs - delta[..., None])).astype(jnp.bfloat16)
        return (grad_scores, probs.astype(jnp.bfloat16), keys_here)

    def key_terms(grad_scores, probs_low, key_count):
        grad_keys = (
            jnp.einsum("hrn,hrd->nhd", grad_scores, query_rows, preferred_element_type=jnp.float32)
            * scale
        )
        grad_values = jnp.einsum(
            "hrn,hrd->nhd", probs_low, grad_rows_out, preferred_element_type=jnp.float32
        )
        return jnp.concatenate(
            [grad_keys.reshape(key_count, kv_width), grad_values.reshape(key_count, kv_width)],
            axis=1,
        )

    start_query = jnp.zeros((KV_HEADS, row_count, HEAD_DIM), jnp.float32)

    def back_step(running, key_part, first_key):
        grad_query_rows, grad_keyvals = running
        grad_scores, probs_low, keys_here = score_grads(key_part, first_key)
        grad_query_rows = (
            grad_query_rows
            + jnp.einsum("hrn,nhd->hrd", grad_scores, keys_here, preferred_element_type=jnp.float32)
            * scale
        )
        fresh = key_terms(grad_scores, probs_low, key_part.shape[0])
        return (grad_query_rows, lax.dynamic_update_slice_in_dim(grad_keyvals, fresh, first_key, 0))

    start_back = (start_query, jnp.zeros((length, 2 * kv_width), jnp.float32))
    grad_query_rows, grad_keyvals = over_keys(
        lax.all_gather(keyval_send, "ctx", axis=0, tiled=True), start_back, back_step
    )
    grad_keyval_mine = lax.psum_scatter(grad_keyvals, "ctx", scatter_dimension=0, tiled=True)
    grad_query = grad_query_rows.reshape(KV_HEADS, group, tokens, HEAD_DIM).transpose(2, 0, 1, 3)
    grad_query_pre = (
        rotate(grad_query.reshape(tokens, HEADS, HEAD_DIM), -angles)
        .reshape(tokens, HEADS * HEAD_DIM)
        .astype(jnp.bfloat16)
    )
    grad_key_pre = rotate(
        grad_keyval_mine[:, :kv_width].reshape(tokens, KV_HEADS, HEAD_DIM), -angles
    ).reshape(tokens, kv_width)
    grad_keyval_pre = jnp.concatenate(
        [grad_key_pre, grad_keyval_mine[:, kv_width:]], axis=1
    ).astype(jnp.bfloat16)
    grad_hidden_one = jnp.dot(
        grad_query_pre, query_matrix.T, preferred_element_type=jnp.float32
    ) + jnp.dot(grad_keyval_pre, keyvalue_matrix.T, preferred_element_type=jnp.float32)
    grad_query_weight = jnp.dot(
        hidden_first_norm.T, grad_query_pre, preferred_element_type=jnp.float32
    )
    grad_keyval_weight = jnp.dot(
        hidden_first_norm.T, grad_keyval_pre, preferred_element_type=jnp.float32
    )
    grad_residual_norm, grad_gain_one = norm_one_back(grad_hidden_one)
    grad_input = (grad_middle + grad_residual_norm).astype(jnp.bfloat16)
    shares = (
        lax.psum_scatter(
            grad_gain_one.astype(jnp.bfloat16), "wa", scatter_dimension=0, tiled=True
        ).astype(jnp.float32),
        lax.psum_scatter(
            grad_query_weight.astype(jnp.bfloat16), "wa", scatter_dimension=0, tiled=True
        ).astype(jnp.float32),
        lax.psum_scatter(
            grad_keyval_weight.astype(jnp.bfloat16), "wa", scatter_dimension=0, tiled=True
        ).astype(jnp.float32),
        lax.psum_scatter(
            grad_attn_weight.astype(jnp.bfloat16), "wa", scatter_dimension=0, tiled=True
        ).astype(jnp.float32),
        lax.psum_scatter(
            grad_gain_two.astype(jnp.bfloat16), "wa", scatter_dimension=0, tiled=True
        ).astype(jnp.float32),
        lax.psum_scatter(
            grad_router.astype(jnp.bfloat16), "wa", scatter_dimension=0, tiled=True
        ).astype(jnp.float32),
        lax.psum_scatter(
            grad_w_in.astype(jnp.bfloat16), "wa", scatter_dimension=3, tiled=True
        ).astype(jnp.float32),
        lax.psum_scatter(
            grad_w_out.astype(jnp.bfloat16), "wa", scatter_dimension=1, tiled=True
        ).astype(jnp.float32),
    )
    summed = lax.psum((shares[0], shares[1], shares[2], shares[3], shares[4], shares[5]), "ctx")
    return (
        output[None],
        grad_input[None],
        summed[0],
        summed[1],
        summed[2],
        summed[3],
        summed[4],
        summed[5],
        shares[6],
        shares[7],
    )

MESH = pl.DeviceIdType.MESH
VMEM_LIMIT = 60 * 1024 * 1024


def chip_place():
    count = lax.axis_size("ctx")
    me = lax.axis_index("ctx")
    return me // 4, lax.rem(me // 2, 2), lax.rem(me, 2), count // 4


def ctx_of(z, y, c):
    return (z * 2 + y) * 2 + c


def greet(across_x=False):
    z, y, c, depth = chip_place()
    barrier = pltpu.get_barrier_semaphore()

    def signal(device):
        pl.semaphore_signal(barrier, 1, device_id=device, device_id_type=MESH)

    signal({"ctx": ctx_of(z, y, 1 - c)})
    signal({"ctx": ctx_of(z, 1 - y, c)})
    if across_x:
        signal({"wa": 1 - lax.axis_index("wa")})
    pl.when(z > 0)(lambda: signal({"ctx": ctx_of(z - 1, y, c)}))
    pl.when(z < depth - 1)(lambda: signal({"ctx": ctx_of(z + 1, y, c)}))
    ends = (z > 0).astype(jnp.int32) + (z < depth - 1).astype(jnp.int32)
    pl.semaphore_wait(barrier, (3 if across_x else 2) + ends)


def remote(source, target_ref, sems, at, device):
    return pltpu.make_async_remote_copy(
        src_ref=source,
        dst_ref=target_ref,
        send_sem=sems.at[(0,) + at],
        recv_sem=sems.at[(1,) + at],
        device_id=device,
        device_id_type=MESH,
    )


def each(step, act):
    z, _, _, depth = chip_place()
    if step == 0:
        act(z)
    else:
        pl.when(z + step < depth)(lambda: act(z + step))
        pl.when(z - step >= 0)(lambda: act(z - step))


def nearest(k):
    z, _, _, depth = chip_place()
    low = jnp.minimum(z, depth - 1 - z)
    step = (k + 1) // 2
    place = jnp.where(k > 2 * low, k, jnp.where(lax.rem(k, 2) == 1, low - step, low + step))
    return jnp.where(z == low, place, depth - 1 - place)


class Gather:
    def __init__(self, out, rows, sems):
        self.out, self.rows = out, rows
        self.z_sems, self.y_sems, self.c_sems = sems
        self.z, self.y, self.c, self.depth = chip_place()

    @staticmethod
    def sems(depth):
        return [
            pltpu.SemaphoreType.DMA((2, 2, depth)),
            pltpu.SemaphoreType.DMA((2, depth)),
            pltpu.SemaphoreType.DMA((2, 2 * depth)),
        ]

    def slot(self, z, y, c):
        return self.out.at[pl.ds(pl.multiple_of(ctx_of(z, y, c) * self.rows, 16), self.rows)]

    def own(self):
        return self.slot(self.z, self.y, self.c)

    def on_z(self, way, of_z, source=None):
        goal = jnp.minimum(self.z + 1, self.depth - 1) if way == 0 else jnp.maximum(self.z - 1, 0)
        block = self.slot(of_z, self.y, self.c)
        target = {"ctx": ctx_of(goal, self.y, self.c)}
        return remote(block if source is None else source, block, self.z_sems, (way, of_z), target)

    def on_y(self, of_z, mine=True, source=None):
        block = self.slot(of_z, self.y if mine else 1 - self.y, self.c)
        target = {"ctx": ctx_of(self.z, 1 - self.y, self.c)}
        return remote(block if source is None else source, block, self.y_sems, (of_z,), target)

    def on_core(self, of_z, of_y, mine=True, source=None):
        block = self.slot(of_z, of_y, self.c if mine else 1 - self.c)
        target = {"ctx": ctx_of(self.z, self.y, 1 - self.c)}
        at = (of_z * 2 + of_y,)
        return remote(block if source is None else source, block, self.c_sems, at, target)

    def start(self, source=None):
        z, depth = self.z, self.depth
        pl.when(z < depth - 1)(lambda: self.on_z(0, z, source).start())
        pl.when(z > 0)(lambda: self.on_z(1, z, source).start())
        self.on_y(z, source=source).start()
        self.on_core(z, self.y, source=source).start()

    def along_z(self, step):
        z, depth = self.z, self.depth

        def from_side(way, of_z, more):
            self.on_z(way, of_z).wait_recv()
            pl.when(more)(lambda: self.on_z(way, of_z).start())
            self.on_y(of_z).start()
            self.on_core(of_z, self.y).start()

        pl.when(z - step >= 0)(lambda: from_side(0, z - step, z < depth - 1))
        pl.when(z + step < depth)(lambda: from_side(1, z + step, z > 0))

    def along_y(self, step):
        def across(of_z):
            self.on_y(of_z, mine=False).wait_recv()
            self.on_core(of_z, 1 - self.y).start()

        each(step, across)

    def finish(self):
        z, depth = self.z, self.depth
        for of_z in range(depth):
            pl.when((z < depth - 1) & (of_z <= z))(lambda: self.on_z(0, of_z).wait_send())
            pl.when((z > 0) & (of_z >= z))(lambda: self.on_z(1, of_z).wait_send())
            self.on_y(of_z).wait_send()
            for of_y in range(2):
                self.on_core(of_z, of_y).wait_send()
                self.on_core(of_z, of_y, mine=False).wait_recv()

    def run(self):
        self.start()
        self.follow()

    def follow(self):
        self.along_z(1)
        self.along_y(0)
        for step in range(1, self.depth):
            if step + 1 < self.depth:
                self.along_z(step + 1)
            self.along_y(step)
        self.finish()


def add_into(target, terms, rows):
    some = 32 if rows % 32 == 0 else 48 if rows % 48 == 0 else 16

    @pl.loop(0, rows // some)
    def _(turn):
        at = pl.ds(pl.multiple_of(turn * some, 16), some)
        total = terms[0][at, :].astype(jnp.float32)
        for term in terms[1:]:
            total = total + term[at, :].astype(jnp.float32)
        target[at, :] = total.astype(target.dtype)


class Scatter:
    def __init__(self, part, scratch, sums=None):
        self.part = part
        self.from_core, self.totals, self.from_y, self.from_z = scratch[:4]
        self.sums = self.totals if sums is None else sums
        self.c_sems, self.y_sems, self.z_sems = scratch[4:]
        self.rows = self.totals.shape[1]
        self.z, self.y, self.c, self.depth = chip_place()

    @staticmethod
    def scratch(depth, rows, columns):
        return [
            pltpu.VMEM((2 * depth, rows, columns), jnp.bfloat16),
            pltpu.VMEM((2 * depth, rows, columns), jnp.bfloat16),
            pltpu.VMEM((depth, rows, columns), jnp.bfloat16),
            pltpu.VMEM((depth + 1, rows, columns), jnp.bfloat16),
            pltpu.SemaphoreType.DMA((2, 2 * depth)),
            pltpu.SemaphoreType.DMA((2, depth)),
            pltpu.SemaphoreType.DMA((2, 2, depth)),
        ]

    def split(self):
        return len(self.part.shape) == 3

    def share(self, chip, c):
        return self.part.at[pl.ds(pl.multiple_of((chip * 2 + c) * self.rows, 16), self.rows)]

    def on_core(self, chip):
        target = {"ctx": ctx_of(self.z, self.y, 1 - self.c)}
        source = self.part.at[chip] if self.split() else self.share(chip, 1 - self.c)
        return remote(source, self.from_core.at[chip], self.c_sems, (chip,), target)

    def on_y(self, of_z):
        target = {"ctx": ctx_of(self.z, 1 - self.y, self.c)}
        source = self.sums.at[of_z * 2 + 1 - self.y]
        return remote(source, self.from_y.at[of_z], self.y_sems, (of_z,), target)

    def on_z(self, way, of_z):
        goal = jnp.minimum(self.z + 1, self.depth - 1) if way == 0 else jnp.maximum(self.z - 1, 0)
        place = of_z if way == 0 else jnp.where(of_z == goal, self.depth, of_z)
        source = self.totals.at[of_z * 2 + self.y]
        target = {"ctx": ctx_of(goal, self.y, self.c)}
        return remote(source, self.from_z.at[place], self.z_sems, (way, of_z), target)

    def start(self):
        def send(of_z):
            self.on_core(of_z * 2 + 1 - self.y).start()
            self.on_core(of_z * 2 + self.y).start()

        for step in range(self.depth - 1, -1, -1):
            each(step, send)

    def add_chip(self, of_z, other, send=True):
        chip = of_z * 2 + (1 - self.y if other else self.y)
        self.on_core(chip).wait_recv()
        own = self.sums.at[chip] if self.split() else self.share(chip, self.c)
        add_into(self.sums.at[chip], (own, self.from_core.at[chip]), self.rows)
        if other and send:
            self.on_y(of_z).start()

    def add_cores(self, step):
        def add(of_z):
            self.add_chip(of_z, True)
            self.add_chip(of_z, False)

        each(step, add)

    def add_y_of(self, of_z):
        z, depth = self.z, self.depth
        self.on_y(of_z).wait_recv()
        place = of_z * 2 + self.y
        total, own, other = self.totals.at[place], self.sums.at[place], self.from_y.at[of_z]
        upward, downward = (of_z > z) & (z > 0), (of_z < z) & (z < depth - 1)
        pl.when(upward)(lambda: self.on_z(0, of_z).wait_recv())
        pl.when(downward)(lambda: self.on_z(1, of_z).wait_recv())

        @pl.when(upward | downward)
        def _():
            add_into(total, (own, other, self.from_z.at[of_z]), self.rows)

        @pl.when(jnp.logical_not(upward | downward))
        def _():
            add_into(total, (own, other), self.rows)

        pl.when(of_z > z)(lambda: self.on_z(0, of_z).start())
        pl.when(of_z < z)(lambda: self.on_z(1, of_z).start())

    def add_y(self, step):
        each(step, self.add_y_of)

    def last(self, result):
        z, depth = self.z, self.depth
        own = self.totals.at[z * 2 + self.y]
        low, high = self.from_z.at[z], self.from_z.at[depth]
        pl.when(z > 0)(lambda: self.on_z(0, z).wait_recv())
        pl.when(z < depth - 1)(lambda: self.on_z(1, z).wait_recv())
        inside = (z > 0) & (z < depth - 1)
        pl.when(inside)(lambda: add_into(result, (own, low, high), self.rows))
        pl.when(z == 0)(lambda: add_into(result, (own, high), self.rows))
        pl.when(z == depth - 1)(lambda: add_into(result, (own, low), self.rows))

    def finish(self, cores=True):
        for of_z in range(self.depth):
            self.on_y(of_z).wait_send()
            if cores:
                self.on_core(of_z * 2).wait_send()
                self.on_core(of_z * 2 + 1).wait_send()
            pl.when(of_z > self.z)(lambda: self.on_z(0, of_z).wait_send())
            pl.when(of_z < self.z)(lambda: self.on_z(1, of_z).wait_send())


def call(kernel, out, scratch, number, name, *operands, outside=(), outside_out=()):
    def spec(position, far):
        return pl.BlockSpec(memory_space=pl.ANY if position in far else pltpu.VMEM)

    many = isinstance(out, (tuple, list))
    out_specs = [spec(i, outside_out) for i in range(len(out) if many else 1)]
    return pl.pallas_call(
        kernel,
        out_shape=out,
        in_specs=[spec(i, outside) for i in range(len(operands))],
        out_specs=out_specs if many else out_specs[0],
        scratch_shapes=scratch,
        compiler_params=pltpu.CompilerParams(
            collective_id=number,
            has_side_effects=number is not None,
            vmem_limit_bytes=VMEM_LIMIT,
        ),
        name=name,
    )(*operands)


class Relay:
    def __init__(self, source, out, sems, parts=1):
        self.source, self.out, self.sems, self.parts = source, out, sems, parts
        self.z, self.y, self.c, _ = chip_place()
        self.rows = source.shape[0] // (2 * parts)

    @staticmethod
    def semaphores():
        return pltpu.SemaphoreType.DMA((2, 4))

    def block(self, ref, part, c):
        return ref.at[pl.ds(pl.multiple_of((c * self.parts + part) * self.rows, 16), self.rows)]

    def on_x(self, part):
        source, target = self.block(self.source, part, self.c), self.block(self.out, part, self.c)
        return remote(source, target, self.sems, (part,), {"wa": 1 - lax.axis_index("wa")})

    def on_core(self, part, c):
        block = self.block(self.out, part, c)
        return remote(
            block, block, self.sems, (2 + part,), {"ctx": ctx_of(self.z, self.y, 1 - self.c)}
        )

    def start(self):
        for part in range(self.parts):
            self.on_x(part).start()

    def pass_on(self, part=0):
        self.on_x(part).wait_recv()
        self.on_core(part, self.c).start()

    def finish(self):
        for part in range(self.parts):
            self.on_x(part).wait_send()
            self.on_core(part, self.c).wait_send()
            self.on_core(part, 1 - self.c).wait_recv()


def front(d_out, w_query, w_keyval, small):
    count, rows = lax.axis_size("ctx"), d_out.shape[0]
    depth = count // 4

    def kernel(
        d_out_ref, query_ref, keyval_ref, small_ref,
        d_out_all, query_there, keyval_there, small_there, *sems,
    ):
        gather = Gather(d_out_all, rows, sems[:3])
        query_sems, keyval_sems, small_sems, own_sem = sems[3:]
        query = Relay(query_ref, query_there, query_sems, parts=2)
        keyval = Relay(keyval_ref, keyval_there, keyval_sems)
        partner = {"wa": 1 - lax.axis_index("wa")}
        swap = remote(small_ref, small_there, small_sems, (0,), partner)
        keep = pltpu.make_async_copy(d_out_ref, gather.own(), own_sem.at[0])
        keep.start()
        greet(across_x=True)
        swap.start()
        query.start()
        keyval.start()
        gather.start(d_out_ref)
        gather.along_z(1)
        gather.along_y(0)
        gather.along_z(2)
        gather.along_y(1)
        query.pass_on(0)
        gather.along_z(3)
        gather.along_y(2)
        query.pass_on(1)
        keyval.pass_on()
        gather.along_y(3)
        gather.finish()
        query.finish()
        keyval.finish()
        swap.wait()
        keep.wait()

    def like(values):
        return jax.ShapeDtypeStruct(values.shape, values.dtype)

    out = [
        jax.ShapeDtypeStruct((count * rows, d_out.shape[1]), d_out.dtype),
        like(w_query), like(w_keyval), like(small),
    ]
    scratch = Gather.sems(depth) + [Relay.semaphores()] * 2
    scratch += [pltpu.SemaphoreType.DMA((2, 1)), pltpu.SemaphoreType.DMA((1,))]
    every = range(4)
    return call(
        kernel, out, scratch, 0, "front",
        d_out, w_query, w_keyval, small, outside=every, outside_out=every,
    )


def rows_by_rows(left, right):
    return lax.dot_general(
        left, right, (((1,), (1,)), ((), ())), preferred_element_type=jnp.float32
    )


def columns_by_columns(left, right):
    return lax.dot_general(
        left, right, (((0,), (0,)), ((), ())), preferred_element_type=jnp.float32
    )


def allowed_bias(doc_row, doc_column, tokens):
    keys = doc_row.shape[1]
    query_block = lax.axis_index("ctx") * tokens // BLOCK
    key_block = lax.broadcasted_iota(jnp.int32, (tokens, keys), 1) // BLOCK
    allowed = (doc_row == doc_column) & (key_block <= query_block)
    return jnp.where(allowed, 0.0, NEGATIVE)


def side_columns(own):
    side = lax.axis_index("wa")
    return pl.ds(pl.multiple_of((side if own else 1 - side) * (D // 2), 128), D // 2)


def turned(values, cosine, sine):
    heads = []
    for head in range(values.shape[1] // HEAD_DIM):
        one = values[:, head * HEAD_DIM : (head + 1) * HEAD_DIM]
        heads.append(one * cosine + pltpu.roll(one, HEAD_DIM // 2, axis=1) * sine)
    return jnp.concatenate(heads, axis=1)


def normed(values, gain_vec):
    return values * lax.rsqrt(jnp.mean(values * values, axis=-1, keepdims=True) + EPSILON) * gain_vec


def fill_small(full, small, small_there):
    full[:, side_columns(True)] = small[...].astype(jnp.float32)
    full[:, side_columns(False)] = small_there[...].astype(jnp.float32)


def router_block(full, experts):
    rows = full[:experts]
    spare = jnp.zeros((128 - 2 * experts, rows.shape[1]), jnp.float32)
    return jnp.concatenate([rows, rows, spare], axis=0).astype(jnp.bfloat16)


def attend(x, small, small_there, projections, w_out_attn, angles, docs, chosen, experts):
    count, tokens, features = lax.axis_size("ctx"), x.shape[0], x.shape[1]
    depth, length = count // 4, count * tokens
    kv_columns, half = projections[2].shape[1], features // 2

    def kernel(
        x_ref, small_ref, small_there_ref, query_own, query_other, keyval_own, keyval_other,
        attn_own, cosine_ref, sine_ref, doc_row, doc_column, chosen_ref,
        query, keyval, level, mixed, hidden_own, hidden_there, mixed_own, mixed_there, middle,
        send, gates_out, attn_other,
        hidden, mixed_low, full, stacked, bias, x_sems, attn_sems, *sems,
    ):
        gather = Gather(keyval, tokens, sems)
        attn = Relay(attn_own, attn_other, attn_sems, parts=2)
        partner = {"wa": 1 - lax.axis_index("wa")}
        greet(across_x=True)
        attn.start()
        fill_small(full, small_ref, small_there_ref)
        residual = x_ref[...].astype(jnp.float32)
        hidden[...] = normed(residual, full[experts : experts + 1]).astype(jnp.bfloat16)
        hidden_own[...] = hidden[:, side_columns(True)]
        own, other = hidden[:, side_columns(True)], hidden[:, side_columns(False)]
        cosine, sine = cosine_ref[...], sine_ref[...]

        def onto(matrix, matrix_other):
            return jnp.dot(own, matrix[...], preferred_element_type=jnp.float32) + jnp.dot(
                other, matrix_other[...], preferred_element_type=jnp.float32
            )

        pre = onto(keyval_own, keyval_other)
        keys = turned(pre[:, : kv_columns // 2], cosine, sine)
        block = jnp.concatenate([keys, pre[:, kv_columns // 2 :]], axis=1)
        gather.own()[...] = block.astype(jnp.bfloat16)
        gather.start()
        swap = remote(hidden.at[:, side_columns(False)], hidden_there, x_sems, (0,), partner)
        swap.start()
        query[...] = turned(onto(query_own, query_other), cosine, sine).astype(jnp.bfloat16)
        bias[...] = allowed_bias(doc_row[...], doc_column[...], tokens)
        for head in range(HEADS):
            rows = slice(head * tokens, (head + 1) * tokens)
            stacked[rows, :] = query[:, head * 128 : (head + 1) * 128]
        gather.follow()

        @pl.loop(0, HEADS // 2)
        def _(pair):
            rows = pl.ds(pl.multiple_of(pair * 2 * tokens, 128), 2 * tokens)
            kind = pair // (HEADS // KV_HEADS // 2)
            key_part = keyval[:, pl.ds(pl.multiple_of(kind * 128, 128), 128)]
            val_part = keyval[:, pl.ds(pl.multiple_of(kind * 128 + 256, 128), 128)]
            scores = rows_by_rows(stacked[rows, :], key_part) * HEAD_DIM**-0.5
            scores = (scores.reshape(2, tokens, -1) + bias[...][None]).reshape(scores.shape)
            top = jnp.max(scores, axis=-1, keepdims=True)
            weights = jnp.exp(scores - top)
            total = jnp.sum(weights, axis=-1, keepdims=True)
            probs = (weights / total).astype(jnp.bfloat16)
            mixture = jnp.dot(probs, val_part, preferred_element_type=jnp.float32)
            for part in range(2):
                columns = pl.ds(pl.multiple_of((pair * 2 + part) * 128, 128), 128)
                mixed[:, columns] = mixture[part * tokens : (part + 1) * tokens]
            level[rows, :] = top + jnp.log(total)
            pl.when(pair == HEADS // 4)(lambda: attn.pass_on(0))

        attn.pass_on(1)
        mixed_low[...] = mixed[...].astype(jnp.bfloat16)
        mixed_own[...] = mixed_low[:, side_columns(True)]
        swap_mixed = remote(
            mixed_low.at[:, side_columns(False)], mixed_there, x_sems, (1,), partner
        )
        swap_mixed.start()
        attn.finish()
        own, other = mixed_low[:, side_columns(True)], mixed_low[:, side_columns(False)]
        middle[...] = residual + onto(attn_own, attn_other)
        hidden_two = normed(middle[...], full[experts + 1 : experts + 2]).astype(jnp.bfloat16)
        send[:, :features] = hidden_two
        logits = rows_by_rows(hidden_two, router_block(full, experts))
        lane = lax.broadcasted_iota(jnp.int32, logits.shape, 1)
        masked = jnp.where(chosen_ref[...] > 0, logits, NEGATIVE)
        weights = jnp.exp(masked - jnp.max(masked, axis=1, keepdims=True))
        total = jnp.sum(jnp.where(lane < experts, weights, 0.0), axis=1, keepdims=True)
        gates = weights / total
        high = gates.astype(jnp.bfloat16).astype(jnp.float32)
        carried = jnp.where(lane < experts, high, jnp.where(lane < 2 * experts, gates - high, 0.0))
        send[:, features:] = carried.astype(jnp.bfloat16)
        gates_out[...] = jnp.where(lane < experts, gates, 0.0)
        swap.wait()
        swap_mixed.wait()

    def shape(rows, columns, kind=jnp.bfloat16):
        return jax.ShapeDtypeStruct((rows, columns), kind)

    wide = features + 128
    out = [
        shape(tokens, features), shape(length, kv_columns), shape(HEADS * tokens, 1, jnp.float32),
        shape(tokens, features, jnp.float32),
        shape(tokens, half), shape(tokens, half), shape(tokens, half), shape(tokens, half),
        shape(tokens, features, jnp.float32), shape(tokens, wide), shape(tokens, 128, jnp.float32),
        shape(*w_out_attn.shape),
    ]
    scratch = [
        pltpu.VMEM((tokens, features), jnp.bfloat16),
        pltpu.VMEM((tokens, features), jnp.bfloat16),
        pltpu.VMEM((small.shape[0], features), jnp.float32),
        pltpu.VMEM((HEADS * tokens, HEAD_DIM), jnp.bfloat16),
        pltpu.VMEM((tokens, length), jnp.float32),
        pltpu.SemaphoreType.DMA((2, 2)),
        Relay.semaphores(),
    ] + Gather.sems(depth)
    return call(
        kernel, out, scratch, 2, "attend",
        x, small, small_there, *projections, w_out_attn, *angles, *docs, chosen,
    )


def norm_back(values, gain_vec, grad):
    scale = lax.rsqrt(jnp.mean(values * values, axis=-1, keepdims=True) + EPSILON)
    through = jnp.mean(gain_vec * grad * values, axis=-1, keepdims=True)
    back = scale * gain_vec * grad - values * (scale * scale * scale * through)
    return back, jnp.sum(grad * values * scale, axis=0, keepdims=True)


def attend_back(
    returned, gates, small, small_there, middle, d_out, send, attn_own, attn_other, query, keyval,
    angles, docs, level, mixed, results, experts,
):
    count, tokens, features = lax.axis_size("ctx"), query.shape[0], query.shape[1]
    depth, length, kv_columns = count // 4, keyval.shape[0], keyval.shape[1]

    def kernel(
        returned_ref, gates_ref, small_ref, small_there_ref, middle_ref, d_out_ref, send_ref,
        attn_own_ref, attn_other_ref, query_ref, keyval_ref, cosine_ref, sine_ref, doc_row,
        doc_column, level_ref, mixed_ref, results_ref,
        output, grad_middle, grad_middle_low, grad_middle_there, grad_query, grad_query_there,
        grad_keyval, grad_keyval_there, small_grads,
        full, grad_mixed, turned_query, own_keyval, result_sum, stacked, grads, bias, delta, total,
        part, x_sems, *scratch,
    ):
        result = Scatter(
            None, (None,) + tuple(scratch[:3]) + (None,) + tuple(scratch[3:5]), results_ref
        )
        keyval_sum = Scatter(part, scratch[5:])
        partner = {"wa": 1 - lax.axis_index("wa")}
        swaps = [
            remote(source, target, x_sems, (i,), partner)
            for i, (source, target) in enumerate(
                [(grad_middle_low, grad_middle_there), (grad_query, grad_query_there),
                 (grad_keyval, grad_keyval_there)]
            )
        ]
        greet(across_x=True)
        for k in (depth - 1, depth - 2):
            result.on_y(nearest(k)).start()
        fill_small(full, small_ref, small_there_ref)
        lane = lax.broadcasted_iota(jnp.int32, (tokens, 128), 1)
        gates = gates_ref[...]
        grad_gates = jnp.where(lane < experts, returned_ref[:, features:], 0.0)
        inner = jnp.sum(gates * grad_gates, axis=1, keepdims=True)
        grad_logits = (gates * (grad_gates - inner)).astype(jnp.bfloat16)
        grad_two = returned_ref[:, :features] + jnp.dot(
            grad_logits, router_block(full, experts), preferred_element_type=jnp.float32
        )
        grad_router = columns_by_columns(grad_logits, send_ref[:, :features])
        back, grad_gain = norm_back(middle_ref[...], full[experts + 1 : experts + 2], grad_two)
        grad_middle[...] = d_out_ref[...].astype(jnp.float32) + back
        grad_middle_low[...] = grad_middle[...].astype(jnp.bfloat16)
        swaps[0].start()
        small_grads[:experts] = grad_router[:experts]
        row = lax.broadcasted_iota(jnp.int32, (small_grads.shape[0] - experts, 1), 0)
        small_grads[experts:] = jnp.where(row == 1, grad_gain, 0.0)
        grad_mixed[:, side_columns(True)] = rows_by_rows(
            grad_middle_low[...], attn_own_ref[...]
        ).astype(jnp.bfloat16)
        grad_mixed[:, side_columns(False)] = rows_by_rows(
            grad_middle_low[...], attn_other_ref[...]
        ).astype(jnp.bfloat16)
        bias[...] = allowed_bias(doc_row[...], doc_column[...], tokens)
        total[...] = jnp.zeros_like(total)
        for head in range(HEADS):
            rows = slice(head * tokens, (head + 1) * tokens)
            columns = slice(head * 128, head * 128 + 128)
            stacked[rows, :] = query_ref[:, columns]
            grads[rows, :] = grad_mixed[:, columns]
            delta[rows, :] = jnp.sum(
                grad_mixed[:, columns].astype(jnp.float32) * mixed_ref[:, columns],
                axis=-1,
                keepdims=True,
            )

        @pl.loop(0, HEADS // 2)
        def _(pair):
            rows = pl.ds(pl.multiple_of(pair * 2 * tokens, 128), 2 * tokens)
            kind = pair // (HEADS // KV_HEADS // 2)
            key_columns = pl.ds(pl.multiple_of(kind * 128, 128), 128)
            val_columns = pl.ds(pl.multiple_of(kind * 128 + 256, 128), 128)
            key_part, val_part = keyval_ref[:, key_columns], keyval_ref[:, val_columns]
            own, grad = stacked[rows, :], grads[rows, :]
            scores = rows_by_rows(own, key_part) * HEAD_DIM**-0.5
            scores = (scores.reshape(2, tokens, -1) + bias[...][None]).reshape(scores.shape)
            probs = jnp.exp(scores - level_ref[rows, :])
            grad_probs = rows_by_rows(grad, val_part)
            grad_scores = (probs * (grad_probs - delta[rows, :])).astype(jnp.bfloat16)
            own_grad = jnp.dot(grad_scores, key_part, preferred_element_type=jnp.float32)
            for half in range(2):
                columns = pl.ds(pl.multiple_of((pair * 2 + half) * 128, 128), 128)
                turned_query[:, columns] = (
                    own_grad[half * tokens : (half + 1) * tokens] * HEAD_DIM**-0.5
                )
            total[:, key_columns] += columns_by_columns(grad_scores, own) * HEAD_DIM**-0.5
            total[:, val_columns] += columns_by_columns(probs.astype(jnp.bfloat16), grad)
            pl.when(pair == 1)(lambda: result.on_y(nearest(depth - 3)).start())
            pl.when(pair == HEADS // 4)(lambda: result.add_y_of(nearest(depth - 1)))

        part[...] = total[...].astype(jnp.bfloat16)
        keyval_sum.start()
        cosine, sine = cosine_ref[...], -sine_ref[...]
        grad_query[...] = turned(turned_query[...], cosine, sine).astype(jnp.bfloat16)
        swaps[1].start()
        steps = range(depth - 1, -1, -1)
        for step in steps:
            keyval_sum.add_cores(step)
        for k in range(depth - 4, -1, -1):
            result.on_y(nearest(k)).start()
        result.add_y_of(nearest(depth - 2))
        for step in steps:
            keyval_sum.add_y(step)
        keyval_sum.last(own_keyval)
        keys = turned(own_keyval[:, : kv_columns // 2], cosine, sine)
        grad_keyval[...] = jnp.concatenate(
            [keys, own_keyval[:, kv_columns // 2 :]], axis=1
        ).astype(jnp.bfloat16)
        swaps[2].start()
        for k in range(depth - 3, -1, -1):
            result.add_y_of(nearest(k))
        result.last(result_sum)
        output[...] = (middle_ref[...] + result_sum[...]).astype(jnp.bfloat16)
        keyval_sum.finish()
        result.finish(cores=False)
        for swap in swaps:
            swap.wait()

    def shape(like, kind=jnp.bfloat16):
        return jax.ShapeDtypeStruct(like, kind)

    rows, narrow = (tokens, features), (tokens, kv_columns)
    small_shape = (small.shape[0], features)
    out = [
        shape(rows), shape(rows, jnp.float32), shape(rows), shape(rows), shape(rows), shape(rows),
        shape(narrow), shape(narrow), shape(small_shape, jnp.float32),
    ]
    scratch = [
        pltpu.VMEM(small_shape, jnp.float32),
        pltpu.VMEM(rows, jnp.bfloat16),
        pltpu.VMEM(rows, jnp.float32),
        pltpu.VMEM(narrow, jnp.float32),
        pltpu.VMEM(rows, jnp.float32),
        pltpu.VMEM((HEADS * tokens, HEAD_DIM), jnp.bfloat16),
        pltpu.VMEM((HEADS * tokens, HEAD_DIM), jnp.bfloat16),
        pltpu.VMEM((tokens, length), jnp.float32),
        pltpu.VMEM((HEADS * tokens, 1), jnp.float32),
        pltpu.VMEM(keyval.shape, jnp.float32),
        pltpu.VMEM(keyval.shape, jnp.bfloat16),
        pltpu.SemaphoreType.DMA((2, 3)),
    ]
    wide = Scatter.scratch(depth, tokens, features)
    scratch += wide[1:4] + wide[5:] + Scatter.scratch(depth, tokens, kv_columns)
    return call(
        kernel, out, scratch, 4, "attend_back",
        returned, gates, small, small_there, middle, d_out, send, attn_own, attn_other, query,
        keyval, *angles, *docs, level, mixed, results,
    )


def gate_unit(first, second):
    root, cube = math.sqrt(2 / math.pi), 0.044715
    square = first * first
    bend = jnp.tanh(root * first * (1 + cube * square))
    lift = 0.5 * (1 + bend)
    slope = lift + 0.5 * first * (1 - bend * bend) * root * (1 + 3 * cube * square)
    gelu = first * lift
    return gelu * second, slope * second, gelu


def run_experts(send, d_out_all, in_own, out_own, experts):
    count, tokens = lax.axis_size("ctx"), send.shape[0]
    depth, chips, length = count // 4, count // 2, count * tokens
    wide, features = send.shape[1], d_out_all.shape[1]
    quarter = out_own.shape[0]
    width = 2 * quarter

    def kernel(
        send_ref, d_out_far, in_own_ref, out_own_ref,
        returned, results, grad_in, grad_in_other, grad_out, grad_out_other,
        hidden_all, grad_both, gated_hidden, other_part, other_result, result_from, result_sems,
        in_ref, out_ref, d_out_ref, x_sems, near_sem, *scratch,
    ):
        gather = Gather(hidden_all, tokens, scratch[:3])
        scatter = Scatter(other_part, scratch[3:])
        z, y, c, _ = chip_place()
        expert = lax.axis_index("ctx") // 2
        lane = lax.broadcasted_iota(jnp.int32, (1, 128), 1)
        gather.own()[...] = send_ref[...]
        partner = {"wa": 1 - lax.axis_index("wa")}
        near = pltpu.make_async_copy(d_out_far, d_out_ref, near_sem.at[0])
        near.start()
        swaps = [
            remote(
                in_own_ref.at[pl.ds(part * quarter, quarter)],
                in_ref.at[pl.ds((2 * part + 1) * quarter, quarter)],
                x_sems,
                (part,),
                partner,
            )
            for part in range(2)
        ]
        swaps.append(
            remote(out_own_ref, out_ref.at[pl.ds(quarter, quarter)], x_sems, (2,), partner)
        )
        greet(across_x=True)
        gather.start()
        for swap in swaps:
            swap.start()
        out_ref[:quarter] = out_own_ref[...]
        in_ref[:quarter] = in_own_ref[:quarter]
        in_ref[width : width + quarter] = in_own_ref[quarter:]
        gather.follow()
        near.wait()
        for swap in swaps:
            swap.wait()

        def chip_rows(chip):
            return pl.ds(pl.multiple_of(chip * 2 * tokens, 16), 2 * tokens)

        def parted(values):
            low, high = values[:tokens], values[tokens:]
            return jnp.where(c == 0, low, high), jnp.where(c == 0, high, low)

        def backward(chip):
            rows = chip_rows(chip)
            carried = hidden_all[rows, features:].astype(jnp.float32)
            mine = (lane == expert) | (lane == expert + experts)
            gate = jnp.sum(jnp.where(mine, carried, 0.0), axis=1, keepdims=True)
            both = rows_by_rows(hidden_all[rows, :features], in_ref[...])
            hidden, by_first, by_second = gate_unit(both[:, :width], both[:, width:])
            gated_hidden[rows, :] = (hidden * gate).astype(jnp.bfloat16)
            grad_hidden = rows_by_rows(d_out_ref[rows, :], out_ref[...])
            grad_gate = jnp.sum(grad_hidden * hidden, axis=1, keepdims=True)
            grad_hidden = grad_hidden * gate
            grad_both[rows, :width] = (grad_hidden * by_first).astype(jnp.bfloat16)
            grad_both[rows, width:] = (grad_hidden * by_second).astype(jnp.bfloat16)
            own, other = parted(
                jnp.dot(grad_both[rows, :], in_ref[...], preferred_element_type=jnp.float32)
            )
            scatter.sums[chip, :, :features] = own.astype(jnp.bfloat16)
            other_part[chip, :, :features] = other.astype(jnp.bfloat16)
            own, other = parted(jnp.where(lane == expert, grad_gate, 0.0))
            scatter.sums[chip, :, features:] = own.astype(jnp.bfloat16)
            other_part[chip, :, features:] = other.astype(jnp.bfloat16)
            scatter.on_core(chip).start()

        @pl.loop(0, depth)
        def _(turn):
            of_z = nearest(depth - 1 - turn)
            backward(of_z * 2 + 1 - y)
            pl.when(turn > 0)(lambda: scatter.add_chip(nearest(depth - turn), False))
            backward(of_z * 2 + y)
            scatter.add_chip(of_z, True)

        scatter.add_chip(nearest(0), False)
        scatter.add_y_of(nearest(depth - 1))

        def result_copy(chip):
            target = {"ctx": ctx_of(z, y, 1 - c)}
            return remote(
                other_result.at[chip], result_from.at[chip], result_sems, (chip,), target
            )

        @pl.loop(0, chips)
        def _(chip):
            result = jnp.dot(
                gated_hidden[chip_rows(chip), :], out_ref[...], preferred_element_type=jnp.float32
            )
            own, other = parted(result)
            results[chip] = own.astype(jnp.bfloat16)
            other_result[chip] = other.astype(jnp.bfloat16)
            result_copy(chip).start()

        scatter.add_y_of(nearest(depth - 2))

        @pl.loop(0, features // 512)
        def _(turn):
            at = pl.ds(pl.multiple_of(turn * 512, 512), 512)
            grad = columns_by_columns(gated_hidden[...], d_out_ref[:, at])
            grad_out[:, at] = grad[:quarter]
            grad_out_other[:, at] = grad[quarter:].astype(jnp.bfloat16)

        for k in range(depth - 3, 0, -1):
            scatter.add_y_of(nearest(k))

        @pl.loop(0, features // 512)
        def _(turn):
            at = pl.ds(pl.multiple_of(turn * 512, 512), 512)
            grad = columns_by_columns(grad_both[...], hidden_all[:, at])
            for part in range(2):
                rows = slice(part * quarter, (part + 1) * quarter)
                first = part * width
                grad_in[rows, at] = grad[first : first + quarter]
                grad_in_other[rows, at] = grad[first + quarter : first + width].astype(jnp.bfloat16)

        scatter.add_y_of(nearest(0))

        @pl.loop(0, chips)
        def _(chip):
            result_copy(chip).wait_recv()
            add_into(results.at[chip], (results.at[chip], result_from.at[chip]), tokens)

        scatter.last(returned)
        scatter.finish()
        for chip in range(chips):
            result_copy(chip).wait_send()

    block = (chips, tokens, features)
    out = [
        jax.ShapeDtypeStruct((tokens, wide), jnp.float32),
        jax.ShapeDtypeStruct(block, jnp.bfloat16),
        jax.ShapeDtypeStruct(in_own.shape, jnp.float32),
        jax.ShapeDtypeStruct(in_own.shape, jnp.bfloat16),
        jax.ShapeDtypeStruct(out_own.shape, jnp.float32),
        jax.ShapeDtypeStruct(out_own.shape, jnp.bfloat16),
    ]
    scratch = [
        pltpu.VMEM((length, wide), jnp.bfloat16),
        pltpu.VMEM((length, 2 * width), jnp.bfloat16),
        pltpu.VMEM((length, width), jnp.bfloat16),
        pltpu.VMEM((chips, tokens, wide), jnp.bfloat16),
        pltpu.VMEM(block, jnp.bfloat16),
        pltpu.VMEM(block, jnp.bfloat16),
        pltpu.SemaphoreType.DMA((2, chips)),
        pltpu.VMEM((2 * width, features), jnp.bfloat16),
        pltpu.VMEM((width, features), jnp.bfloat16),
        pltpu.VMEM(d_out_all.shape, jnp.bfloat16),
        pltpu.SemaphoreType.DMA((2, 3)),
        pltpu.SemaphoreType.DMA((1,)),
    ]
    scratch += Gather.sems(depth) + Scatter.scratch(depth, tokens, wide)
    return call(
        kernel, out, scratch, 3, "experts", send, d_out_all, in_own, out_own, outside=(1,)
    )


def finish(
    x, grad_middle, small, small_there, small_grads, matrices, hidden, mixed, middle, query, keyval,
    expert_in, expert_out,
):
    count, tokens, half = lax.axis_size("ctx"), x.shape[0], x.shape[1] // 2
    depth, rows = count // 4, half // count
    widths = (middle[0].shape[1], query[0].shape[1], keyval[0].shape[1])
    experts = small.shape[0] // 2

    def kernel(
        x_ref, grad_middle_ref, small_ref, small_there_ref, small_grads_ref,
        query_own, query_other, keyval_own, keyval_other,
        hidden_ref, hidden_there, mixed_ref, mixed_there, middle_ref, middle_there,
        query_ref, query_there, keyval_ref, keyval_there, in_ref, out_ref,
        attn_sum, query_sum, keyval_sum, small_sum, grad_input, in_there, out_there,
        attn_part, query_part, keyval_part, pair, full, grad_one, small_mine, small_came, small_all,
        x_sems, *scratch,
    ):
        scatters, gathers = [], []
        parts, sums = (attn_part, query_part, keyval_part), (attn_sum, query_sum, keyval_sum)
        for part, total in zip(parts, sums):
            scatters.append(Scatter(part, scratch[:7]))
            gathers.append(Gather(total, rows, scratch[7:10]))
            scratch = scratch[10:]
        small_out = Gather(small_all, small_came.shape[0], scratch)
        (attn, query_, keyval_), (attn_out, query_out, keyval_out) = scatters, gathers
        partner = {"wa": 1 - lax.axis_index("wa")}
        swaps = [
            remote(source, target, x_sems, (i,), partner)
            for i, (source, target) in enumerate(
                [(small_mine.at[:, side_columns(False)], small_came), (in_ref, in_there),
                 (out_ref, out_there)]
            )
        ]
        steps = range(depth - 1, -1, -1)

        def products(left, left_there, right, right_there, part):
            pair[:tokens] = left[...]
            pair[tokens:] = left_there[...]

            @pl.loop(0, part.shape[1] // 512)
            def _(turn):
                at = pl.ds(pl.multiple_of(turn * 512, 512), 512)
                both = jnp.concatenate([right[:, at], right_there[:, at]], axis=0)
                part[:, at] = columns_by_columns(pair[...], both).astype(jnp.bfloat16)

        products(mixed_ref, mixed_there, middle_ref, middle_there, attn_part)
        greet(across_x=True)
        attn.start()
        products(hidden_ref, hidden_there, query_ref, query_there, query_part)
        for step in steps:
            attn.add_cores(step)
        query_.start()
        products(hidden_ref, hidden_there, keyval_ref, keyval_there, keyval_part)
        keyval_.start()
        for step in steps:
            query_.add_cores(step)
        attn.add_y(depth - 1)
        fill_small(full, small_ref, small_there_ref)
        grad_one[:, side_columns(True)] = rows_by_rows(
            query_ref[...], query_own[...]
        ) + rows_by_rows(keyval_ref[...], keyval_own[...])
        attn.add_y(depth - 2)
        grad_one[:, side_columns(False)] = rows_by_rows(
            query_ref[...], query_other[...]
        ) + rows_by_rows(keyval_ref[...], keyval_other[...])
        back, grad_gain = norm_back(
            x_ref[...].astype(jnp.float32), full[experts : experts + 1], grad_one[...]
        )
        grad_input[...] = (grad_middle_ref[...] + back).astype(jnp.bfloat16)
        row = lax.broadcasted_iota(jnp.int32, (small_mine.shape[0], 1), 0)
        small_mine[...] = jnp.where(row == experts, grad_gain, small_grads_ref[...])
        swaps[0].start()
        for step in range(depth - 3, -1, -1):
            attn.add_y(step)
        for step in steps:
            keyval_.add_cores(step)
        attn.last(attn_out.own())
        attn_out.start()
        swaps[1].start()
        swaps[2].start()
        swaps[0].wait()
        small_out.own()[...] = (small_mine[:, side_columns(True)] + small_came[...]).astype(
            jnp.bfloat16
        )
        small_out.start()
        for step in steps:
            query_.add_y(step)
        attn_out.along_z(1)
        query_.last(query_out.own())
        query_out.start()
        attn_out.along_z(2)
        attn_out.along_y(0)
        small_out.along_z(1)
        for step in steps:
            keyval_.add_y(step)
        attn_out.along_z(3)
        attn_out.along_y(1)
        keyval_.last(keyval_out.own())
        keyval_out.start()
        query_out.along_z(1)
        small_out.along_z(2)
        attn_out.along_y(2)
        query_out.along_z(2)
        small_out.along_z(3)
        query_out.along_y(0)
        keyval_out.along_z(1)
        query_out.along_z(3)
        attn_out.along_y(3)
        keyval_out.along_z(2)
        query_out.along_y(1)
        keyval_out.along_z(3)
        query_out.along_y(2)
        small_out.along_y(0)
        keyval_out.along_y(0)
        small_out.along_y(1)
        query_out.along_y(3)
        keyval_out.along_y(1)
        small_out.along_y(2)
        keyval_out.along_y(2)
        small_out.along_y(3)
        keyval_out.along_y(3)
        for one in [small_out] + gathers + scatters:
            one.finish()
        small_rows = small_came.shape[0]
        total = small_all[:small_rows].astype(jnp.float32)
        for device in range(1, count):
            rows_of = slice(device * small_rows, (device + 1) * small_rows)
            total = total + small_all[rows_of].astype(jnp.float32)
        small_sum[...] = total
        swaps[1].wait()
        swaps[2].wait()

    small_shape = (small.shape[0], half)
    out = [jax.ShapeDtypeStruct((half, width), jnp.bfloat16) for width in widths]
    out += [
        jax.ShapeDtypeStruct(small_shape, jnp.float32),
        jax.ShapeDtypeStruct(x.shape, jnp.bfloat16),
        jax.ShapeDtypeStruct(expert_in.shape, expert_in.dtype),
        jax.ShapeDtypeStruct(expert_out.shape, expert_out.dtype),
    ]
    scratch = [pltpu.VMEM((half, width), jnp.bfloat16) for width in widths]
    scratch += [
        pltpu.VMEM((2 * tokens, half), jnp.bfloat16),
        pltpu.VMEM(small_grads.shape, jnp.float32),
        pltpu.VMEM(x.shape, jnp.float32),
        pltpu.VMEM(small_grads.shape, jnp.float32),
        pltpu.VMEM(small_shape, jnp.float32),
        pltpu.VMEM((count * small.shape[0], half), jnp.bfloat16),
        pltpu.SemaphoreType.DMA((2, 3)),
    ]
    for width in widths:
        scratch += Scatter.scratch(depth, rows, width) + Gather.sems(depth)
    scratch += Gather.sems(depth)
    return call(
        kernel, out, scratch, 1, "finish",
        x, grad_middle, small, small_there, small_grads, *matrices, *hidden, *mixed, *middle,
        *query, *keyval, expert_in, expert_out, outside=(19, 20), outside_out=(5, 6),
    )


def widen(query, keyval, attn, grad_in, in_there, grad_out, out_there):
    quarter, features = grad_out.shape
    steps = 4

    def kernel(*refs):
        query_ref, keyval_ref, attn_ref, in_ref, in_there_ref, out_ref, out_there_ref = refs[:7]
        query_out, keyval_out, attn_out, in_out, out_out = refs[7:]
        query_out[...] = query_ref[...].astype(jnp.float32)
        keyval_out[...] = keyval_ref[...].astype(jnp.float32)
        attn_out[...] = attn_ref[...].astype(jnp.float32)
        both = in_ref[...] + in_there_ref[...].astype(jnp.float32)
        in_out[...] = both
        out_out[0] = out_ref[...] + out_there_ref[...].astype(jnp.float32)

    def rows(values):
        return pl.BlockSpec((values.shape[0] // steps, values.shape[1]), lambda i: (i, 0))

    operands = (query, keyval, attn, grad_in, in_there, grad_out, out_there)
    return pl.pallas_call(
        kernel,
        grid=(steps,),
        out_shape=[
            jax.ShapeDtypeStruct(query.shape, jnp.float32),
            jax.ShapeDtypeStruct(keyval.shape, jnp.float32),
            jax.ShapeDtypeStruct(attn.shape, jnp.float32),
            jax.ShapeDtypeStruct(grad_in.shape, jnp.float32),
            jax.ShapeDtypeStruct((1, quarter, features), jnp.float32),
        ],
        in_specs=[rows(values) for values in operands],
        out_specs=[
            rows(query), rows(keyval), rows(attn),
            rows(grad_in),
            pl.BlockSpec((1, quarter // steps, features), lambda i: (0, i, 0)),
        ],
        compiler_params=pltpu.CompilerParams(vmem_limit_bytes=VMEM_LIMIT),
        name="widen",
    )(*operands)


def gathered_body(
    layer_input, seq_ids, routes, gain_attn, w_query, w_keyval, w_out_attn, gain_ffn, router,
    w_in, w_out, d_out,
):
    me = lax.axis_index("ctx")
    tokens, experts = layer_input.shape[1], router.shape[1]
    x, grad_out = layer_input[0], d_out[0]
    small = jnp.concatenate(
        [router.T, gain_attn[None], gain_ffn[None], jnp.zeros((experts - 2, D // 2), jnp.bfloat16)]
    )
    turns = angle_table(me * tokens + jnp.arange(tokens, dtype=jnp.int32))[:, 0]
    cosine, sine = jnp.cos(turns), jnp.sin(turns)
    angles = (
        jnp.concatenate([cosine, cosine], axis=1), jnp.concatenate([-sine, sine], axis=1)
    )
    docs = (seq_ids, lax.dynamic_slice_in_dim(seq_ids[0], me * tokens, tokens, 0)[:, None])
    numbers = jnp.arange(128, dtype=jnp.int32)
    named = jnp.any(routes[0][:, :, None] == (numbers % experts)[None, None, :], axis=1)
    chosen = (named & (numbers < 2 * experts)[None, :]).astype(jnp.float32)
    in_own = jnp.swapaxes(w_in[0], 1, 2).reshape(-1, D)

    d_out_all, w_query_there, w_keyval_there, small_there = front(
        grad_out, w_query, w_keyval, small
    )
    projections = (w_query, w_query_there, w_keyval, w_keyval_there)
    (
        query, keyval, level, mixed, hidden_own, hidden_there, mixed_own, mixed_there, middle,
        send, gates, w_out_attn_there,
    ) = attend(
        x, small, small_there, projections, w_out_attn, angles, docs, chosen, experts
    )
    returned, results, grad_in, grad_in_other, grad_out_matrix, grad_out_other = run_experts(
        send, d_out_all, in_own, w_out[0], experts
    )
    (
        output, grad_middle, middle_low, middle_there, grad_query, query_there, grad_keyval,
        keyval_there, small_grads,
    ) = attend_back(
        returned, gates, small, small_there, middle, grad_out, send, w_out_attn, w_out_attn_there,
        query, keyval, angles, docs, level, mixed, results, experts,
    )
    attn_sum, query_sum, keyval_sum, small_sum, grad_input, in_there, out_there = finish(
        x, grad_middle, small, small_there, small_grads, projections, (hidden_own, hidden_there),
        (mixed_own, mixed_there), (middle_low, middle_there), (grad_query, query_there),
        (grad_keyval, keyval_there), grad_in_other, grad_out_other,
    )
    query_sum, keyval_sum, attn_sum, grad_w_in, grad_w_out = widen(
        query_sum, keyval_sum, attn_sum, grad_in, in_there, grad_out_matrix, out_there
    )
    return (
        output[None],
        grad_input[None],
        small_sum[experts],
        query_sum,
        keyval_sum,
        attn_sum,
        small_sum[experts + 1],
        small_sum[:experts].T,
        jnp.swapaxes(grad_w_in.reshape(2, -1, D), 1, 2)[None],
        grad_w_out,
    )


def solution(mesh):
    in_specs = (
        P("wa", "ctx", None),
        P("wa", None),
        P("wa", "ctx", None),
        P("wa"),
        P("wa", None),
        P("wa", None),
        P("wa", None),
        P("wa"),
        P("wa", None),
        P("ctx", None, None, "wa"),
        P("ctx", "wa", None),
        P("wa", "ctx", None),
    )
    out_specs = (
        P("wa", "ctx", None),
        P("wa", "ctx", None),
        P("wa"),
        P("wa", None),
        P("wa", None),
        P("wa", None),
        P("wa"),
        P("wa", None),
        P("ctx", None, None, "wa"),
        P("ctx", "wa", None),
    )
    depth = mesh.shape["ctx"]
    body = gathered_body if depth == 16 else routed_body
    return jax.shard_map(body, mesh=mesh, in_specs=in_specs, out_specs=out_specs, check_vma=False)
```

```python
import functools
import math

import jax
import jax.numpy as jnp
from jax import lax
from jax.experimental import pallas as pl
from jax.experimental.pallas import tpu as pltpu
from jax.sharding import PartitionSpec as P

D = 1536
HEADS = 12
KV_HEADS = 2
HEAD_DIM = 128
TOP = 4
BLOCK = 256


EPSILON = 1e-06
THETA = 1000000.0
NEGATIVE = -1e30


def rms_scale(values, gain_vec):
    return (
        values * lax.rsqrt(jnp.mean(values * values, axis=-1, keepdims=True) + EPSILON) * gain_vec
    )


def rotate(values, angles):
    half_dim = values.shape[-1] // 2
    cosine = jnp.cos(angles)
    sine_part = jnp.sin(angles)
    first_half = values[..., :half_dim]
    second = values[..., half_dim:]
    return jnp.concatenate(
        [first_half * cosine - second * sine_part, second * cosine + first_half * sine_part],
        axis=-1,
    )


def angle_table(positions):
    half_dim = HEAD_DIM // 2
    frequency = THETA ** (-2.0 * jnp.arange(half_dim, dtype=jnp.float32) / HEAD_DIM)
    return (positions.astype(jnp.float32)[:, None] * frequency[None, :])[:, None, :]


def gated(stacked):
    return jax.nn.gelu(stacked[..., 0, :], approximate=True) * stacked[..., 1, :]


def over_keys(key_rows, running, advance):
    key_count = key_rows.shape[0]
    key_width = math.gcd(key_count, 512)

    def one_turn(state_now, block_index):
        key_offset = block_index * key_width
        key_part = lax.dynamic_slice_in_dim(key_rows, key_offset, key_width, 0)
        return (advance(state_now, key_part, key_offset), None)

    running, unused = lax.scan(
        one_turn, running, jnp.arange(key_count // key_width, dtype=jnp.int32)
    )
    return running


def routed_body(
    layer_input,
    seq_ids,
    routes,
    gain_attn,
    w_query,
    w_keyval,
    w_out_attn,
    gain_ffn,
    router,
    w_in,
    w_out,
    d_out,
):
    ctx_count = lax.axis_size("ctx")
    ctx_index = lax.axis_index("ctx")
    tokens = layer_input.shape[1]
    length = tokens * ctx_count
    experts_all = ctx_count // 2
    capacity = 2 * tokens * TOP // experts_all
    group = HEADS // KV_HEADS
    kv_width = KV_HEADS * HEAD_DIM
    row_count = group * tokens
    scale = HEAD_DIM ** (-0.5)
    gain_one, query_matrix, keyvalue_matrix, attention_matrix = (
        lax.all_gather(gain_attn, "wa", axis=0, tiled=True),
        lax.all_gather(w_query, "wa", axis=0, tiled=True),
        lax.all_gather(w_keyval, "wa", axis=0, tiled=True),
        lax.all_gather(w_out_attn, "wa", axis=0, tiled=True),
    )
    residual = layer_input[0].astype(jnp.float32)
    normed_one, norm_one_back = jax.vjp(rms_scale, residual, gain_one.astype(jnp.float32))
    hidden_first_norm = normed_one.astype(jnp.bfloat16)
    positions = ctx_index * tokens + jnp.arange(tokens, dtype=jnp.int32)
    angles = angle_table(positions)
    query_projected = jnp.dot(
        hidden_first_norm, query_matrix, preferred_element_type=jnp.float32
    ).reshape(tokens, HEADS, HEAD_DIM)
    keyvalue_projected = jnp.dot(
        hidden_first_norm, keyvalue_matrix, preferred_element_type=jnp.float32
    )
    key_pre = keyvalue_projected[:, :kv_width].reshape(tokens, KV_HEADS, HEAD_DIM)
    query_low = rotate(query_projected, angles).astype(jnp.bfloat16)
    key_low = rotate(key_pre, angles).astype(jnp.bfloat16)
    value_low = keyvalue_projected[:, kv_width:].astype(jnp.bfloat16)
    keyval_send = jnp.concatenate([key_low.reshape(tokens, kv_width), value_low], axis=1)
    query_rows = (
        query_low.reshape(tokens, KV_HEADS, group, HEAD_DIM)
        .transpose(1, 2, 0, 3)
        .reshape(KV_HEADS, row_count, HEAD_DIM)
    )
    doc_row = seq_ids[0]
    query_docs = lax.dynamic_slice_in_dim(doc_row, ctx_index * tokens, tokens, 0)
    query_blocks = positions // BLOCK

    def block_scores(key_part, first_key):
        key_count = key_part.shape[0]
        split_part = key_part.reshape(key_count, 2, KV_HEADS, HEAD_DIM)
        keys_here = split_part[:, 0]
        values_here = split_part[:, 1]
        scores = (
            jnp.einsum("hrd,nhd->hrn", query_rows, keys_here, preferred_element_type=jnp.float32)
            * scale
        )
        key_docs = lax.dynamic_slice_in_dim(doc_row, first_key, key_count, 0)
        key_blocks = (first_key + jnp.arange(key_count, dtype=jnp.int32)) // BLOCK
        allowed = (query_docs[:, None] == key_docs[None, :]) & (
            key_blocks[None, :] <= query_blocks[:, None]
        )
        allowed = jnp.broadcast_to(allowed[None], (group, tokens, key_count)).reshape(
            1, row_count, key_count
        )
        return (jnp.where(allowed, scores, NEGATIVE), allowed, keys_here, values_here)

    def probs_of(masked, allowed, largest, totals):
        return jnp.where(allowed, jnp.exp(masked - largest[..., None]) / totals[..., None], 0.0)

    def stats_step(running, key_part, first_key):
        largest, totals = running
        masked, allowed, keys_here, values_here = block_scores(key_part, first_key)
        new_largest = jnp.maximum(largest, jnp.max(masked, axis=-1))
        weights = jnp.where(allowed, jnp.exp(masked - new_largest[..., None]), 0.0)
        return (new_largest, totals * jnp.exp(largest - new_largest) + jnp.sum(weights, axis=-1))

    start_stats = (
        jnp.full((KV_HEADS, row_count), NEGATIVE, jnp.float32),
        jnp.zeros((KV_HEADS, row_count), jnp.float32),
    )
    largest, totals = over_keys(
        lax.all_gather(keyval_send, "ctx", axis=0, tiled=True), start_stats, stats_step
    )

    def values_step(running, key_part, first_key):
        masked, allowed, keys_here, values_here = block_scores(key_part, first_key)
        probs_low = probs_of(masked, allowed, largest, totals).astype(jnp.bfloat16)
        return running + jnp.einsum(
            "hrn,nhd->hrd", probs_low, values_here, preferred_element_type=jnp.float32
        )

    start_values = jnp.zeros((KV_HEADS, row_count, HEAD_DIM), jnp.float32)
    mixed_rows = over_keys(
        lax.all_gather(keyval_send, "ctx", axis=0, tiled=True), start_values, values_step
    )
    mixed_low = (
        mixed_rows.reshape(KV_HEADS, group, tokens, HEAD_DIM)
        .transpose(2, 0, 1, 3)
        .reshape(tokens, HEADS * HEAD_DIM)
        .astype(jnp.bfloat16)
    )
    middle_activation = residual + jnp.dot(
        mixed_low, attention_matrix, preferred_element_type=jnp.float32
    )
    gain_two, router_full, w_in_full, w_out_full = (
        lax.all_gather(gain_ffn, "wa", axis=0, tiled=True),
        lax.all_gather(router, "wa", axis=0, tiled=True),
        lax.all_gather(w_in, "wa", axis=3, tiled=True),
        lax.all_gather(w_out, "wa", axis=1, tiled=True),
    )
    in_half = w_in_full[0]
    out_half = w_out_full[0]
    normed_two, norm_two_back = jax.vjp(rms_scale, middle_activation, gain_two.astype(jnp.float32))
    hidden_second_norm = normed_two.astype(jnp.bfloat16)
    router_logits = jnp.dot(hidden_second_norm, router_full, preferred_element_type=jnp.float32)
    route_ids = routes[0]

    def gate_values(logit_rows):
        return jax.nn.softmax(jnp.take_along_axis(logit_rows, route_ids, axis=-1), axis=-1)

    gates, gate_back = jax.vjp(gate_values, router_logits)
    flat_ids = route_ids.reshape(tokens * TOP)
    expert_hits = (flat_ids[:, None] == jnp.arange(experts_all, dtype=jnp.int32)[None, :]).astype(
        jnp.int32
    )
    ranks = jnp.sum(expert_hits * (jnp.cumsum(expert_hits, axis=0) - expert_hits), axis=1)
    slot_first = 2 * flat_ids * capacity + ranks
    slot_second = slot_first + capacity
    slot_total = ctx_count * capacity
    slot_numbers = jnp.arange(slot_total, dtype=jnp.int32)[:, None]
    placed = (
        (slot_first[None, :] == slot_numbers) | (slot_second[None, :] == slot_numbers)
    ).astype(jnp.bfloat16)
    dispatch = jnp.sum(placed.reshape(slot_total, tokens, TOP), axis=2)
    send_rows = (
        jnp.dot(dispatch, hidden_second_norm, preferred_element_type=jnp.float32)
        .astype(jnp.bfloat16)
        .reshape(ctx_count, capacity, D)
    )
    arrived = lax.all_to_all(send_rows, "ctx", split_axis=0, concat_axis=0, tiled=True)
    stacked = jnp.einsum("ncd,gdf->ncgf", arrived, in_half, preferred_element_type=jnp.float32)
    hidden_low = gated(stacked).astype(jnp.bfloat16)
    result = jnp.einsum(
        "ncf,fd->ncd", hidden_low, out_half, preferred_element_type=jnp.float32
    ).astype(jnp.bfloat16)
    returned_rows = lax.all_to_all(result, "ctx", split_axis=0, concat_axis=0, tiled=True)
    returned_flat = returned_rows.reshape(slot_total, D)
    pair_rows = (
        returned_flat[slot_first].astype(jnp.float32)
        + returned_flat[slot_second].astype(jnp.float32)
    ).reshape(tokens, TOP, D)
    output = (middle_activation + jnp.sum(gates[:, :, None] * pair_rows, axis=1)).astype(
        jnp.bfloat16
    )
    grad_out = d_out[0].astype(jnp.float32)
    grad_gates = jnp.sum(pair_rows * grad_out[:, None, :], axis=-1)
    (grad_logits,) = gate_back(grad_gates)
    grad_logits_low = grad_logits.astype(jnp.bfloat16)
    gate_slots = jnp.dot(
        placed.astype(jnp.float32), gates.reshape(tokens * TOP), precision=lax.Precision.HIGHEST
    )
    routed_grad = jnp.dot(dispatch, d_out[0], preferred_element_type=jnp.float32)
    grad_send_rows = (
        (gate_slots[:, None] * routed_grad).astype(jnp.bfloat16).reshape(ctx_count, capacity, D)
    )
    grad_arrived = lax.all_to_all(grad_send_rows, "ctx", split_axis=0, concat_axis=0, tiled=True)
    grad_hidden = jnp.einsum(
        "ncd,fd->ncf", grad_arrived, out_half, preferred_element_type=jnp.float32
    )
    hidden_again, gated_back = jax.vjp(gated, stacked)
    (grad_stacked,) = gated_back(grad_hidden)
    grad_stacked_low = grad_stacked.astype(jnp.bfloat16)
    grad_rows = jnp.einsum(
        "ncgf,gdf->ncd", grad_stacked_low, in_half, preferred_element_type=jnp.float32
    ).astype(jnp.bfloat16)
    grad_returned = lax.all_to_all(grad_rows, "ctx", split_axis=0, concat_axis=0, tiled=True)
    grad_w_in = jnp.einsum(
        "ncd,ncgf->gdf", arrived, grad_stacked_low, preferred_element_type=jnp.float32
    )[None]
    grad_w_out = jnp.einsum(
        "ncf,ncd->fd",
        hidden_again.astype(jnp.bfloat16),
        grad_arrived,
        preferred_element_type=jnp.float32,
    )[None]
    grad_hidden_two = jnp.einsum(
        "st,sd->td",
        dispatch,
        grad_returned.reshape(slot_total, D),
        preferred_element_type=jnp.float32,
    )
    grad_hidden_two = grad_hidden_two + jnp.dot(
        grad_logits_low, router_full.T, preferred_element_type=jnp.float32
    )
    grad_router = jnp.dot(hidden_second_norm.T, grad_logits_low, preferred_element_type=jnp.float32)
    grad_middle_norm, grad_gain_two = norm_two_back(grad_hidden_two)
    grad_middle = grad_out + grad_middle_norm
    grad_middle_low = grad_middle.astype(jnp.bfloat16)
    grad_attn_weight = jnp.dot(mixed_low.T, grad_middle_low, preferred_element_type=jnp.float32)
    grad_mixed = jnp.dot(
        grad_middle_low, attention_matrix.T, preferred_element_type=jnp.float32
    ).astype(jnp.bfloat16)
    grad_rows_out = (
        grad_mixed.reshape(tokens, KV_HEADS, group, HEAD_DIM)
        .transpose(1, 2, 0, 3)
        .reshape(KV_HEADS, row_count, HEAD_DIM)
    )
    delta = jnp.sum(grad_rows_out.astype(jnp.float32) * mixed_rows, axis=-1)

    def score_grads(key_part, first_key):
        masked, allowed, keys_here, values_here = block_scores(key_part, first_key)
        probs = probs_of(masked, allowed, largest, totals)
        grad_probs = jnp.einsum(
            "hrd,nhd->hrn", grad_rows_out, values_here, preferred_element_type=jnp.float32
        )
        grad_scores = (probs * (grad_probs - delta[..., None])).astype(jnp.bfloat16)
        return (grad_scores, probs.astype(jnp.bfloat16), keys_here)

    def key_terms(grad_scores, probs_low, key_count):
        grad_keys = (
            jnp.einsum("hrn,hrd->nhd", grad_scores, query_rows, preferred_element_type=jnp.float32)
            * scale
        )
        grad_values = jnp.einsum(
            "hrn,hrd->nhd", probs_low, grad_rows_out, preferred_element_type=jnp.float32
        )
        return jnp.concatenate(
            [grad_keys.reshape(key_count, kv_width), grad_values.reshape(key_count, kv_width)],
            axis=1,
        )

    start_query = jnp.zeros((KV_HEADS, row_count, HEAD_DIM), jnp.float32)

    def back_step(running, key_part, first_key):
        grad_query_rows, grad_keyvals = running
        grad_scores, probs_low, keys_here = score_grads(key_part, first_key)
        grad_query_rows = (
            grad_query_rows
            + jnp.einsum("hrn,nhd->hrd", grad_scores, keys_here, preferred_element_type=jnp.float32)
            * scale
        )
        fresh = key_terms(grad_scores, probs_low, key_part.shape[0])
        return (grad_query_rows, lax.dynamic_update_slice_in_dim(grad_keyvals, fresh, first_key, 0))

    start_back = (start_query, jnp.zeros((length, 2 * kv_width), jnp.float32))
    grad_query_rows, grad_keyvals = over_keys(
        lax.all_gather(keyval_send, "ctx", axis=0, tiled=True), start_back, back_step
    )
    grad_keyval_mine = lax.psum_scatter(grad_keyvals, "ctx", scatter_dimension=0, tiled=True)
    grad_query = grad_query_rows.reshape(KV_HEADS, group, tokens, HEAD_DIM).transpose(2, 0, 1, 3)
    grad_query_pre = (
        rotate(grad_query.reshape(tokens, HEADS, HEAD_DIM), -angles)
        .reshape(tokens, HEADS * HEAD_DIM)
        .astype(jnp.bfloat16)
    )
    grad_key_pre = rotate(
        grad_keyval_mine[:, :kv_width].reshape(tokens, KV_HEADS, HEAD_DIM), -angles
    ).reshape(tokens, kv_width)
    grad_keyval_pre = jnp.concatenate(
        [grad_key_pre, grad_keyval_mine[:, kv_width:]], axis=1
    ).astype(jnp.bfloat16)
    grad_hidden_one = jnp.dot(
        grad_query_pre, query_matrix.T, preferred_element_type=jnp.float32
    ) + jnp.dot(grad_keyval_pre, keyvalue_matrix.T, preferred_element_type=jnp.float32)
    grad_query_weight = jnp.dot(
        hidden_first_norm.T, grad_query_pre, preferred_element_type=jnp.float32
    )
    grad_keyval_weight = jnp.dot(
        hidden_first_norm.T, grad_keyval_pre, preferred_element_type=jnp.float32
    )
    grad_residual_norm, grad_gain_one = norm_one_back(grad_hidden_one)
    grad_input = (grad_middle + grad_residual_norm).astype(jnp.bfloat16)
    shares = (
        lax.psum_scatter(
            grad_gain_one.astype(jnp.bfloat16), "wa", scatter_dimension=0, tiled=True
        ).astype(jnp.float32),
        lax.psum_scatter(
            grad_query_weight.astype(jnp.bfloat16), "wa", scatter_dimension=0, tiled=True
        ).astype(jnp.float32),
        lax.psum_scatter(
            grad_keyval_weight.astype(jnp.bfloat16), "wa", scatter_dimension=0, tiled=True
        ).astype(jnp.float32),
        lax.psum_scatter(
            grad_attn_weight.astype(jnp.bfloat16), "wa", scatter_dimension=0, tiled=True
        ).astype(jnp.float32),
        lax.psum_scatter(
            grad_gain_two.astype(jnp.bfloat16), "wa", scatter_dimension=0, tiled=True
        ).astype(jnp.float32),
        lax.psum_scatter(
            grad_router.astype(jnp.bfloat16), "wa", scatter_dimension=0, tiled=True
        ).astype(jnp.float32),
        lax.psum_scatter(
            grad_w_in.astype(jnp.bfloat16), "wa", scatter_dimension=3, tiled=True
        ).astype(jnp.float32),
        lax.psum_scatter(
            grad_w_out.astype(jnp.bfloat16), "wa", scatter_dimension=1, tiled=True
        ).astype(jnp.float32),
    )
    summed = lax.psum((shares[0], shares[1], shares[2], shares[3], shares[4], shares[5]), "ctx")
    return (
        output[None],
        grad_input[None],
        summed[0],
        summed[1],
        summed[2],
        summed[3],
        summed[4],
        summed[5],
        shares[6],
        shares[7],
    )

MESH = pl.DeviceIdType.MESH
VMEM_LIMIT = 60 * 1024 * 1024


def chip_place():
    count = lax.axis_size("ctx")
    me = lax.axis_index("ctx")
    return me // 4, lax.rem(me // 2, 2), lax.rem(me, 2), count // 4


def ctx_of(z, y, c):
    return (z * 2 + y) * 2 + c


def greet(across_x=False):
    z, y, c, depth = chip_place()
    barrier = pltpu.get_barrier_semaphore()

    def signal(device):
        pl.semaphore_signal(barrier, 1, device_id=device, device_id_type=MESH)

    signal({"ctx": ctx_of(z, y, 1 - c)})
    signal({"ctx": ctx_of(z, 1 - y, c)})
    if across_x:
        signal({"wa": 1 - lax.axis_index("wa")})
    pl.when(z > 0)(lambda: signal({"ctx": ctx_of(z - 1, y, c)}))
    pl.when(z < depth - 1)(lambda: signal({"ctx": ctx_of(z + 1, y, c)}))
    ends = (z > 0).astype(jnp.int32) + (z < depth - 1).astype(jnp.int32)
    pl.semaphore_wait(barrier, (3 if across_x else 2) + ends)


def remote(source, target_ref, sems, at, device):
    return pltpu.make_async_remote_copy(
        src_ref=source,
        dst_ref=target_ref,
        send_sem=sems.at[(0,) + at],
        recv_sem=sems.at[(1,) + at],
        device_id=device,
        device_id_type=MESH,
    )


def each(step, act):
    z, _, _, depth = chip_place()
    if step == 0:
        act(z)
    else:
        pl.when(z + step < depth)(lambda: act(z + step))
        pl.when(z - step >= 0)(lambda: act(z - step))


def nearest(k):
    z, _, _, depth = chip_place()
    low = jnp.minimum(z, depth - 1 - z)
    step = (k + 1) // 2
    place = jnp.where(k > 2 * low, k, jnp.where(lax.rem(k, 2) == 1, low - step, low + step))
    return jnp.where(z == low, place, depth - 1 - place)


class Gather:
    def __init__(self, out, rows, sems, part=0, parts=1):
        self.out, self.block, self.rows = out, rows, rows // parts
        self.first = part * self.rows
        self.z_sems, self.y_sems, self.c_sems = sems
        self.z, self.y, self.c, self.depth = chip_place()

    @staticmethod
    def sems(depth):
        return [
            pltpu.SemaphoreType.DMA((2, 2, depth)),
            pltpu.SemaphoreType.DMA((2, depth)),
            pltpu.SemaphoreType.DMA((2, 2 * depth)),
        ]

    def slot(self, z, y, c):
        start = ctx_of(z, y, c) * self.block + self.first
        return self.out.at[pl.ds(pl.multiple_of(start, 16), self.rows)]

    def own(self):
        return self.slot(self.z, self.y, self.c)

    def on_z(self, way, of_z, source=None):
        goal = jnp.minimum(self.z + 1, self.depth - 1) if way == 0 else jnp.maximum(self.z - 1, 0)
        block = self.slot(of_z, self.y, self.c)
        target = {"ctx": ctx_of(goal, self.y, self.c)}
        return remote(block if source is None else source, block, self.z_sems, (way, of_z), target)

    def on_y(self, of_z, mine=True, source=None):
        block = self.slot(of_z, self.y if mine else 1 - self.y, self.c)
        target = {"ctx": ctx_of(self.z, 1 - self.y, self.c)}
        return remote(block if source is None else source, block, self.y_sems, (of_z,), target)

    def on_core(self, of_z, of_y, mine=True, source=None):
        block = self.slot(of_z, of_y, self.c if mine else 1 - self.c)
        target = {"ctx": ctx_of(self.z, self.y, 1 - self.c)}
        at = (of_z * 2 + of_y,)
        return remote(block if source is None else source, block, self.c_sems, at, target)

    def start(self, source=None):
        z, depth = self.z, self.depth
        if source is not None:
            source = source.at[pl.ds(self.first, self.rows)]
        pl.when(z < depth - 1)(lambda: self.on_z(0, z, source).start())
        pl.when(z > 0)(lambda: self.on_z(1, z, source).start())
        self.on_y(z, source=source).start()
        self.on_core(z, self.y, source=source).start()

    def along_z(self, step):
        z, depth = self.z, self.depth

        def from_side(way, of_z, more):
            self.on_z(way, of_z).wait_recv()
            pl.when(more)(lambda: self.on_z(way, of_z).start())
            self.on_y(of_z).start()
            self.on_core(of_z, self.y).start()

        pl.when(z - step >= 0)(lambda: from_side(0, z - step, z < depth - 1))
        pl.when(z + step < depth)(lambda: from_side(1, z + step, z > 0))

    def along_y(self, step):
        def across(of_z):
            self.on_y(of_z, mine=False).wait_recv()
            self.on_core(of_z, 1 - self.y).start()

        each(step, across)

    def finish(self):
        z, depth = self.z, self.depth
        for of_z in range(depth):
            pl.when((z < depth - 1) & (of_z <= z))(lambda: self.on_z(0, of_z).wait_send())
            pl.when((z > 0) & (of_z >= z))(lambda: self.on_z(1, of_z).wait_send())
            self.on_y(of_z).wait_send()
            for of_y in range(2):
                self.on_core(of_z, of_y).wait_send()
                self.on_core(of_z, of_y, mine=False).wait_recv()


class Several:
    def __init__(self, members):
        self.members = members

    def __getattr__(self, name):
        def every(*given, **named):
            for member in self.members:
                getattr(member, name)(*given, **named)

        return every


def gather_parts(out, rows, sems, parts):
    return Several(
        [Gather(out, rows, sems[3 * i : 3 * i + 3], i, parts) for i in range(parts)]
    )


def follow(gather):
    depth = chip_place()[3]
    gather.along_z(1)
    for step in range(depth):
        if step >= 1 and step + 1 < depth:
            gather.along_z(step + 1)
        gather.along_y(step)
    gather.finish()


def add_into(target, terms, rows):
    some = 32 if rows % 32 == 0 else 48 if rows % 48 == 0 else 16

    @pl.loop(0, rows // some)
    def _(turn):
        at = pl.ds(pl.multiple_of(turn * some, 16), some)
        total = terms[0][at, :].astype(jnp.float32)
        for term in terms[1:]:
            total = total + term[at, :].astype(jnp.float32)
        target[at, :] = total.astype(target.dtype)


class Scatter:
    def __init__(self, part, scratch, sums=None, piece=0, pieces=1):
        self.part = part
        self.from_core, self.totals, self.from_y, self.from_z = scratch[:4]
        self.sums = self.totals if sums is None else sums
        self.c_sems, self.y_sems, self.z_sems = scratch[4:]
        self.block = self.totals.shape[1]
        self.rows = self.block // pieces
        self.first = piece * self.rows
        self.z, self.y, self.c, self.depth = chip_place()

    @staticmethod
    def sems(depth):
        return [
            pltpu.SemaphoreType.DMA((2, 2 * depth)),
            pltpu.SemaphoreType.DMA((2, depth)),
            pltpu.SemaphoreType.DMA((2, 2, depth)),
        ]

    @staticmethod
    def scratch(depth, rows, columns, pieces=1):
        return [
            pltpu.VMEM((2 * depth, rows, columns), jnp.bfloat16),
            pltpu.VMEM((2 * depth, rows, columns), jnp.bfloat16),
            pltpu.VMEM((depth, rows, columns), jnp.bfloat16),
            pltpu.VMEM((depth + 1, rows, columns), jnp.bfloat16),
        ] + Scatter.sems(depth) * pieces

    def of(self, ref, place):
        return ref.at[place, pl.ds(self.first, self.rows)]

    def split(self):
        return len(self.part.shape) == 3

    def share(self, chip, c):
        start = (chip * 2 + c) * self.block + self.first
        return self.part.at[pl.ds(pl.multiple_of(start, 16), self.rows)]

    def on_core(self, chip):
        target = {"ctx": ctx_of(self.z, self.y, 1 - self.c)}
        source = self.of(self.part, chip) if self.split() else self.share(chip, 1 - self.c)
        return remote(source, self.of(self.from_core, chip), self.c_sems, (chip,), target)

    def send_core(self, chip):
        self.on_core(chip).start()

    def send_y(self, of_z):
        self.on_y(of_z).start()

    def on_y(self, of_z):
        target = {"ctx": ctx_of(self.z, 1 - self.y, self.c)}
        source = self.of(self.sums, of_z * 2 + 1 - self.y)
        return remote(source, self.of(self.from_y, of_z), self.y_sems, (of_z,), target)

    def on_z(self, way, of_z):
        goal = jnp.minimum(self.z + 1, self.depth - 1) if way == 0 else jnp.maximum(self.z - 1, 0)
        place = of_z if way == 0 else jnp.where(of_z == goal, self.depth, of_z)
        source = self.of(self.totals, of_z * 2 + self.y)
        target = {"ctx": ctx_of(goal, self.y, self.c)}
        return remote(source, self.of(self.from_z, place), self.z_sems, (way, of_z), target)

    def start(self):
        def send(of_z):
            self.on_core(of_z * 2 + 1 - self.y).start()
            self.on_core(of_z * 2 + self.y).start()

        for step in range(self.depth - 1, -1, -1):
            each(step, send)

    def add_chip(self, of_z, other, send=True):
        chip = of_z * 2 + (1 - self.y if other else self.y)
        self.on_core(chip).wait_recv()
        total = self.of(self.sums, chip)
        own = total if self.split() else self.share(chip, self.c)
        add_into(total, (own, self.of(self.from_core, chip)), self.rows)
        if other and send:
            self.on_y(of_z).start()

    def add_cores(self, step):
        def add(of_z):
            self.add_chip(of_z, True)
            self.add_chip(of_z, False)

        each(step, add)

    def add_y_of(self, of_z):
        z, depth = self.z, self.depth
        self.on_y(of_z).wait_recv()
        place = of_z * 2 + self.y
        total, own = self.of(self.totals, place), self.of(self.sums, place)
        other = self.of(self.from_y, of_z)
        upward, downward = (of_z > z) & (z > 0), (of_z < z) & (z < depth - 1)
        pl.when(upward)(lambda: self.on_z(0, of_z).wait_recv())
        pl.when(downward)(lambda: self.on_z(1, of_z).wait_recv())

        @pl.when(upward | downward)
        def _():
            add_into(total, (own, other, self.of(self.from_z, of_z)), self.rows)

        @pl.when(jnp.logical_not(upward | downward))
        def _():
            add_into(total, (own, other), self.rows)

        pl.when(of_z > z)(lambda: self.on_z(0, of_z).start())
        pl.when(of_z < z)(lambda: self.on_z(1, of_z).start())

    def add_y(self, step):
        each(step, self.add_y_of)

    def last(self, result):
        z, depth = self.z, self.depth
        own = self.of(self.totals, z * 2 + self.y)
        low, high = self.of(self.from_z, z), self.of(self.from_z, depth)
        result = result.at[pl.ds(self.first, self.rows)]
        pl.when(z > 0)(lambda: self.on_z(0, z).wait_recv())
        pl.when(z < depth - 1)(lambda: self.on_z(1, z).wait_recv())
        inside = (z > 0) & (z < depth - 1)
        pl.when(inside)(lambda: add_into(result, (own, low, high), self.rows))
        pl.when(z == 0)(lambda: add_into(result, (own, high), self.rows))
        pl.when(z == depth - 1)(lambda: add_into(result, (own, low), self.rows))

    def finish(self, cores=True):
        for of_z in range(self.depth):
            self.on_y(of_z).wait_send()
            if cores:
                self.on_core(of_z * 2).wait_send()
                self.on_core(of_z * 2 + 1).wait_send()
            pl.when(of_z > self.z)(lambda: self.on_z(0, of_z).wait_send())
            pl.when(of_z < self.z)(lambda: self.on_z(1, of_z).wait_send())


def scatter_parts(part, scratch, pieces, sums=None):
    arrays, sems = tuple(scratch[:4]), tuple(scratch[4:])
    return Several(
        [
            Scatter(part, arrays + sems[3 * i : 3 * i + 3], sums, i, pieces)
            for i in range(pieces)
        ]
    )


def call(kernel, out, scratch, number, name, *operands, outside=(), outside_out=(), late=()):
    many = isinstance(out, (tuple, list))
    count, results = len(operands), len(out) if many else 1
    late = tuple(late)

    def spec(position, far):
        return pl.BlockSpec(memory_space=pl.ANY if position in far else pltpu.VMEM)

    def with_late(*refs):
        near, sems = refs[-len(late) - 1 : -1], refs[-1]
        copies = {
            i: pltpu.make_async_copy(refs[i], near[k], sems.at[k]) for k, i in enumerate(late)
        }
        for copy in copies.values():
            copy.start()
        held = [near[late.index(i)] if i in late else refs[i] for i in range(count)]

        def arrive(*which):
            for i in which:
                copies[i].wait()

        kernel(arrive, *held, *refs[count : -len(late) - 1])

    if late:
        scratch = list(scratch) + [pltpu.VMEM(operands[i].shape, operands[i].dtype) for i in late]
        scratch.append(pltpu.SemaphoreType.DMA((len(late),)))
    far = tuple(outside) + late
    out_specs = [spec(i, outside_out) for i in range(results)]
    return pl.pallas_call(
        with_late if late else kernel,
        out_shape=out,
        in_specs=[spec(i, far) for i in range(count)],
        out_specs=out_specs if many else out_specs[0],
        scratch_shapes=scratch,
        compiler_params=pltpu.CompilerParams(
            collective_id=number,
            has_side_effects=number is not None,
            vmem_limit_bytes=VMEM_LIMIT,
        ),
        name=name,
    )(*operands)


class Relay:
    def __init__(self, source, out, sems, parts=1):
        self.source, self.out, self.sems, self.parts = source, out, sems, parts
        self.z, self.y, self.c, _ = chip_place()
        self.rows = source.shape[0] // (2 * parts)

    @staticmethod
    def semaphores():
        return pltpu.SemaphoreType.DMA((2, 4))

    def block(self, ref, part, c):
        return ref.at[pl.ds(pl.multiple_of((c * self.parts + part) * self.rows, 16), self.rows)]

    def on_x(self, part):
        source, target = self.block(self.source, part, self.c), self.block(self.out, part, self.c)
        return remote(source, target, self.sems, (part,), {"wa": 1 - lax.axis_index("wa")})

    def on_core(self, part, c):
        block = self.block(self.out, part, c)
        return remote(
            block, block, self.sems, (2 + part,), {"ctx": ctx_of(self.z, self.y, 1 - self.c)}
        )

    def start(self):
        for part in range(self.parts):
            self.on_x(part).start()

    def pass_on(self, part=0):
        self.on_x(part).wait_recv()
        self.on_core(part, self.c).start()

    def finish(self):
        for part in range(self.parts):
            self.on_x(part).wait_send()
            self.on_core(part, self.c).wait_send()
            self.on_core(part, 1 - self.c).wait_recv()


def front(d_out, w_query, w_keyval, small):
    count, rows = lax.axis_size("ctx"), d_out.shape[0]
    depth = count // 4

    def kernel(
        d_out_ref, query_ref, keyval_ref, small_ref,
        d_out_all, query_there, keyval_there, small_there, *sems,
    ):
        gather = gather_parts(d_out_all, rows, sems[:6], 2)
        query_sems, keyval_sems, small_sems, own_sem = sems[6:]
        query = Relay(query_ref, query_there, query_sems, parts=2)
        keyval = Relay(keyval_ref, keyval_there, keyval_sems)
        partner = {"wa": 1 - lax.axis_index("wa")}
        swap = remote(small_ref, small_there, small_sems, (0,), partner)
        keep = pltpu.make_async_copy(
            d_out_ref, Gather(d_out_all, rows, sems[:3]).own(), own_sem.at[0]
        )
        keep.start()
        greet(across_x=True)
        swap.start()
        query.start()
        keyval.start()
        gather.start(d_out_ref)
        gather.along_z(1)
        gather.along_y(0)
        gather.along_z(2)
        gather.along_y(1)
        query.pass_on(0)
        gather.along_z(3)
        gather.along_y(2)
        query.pass_on(1)
        keyval.pass_on()
        gather.along_y(3)
        gather.finish()
        query.finish()
        keyval.finish()
        swap.wait()
        keep.wait()

    def like(values):
        return jax.ShapeDtypeStruct(values.shape, values.dtype)

    out = [
        jax.ShapeDtypeStruct((count * rows, d_out.shape[1]), d_out.dtype),
        like(w_query), like(w_keyval), like(small),
    ]
    scratch = Gather.sems(depth) * 2 + [Relay.semaphores()] * 2
    scratch += [pltpu.SemaphoreType.DMA((2, 1)), pltpu.SemaphoreType.DMA((1,))]
    every = range(4)
    return call(
        kernel, out, scratch, 0, "front",
        d_out, w_query, w_keyval, small, outside=every, outside_out=every,
    )


def rows_by_rows(left, right):
    return lax.dot_general(
        left, right, (((1,), (1,)), ((), ())), preferred_element_type=jnp.float32
    )


def columns_by_columns(left, right):
    return lax.dot_general(
        left, right, (((0,), (0,)), ((), ())), preferred_element_type=jnp.float32
    )


def allowed_bias(doc_row, doc_column, tokens):
    keys = doc_row.shape[1]
    query_block = lax.axis_index("ctx") * tokens // BLOCK
    key_block = lax.broadcasted_iota(jnp.int32, (tokens, keys), 1) // BLOCK
    allowed = (doc_row == doc_column) & (key_block <= query_block)
    return jnp.where(allowed, 0.0, NEGATIVE)


def side_columns(own):
    side = lax.axis_index("wa")
    return pl.ds(pl.multiple_of((side if own else 1 - side) * (D // 2), 128), D // 2)


def turned(values, cosine, sine):
    heads = []
    for head in range(values.shape[1] // HEAD_DIM):
        one = values[:, head * HEAD_DIM : (head + 1) * HEAD_DIM]
        heads.append(one * cosine + pltpu.roll(one, HEAD_DIM // 2, axis=1) * sine)
    return jnp.concatenate(heads, axis=1)


def normed(values, gain_vec):
    return values * lax.rsqrt(jnp.mean(values * values, axis=-1, keepdims=True) + EPSILON) * gain_vec


def fill_small(full, small, small_there):
    full[:, side_columns(True)] = small[...].astype(jnp.float32)
    full[:, side_columns(False)] = small_there[...].astype(jnp.float32)


def router_block(full, experts):
    rows = full[:experts]
    spare = jnp.zeros((128 - 2 * experts, rows.shape[1]), jnp.float32)
    return jnp.concatenate([rows, rows, spare], axis=0).astype(jnp.bfloat16)


def attend(x, small, small_there, projections, w_out_attn, angles, docs, chosen, experts):
    count, tokens, features = lax.axis_size("ctx"), x.shape[0], x.shape[1]
    depth, length = count // 4, count * tokens
    kv_columns = projections[2].shape[1]

    def kernel(
        arrive, x_ref, small_ref, small_there_ref, query_own, query_other, keyval_own, keyval_other,
        attn_own, attn_own_far, cosine_ref, sine_ref, doc_row, doc_column, chosen_ref,
        query, keyval, level, mixed, hidden, mixed_low, middle, send, gates_out, attn_other,
        full, stacked, bias, attn_sems, *sems,
    ):
        gather = gather_parts(keyval, tokens, sems, 2)
        attn = Relay(attn_own_far, attn_other, attn_sems, parts=2)
        greet(across_x=True)
        attn.start()
        fill_small(full, small_ref, small_there_ref)
        residual = x_ref[...].astype(jnp.float32)
        hidden[...] = normed(residual, full[experts : experts + 1]).astype(jnp.bfloat16)
        own, other = hidden[:, side_columns(True)], hidden[:, side_columns(False)]
        cosine, sine = cosine_ref[...], sine_ref[...]

        def onto(matrix, matrix_other):
            return jnp.dot(own, matrix[...], preferred_element_type=jnp.float32) + jnp.dot(
                other, matrix_other[...], preferred_element_type=jnp.float32
            )

        arrive(5, 6)
        pre = onto(keyval_own, keyval_other)
        keys = turned(pre[:, : kv_columns // 2], cosine, sine)
        block = jnp.concatenate([keys, pre[:, kv_columns // 2 :]], axis=1)
        Gather(keyval, tokens, sems[:3]).own()[...] = block.astype(jnp.bfloat16)
        gather.start()
        arrive(3, 4)
        query[...] = turned(onto(query_own, query_other), cosine, sine).astype(jnp.bfloat16)
        bias[...] = allowed_bias(doc_row[...], doc_column[...], tokens)
        for head in range(HEADS):
            rows = slice(head * tokens, (head + 1) * tokens)
            stacked[rows, :] = query[:, head * 128 : (head + 1) * 128]
        follow(gather)

        @pl.loop(0, HEADS // 2)
        def _(pair):
            rows = pl.ds(pl.multiple_of(pair * 2 * tokens, 128), 2 * tokens)
            kind = pair // (HEADS // KV_HEADS // 2)
            key_part = keyval[:, pl.ds(pl.multiple_of(kind * 128, 128), 128)]
            val_part = keyval[:, pl.ds(pl.multiple_of(kind * 128 + 256, 128), 128)]
            scores = rows_by_rows(stacked[rows, :], key_part) * HEAD_DIM**-0.5
            scores = (scores.reshape(2, tokens, -1) + bias[...][None]).reshape(scores.shape)
            top = jnp.max(scores, axis=-1, keepdims=True)
            weights = jnp.exp(scores - top)
            total = jnp.sum(weights, axis=-1, keepdims=True)
            probs = (weights * (1 / total)).astype(jnp.bfloat16)
            mixture = jnp.dot(probs, val_part, preferred_element_type=jnp.float32)
            for part in range(2):
                columns = pl.ds(pl.multiple_of((pair * 2 + part) * 128, 128), 128)
                mixed[:, columns] = mixture[part * tokens : (part + 1) * tokens]
            column = jnp.broadcast_to(top + jnp.log(total), (2 * tokens, 128))
            level[pl.ds(pair, 1), :] = jnp.transpose(column)[:1]
            pl.when(pair == HEADS // 4)(lambda: attn.pass_on(0))

        attn.pass_on(1)
        mixed_low[...] = mixed[...].astype(jnp.bfloat16)
        attn.finish()
        arrive(7)
        own, other = mixed_low[:, side_columns(True)], mixed_low[:, side_columns(False)]
        middle[...] = residual + onto(attn_own, attn_other)
        hidden_two = normed(middle[...], full[experts + 1 : experts + 2]).astype(jnp.bfloat16)
        send[:, :features] = hidden_two
        logits = rows_by_rows(hidden_two, router_block(full, experts))
        lane = lax.broadcasted_iota(jnp.int32, logits.shape, 1)
        masked = jnp.where(chosen_ref[...] > 0, logits, NEGATIVE)
        weights = jnp.exp(masked - jnp.max(masked, axis=1, keepdims=True))
        total = jnp.sum(jnp.where(lane < experts, weights, 0.0), axis=1, keepdims=True)
        gates = weights / total
        high = gates.astype(jnp.bfloat16).astype(jnp.float32)
        carried = jnp.where(lane < experts, high, jnp.where(lane < 2 * experts, gates - high, 0.0))
        send[:, features:] = carried.astype(jnp.bfloat16)
        gates_out[...] = jnp.where(lane < experts, gates, 0.0)

    def shape(rows, columns, kind=jnp.bfloat16):
        return jax.ShapeDtypeStruct((rows, columns), kind)

    wide = features + 128
    out = [
        shape(tokens, features), shape(length, kv_columns), shape(8, 2 * tokens, jnp.float32),
        shape(tokens, features, jnp.float32), shape(tokens, features), shape(tokens, features),
        shape(tokens, features, jnp.float32), shape(tokens, wide), shape(tokens, 128, jnp.float32),
        shape(*w_out_attn.shape),
    ]
    scratch = [
        pltpu.VMEM((small.shape[0], features), jnp.float32),
        pltpu.VMEM((HEADS * tokens, HEAD_DIM), jnp.bfloat16),
        pltpu.VMEM((tokens, length), jnp.float32),
        Relay.semaphores(),
    ] + Gather.sems(depth) * 2
    return call(
        kernel, out, scratch, 2, "attend",
        x, small, small_there, *projections, w_out_attn, w_out_attn, *angles, *docs, chosen,
        outside=(8,), late=(5, 6, 3, 4, 7),
    )


def norm_back(values, gain_vec, grad):
    scale = lax.rsqrt(jnp.mean(values * values, axis=-1, keepdims=True) + EPSILON)
    through = jnp.mean(gain_vec * grad * values, axis=-1, keepdims=True)
    back = scale * gain_vec * grad - values * (scale * scale * scale * through)
    return back, jnp.sum(grad * values * scale, axis=0, keepdims=True)


def attend_back(
    returned, gates, small, small_there, middle, d_out, send, attn_own, attn_other, query, keyval,
    angles, docs, level, mixed, hidden, mixed_low, results, experts,
):
    count, tokens, features = lax.axis_size("ctx"), query.shape[0], query.shape[1]
    depth, length, kv_columns = count // 4, keyval.shape[0], keyval.shape[1]

    def kernel(
        arrive, returned_ref, gates_ref, small_ref, small_there_ref, middle_ref, d_out_ref, send_ref,
        attn_own_ref, attn_other_ref, query_ref, keyval_ref, cosine_ref, sine_ref, doc_row,
        doc_column, level_ref, mixed_ref, hidden_ref, mixed_low_ref, results_ref,
        output, grad_middle, grad_middle_low, grad_middle_there, grad_query, grad_query_there,
        grad_keyval, grad_keyval_there, small_grads, hidden_own, hidden_there, mixed_own,
        mixed_there,
        full, grad_mixed, turned_query, own_keyval, result_sum, stacked, grads, bias, delta, total,
        part, x_sems, *scratch,
    ):
        result = scatter_parts(
            None, (None,) + tuple(scratch[:3]) + tuple(scratch[3:9]), 2, results_ref
        )
        keyval_sum = scatter_parts(part, scratch[9:], 2)
        partner = {"wa": 1 - lax.axis_index("wa")}
        swaps = [
            remote(source, target, x_sems, (i,), partner)
            for i, (source, target) in enumerate(
                [(grad_middle_low, grad_middle_there), (grad_query, grad_query_there),
                 (grad_keyval, grad_keyval_there),
                 (hidden_ref.at[:, side_columns(False)], hidden_there),
                 (mixed_low_ref.at[:, side_columns(False)], mixed_there)]
            )
        ]
        greet(across_x=True)
        arrive(19)
        for k in range(depth - 1, 0, -1):
            result.send_y(nearest(k))
        swaps[3].start()
        swaps[4].start()
        hidden_own[...] = hidden_ref[:, side_columns(True)]
        mixed_own[...] = mixed_low_ref[:, side_columns(True)]
        fill_small(full, small_ref, small_there_ref)
        arrive(0, 4, 5, 6)
        lane = lax.broadcasted_iota(jnp.int32, (tokens, 128), 1)
        gates = gates_ref[...]
        grad_gates = jnp.where(lane < experts, returned_ref[:, features:], 0.0)
        inner = jnp.sum(gates * grad_gates, axis=1, keepdims=True)
        grad_logits = (gates * (grad_gates - inner)).astype(jnp.bfloat16)
        z = chip_place()[0]
        at_end = (z == 0) | (z == depth - 1)
        within = jnp.logical_not(at_end)
        grad_two = returned_ref[:, :features] + jnp.dot(
            grad_logits, router_block(full, experts), preferred_element_type=jnp.float32
        )
        grad_router = columns_by_columns(grad_logits, send_ref[:, :features])
        back, grad_gain = norm_back(middle_ref[...], full[experts + 1 : experts + 2], grad_two)
        grad_middle[...] = d_out_ref[...].astype(jnp.float32) + back
        grad_middle_low[...] = grad_middle[...].astype(jnp.bfloat16)
        swaps[0].start()
        small_grads[:experts] = grad_router[:experts]
        row = lax.broadcasted_iota(jnp.int32, (small_grads.shape[0] - experts, 1), 0)
        small_grads[experts:] = jnp.where(row == 1, grad_gain, 0.0)
        arrive(7, 8)
        grad_mixed[:, side_columns(True)] = rows_by_rows(
            grad_middle_low[...], attn_own_ref[...]
        ).astype(jnp.bfloat16)
        grad_mixed[:, side_columns(False)] = rows_by_rows(
            grad_middle_low[...], attn_other_ref[...]
        ).astype(jnp.bfloat16)
        allowed = jnp.transpose(allowed_bias(doc_row[...], doc_column[...], tokens))
        bias[:, :tokens] = allowed
        bias[:, tokens:] = allowed
        total[...] = jnp.zeros_like(total)
        arrive(9, 10, 16)
        for head in range(HEADS):
            rows = slice(head * tokens, (head + 1) * tokens)
            columns = slice(head * 128, head * 128 + 128)
            stacked[rows, :] = query_ref[:, columns]
            grads[rows, :] = grad_mixed[:, columns]
            product = grad_mixed[:, columns].astype(jnp.float32) * mixed_ref[:, columns]
            delta[head // 2 : head // 2 + 1, (head % 2) * tokens : (head % 2 + 1) * tokens] = (
                jnp.sum(jnp.transpose(product), axis=0, keepdims=True)
            )

        @pl.loop(0, HEADS // 2)
        def _(pair):
            rows = pl.ds(pl.multiple_of(pair * 2 * tokens, 128), 2 * tokens)
            kind = pair // (HEADS // KV_HEADS // 2)
            key_columns = pl.ds(pl.multiple_of(kind * 128, 128), 128)
            val_columns = pl.ds(pl.multiple_of(kind * 128 + 256, 128), 128)
            key_part, val_part = keyval_ref[:, key_columns], keyval_ref[:, val_columns]
            own, grad = stacked[rows, :], grads[rows, :]
            pair_row = pl.ds(pair, 1)
            scores = rows_by_rows(key_part, own) * HEAD_DIM**-0.5 + bias[...]
            probs = jnp.exp(scores - level_ref[pair_row, :])
            grad_probs = rows_by_rows(val_part, grad)
            grad_scores = (probs * (grad_probs - delta[pair_row, :])).astype(jnp.bfloat16)
            own_grad = jnp.transpose(columns_by_columns(key_part, grad_scores))
            for half in range(2):
                columns = pl.ds(pl.multiple_of((pair * 2 + half) * 128, 128), 128)
                turned_query[:, columns] = (
                    own_grad[half * tokens : (half + 1) * tokens] * HEAD_DIM**-0.5
                )
            total[:, key_columns] += (
                jnp.dot(grad_scores, own, preferred_element_type=jnp.float32) * HEAD_DIM**-0.5
            )
            total[:, val_columns] += jnp.dot(
                probs.astype(jnp.bfloat16), grad, preferred_element_type=jnp.float32
            )
            pl.when((pair == HEADS // 4) & at_end)(lambda: result.add_y_of(nearest(depth - 1)))

        part[...] = total[...].astype(jnp.bfloat16)
        keyval_sum.start()
        cosine, sine = cosine_ref[...], -sine_ref[...]
        grad_query[...] = turned(turned_query[...], cosine, sine).astype(jnp.bfloat16)
        swaps[1].start()
        steps = range(depth - 1, -1, -1)
        for step in steps:
            keyval_sum.add_cores(step)
        result.send_y(nearest(0))
        pl.when(within)(lambda: result.add_y_of(nearest(depth - 1)))
        for k in range(depth - 2, 0, -1):
            result.add_y_of(nearest(k))
        for step in steps:
            keyval_sum.add_y(step)
        keyval_sum.last(own_keyval)
        keys = turned(own_keyval[:, : kv_columns // 2], cosine, sine)
        grad_keyval[...] = jnp.concatenate(
            [keys, own_keyval[:, kv_columns // 2 :]], axis=1
        ).astype(jnp.bfloat16)
        swaps[2].start()
        result.add_y_of(nearest(0))
        result.last(result_sum)
        output[...] = (middle_ref[...] + result_sum[...]).astype(jnp.bfloat16)
        keyval_sum.finish()
        result.finish(cores=False)
        for swap in swaps:
            swap.wait()

    def shape(like, kind=jnp.bfloat16):
        return jax.ShapeDtypeStruct(like, kind)

    rows, narrow = (tokens, features), (tokens, kv_columns)
    small_shape = (small.shape[0], features)
    out = [
        shape(rows), shape(rows, jnp.float32), shape(rows), shape(rows), shape(rows), shape(rows),
        shape(narrow), shape(narrow), shape(small_shape, jnp.float32),
    ] + [shape((tokens, features // 2))] * 4
    scratch = [
        pltpu.VMEM(small_shape, jnp.float32),
        pltpu.VMEM(rows, jnp.bfloat16),
        pltpu.VMEM(rows, jnp.float32),
        pltpu.VMEM(narrow, jnp.float32),
        pltpu.VMEM(rows, jnp.float32),
        pltpu.VMEM((HEADS * tokens, HEAD_DIM), jnp.bfloat16),
        pltpu.VMEM((HEADS * tokens, HEAD_DIM), jnp.bfloat16),
        pltpu.VMEM((length, 2 * tokens), jnp.float32),
        pltpu.VMEM((8, 2 * tokens), jnp.float32),
        pltpu.VMEM(keyval.shape, jnp.float32),
        pltpu.VMEM(keyval.shape, jnp.bfloat16),
        pltpu.SemaphoreType.DMA((2, 5)),
    ]
    wide = Scatter.scratch(depth, tokens, features)
    scratch += wide[1:4] + Scatter.sems(depth) * 2 + Scatter.scratch(depth, tokens, kv_columns, 2)
    return call(
        kernel, out, scratch, 4, "attend_back",
        returned, gates, small, small_there, middle, d_out, send, attn_own, attn_other, query,
        keyval, *angles, *docs, level, mixed, hidden, mixed_low, results,
        late=(19, 0, 4, 5, 6, 7, 8, 9, 10, 16),
    )


def gate_unit(first, second):
    root, cube = math.sqrt(2 / math.pi), 0.044715
    square = first * first
    bend = jnp.tanh(root * first * (1 + cube * square))
    lift = 0.5 * (1 + bend)
    slope = lift + 0.5 * first * (1 - bend * bend) * root * (1 + 3 * cube * square)
    gelu = first * lift
    return gelu * second, slope * second, gelu


def run_experts(send, d_out_all, in_own, out_own, experts):
    count, tokens = lax.axis_size("ctx"), send.shape[0]
    depth, chips, length = count // 4, count // 2, count * tokens
    wide, features = send.shape[1], d_out_all.shape[1]
    quarter = out_own.shape[0]
    width = 2 * quarter

    def kernel(
        send_ref, d_out_far, in_own_ref, out_own_ref,
        returned, results_far, grad_in_far, grad_in_other_far, grad_out_far, grad_out_other_far,
        hidden_all, grad_both, gated_hidden, other_part, other_result, result_from, result_sems,
        in_ref, out_ref, d_out_ref, x_sems, near_sem, results, grad_in, grad_in_other, grad_out,
        grad_out_other, far_sems, *scratch,
    ):
        gather = gather_parts(hidden_all, tokens, scratch[:6], 2)
        scatter = scatter_parts(other_part, scratch[6:], 2)
        chip_sums = scratch[7]
        z, y, c, _ = chip_place()
        expert = lax.axis_index("ctx") // 2
        lane = lax.broadcasted_iota(jnp.int32, (1, 128), 1)
        Gather(hidden_all, tokens, scratch[:3]).own()[...] = send_ref[...]
        partner = {"wa": 1 - lax.axis_index("wa")}
        stores = [
            pltpu.make_async_copy(source, target, far_sems.at[i])
            for i, (source, target) in enumerate(
                [(results, results_far), (grad_in, grad_in_far),
                 (grad_in_other, grad_in_other_far), (grad_out, grad_out_far),
                 (grad_out_other, grad_out_other_far)]
            )
        ]
        near = pltpu.make_async_copy(d_out_far, d_out_ref, near_sem.at[0])
        near.start()
        swaps = [
            remote(
                in_own_ref.at[pl.ds(part * quarter, quarter)],
                in_ref.at[pl.ds((2 * part + 1) * quarter, quarter)],
                x_sems,
                (part,),
                partner,
            )
            for part in range(2)
        ]
        swaps.append(
            remote(out_own_ref, out_ref.at[pl.ds(quarter, quarter)], x_sems, (2,), partner)
        )
        greet(across_x=True)
        gather.start()
        for swap in swaps:
            swap.start()
        out_ref[:quarter] = out_own_ref[...]
        in_ref[:quarter] = in_own_ref[:quarter]
        in_ref[width : width + quarter] = in_own_ref[quarter:]
        def chip_rows(chip):
            return pl.ds(pl.multiple_of(chip * 2 * tokens, 16), 2 * tokens)

        def parted(values):
            low, high = values[:tokens], values[tokens:]
            return jnp.where(c == 0, low, high), jnp.where(c == 0, high, low)

        def backward(chip):
            rows = chip_rows(chip)
            carried = hidden_all[rows, features:].astype(jnp.float32)
            mine = (lane == expert) | (lane == expert + experts)
            gate = jnp.sum(jnp.where(mine, carried, 0.0), axis=1, keepdims=True)
            both = rows_by_rows(hidden_all[rows, :features], in_ref[...])
            hidden, by_first, by_second = gate_unit(both[:, :width], both[:, width:])
            gated_hidden[rows, :] = (hidden * gate).astype(jnp.bfloat16)
            grad_hidden = rows_by_rows(d_out_ref[rows, :], out_ref[...])
            grad_gate = jnp.sum(grad_hidden * hidden, axis=1, keepdims=True)
            grad_hidden = grad_hidden * gate
            grad_both[rows, :width] = (grad_hidden * by_first).astype(jnp.bfloat16)
            grad_both[rows, width:] = (grad_hidden * by_second).astype(jnp.bfloat16)
            own, other = parted(
                jnp.dot(grad_both[rows, :], in_ref[...], preferred_element_type=jnp.float32)
            )
            chip_sums[chip, :, :features] = own.astype(jnp.bfloat16)
            other_part[chip, :, :features] = other.astype(jnp.bfloat16)
            own, other = parted(jnp.where(lane == expert, grad_gate, 0.0))
            chip_sums[chip, :, features:] = own.astype(jnp.bfloat16)
            other_part[chip, :, features:] = other.astype(jnp.bfloat16)
            scatter.send_core(chip)

        follow(gather)
        near.wait()
        for swap in swaps:
            swap.wait()
        backward(nearest(1) * 2 + 1 - y)
        backward(nearest(1) * 2 + y)
        scatter.add_chip(nearest(1), True)

        def next_chip(turn, of_z):
            backward(of_z * 2 + 1 - y)
            scatter.add_chip(nearest(jnp.where(turn == 0, 1, depth - turn)), False)
            backward(of_z * 2 + y)
            scatter.add_chip(of_z, True)

        @pl.loop(0, depth - 1)
        def _(turn):
            next_chip(turn, nearest(jnp.where(turn == depth - 2, 0, depth - 1 - turn)))

        scatter.add_chip(nearest(0), False)
        scatter.add_y_of(nearest(depth - 1))

        def result_copy(chip):
            target = {"ctx": ctx_of(z, y, 1 - c)}
            return remote(
                other_result.at[chip], result_from.at[chip], result_sems, (chip,), target
            )

        @pl.loop(0, chips)
        def _(chip):
            result = jnp.dot(
                gated_hidden[chip_rows(chip), :], out_ref[...], preferred_element_type=jnp.float32
            )
            own, other = parted(result)
            results[chip] = own.astype(jnp.bfloat16)
            other_result[chip] = other.astype(jnp.bfloat16)
            result_copy(chip).start()

        scatter.add_y_of(nearest(depth - 2))

        @pl.loop(0, features // 512)
        def _(turn):
            at = pl.ds(pl.multiple_of(turn * 512, 512), 512)
            grad = columns_by_columns(gated_hidden[...], d_out_ref[:, at])
            grad_out[:, at] = grad[:quarter]
            grad_out_other[:, at] = grad[quarter:].astype(jnp.bfloat16)

        stores[3].start()
        stores[4].start()
        for k in range(depth - 3, 0, -1):
            scatter.add_y_of(nearest(k))

        @pl.loop(0, features // 512)
        def _(turn):
            at = pl.ds(pl.multiple_of(turn * 512, 512), 512)
            grad = columns_by_columns(grad_both[...], hidden_all[:, at])
            for part in range(2):
                rows = slice(part * quarter, (part + 1) * quarter)
                first = part * width
                grad_in[rows, at] = grad[first : first + quarter]
                grad_in_other[rows, at] = grad[first + quarter : first + width].astype(jnp.bfloat16)

        stores[1].start()
        stores[2].start()

        @pl.loop(0, chips)
        def _(chip):
            result_copy(chip).wait_recv()
            add_into(results.at[chip], (results.at[chip], result_from.at[chip]), tokens)

        stores[0].start()
        scatter.add_y_of(nearest(0))
        scatter.last(returned)
        scatter.finish()
        for chip in range(chips):
            result_copy(chip).wait_send()
        for store in stores:
            store.wait()

    block = (chips, tokens, features)
    out = [
        jax.ShapeDtypeStruct((tokens, wide), jnp.float32),
        jax.ShapeDtypeStruct(block, jnp.bfloat16),
        jax.ShapeDtypeStruct(in_own.shape, jnp.float32),
        jax.ShapeDtypeStruct(in_own.shape, jnp.bfloat16),
        jax.ShapeDtypeStruct(out_own.shape, jnp.float32),
        jax.ShapeDtypeStruct(out_own.shape, jnp.bfloat16),
    ]
    scratch = [
        pltpu.VMEM((length, wide), jnp.bfloat16),
        pltpu.VMEM((length, 2 * width), jnp.bfloat16),
        pltpu.VMEM((length, width), jnp.bfloat16),
        pltpu.VMEM((chips, tokens, wide), jnp.bfloat16),
        pltpu.VMEM(block, jnp.bfloat16),
        pltpu.VMEM(block, jnp.bfloat16),
        pltpu.SemaphoreType.DMA((2, chips)),
        pltpu.VMEM((2 * width, features), jnp.bfloat16),
        pltpu.VMEM((width, features), jnp.bfloat16),
        pltpu.VMEM(d_out_all.shape, jnp.bfloat16),
        pltpu.SemaphoreType.DMA((2, 3)),
        pltpu.SemaphoreType.DMA((1,)),
    ]
    scratch += [pltpu.VMEM(one.shape, one.dtype) for one in out[1:]]
    scratch.append(pltpu.SemaphoreType.DMA((5,)))
    scratch += Gather.sems(depth) * 2 + Scatter.scratch(depth, tokens, wide, 2)
    return call(
        kernel, out, scratch, 3, "experts", send, d_out_all, in_own, out_own, outside=(1,),
        outside_out=range(1, 6),
    )


def finish(
    x, grad_middle, small, small_there, small_grads, matrices, hidden, mixed, middle, query, keyval,
    expert_in, expert_out,
):
    count, tokens, half = lax.axis_size("ctx"), x.shape[0], x.shape[1] // 2
    depth, rows = count // 4, half // count
    widths = (middle[0].shape[1], query[0].shape[1], keyval[0].shape[1])
    experts = small.shape[0] // 2

    def kernel(
        arrive, x_ref, grad_middle_ref, small_ref, small_there_ref, small_grads_ref,
        query_own, query_other, keyval_own, keyval_other,
        hidden_ref, hidden_there, mixed_ref, mixed_there, middle_ref, middle_there,
        query_ref, query_there, keyval_ref, keyval_there, in_ref, out_ref,
        attn_sum, query_sum, keyval_sum, small_sum, grad_input, in_there, out_there,
        attn_part, query_part, keyval_part, pair, full, grad_one, small_mine, small_came, small_all,
        x_sems, *scratch,
    ):
        scatters, gathers = [], []
        parts, sums = (attn_part, query_part, keyval_part), (attn_sum, query_sum, keyval_sum)
        for part, total in zip(parts, sums):
            scatters.append(Scatter(part, scratch[:7]))
            gathers.append(Gather(total, rows, scratch[7:10]))
            scratch = scratch[10:]
        small_out = Gather(small_all, small_came.shape[0], scratch)
        (attn, query_, keyval_), (attn_out, query_out, keyval_out) = scatters, gathers
        partner = {"wa": 1 - lax.axis_index("wa")}
        swaps = [
            remote(source, target, x_sems, (i,), partner)
            for i, (source, target) in enumerate(
                [(small_mine.at[:, side_columns(False)], small_came), (in_ref, in_there),
                 (out_ref, out_there)]
            )
        ]
        steps = range(depth - 1, -1, -1)

        def products(left, left_there, right, right_there, part):
            pair[:tokens] = left[...]
            pair[tokens:] = left_there[...]

            @pl.loop(0, part.shape[1] // 512)
            def _(turn):
                at = pl.ds(pl.multiple_of(turn * 512, 512), 512)
                both = jnp.concatenate([right[:, at], right_there[:, at]], axis=0)
                part[:, at] = columns_by_columns(pair[...], both).astype(jnp.bfloat16)

        products(mixed_ref, mixed_there, middle_ref, middle_there, attn_part)
        greet(across_x=True)
        attn.start()
        products(hidden_ref, hidden_there, query_ref, query_there, query_part)
        for step in steps:
            attn.add_cores(step)
        query_.start()
        products(hidden_ref, hidden_there, keyval_ref, keyval_there, keyval_part)
        keyval_.start()
        for step in steps:
            query_.add_cores(step)
        attn.add_y(depth - 1)
        fill_small(full, small_ref, small_there_ref)
        arrive(0, 1, 5, 6, 7, 8)
        grad_one[:, side_columns(True)] = rows_by_rows(
            query_ref[...], query_own[...]
        ) + rows_by_rows(keyval_ref[...], keyval_own[...])
        attn.add_y(depth - 2)
        grad_one[:, side_columns(False)] = rows_by_rows(
            query_ref[...], query_other[...]
        ) + rows_by_rows(keyval_ref[...], keyval_other[...])
        back, grad_gain = norm_back(
            x_ref[...].astype(jnp.float32), full[experts : experts + 1], grad_one[...]
        )
        grad_input[...] = (grad_middle_ref[...] + back).astype(jnp.bfloat16)
        row = lax.broadcasted_iota(jnp.int32, (small_mine.shape[0], 1), 0)
        small_mine[...] = jnp.where(row == experts, grad_gain, small_grads_ref[...])
        swaps[0].start()
        for step in range(depth - 3, -1, -1):
            attn.add_y(step)
        for step in steps:
            keyval_.add_cores(step)
        attn.last(attn_out.own())
        attn_out.start()
        swaps[1].start()
        swaps[2].start()
        swaps[0].wait()
        small_out.own()[...] = (small_mine[:, side_columns(True)] + small_came[...]).astype(
            jnp.bfloat16
        )
        small_out.start()
        for step in steps:
            query_.add_y(step)
        attn_out.along_z(1)
        query_.last(query_out.own())
        query_out.start()
        attn_out.along_z(2)
        attn_out.along_y(0)
        small_out.along_z(1)
        for step in steps:
            keyval_.add_y(step)
        attn_out.along_z(3)
        attn_out.along_y(1)
        keyval_.last(keyval_out.own())
        keyval_out.start()
        query_out.along_z(1)
        small_out.along_z(2)
        attn_out.along_y(2)
        query_out.along_z(2)
        small_out.along_z(3)
        query_out.along_y(0)
        keyval_out.along_z(1)
        query_out.along_z(3)
        attn_out.along_y(3)
        keyval_out.along_z(2)
        query_out.along_y(1)
        keyval_out.along_z(3)
        query_out.along_y(2)
        small_out.along_y(0)
        keyval_out.along_y(0)
        small_out.along_y(1)
        query_out.along_y(3)
        keyval_out.along_y(1)
        small_out.along_y(2)
        keyval_out.along_y(2)
        small_out.along_y(3)
        keyval_out.along_y(3)
        for one in [small_out] + gathers + scatters:
            one.finish()
        small_rows = small_came.shape[0]
        total = small_all[:small_rows].astype(jnp.float32)
        for device in range(1, count):
            rows_of = slice(device * small_rows, (device + 1) * small_rows)
            total = total + small_all[rows_of].astype(jnp.float32)
        small_sum[...] = total
        swaps[1].wait()
        swaps[2].wait()

    small_shape = (small.shape[0], half)
    out = [jax.ShapeDtypeStruct((half, width), jnp.bfloat16) for width in widths]
    out += [
        jax.ShapeDtypeStruct(small_shape, jnp.float32),
        jax.ShapeDtypeStruct(x.shape, jnp.bfloat16),
        jax.ShapeDtypeStruct(expert_in.shape, expert_in.dtype),
        jax.ShapeDtypeStruct(expert_out.shape, expert_out.dtype),
    ]
    scratch = [pltpu.VMEM((half, width), jnp.bfloat16) for width in widths]
    scratch += [
        pltpu.VMEM((2 * tokens, half), jnp.bfloat16),
        pltpu.VMEM(small_grads.shape, jnp.float32),
        pltpu.VMEM(x.shape, jnp.float32),
        pltpu.VMEM(small_grads.shape, jnp.float32),
        pltpu.VMEM(small_shape, jnp.float32),
        pltpu.VMEM((count * small.shape[0], half), jnp.bfloat16),
        pltpu.SemaphoreType.DMA((2, 3)),
    ]
    for width in widths:
        scratch += Scatter.scratch(depth, rows, width) + Gather.sems(depth)
    scratch += Gather.sems(depth)
    return call(
        kernel, out, scratch, 1, "finish",
        x, grad_middle, small, small_there, small_grads, *matrices, *hidden, *mixed, *middle,
        *query, *keyval, expert_in, expert_out, outside=(19, 20), outside_out=(5, 6),
        late=(0, 1, 5, 6, 7, 8),
    )


def widen(query, keyval, attn, grad_in, in_there, grad_out, out_there):
    quarter, features = grad_out.shape
    steps = 4

    def kernel(*refs):
        query_ref, keyval_ref, attn_ref, in_ref, in_there_ref, out_ref, out_there_ref = refs[:7]
        query_out, keyval_out, attn_out, in_out, out_out = refs[7:]
        query_out[...] = query_ref[...].astype(jnp.float32)
        keyval_out[...] = keyval_ref[...].astype(jnp.float32)
        attn_out[...] = attn_ref[...].astype(jnp.float32)
        both = in_ref[...] + in_there_ref[...].astype(jnp.float32)
        in_out[...] = both
        out_out[0] = out_ref[...] + out_there_ref[...].astype(jnp.float32)

    def rows(values):
        return pl.BlockSpec((values.shape[0] // steps, values.shape[1]), lambda i: (i, 0))

    operands = (query, keyval, attn, grad_in, in_there, grad_out, out_there)
    return pl.pallas_call(
        kernel,
        grid=(steps,),
        out_shape=[
            jax.ShapeDtypeStruct(query.shape, jnp.float32),
            jax.ShapeDtypeStruct(keyval.shape, jnp.float32),
            jax.ShapeDtypeStruct(attn.shape, jnp.float32),
            jax.ShapeDtypeStruct(grad_in.shape, jnp.float32),
            jax.ShapeDtypeStruct((1, quarter, features), jnp.float32),
        ],
        in_specs=[rows(values) for values in operands],
        out_specs=[
            rows(query), rows(keyval), rows(attn),
            rows(grad_in),
            pl.BlockSpec((1, quarter // steps, features), lambda i: (0, i, 0)),
        ],
        compiler_params=pltpu.CompilerParams(vmem_limit_bytes=VMEM_LIMIT),
        name="widen",
    )(*operands)


def gathered_body(
    layer_input, seq_ids, routes, gain_attn, w_query, w_keyval, w_out_attn, gain_ffn, router,
    w_in, w_out, d_out,
):
    me = lax.axis_index("ctx")
    tokens, experts = layer_input.shape[1], router.shape[1]
    x, grad_out = layer_input[0], d_out[0]
    small = jnp.concatenate(
        [router.T, gain_attn[None], gain_ffn[None], jnp.zeros((experts - 2, D // 2), jnp.bfloat16)]
    )
    turns = angle_table(me * tokens + jnp.arange(tokens, dtype=jnp.int32))[:, 0]
    cosine, sine = jnp.cos(turns), jnp.sin(turns)
    angles = (
        jnp.concatenate([cosine, cosine], axis=1), jnp.concatenate([-sine, sine], axis=1)
    )
    docs = (seq_ids, lax.dynamic_slice_in_dim(seq_ids[0], me * tokens, tokens, 0)[:, None])
    numbers = jnp.arange(128, dtype=jnp.int32)
    named = jnp.any(routes[0][:, :, None] == (numbers % experts)[None, None, :], axis=1)
    chosen = (named & (numbers < 2 * experts)[None, :]).astype(jnp.float32)
    in_own = jnp.swapaxes(w_in[0], 1, 2).reshape(-1, D)

    d_out_all, w_query_there, w_keyval_there, small_there = front(
        grad_out, w_query, w_keyval, small
    )
    projections = (w_query, w_query_there, w_keyval, w_keyval_there)
    (
        query, keyval, level, mixed, hidden, mixed_low, middle, send, gates, w_out_attn_there,
    ) = attend(x, small, small_there, projections, w_out_attn, angles, docs, chosen, experts)
    returned, results, grad_in, grad_in_other, grad_out_matrix, grad_out_other = run_experts(
        send, d_out_all, in_own, w_out[0], experts
    )
    (
        output, grad_middle, middle_low, middle_there, grad_query, query_there, grad_keyval,
        keyval_there, small_grads, *halves,
    ) = attend_back(
        returned, gates, small, small_there, middle, grad_out, send, w_out_attn, w_out_attn_there,
        query, keyval, angles, docs, level, mixed, hidden, mixed_low, results, experts,
    )
    attn_sum, query_sum, keyval_sum, small_sum, grad_input, in_there, out_there = finish(
        x, grad_middle, small, small_there, small_grads, projections, halves[:2], halves[2:],
        (middle_low, middle_there), (grad_query, query_there),
        (grad_keyval, keyval_there), grad_in_other, grad_out_other,
    )
    query_sum, keyval_sum, attn_sum, grad_w_in, grad_w_out = widen(
        query_sum, keyval_sum, attn_sum, grad_in, in_there, grad_out_matrix, out_there
    )
    return (
        output[None],
        grad_input[None],
        small_sum[experts],
        query_sum,
        keyval_sum,
        attn_sum,
        small_sum[experts + 1],
        small_sum[:experts].T,
        jnp.swapaxes(grad_w_in.reshape(2, -1, D), 1, 2)[None],
        grad_w_out,
    )


def solution(mesh):
    in_specs = (
        P("wa", "ctx", None),
        P("wa", None),
        P("wa", "ctx", None),
        P("wa"),
        P("wa", None),
        P("wa", None),
        P("wa", None),
        P("wa"),
        P("wa", None),
        P("ctx", None, None, "wa"),
        P("ctx", "wa", None),
        P("wa", "ctx", None),
    )
    out_specs = (
        P("wa", "ctx", None),
        P("wa", "ctx", None),
        P("wa"),
        P("wa", None),
        P("wa", None),
        P("wa", None),
        P("wa"),
        P("wa", None),
        P("ctx", None, None, "wa"),
        P("ctx", "wa", None),
    )
    depth = mesh.shape["ctx"]
    body = gathered_body if depth == 16 else routed_body
    return jax.shard_map(body, mesh=mesh, in_specs=in_specs, out_specs=out_specs, check_vma=False)
```

```python
import functools
import math

import jax
import jax.numpy as jnp
from jax import lax
from jax.experimental import pallas as pl
from jax.experimental.pallas import tpu as pltpu
from jax.sharding import PartitionSpec as P

D = 1536
HEADS = 12
KV_HEADS = 2
HEAD_DIM = 128
TOP = 4
BLOCK = 256


EPSILON = 1e-06
THETA = 1000000.0
NEGATIVE = -1e30


def rms_scale(values, gain_vec):
    return (
        values * lax.rsqrt(jnp.mean(values * values, axis=-1, keepdims=True) + EPSILON) * gain_vec
    )


def rotate(values, angles):
    half_dim = values.shape[-1] // 2
    cosine = jnp.cos(angles)
    sine_part = jnp.sin(angles)
    first_half = values[..., :half_dim]
    second = values[..., half_dim:]
    return jnp.concatenate(
        [first_half * cosine - second * sine_part, second * cosine + first_half * sine_part],
        axis=-1,
    )


def angle_table(positions):
    half_dim = HEAD_DIM // 2
    frequency = THETA ** (-2.0 * jnp.arange(half_dim, dtype=jnp.float32) / HEAD_DIM)
    return (positions.astype(jnp.float32)[:, None] * frequency[None, :])[:, None, :]


def gated(stacked):
    return jax.nn.gelu(stacked[..., 0, :], approximate=True) * stacked[..., 1, :]


def over_keys(key_rows, running, advance):
    key_count = key_rows.shape[0]
    key_width = math.gcd(key_count, 512)

    def one_turn(state_now, block_index):
        key_offset = block_index * key_width
        key_part = lax.dynamic_slice_in_dim(key_rows, key_offset, key_width, 0)
        return (advance(state_now, key_part, key_offset), None)

    running, unused = lax.scan(
        one_turn, running, jnp.arange(key_count // key_width, dtype=jnp.int32)
    )
    return running


def routed_body(
    layer_input,
    seq_ids,
    routes,
    gain_attn,
    w_query,
    w_keyval,
    w_out_attn,
    gain_ffn,
    router,
    w_in,
    w_out,
    d_out,
):
    ctx_count = lax.axis_size("ctx")
    ctx_index = lax.axis_index("ctx")
    tokens = layer_input.shape[1]
    length = tokens * ctx_count
    experts_all = ctx_count // 2
    capacity = 2 * tokens * TOP // experts_all
    group = HEADS // KV_HEADS
    kv_width = KV_HEADS * HEAD_DIM
    row_count = group * tokens
    scale = HEAD_DIM ** (-0.5)
    gain_one, query_matrix, keyvalue_matrix, attention_matrix = (
        lax.all_gather(gain_attn, "wa", axis=0, tiled=True),
        lax.all_gather(w_query, "wa", axis=0, tiled=True),
        lax.all_gather(w_keyval, "wa", axis=0, tiled=True),
        lax.all_gather(w_out_attn, "wa", axis=0, tiled=True),
    )
    residual = layer_input[0].astype(jnp.float32)
    normed_one, norm_one_back = jax.vjp(rms_scale, residual, gain_one.astype(jnp.float32))
    hidden_first_norm = normed_one.astype(jnp.bfloat16)
    positions = ctx_index * tokens + jnp.arange(tokens, dtype=jnp.int32)
    angles = angle_table(positions)
    query_projected = jnp.dot(
        hidden_first_norm, query_matrix, preferred_element_type=jnp.float32
    ).reshape(tokens, HEADS, HEAD_DIM)
    keyvalue_projected = jnp.dot(
        hidden_first_norm, keyvalue_matrix, preferred_element_type=jnp.float32
    )
    key_pre = keyvalue_projected[:, :kv_width].reshape(tokens, KV_HEADS, HEAD_DIM)
    query_low = rotate(query_projected, angles).astype(jnp.bfloat16)
    key_low = rotate(key_pre, angles).astype(jnp.bfloat16)
    value_low = keyvalue_projected[:, kv_width:].astype(jnp.bfloat16)
    keyval_send = jnp.concatenate([key_low.reshape(tokens, kv_width), value_low], axis=1)
    query_rows = (
        query_low.reshape(tokens, KV_HEADS, group, HEAD_DIM)
        .transpose(1, 2, 0, 3)
        .reshape(KV_HEADS, row_count, HEAD_DIM)
    )
    doc_row = seq_ids[0]
    query_docs = lax.dynamic_slice_in_dim(doc_row, ctx_index * tokens, tokens, 0)
    query_blocks = positions // BLOCK

    def block_scores(key_part, first_key):
        key_count = key_part.shape[0]
        split_part = key_part.reshape(key_count, 2, KV_HEADS, HEAD_DIM)
        keys_here = split_part[:, 0]
        values_here = split_part[:, 1]
        scores = (
            jnp.einsum("hrd,nhd->hrn", query_rows, keys_here, preferred_element_type=jnp.float32)
            * scale
        )
        key_docs = lax.dynamic_slice_in_dim(doc_row, first_key, key_count, 0)
        key_blocks = (first_key + jnp.arange(key_count, dtype=jnp.int32)) // BLOCK
        allowed = (query_docs[:, None] == key_docs[None, :]) & (
            key_blocks[None, :] <= query_blocks[:, None]
        )
        allowed = jnp.broadcast_to(allowed[None], (group, tokens, key_count)).reshape(
            1, row_count, key_count
        )
        return (jnp.where(allowed, scores, NEGATIVE), allowed, keys_here, values_here)

    def probs_of(masked, allowed, largest, totals):
        return jnp.where(allowed, jnp.exp(masked - largest[..., None]) / totals[..., None], 0.0)

    def stats_step(running, key_part, first_key):
        largest, totals = running
        masked, allowed, keys_here, values_here = block_scores(key_part, first_key)
        new_largest = jnp.maximum(largest, jnp.max(masked, axis=-1))
        weights = jnp.where(allowed, jnp.exp(masked - new_largest[..., None]), 0.0)
        return (new_largest, totals * jnp.exp(largest - new_largest) + jnp.sum(weights, axis=-1))

    start_stats = (
        jnp.full((KV_HEADS, row_count), NEGATIVE, jnp.float32),
        jnp.zeros((KV_HEADS, row_count), jnp.float32),
    )
    largest, totals = over_keys(
        lax.all_gather(keyval_send, "ctx", axis=0, tiled=True), start_stats, stats_step
    )

    def values_step(running, key_part, first_key):
        masked, allowed, keys_here, values_here = block_scores(key_part, first_key)
        probs_low = probs_of(masked, allowed, largest, totals).astype(jnp.bfloat16)
        return running + jnp.einsum(
            "hrn,nhd->hrd", probs_low, values_here, preferred_element_type=jnp.float32
        )

    start_values = jnp.zeros((KV_HEADS, row_count, HEAD_DIM), jnp.float32)
    mixed_rows = over_keys(
        lax.all_gather(keyval_send, "ctx", axis=0, tiled=True), start_values, values_step
    )
    mixed_low = (
        mixed_rows.reshape(KV_HEADS, group, tokens, HEAD_DIM)
        .transpose(2, 0, 1, 3)
        .reshape(tokens, HEADS * HEAD_DIM)
        .astype(jnp.bfloat16)
    )
    middle_activation = residual + jnp.dot(
        mixed_low, attention_matrix, preferred_element_type=jnp.float32
    )
    gain_two, router_full, w_in_full, w_out_full = (
        lax.all_gather(gain_ffn, "wa", axis=0, tiled=True),
        lax.all_gather(router, "wa", axis=0, tiled=True),
        lax.all_gather(w_in, "wa", axis=3, tiled=True),
        lax.all_gather(w_out, "wa", axis=1, tiled=True),
    )
    in_half = w_in_full[0]
    out_half = w_out_full[0]
    normed_two, norm_two_back = jax.vjp(rms_scale, middle_activation, gain_two.astype(jnp.float32))
    hidden_second_norm = normed_two.astype(jnp.bfloat16)
    router_logits = jnp.dot(hidden_second_norm, router_full, preferred_element_type=jnp.float32)
    route_ids = routes[0]

    def gate_values(logit_rows):
        return jax.nn.softmax(jnp.take_along_axis(logit_rows, route_ids, axis=-1), axis=-1)

    gates, gate_back = jax.vjp(gate_values, router_logits)
    flat_ids = route_ids.reshape(tokens * TOP)
    expert_hits = (flat_ids[:, None] == jnp.arange(experts_all, dtype=jnp.int32)[None, :]).astype(
        jnp.int32
    )
    ranks = jnp.sum(expert_hits * (jnp.cumsum(expert_hits, axis=0) - expert_hits), axis=1)
    slot_first = 2 * flat_ids * capacity + ranks
    slot_second = slot_first + capacity
    slot_total = ctx_count * capacity
    slot_numbers = jnp.arange(slot_total, dtype=jnp.int32)[:, None]
    placed = (
        (slot_first[None, :] == slot_numbers) | (slot_second[None, :] == slot_numbers)
    ).astype(jnp.bfloat16)
    dispatch = jnp.sum(placed.reshape(slot_total, tokens, TOP), axis=2)
    send_rows = (
        jnp.dot(dispatch, hidden_second_norm, preferred_element_type=jnp.float32)
        .astype(jnp.bfloat16)
        .reshape(ctx_count, capacity, D)
    )
    arrived = lax.all_to_all(send_rows, "ctx", split_axis=0, concat_axis=0, tiled=True)
    stacked = jnp.einsum("ncd,gdf->ncgf", arrived, in_half, preferred_element_type=jnp.float32)
    hidden_low = gated(stacked).astype(jnp.bfloat16)
    result = jnp.einsum(
        "ncf,fd->ncd", hidden_low, out_half, preferred_element_type=jnp.float32
    ).astype(jnp.bfloat16)
    returned_rows = lax.all_to_all(result, "ctx", split_axis=0, concat_axis=0, tiled=True)
    returned_flat = returned_rows.reshape(slot_total, D)
    pair_rows = (
        returned_flat[slot_first].astype(jnp.float32)
        + returned_flat[slot_second].astype(jnp.float32)
    ).reshape(tokens, TOP, D)
    output = (middle_activation + jnp.sum(gates[:, :, None] * pair_rows, axis=1)).astype(
        jnp.bfloat16
    )
    grad_out = d_out[0].astype(jnp.float32)
    grad_gates = jnp.sum(pair_rows * grad_out[:, None, :], axis=-1)
    (grad_logits,) = gate_back(grad_gates)
    grad_logits_low = grad_logits.astype(jnp.bfloat16)
    gate_slots = jnp.dot(
        placed.astype(jnp.float32), gates.reshape(tokens * TOP), precision=lax.Precision.HIGHEST
    )
    routed_grad = jnp.dot(dispatch, d_out[0], preferred_element_type=jnp.float32)
    grad_send_rows = (
        (gate_slots[:, None] * routed_grad).astype(jnp.bfloat16).reshape(ctx_count, capacity, D)
    )
    grad_arrived = lax.all_to_all(grad_send_rows, "ctx", split_axis=0, concat_axis=0, tiled=True)
    grad_hidden = jnp.einsum(
        "ncd,fd->ncf", grad_arrived, out_half, preferred_element_type=jnp.float32
    )
    hidden_again, gated_back = jax.vjp(gated, stacked)
    (grad_stacked,) = gated_back(grad_hidden)
    grad_stacked_low = grad_stacked.astype(jnp.bfloat16)
    grad_rows = jnp.einsum(
        "ncgf,gdf->ncd", grad_stacked_low, in_half, preferred_element_type=jnp.float32
    ).astype(jnp.bfloat16)
    grad_returned = lax.all_to_all(grad_rows, "ctx", split_axis=0, concat_axis=0, tiled=True)
    grad_w_in = jnp.einsum(
        "ncd,ncgf->gdf", arrived, grad_stacked_low, preferred_element_type=jnp.float32
    )[None]
    grad_w_out = jnp.einsum(
        "ncf,ncd->fd",
        hidden_again.astype(jnp.bfloat16),
        grad_arrived,
        preferred_element_type=jnp.float32,
    )[None]
    grad_hidden_two = jnp.einsum(
        "st,sd->td",
        dispatch,
        grad_returned.reshape(slot_total, D),
        preferred_element_type=jnp.float32,
    )
    grad_hidden_two = grad_hidden_two + jnp.dot(
        grad_logits_low, router_full.T, preferred_element_type=jnp.float32
    )
    grad_router = jnp.dot(hidden_second_norm.T, grad_logits_low, preferred_element_type=jnp.float32)
    grad_middle_norm, grad_gain_two = norm_two_back(grad_hidden_two)
    grad_middle = grad_out + grad_middle_norm
    grad_middle_low = grad_middle.astype(jnp.bfloat16)
    grad_attn_weight = jnp.dot(mixed_low.T, grad_middle_low, preferred_element_type=jnp.float32)
    grad_mixed = jnp.dot(
        grad_middle_low, attention_matrix.T, preferred_element_type=jnp.float32
    ).astype(jnp.bfloat16)
    grad_rows_out = (
        grad_mixed.reshape(tokens, KV_HEADS, group, HEAD_DIM)
        .transpose(1, 2, 0, 3)
        .reshape(KV_HEADS, row_count, HEAD_DIM)
    )
    delta = jnp.sum(grad_rows_out.astype(jnp.float32) * mixed_rows, axis=-1)

    def score_grads(key_part, first_key):
        masked, allowed, keys_here, values_here = block_scores(key_part, first_key)
        probs = probs_of(masked, allowed, largest, totals)
        grad_probs = jnp.einsum(
            "hrd,nhd->hrn", grad_rows_out, values_here, preferred_element_type=jnp.float32
        )
        grad_scores = (probs * (grad_probs - delta[..., None])).astype(jnp.bfloat16)
        return (grad_scores, probs.astype(jnp.bfloat16), keys_here)

    def key_terms(grad_scores, probs_low, key_count):
        grad_keys = (
            jnp.einsum("hrn,hrd->nhd", grad_scores, query_rows, preferred_element_type=jnp.float32)
            * scale
        )
        grad_values = jnp.einsum(
            "hrn,hrd->nhd", probs_low, grad_rows_out, preferred_element_type=jnp.float32
        )
        return jnp.concatenate(
            [grad_keys.reshape(key_count, kv_width), grad_values.reshape(key_count, kv_width)],
            axis=1,
        )

    start_query = jnp.zeros((KV_HEADS, row_count, HEAD_DIM), jnp.float32)

    def back_step(running, key_part, first_key):
        grad_query_rows, grad_keyvals = running
        grad_scores, probs_low, keys_here = score_grads(key_part, first_key)
        grad_query_rows = (
            grad_query_rows
            + jnp.einsum("hrn,nhd->hrd", grad_scores, keys_here, preferred_element_type=jnp.float32)
            * scale
        )
        fresh = key_terms(grad_scores, probs_low, key_part.shape[0])
        return (grad_query_rows, lax.dynamic_update_slice_in_dim(grad_keyvals, fresh, first_key, 0))

    start_back = (start_query, jnp.zeros((length, 2 * kv_width), jnp.float32))
    grad_query_rows, grad_keyvals = over_keys(
        lax.all_gather(keyval_send, "ctx", axis=0, tiled=True), start_back, back_step
    )
    grad_keyval_mine = lax.psum_scatter(grad_keyvals, "ctx", scatter_dimension=0, tiled=True)
    grad_query = grad_query_rows.reshape(KV_HEADS, group, tokens, HEAD_DIM).transpose(2, 0, 1, 3)
    grad_query_pre = (
        rotate(grad_query.reshape(tokens, HEADS, HEAD_DIM), -angles)
        .reshape(tokens, HEADS * HEAD_DIM)
        .astype(jnp.bfloat16)
    )
    grad_key_pre = rotate(
        grad_keyval_mine[:, :kv_width].reshape(tokens, KV_HEADS, HEAD_DIM), -angles
    ).reshape(tokens, kv_width)
    grad_keyval_pre = jnp.concatenate(
        [grad_key_pre, grad_keyval_mine[:, kv_width:]], axis=1
    ).astype(jnp.bfloat16)
    grad_hidden_one = jnp.dot(
        grad_query_pre, query_matrix.T, preferred_element_type=jnp.float32
    ) + jnp.dot(grad_keyval_pre, keyvalue_matrix.T, preferred_element_type=jnp.float32)
    grad_query_weight = jnp.dot(
        hidden_first_norm.T, grad_query_pre, preferred_element_type=jnp.float32
    )
    grad_keyval_weight = jnp.dot(
        hidden_first_norm.T, grad_keyval_pre, preferred_element_type=jnp.float32
    )
    grad_residual_norm, grad_gain_one = norm_one_back(grad_hidden_one)
    grad_input = (grad_middle + grad_residual_norm).astype(jnp.bfloat16)
    shares = (
        lax.psum_scatter(
            grad_gain_one.astype(jnp.bfloat16), "wa", scatter_dimension=0, tiled=True
        ).astype(jnp.float32),
        lax.psum_scatter(
            grad_query_weight.astype(jnp.bfloat16), "wa", scatter_dimension=0, tiled=True
        ).astype(jnp.float32),
        lax.psum_scatter(
            grad_keyval_weight.astype(jnp.bfloat16), "wa", scatter_dimension=0, tiled=True
        ).astype(jnp.float32),
        lax.psum_scatter(
            grad_attn_weight.astype(jnp.bfloat16), "wa", scatter_dimension=0, tiled=True
        ).astype(jnp.float32),
        lax.psum_scatter(
            grad_gain_two.astype(jnp.bfloat16), "wa", scatter_dimension=0, tiled=True
        ).astype(jnp.float32),
        lax.psum_scatter(
            grad_router.astype(jnp.bfloat16), "wa", scatter_dimension=0, tiled=True
        ).astype(jnp.float32),
        lax.psum_scatter(
            grad_w_in.astype(jnp.bfloat16), "wa", scatter_dimension=3, tiled=True
        ).astype(jnp.float32),
        lax.psum_scatter(
            grad_w_out.astype(jnp.bfloat16), "wa", scatter_dimension=1, tiled=True
        ).astype(jnp.float32),
    )
    summed = lax.psum((shares[0], shares[1], shares[2], shares[3], shares[4], shares[5]), "ctx")
    return (
        output[None],
        grad_input[None],
        summed[0],
        summed[1],
        summed[2],
        summed[3],
        summed[4],
        summed[5],
        shares[6],
        shares[7],
    )

MESH = pl.DeviceIdType.MESH
VMEM_LIMIT = 60 * 1024 * 1024


def chip_place():
    count = lax.axis_size("ctx")
    me = lax.axis_index("ctx")
    return me // 4, lax.rem(me // 2, 2), lax.rem(me, 2), count // 4


def ctx_of(z, y, c):
    return (z * 2 + y) * 2 + c


def greet(across_x=False):
    z, y, c, depth = chip_place()
    barrier = pltpu.get_barrier_semaphore()

    def signal(device):
        pl.semaphore_signal(barrier, 1, device_id=device, device_id_type=MESH)

    signal({"ctx": ctx_of(z, y, 1 - c)})
    signal({"ctx": ctx_of(z, 1 - y, c)})
    if across_x:
        signal({"wa": 1 - lax.axis_index("wa")})
    pl.when(z > 0)(lambda: signal({"ctx": ctx_of(z - 1, y, c)}))
    pl.when(z < depth - 1)(lambda: signal({"ctx": ctx_of(z + 1, y, c)}))
    ends = (z > 0).astype(jnp.int32) + (z < depth - 1).astype(jnp.int32)
    pl.semaphore_wait(barrier, (3 if across_x else 2) + ends)


def remote(source, target_ref, sems, at, device):
    return pltpu.make_async_remote_copy(
        src_ref=source,
        dst_ref=target_ref,
        send_sem=sems.at[(0,) + at],
        recv_sem=sems.at[(1,) + at],
        device_id=device,
        device_id_type=MESH,
    )


def each(step, act):
    z, _, _, depth = chip_place()
    if step == 0:
        act(z)
    else:
        pl.when(z + step < depth)(lambda: act(z + step))
        pl.when(z - step >= 0)(lambda: act(z - step))


def nearest(k):
    z, _, _, depth = chip_place()
    low = jnp.minimum(z, depth - 1 - z)
    step = (k + 1) // 2
    place = jnp.where(k > 2 * low, k, jnp.where(lax.rem(k, 2) == 1, low - step, low + step))
    return jnp.where(z == low, place, depth - 1 - place)


class Gather:
    def __init__(self, out, rows, sems, part=0, parts=1):
        self.out, self.block, self.rows = out, rows, rows // parts
        self.first = part * self.rows
        self.z_sems, self.y_sems, self.c_sems = sems
        self.z, self.y, self.c, self.depth = chip_place()

    @staticmethod
    def sems(depth):
        return [
            pltpu.SemaphoreType.DMA((2, 2, depth)),
            pltpu.SemaphoreType.DMA((2, depth)),
            pltpu.SemaphoreType.DMA((2, 2 * depth)),
        ]

    def slot(self, z, y, c):
        start = ctx_of(z, y, c) * self.block + self.first
        return self.out.at[pl.ds(pl.multiple_of(start, 16), self.rows)]

    def own(self):
        return self.slot(self.z, self.y, self.c)

    def on_z(self, way, of_z, source=None):
        goal = jnp.minimum(self.z + 1, self.depth - 1) if way == 0 else jnp.maximum(self.z - 1, 0)
        block = self.slot(of_z, self.y, self.c)
        target = {"ctx": ctx_of(goal, self.y, self.c)}
        return remote(block if source is None else source, block, self.z_sems, (way, of_z), target)

    def on_y(self, of_z, mine=True, source=None):
        block = self.slot(of_z, self.y if mine else 1 - self.y, self.c)
        target = {"ctx": ctx_of(self.z, 1 - self.y, self.c)}
        return remote(block if source is None else source, block, self.y_sems, (of_z,), target)

    def on_core(self, of_z, of_y, mine=True, source=None):
        block = self.slot(of_z, of_y, self.c if mine else 1 - self.c)
        target = {"ctx": ctx_of(self.z, self.y, 1 - self.c)}
        at = (of_z * 2 + of_y,)
        return remote(block if source is None else source, block, self.c_sems, at, target)

    def start(self, source=None):
        z, depth = self.z, self.depth
        if source is not None:
            source = source.at[pl.ds(self.first, self.rows)]
        pl.when(z < depth - 1)(lambda: self.on_z(0, z, source).start())
        pl.when(z > 0)(lambda: self.on_z(1, z, source).start())
        self.on_y(z, source=source).start()
        self.on_core(z, self.y, source=source).start()

    def along_z(self, step):
        z, depth = self.z, self.depth

        def from_side(way, of_z, more):
            self.on_z(way, of_z).wait_recv()
            pl.when(more)(lambda: self.on_z(way, of_z).start())
            self.on_y(of_z).start()
            self.on_core(of_z, self.y).start()

        pl.when(z - step >= 0)(lambda: from_side(0, z - step, z < depth - 1))
        pl.when(z + step < depth)(lambda: from_side(1, z + step, z > 0))

    def along_y(self, step):
        def across(of_z):
            self.on_y(of_z, mine=False).wait_recv()
            self.on_core(of_z, 1 - self.y).start()

        each(step, across)

    def take_core(self, of_z):
        for of_y in range(2):
            self.on_core(of_z, of_y, mine=False).wait_recv()

    def finish(self, *taken):
        z, depth = self.z, self.depth
        for of_z in range(depth):
            pl.when((z < depth - 1) & (of_z <= z))(lambda: self.on_z(0, of_z).wait_send())
            pl.when((z > 0) & (of_z >= z))(lambda: self.on_z(1, of_z).wait_send())
            self.on_y(of_z).wait_send()
            for of_y in range(2):
                self.on_core(of_z, of_y).wait_send()
            open_still = of_z >= 0
            for one in taken:
                open_still = (of_z != one) & open_still
            pl.when(open_still)(lambda: self.take_core(of_z))


class Several:
    def __init__(self, members):
        self.members = members

    def __getattr__(self, name):
        def every(*given, **named):
            for member in self.members:
                getattr(member, name)(*given, **named)

        return every


def gather_parts(out, rows, sems, parts):
    return Several(
        [Gather(out, rows, sems[3 * i : 3 * i + 3], i, parts) for i in range(parts)]
    )


def follow(gather):
    depth = chip_place()[3]
    gather.along_z(1)
    for step in range(depth):
        if step >= 1 and step + 1 < depth:
            gather.along_z(step + 1)
        gather.along_y(step)
    gather.finish()


def add_into(target, terms, rows):
    some = 32 if rows % 32 == 0 else 48 if rows % 48 == 0 else 16

    @pl.loop(0, rows // some)
    def _(turn):
        at = pl.ds(pl.multiple_of(turn * some, 16), some)
        total = terms[0][at, :].astype(jnp.float32)
        for term in terms[1:]:
            total = total + term[at, :].astype(jnp.float32)
        target[at, :] = total.astype(target.dtype)


class Scatter:
    def __init__(self, part, scratch, sums=None, piece=0, pieces=1):
        self.part = part
        self.from_core, self.totals, self.from_y, self.from_z = scratch[:4]
        self.sums = self.totals if sums is None else sums
        self.c_sems, self.y_sems, self.z_sems = scratch[4:]
        self.block = self.totals.shape[1]
        self.rows = self.block // pieces
        self.first = piece * self.rows
        self.z, self.y, self.c, self.depth = chip_place()

    @staticmethod
    def sems(depth):
        return [
            pltpu.SemaphoreType.DMA((2, 2 * depth)),
            pltpu.SemaphoreType.DMA((2, depth)),
            pltpu.SemaphoreType.DMA((2, 2, depth)),
        ]

    @staticmethod
    def scratch(depth, rows, columns, pieces=1):
        return [
            pltpu.VMEM((2 * depth, rows, columns), jnp.bfloat16),
            pltpu.VMEM((2 * depth, rows, columns), jnp.bfloat16),
            pltpu.VMEM((depth, rows, columns), jnp.bfloat16),
            pltpu.VMEM((depth + 1, rows, columns), jnp.bfloat16),
        ] + Scatter.sems(depth) * pieces

    def of(self, ref, place):
        return ref.at[place, pl.ds(self.first, self.rows)]

    def split(self):
        return len(self.part.shape) == 3

    def share(self, chip, c):
        start = (chip * 2 + c) * self.block + self.first
        return self.part.at[pl.ds(pl.multiple_of(start, 16), self.rows)]

    def on_core(self, chip):
        target = {"ctx": ctx_of(self.z, self.y, 1 - self.c)}
        source = self.of(self.part, chip) if self.split() else self.share(chip, 1 - self.c)
        return remote(source, self.of(self.from_core, chip), self.c_sems, (chip,), target)

    def send_core(self, chip):
        self.on_core(chip).start()

    def send_y(self, of_z):
        self.on_y(of_z).start()

    def on_y(self, of_z):
        target = {"ctx": ctx_of(self.z, 1 - self.y, self.c)}
        source = self.of(self.sums, of_z * 2 + 1 - self.y)
        return remote(source, self.of(self.from_y, of_z), self.y_sems, (of_z,), target)

    def on_z(self, way, of_z):
        goal = jnp.minimum(self.z + 1, self.depth - 1) if way == 0 else jnp.maximum(self.z - 1, 0)
        place = of_z if way == 0 else jnp.where(of_z == goal, self.depth, of_z)
        source = self.of(self.totals, of_z * 2 + self.y)
        target = {"ctx": ctx_of(goal, self.y, self.c)}
        return remote(source, self.of(self.from_z, place), self.z_sems, (way, of_z), target)

    def start(self):
        def send(of_z):
            self.on_core(of_z * 2 + 1 - self.y).start()
            self.on_core(of_z * 2 + self.y).start()

        for step in range(self.depth - 1, -1, -1):
            each(step, send)

    def add_chip(self, of_z, other, send=True):
        chip = of_z * 2 + (1 - self.y if other else self.y)
        self.on_core(chip).wait_recv()
        total = self.of(self.sums, chip)
        own = total if self.split() else self.share(chip, self.c)
        add_into(total, (own, self.of(self.from_core, chip)), self.rows)
        if other and send:
            self.on_y(of_z).start()

    def add_cores(self, step):
        def add(of_z):
            self.add_chip(of_z, True)
            self.add_chip(of_z, False)

        each(step, add)

    def add_y_of(self, of_z):
        z, depth = self.z, self.depth
        self.on_y(of_z).wait_recv()
        place = of_z * 2 + self.y
        total, own = self.of(self.totals, place), self.of(self.sums, place)
        other = self.of(self.from_y, of_z)
        upward, downward = (of_z > z) & (z > 0), (of_z < z) & (z < depth - 1)
        pl.when(upward)(lambda: self.on_z(0, of_z).wait_recv())
        pl.when(downward)(lambda: self.on_z(1, of_z).wait_recv())

        @pl.when(upward | downward)
        def _():
            add_into(total, (own, other, self.of(self.from_z, of_z)), self.rows)

        @pl.when(jnp.logical_not(upward | downward))
        def _():
            add_into(total, (own, other), self.rows)

        pl.when(of_z > z)(lambda: self.on_z(0, of_z).start())
        pl.when(of_z < z)(lambda: self.on_z(1, of_z).start())

    def add_y(self, step):
        each(step, self.add_y_of)

    def last(self, result):
        z, depth = self.z, self.depth
        own = self.of(self.totals, z * 2 + self.y)
        low, high = self.of(self.from_z, z), self.of(self.from_z, depth)
        result = result.at[pl.ds(self.first, self.rows)]
        pl.when(z > 0)(lambda: self.on_z(0, z).wait_recv())
        pl.when(z < depth - 1)(lambda: self.on_z(1, z).wait_recv())
        inside = (z > 0) & (z < depth - 1)
        pl.when(inside)(lambda: add_into(result, (own, low, high), self.rows))
        pl.when(z == 0)(lambda: add_into(result, (own, high), self.rows))
        pl.when(z == depth - 1)(lambda: add_into(result, (own, low), self.rows))

    def finish(self, cores=True):
        for of_z in range(self.depth):
            self.on_y(of_z).wait_send()
            if cores:
                self.on_core(of_z * 2).wait_send()
                self.on_core(of_z * 2 + 1).wait_send()
            pl.when(of_z > self.z)(lambda: self.on_z(0, of_z).wait_send())
            pl.when(of_z < self.z)(lambda: self.on_z(1, of_z).wait_send())


def scatter_parts(part, scratch, pieces, sums=None):
    arrays, sems = tuple(scratch[:4]), tuple(scratch[4:])
    return Several(
        [
            Scatter(part, arrays + sems[3 * i : 3 * i + 3], sums, i, pieces)
            for i in range(pieces)
        ]
    )


def call(kernel, out, scratch, number, name, *operands, outside=(), outside_out=(), late=()):
    many = isinstance(out, (tuple, list))
    count, results = len(operands), len(out) if many else 1
    late = tuple(late)

    def spec(position, far):
        return pl.BlockSpec(memory_space=pl.ANY if position in far else pltpu.VMEM)

    def with_late(*refs):
        near, sems = refs[-len(late) - 1 : -1], refs[-1]
        copies = {
            i: pltpu.make_async_copy(refs[i], near[k], sems.at[k]) for k, i in enumerate(late)
        }
        for copy in copies.values():
            copy.start()
        held = [near[late.index(i)] if i in late else refs[i] for i in range(count)]

        def arrive(*which):
            for i in which:
                copies[i].wait()

        kernel(arrive, *held, *refs[count : -len(late) - 1])

    if late:
        scratch = list(scratch) + [pltpu.VMEM(operands[i].shape, operands[i].dtype) for i in late]
        scratch.append(pltpu.SemaphoreType.DMA((len(late),)))
    far = tuple(outside) + late
    out_specs = [spec(i, outside_out) for i in range(results)]
    return pl.pallas_call(
        with_late if late else kernel,
        out_shape=out,
        in_specs=[spec(i, far) for i in range(count)],
        out_specs=out_specs if many else out_specs[0],
        scratch_shapes=scratch,
        compiler_params=pltpu.CompilerParams(
            collective_id=number,
            has_side_effects=number is not None,
            vmem_limit_bytes=VMEM_LIMIT,
        ),
        name=name,
    )(*operands)


class Relay:
    def __init__(self, source, out, sems, parts=1, paired=False):
        self.source, self.out, self.sems, self.parts = source, out, sems, parts
        self.paired = paired
        self.z, self.y, self.c, _ = chip_place()
        self.odd = lax.rem(self.z, 2)
        self.rows = source.shape[0] // ((4 if paired else 2) * parts)

    @staticmethod
    def semaphores():
        return pltpu.SemaphoreType.DMA((2, 8))

    def block(self, ref, part, c, odd):
        place = (c * 2 + odd if self.paired else c) * self.parts + part
        return ref.at[pl.ds(pl.multiple_of(place * self.rows, 16), self.rows)]

    def on_x(self, part):
        source = self.block(self.source, part, self.c, self.odd)
        target = self.block(self.out, part, self.c, self.odd)
        return remote(source, target, self.sems, (part,), {"wa": 1 - lax.axis_index("wa")})

    def on_core(self, part, c, other_z=False):
        block = self.block(self.out, part, c, 1 - self.odd if other_z else self.odd)
        at = ((4 if other_z else 2) + part,)
        return remote(block, block, self.sems, at, {"ctx": ctx_of(self.z, self.y, 1 - self.c)})

    def on_pair(self, part, mine=True):
        block = self.block(self.out, part, self.c, self.odd if mine else 1 - self.odd)
        target = {"ctx": ctx_of(self.z + 1 - 2 * self.odd, self.y, self.c)}
        return remote(block, block, self.sems, (6 + part,), target)

    def start(self):
        for part in range(self.parts):
            self.on_x(part).start()

    def pass_on(self, part=0):
        self.on_x(part).wait_recv()
        if self.paired:
            self.on_pair(part).start()
        self.on_core(part, self.c).start()

    def pass_on_pair(self, part):
        self.on_pair(part, mine=False).wait_recv()
        self.on_core(part, self.c, other_z=True).start()

    def finish(self):
        for part in range(self.parts):
            self.on_x(part).wait_send()
            self.on_core(part, self.c).wait_send()
            self.on_core(part, 1 - self.c).wait_recv()
            if self.paired:
                self.on_pair(part).wait_send()
                self.on_core(part, self.c, other_z=True).wait_send()
                self.on_core(part, 1 - self.c, other_z=True).wait_recv()


def front(d_out, w_query, w_keyval, small):
    count, rows = lax.axis_size("ctx"), d_out.shape[0]
    depth = count // 4

    def kernel(
        d_out_ref, query_ref, keyval_ref, small_ref,
        d_out_all, query_there, keyval_there, small_there, *sems,
    ):
        gather = gather_parts(d_out_all, rows, sems[:6], 2)
        query_sems, keyval_sems, small_sems, own_sem = sems[6:]
        query = Relay(query_ref, query_there, query_sems, parts=2)
        keyval = Relay(keyval_ref, keyval_there, keyval_sems)
        partner = {"wa": 1 - lax.axis_index("wa")}
        swap = remote(small_ref, small_there, small_sems, (0,), partner)
        keep = pltpu.make_async_copy(
            d_out_ref, Gather(d_out_all, rows, sems[:3]).own(), own_sem.at[0]
        )
        keep.start()
        greet(across_x=True)
        swap.start()
        query.start()
        keyval.start()
        gather.start(d_out_ref)
        gather.along_z(1)
        gather.along_y(0)
        gather.along_z(2)
        gather.along_y(1)
        query.pass_on(0)
        gather.along_z(3)
        gather.along_y(2)
        query.pass_on(1)
        keyval.pass_on()
        gather.along_y(3)
        gather.finish()
        query.finish()
        keyval.finish()
        swap.wait()
        keep.wait()

    def like(values):
        return jax.ShapeDtypeStruct(values.shape, values.dtype)

    out = [
        jax.ShapeDtypeStruct((count * rows, d_out.shape[1]), d_out.dtype),
        like(w_query), like(w_keyval), like(small),
    ]
    scratch = Gather.sems(depth) * 2 + [Relay.semaphores()] * 2
    scratch += [pltpu.SemaphoreType.DMA((2, 1)), pltpu.SemaphoreType.DMA((1,))]
    every = range(4)
    return call(
        kernel, out, scratch, 0, "front",
        d_out, w_query, w_keyval, small, outside=every, outside_out=every,
    )


def rows_by_rows(left, right):
    return lax.dot_general(
        left, right, (((1,), (1,)), ((), ())), preferred_element_type=jnp.float32
    )


def columns_by_columns(left, right):
    return lax.dot_general(
        left, right, (((0,), (0,)), ((), ())), preferred_element_type=jnp.float32
    )


def down(row):
    return jnp.transpose(jnp.broadcast_to(row.astype(jnp.float32), (128, 128)))


def allowed_bias(doc_row, tokens):
    keys, me = doc_row.shape[1], lax.axis_index("ctx")
    own = down(doc_row[:, pl.ds(pl.multiple_of(me * tokens, 128), tokens)])[:, :1]
    key_block = lax.broadcasted_iota(jnp.int32, (tokens, keys), 1) // BLOCK
    same = doc_row[...].astype(jnp.float32) == own
    return jnp.where(same & (key_block <= me * tokens // BLOCK), 0.0, NEGATIVE)


def chosen_by(routes, lanes, experts):
    numbers = lax.rem(lanes, experts).astype(jnp.float32)
    found = down(routes[:1]) == numbers
    for k in range(1, routes.shape[0]):
        found = found | (down(routes[k : k + 1]) == numbers)
    return found & (lanes < 2 * experts)


def side_columns(own):
    side = lax.axis_index("wa")
    return pl.ds(pl.multiple_of((side if own else 1 - side) * (D // 2), 128), D // 2)


def turned(values, cosine, sine):
    heads = []
    for head in range(values.shape[1] // HEAD_DIM):
        one = values[:, head * HEAD_DIM : (head + 1) * HEAD_DIM]
        heads.append(one * cosine + pltpu.roll(one, HEAD_DIM // 2, axis=1) * sine)
    return jnp.concatenate(heads, axis=1)


def normed(values, gain_vec):
    return values * lax.rsqrt(jnp.mean(values * values, axis=-1, keepdims=True) + EPSILON) * gain_vec


def fill_small(full, small, small_there):
    full[:, side_columns(True)] = small[...].astype(jnp.float32)
    full[:, side_columns(False)] = small_there[...].astype(jnp.float32)


def router_block(full, experts):
    rows = full[:experts]
    spare = jnp.zeros((128 - 2 * experts, rows.shape[1]), jnp.float32)
    return jnp.concatenate([rows, rows, spare], axis=0).astype(jnp.bfloat16)


def attend(
    x, small, small_there, projections, w_out_attn, w_out, angles, doc_row, routes, experts
):
    count, tokens, features = lax.axis_size("ctx"), x.shape[0], x.shape[1]
    depth, length = count // 4, count * tokens
    kv_columns = projections[2].shape[1]

    def kernel(
        arrive, x_ref, small_ref, small_there_ref, query_own, query_other, keyval_own, keyval_other,
        attn_own, attn_own_far, out_own, cosine_ref, sine_ref, doc_row_ref, routes_ref,
        query, keyval, level, mixed, hidden, mixed_low, middle, send, gates_out, attn_other,
        out_other,
        full, stacked, bias, x_sems, attn_sems, *sems,
    ):
        gather = gather_parts(keyval, tokens, sems, 2)
        attn = Relay(attn_own_far, attn_other, attn_sems, parts=2, paired=True)
        greet(across_x=True)
        attn.start()
        partner = {"wa": 1 - lax.axis_index("wa")}
        swap_out = remote(out_own, out_other, x_sems, (0,), partner)
        swap_out.start()
        fill_small(full, small_ref, small_there_ref)
        residual = x_ref[...].astype(jnp.float32)
        hidden[...] = normed(residual, full[experts : experts + 1]).astype(jnp.bfloat16)
        own, other = hidden[:, side_columns(True)], hidden[:, side_columns(False)]
        cosine, sine = cosine_ref[...], sine_ref[...]

        def onto(matrix, matrix_other):
            return jnp.dot(own, matrix[...], preferred_element_type=jnp.float32) + jnp.dot(
                other, matrix_other[...], preferred_element_type=jnp.float32
            )

        arrive(5, 6)
        pre = onto(keyval_own, keyval_other)
        keys = turned(pre[:, : kv_columns // 2], cosine, sine)
        block = jnp.concatenate([keys, pre[:, kv_columns // 2 :]], axis=1)
        Gather(keyval, tokens, sems[:3]).own()[...] = block.astype(jnp.bfloat16)
        gather.start()
        arrive(3, 4)
        query[...] = turned(onto(query_own, query_other), cosine, sine).astype(jnp.bfloat16)
        bias[...] = allowed_bias(doc_row_ref, tokens)
        for head in range(HEADS):
            rows = slice(head * tokens, (head + 1) * tokens)
            stacked[rows, :] = query[:, head * 128 : (head + 1) * 128]
        gather.along_z(1)
        gather.along_y(0)
        gather.along_z(2)
        gather.along_y(1)
        gather.along_z(3)
        attn.pass_on(0)
        gather.along_y(2)
        attn.pass_on(1)
        gather.along_y(3)
        gather.finish()

        @pl.loop(0, HEADS // 2)
        def _(pair):
            rows = pl.ds(pl.multiple_of(pair * 2 * tokens, 128), 2 * tokens)
            kind = pair // (HEADS // KV_HEADS // 2)
            key_part = keyval[:, pl.ds(pl.multiple_of(kind * 128, 128), 128)]
            val_part = keyval[:, pl.ds(pl.multiple_of(kind * 128 + 256, 128), 128)]
            scores = rows_by_rows(stacked[rows, :], key_part) * HEAD_DIM**-0.5
            scores = (scores.reshape(2, tokens, -1) + bias[...][None]).reshape(scores.shape)
            top = jnp.max(scores, axis=-1, keepdims=True)
            weights = jnp.exp(scores - top)
            total = jnp.sum(weights, axis=-1, keepdims=True)
            probs = (weights * (1 / total)).astype(jnp.bfloat16)
            mixture = jnp.dot(probs, val_part, preferred_element_type=jnp.float32)
            for part in range(2):
                columns = pl.ds(pl.multiple_of((pair * 2 + part) * 128, 128), 128)
                mixed[:, columns] = mixture[part * tokens : (part + 1) * tokens]
            column = jnp.broadcast_to(top + jnp.log(total), (2 * tokens, 128))
            level[pl.ds(pair, 1), :] = jnp.transpose(column)[:1]
            pl.when(pair == HEADS // 4)(lambda: attn.pass_on_pair(0))

        attn.pass_on_pair(1)
        mixed_low[...] = mixed[...].astype(jnp.bfloat16)
        attn.finish()
        arrive(7)
        own, other = mixed_low[:, side_columns(True)], mixed_low[:, side_columns(False)]
        middle[...] = residual + onto(attn_own, attn_other)
        hidden_two = normed(middle[...], full[experts + 1 : experts + 2]).astype(jnp.bfloat16)
        send[:, :features] = hidden_two
        logits = rows_by_rows(hidden_two, router_block(full, experts))
        lane = lax.broadcasted_iota(jnp.int32, logits.shape, 1)
        masked = jnp.where(chosen_by(routes_ref[...], lane, experts), logits, NEGATIVE)
        weights = jnp.exp(masked - jnp.max(masked, axis=1, keepdims=True))
        total = jnp.sum(jnp.where(lane < experts, weights, 0.0), axis=1, keepdims=True)
        gates = weights / total
        high = gates.astype(jnp.bfloat16).astype(jnp.float32)
        carried = jnp.where(lane < experts, high, jnp.where(lane < 2 * experts, gates - high, 0.0))
        send[:, features:] = carried.astype(jnp.bfloat16)
        gates_out[...] = jnp.where(lane < experts, gates, 0.0)
        swap_out.wait()

    def shape(rows, columns, kind=jnp.bfloat16):
        return jax.ShapeDtypeStruct((rows, columns), kind)

    wide = features + 128
    out = [
        shape(tokens, features), shape(length, kv_columns), shape(8, 2 * tokens, jnp.float32),
        shape(tokens, features, jnp.float32), shape(tokens, features), shape(tokens, features),
        shape(tokens, features, jnp.float32), shape(tokens, wide), shape(tokens, 128, jnp.float32),
        shape(*w_out_attn.shape), shape(*w_out.shape),
    ]
    scratch = [
        pltpu.VMEM((small.shape[0], features), jnp.float32),
        pltpu.VMEM((HEADS * tokens, HEAD_DIM), jnp.bfloat16),
        pltpu.VMEM((tokens, length), jnp.float32),
        pltpu.SemaphoreType.DMA((2, 1)),
        Relay.semaphores(),
    ] + Gather.sems(depth) * 2
    return call(
        kernel, out, scratch, 2, "attend",
        x, small, small_there, *projections, w_out_attn, w_out_attn, w_out, *angles, doc_row,
        routes, outside=(8, 9), outside_out=(10,), late=(5, 6, 3, 4, 7),
    )


def norm_back(values, gain_vec, grad):
    scale = lax.rsqrt(jnp.mean(values * values, axis=-1, keepdims=True) + EPSILON)
    through = jnp.mean(gain_vec * grad * values, axis=-1, keepdims=True)
    back = scale * gain_vec * grad - values * (scale * scale * scale * through)
    return back, jnp.sum(grad * values * scale, axis=0, keepdims=True)


def attend_back(
    returned, gates, small, small_there, middle, d_out, send, attn_own, attn_other, query, keyval,
    angles, doc_row, level, mixed, hidden, mixed_low, results, experts,
):
    count, tokens, features = lax.axis_size("ctx"), query.shape[0], query.shape[1]
    depth, length, kv_columns = count // 4, keyval.shape[0], keyval.shape[1]

    def kernel(
        arrive, returned_ref, gates_ref, small_ref, small_there_ref, middle_ref, d_out_ref, send_ref,
        attn_own_ref, attn_other_ref, query_ref, keyval_ref, cosine_ref, sine_ref, doc_row_ref,
        level_ref, mixed_ref, hidden_ref, mixed_low_ref, results_ref,
        output, grad_middle, grad_middle_low, grad_middle_there, grad_query, grad_query_there,
        grad_keyval, grad_keyval_there, small_grads, hidden_own, hidden_there, mixed_own,
        mixed_there,
        full, grad_mixed, turned_query, own_keyval, result_sum, stacked, grads, bias, delta, total,
        part, x_sems, *scratch,
    ):
        result = scatter_parts(
            None, (None,) + tuple(scratch[:3]) + tuple(scratch[3:9]), 2, results_ref
        )
        keyval_sum = scatter_parts(part, scratch[9:], 2)
        partner = {"wa": 1 - lax.axis_index("wa")}
        swaps = [
            remote(source, target, x_sems, (i,), partner)
            for i, (source, target) in enumerate(
                [(grad_middle_low, grad_middle_there), (grad_query, grad_query_there),
                 (grad_keyval, grad_keyval_there),
                 (hidden_ref.at[:, side_columns(False)], hidden_there),
                 (mixed_low_ref.at[:, side_columns(False)], mixed_there)]
            )
        ]
        greet(across_x=True)
        arrive(18)
        for k in range(depth - 1, 0, -1):
            result.send_y(nearest(k))
        swaps[3].start()
        swaps[4].start()
        hidden_own[...] = hidden_ref[:, side_columns(True)]
        mixed_own[...] = mixed_low_ref[:, side_columns(True)]
        fill_small(full, small_ref, small_there_ref)
        arrive(0, 4, 5, 6)
        lane = lax.broadcasted_iota(jnp.int32, (tokens, 128), 1)
        gates = gates_ref[...]
        grad_gates = jnp.where(lane < experts, returned_ref[:, features:], 0.0)
        inner = jnp.sum(gates * grad_gates, axis=1, keepdims=True)
        grad_logits = (gates * (grad_gates - inner)).astype(jnp.bfloat16)
        z = chip_place()[0]
        at_end = (z == 0) | (z == depth - 1)
        within = jnp.logical_not(at_end)
        grad_two = returned_ref[:, :features] + jnp.dot(
            grad_logits, router_block(full, experts), preferred_element_type=jnp.float32
        )
        grad_router = columns_by_columns(grad_logits, send_ref[:, :features])
        back, grad_gain = norm_back(middle_ref[...], full[experts + 1 : experts + 2], grad_two)
        grad_middle[...] = d_out_ref[...].astype(jnp.float32) + back
        grad_middle_low[...] = grad_middle[...].astype(jnp.bfloat16)
        swaps[0].start()
        small_grads[:experts] = grad_router[:experts]
        row = lax.broadcasted_iota(jnp.int32, (small_grads.shape[0] - experts, 1), 0)
        small_grads[experts:] = jnp.where(row == 1, grad_gain, 0.0)
        arrive(7, 8)
        grad_mixed[:, side_columns(True)] = rows_by_rows(
            grad_middle_low[...], attn_own_ref[...]
        ).astype(jnp.bfloat16)
        grad_mixed[:, side_columns(False)] = rows_by_rows(
            grad_middle_low[...], attn_other_ref[...]
        ).astype(jnp.bfloat16)
        allowed = jnp.transpose(allowed_bias(doc_row_ref, tokens))
        bias[:, :tokens] = allowed
        bias[:, tokens:] = allowed
        total[...] = jnp.zeros_like(total)
        arrive(9, 10, 15)
        for head in range(HEADS):
            rows = slice(head * tokens, (head + 1) * tokens)
            columns = slice(head * 128, head * 128 + 128)
            stacked[rows, :] = query_ref[:, columns]
            grads[rows, :] = grad_mixed[:, columns]
            product = grad_mixed[:, columns].astype(jnp.float32) * mixed_ref[:, columns]
            delta[head // 2 : head // 2 + 1, (head % 2) * tokens : (head % 2 + 1) * tokens] = (
                jnp.sum(jnp.transpose(product), axis=0, keepdims=True)
            )

        @pl.loop(0, HEADS // 2)
        def _(pair):
            rows = pl.ds(pl.multiple_of(pair * 2 * tokens, 128), 2 * tokens)
            kind = pair // (HEADS // KV_HEADS // 2)
            key_columns = pl.ds(pl.multiple_of(kind * 128, 128), 128)
            val_columns = pl.ds(pl.multiple_of(kind * 128 + 256, 128), 128)
            key_part, val_part = keyval_ref[:, key_columns], keyval_ref[:, val_columns]
            own, grad = stacked[rows, :], grads[rows, :]
            pair_row = pl.ds(pair, 1)
            scores = rows_by_rows(key_part, own) * HEAD_DIM**-0.5 + bias[...]
            probs = jnp.exp(scores - level_ref[pair_row, :])
            grad_probs = rows_by_rows(val_part, grad)
            grad_scores = (probs * (grad_probs - delta[pair_row, :])).astype(jnp.bfloat16)
            own_grad = jnp.transpose(columns_by_columns(key_part, grad_scores))
            for half in range(2):
                columns = pl.ds(pl.multiple_of((pair * 2 + half) * 128, 128), 128)
                turned_query[:, columns] = (
                    own_grad[half * tokens : (half + 1) * tokens] * HEAD_DIM**-0.5
                )
            total[:, key_columns] += (
                jnp.dot(grad_scores, own, preferred_element_type=jnp.float32) * HEAD_DIM**-0.5
            )
            total[:, val_columns] += jnp.dot(
                probs.astype(jnp.bfloat16), grad, preferred_element_type=jnp.float32
            )
            pl.when((pair == HEADS // 4) & at_end)(lambda: result.add_y_of(nearest(depth - 1)))

        part[...] = total[...].astype(jnp.bfloat16)
        keyval_sum.start()
        cosine, sine = cosine_ref[...], -sine_ref[...]
        grad_query[...] = turned(turned_query[...], cosine, sine).astype(jnp.bfloat16)
        swaps[1].start()
        steps = range(depth - 1, -1, -1)
        for step in steps:
            keyval_sum.add_cores(step)
        result.send_y(nearest(0))
        pl.when(within)(lambda: result.add_y_of(nearest(depth - 1)))
        for k in range(depth - 2, 0, -1):
            result.add_y_of(nearest(k))
        for step in steps:
            keyval_sum.add_y(step)
        keyval_sum.last(own_keyval)
        keys = turned(own_keyval[:, : kv_columns // 2], cosine, sine)
        grad_keyval[...] = jnp.concatenate(
            [keys, own_keyval[:, kv_columns // 2 :]], axis=1
        ).astype(jnp.bfloat16)
        swaps[2].start()
        result.add_y_of(nearest(0))
        result.last(result_sum)
        output[...] = (middle_ref[...] + result_sum[...]).astype(jnp.bfloat16)
        keyval_sum.finish()
        result.finish(cores=False)
        for swap in swaps:
            swap.wait()

    def shape(like, kind=jnp.bfloat16):
        return jax.ShapeDtypeStruct(like, kind)

    rows, narrow = (tokens, features), (tokens, kv_columns)
    small_shape = (small.shape[0], features)
    out = [
        shape(rows), shape(rows, jnp.float32), shape(rows), shape(rows), shape(rows), shape(rows),
        shape(narrow), shape(narrow), shape(small_shape, jnp.float32),
    ] + [shape((tokens, features // 2))] * 4
    scratch = [
        pltpu.VMEM(small_shape, jnp.float32),
        pltpu.VMEM(rows, jnp.bfloat16),
        pltpu.VMEM(rows, jnp.float32),
        pltpu.VMEM(narrow, jnp.float32),
        pltpu.VMEM(rows, jnp.float32),
        pltpu.VMEM((HEADS * tokens, HEAD_DIM), jnp.bfloat16),
        pltpu.VMEM((HEADS * tokens, HEAD_DIM), jnp.bfloat16),
        pltpu.VMEM((length, 2 * tokens), jnp.float32),
        pltpu.VMEM((8, 2 * tokens), jnp.float32),
        pltpu.VMEM(keyval.shape, jnp.float32),
        pltpu.VMEM(keyval.shape, jnp.bfloat16),
        pltpu.SemaphoreType.DMA((2, 5)),
    ]
    wide = Scatter.scratch(depth, tokens, features)
    scratch += wide[1:4] + Scatter.sems(depth) * 2 + Scatter.scratch(depth, tokens, kv_columns, 2)
    return call(
        kernel, out, scratch, 4, "attend_back",
        returned, gates, small, small_there, middle, d_out, send, attn_own, attn_other, query,
        keyval, *angles, doc_row, level, mixed, hidden, mixed_low, results,
        late=(18, 0, 4, 5, 6, 7, 8, 9, 10, 15),
    )


def gate_unit(first, second):
    root, cube = math.sqrt(2 / math.pi), 0.044715
    square = first * first
    bend = jnp.tanh(root * first * (1 + cube * square))
    lift = 0.5 * (1 + bend)
    slope = lift + 0.5 * first * (1 - bend * bend) * root * (1 + 3 * cube * square)
    gelu = first * lift
    return gelu * second, slope * second, gelu


def run_experts(send, d_out_all, in_own, out_own, out_other, experts):
    count, tokens = lax.axis_size("ctx"), send.shape[0]
    depth, chips, length = count // 4, count // 2, count * tokens
    wide, features = send.shape[1], d_out_all.shape[1]
    quarter = out_own.shape[0]
    width = 2 * quarter

    def kernel(
        send_ref, d_out_far, in_own_ref, out_own_ref, out_other_ref,
        returned, results_far, grad_in_far, grad_in_other_far, grad_out_far, grad_out_other_far,
        hidden_all, grad_both, gated_hidden, other_part, other_result, result_from, result_sems,
        in_ref, out_ref, d_out_ref, x_sems, near_sem, results, grad_in, grad_in_other, grad_out,
        grad_out_other, far_sems, *scratch,
    ):
        gather = gather_parts(hidden_all, tokens, scratch[:6], 2)
        scatter = scatter_parts(other_part, scratch[6:], 2)
        chip_sums = scratch[7]
        z, y, c, _ = chip_place()
        expert = lax.axis_index("ctx") // 2
        lane = lax.broadcasted_iota(jnp.int32, (1, 128), 1)
        Gather(hidden_all, tokens, scratch[:3]).own()[...] = send_ref[...]
        partner = {"wa": 1 - lax.axis_index("wa")}
        stores = [
            pltpu.make_async_copy(source, target, far_sems.at[i])
            for i, (source, target) in enumerate(
                [(results, results_far), (grad_in, grad_in_far),
                 (grad_in_other, grad_in_other_far), (grad_out, grad_out_far),
                 (grad_out_other, grad_out_other_far)]
            )
        ]
        near = pltpu.make_async_copy(d_out_far, d_out_ref, near_sem.at[0])
        near.start()
        swaps = [
            remote(
                in_own_ref.at[pl.ds(part * quarter, quarter)],
                in_ref.at[pl.ds((2 * part + 1) * quarter, quarter)],
                x_sems,
                (part,),
                partner,
            )
            for part in range(2)
        ]
        greet(across_x=True)
        gather.start()
        for swap in swaps:
            swap.start()
        out_ref[:quarter] = out_own_ref[...]
        out_ref[quarter:] = out_other_ref[...]
        in_ref[:quarter] = in_own_ref[:quarter]
        in_ref[width : width + quarter] = in_own_ref[quarter:]
        def chip_rows(chip):
            return pl.ds(pl.multiple_of(chip * 2 * tokens, 16), 2 * tokens)

        def parted(values):
            low, high = values[:tokens], values[tokens:]
            return jnp.where(c == 0, low, high), jnp.where(c == 0, high, low)

        def backward(chip):
            rows = chip_rows(chip)
            carried = hidden_all[rows, features:].astype(jnp.float32)
            mine = (lane == expert) | (lane == expert + experts)
            gate = jnp.sum(jnp.where(mine, carried, 0.0), axis=1, keepdims=True)
            both = rows_by_rows(hidden_all[rows, :features], in_ref[...])
            hidden, by_first, by_second = gate_unit(both[:, :width], both[:, width:])
            gated_hidden[rows, :] = (hidden * gate).astype(jnp.bfloat16)
            grad_hidden = rows_by_rows(d_out_ref[rows, :], out_ref[...])
            grad_gate = jnp.sum(grad_hidden * hidden, axis=1, keepdims=True)
            grad_hidden = grad_hidden * gate
            grad_both[rows, :width] = (grad_hidden * by_first).astype(jnp.bfloat16)
            grad_both[rows, width:] = (grad_hidden * by_second).astype(jnp.bfloat16)
            own, other = parted(
                jnp.dot(grad_both[rows, :], in_ref[...], preferred_element_type=jnp.float32)
            )
            chip_sums[chip, :, :features] = own.astype(jnp.bfloat16)
            other_part[chip, :, :features] = other.astype(jnp.bfloat16)
            own, other = parted(jnp.where(lane == expert, grad_gate, 0.0))
            chip_sums[chip, :, features:] = own.astype(jnp.bfloat16)
            other_part[chip, :, features:] = other.astype(jnp.bfloat16)
            scatter.send_core(chip)

        gather.along_z(1)
        for step in range(2, depth):
            gather.along_y(step - 2)
            gather.along_z(step)
        near.wait()
        for swap in swaps:
            swap.wait()
        for of_z in (nearest(1), z):
            gather.take_core(of_z)
        backward(nearest(1) * 2 + 1 - y)
        backward(nearest(1) * 2 + y)
        scatter.add_chip(nearest(1), True)
        gather.along_y(depth - 2)
        backward(z * 2 + 1 - y)
        gather.along_y(depth - 1)
        backward(z * 2 + y)
        gather.finish(nearest(1), z)
        scatter.add_chip(nearest(1), False)

        @pl.loop(0, depth - 2)
        def _(turn):
            of_z = nearest(depth - 1 - turn)
            backward(of_z * 2 + 1 - y)
            pl.when(turn > 0)(lambda: scatter.add_chip(nearest(depth - turn), False))
            backward(of_z * 2 + y)
            scatter.add_chip(of_z, True)

        scatter.add_chip(nearest(2), False)
        scatter.add_chip(z, True)
        scatter.add_chip(nearest(0), False)
        scatter.add_y_of(nearest(depth - 1))

        def result_copy(chip):
            target = {"ctx": ctx_of(z, y, 1 - c)}
            return remote(
                other_result.at[chip], result_from.at[chip], result_sems, (chip,), target
            )

        @pl.loop(0, chips)
        def _(chip):
            result = jnp.dot(
                gated_hidden[chip_rows(chip), :], out_ref[...], preferred_element_type=jnp.float32
            )
            own, other = parted(result)
            results[chip] = own.astype(jnp.bfloat16)
            other_result[chip] = other.astype(jnp.bfloat16)
            result_copy(chip).start()

        scatter.add_y_of(nearest(depth - 2))

        @pl.loop(0, features // 512)
        def _(turn):
            at = pl.ds(pl.multiple_of(turn * 512, 512), 512)
            grad = columns_by_columns(gated_hidden[...], d_out_ref[:, at])
            grad_out[:, at] = grad[:quarter]
            grad_out_other[:, at] = grad[quarter:].astype(jnp.bfloat16)

        stores[3].start()
        stores[4].start()
        for k in range(depth - 3, 0, -1):
            scatter.add_y_of(nearest(k))

        @pl.loop(0, features // 512)
        def _(turn):
            at = pl.ds(pl.multiple_of(turn * 512, 512), 512)
            grad = columns_by_columns(grad_both[...], hidden_all[:, at])
            for part in range(2):
                rows = slice(part * quarter, (part + 1) * quarter)
                first = part * width
                grad_in[rows, at] = grad[first : first + quarter]
                grad_in_other[rows, at] = grad[first + quarter : first + width].astype(jnp.bfloat16)

        stores[1].start()
        stores[2].start()

        @pl.loop(0, chips)
        def _(chip):
            result_copy(chip).wait_recv()
            add_into(results.at[chip], (results.at[chip], result_from.at[chip]), tokens)

        stores[0].start()
        scatter.add_y_of(nearest(0))
        scatter.last(returned)
        scatter.finish()
        for chip in range(chips):
            result_copy(chip).wait_send()
        for store in stores:
            store.wait()

    block = (chips, tokens, features)
    out = [
        jax.ShapeDtypeStruct((tokens, wide), jnp.float32),
        jax.ShapeDtypeStruct(block, jnp.bfloat16),
        jax.ShapeDtypeStruct(in_own.shape, jnp.float32),
        jax.ShapeDtypeStruct(in_own.shape, jnp.bfloat16),
        jax.ShapeDtypeStruct(out_own.shape, jnp.float32),
        jax.ShapeDtypeStruct(out_own.shape, jnp.bfloat16),
    ]
    scratch = [
        pltpu.VMEM((length, wide), jnp.bfloat16),
        pltpu.VMEM((length, 2 * width), jnp.bfloat16),
        pltpu.VMEM((length, width), jnp.bfloat16),
        pltpu.VMEM((chips, tokens, wide), jnp.bfloat16),
        pltpu.VMEM(block, jnp.bfloat16),
        pltpu.VMEM(block, jnp.bfloat16),
        pltpu.SemaphoreType.DMA((2, chips)),
        pltpu.VMEM((2 * width, features), jnp.bfloat16),
        pltpu.VMEM((width, features), jnp.bfloat16),
        pltpu.VMEM(d_out_all.shape, jnp.bfloat16),
        pltpu.SemaphoreType.DMA((2, 2)),
        pltpu.SemaphoreType.DMA((1,)),
    ]
    scratch += [pltpu.VMEM(one.shape, one.dtype) for one in out[1:]]
    scratch.append(pltpu.SemaphoreType.DMA((5,)))
    scratch += Gather.sems(depth) * 2 + Scatter.scratch(depth, tokens, wide, 2)
    return call(
        kernel, out, scratch, 3, "experts", send, d_out_all, in_own, out_own, out_other, outside=(1,),
        outside_out=range(1, 6),
    )


def finish(
    x, grad_middle, small, small_there, small_grads, matrices, hidden, mixed, middle, query, keyval,
    expert_in, expert_out,
):
    count, tokens, half = lax.axis_size("ctx"), x.shape[0], x.shape[1] // 2
    depth, rows = count // 4, half // count
    widths = (middle[0].shape[1], query[0].shape[1], keyval[0].shape[1])
    experts = small.shape[0] // 2

    def kernel(
        arrive, x_ref, grad_middle_ref, small_ref, small_there_ref, small_grads_ref,
        query_own, query_other, keyval_own, keyval_other,
        hidden_ref, hidden_there, mixed_ref, mixed_there, middle_ref, middle_there,
        query_ref, query_there, keyval_ref, keyval_there, in_ref, out_ref,
        attn_sum, query_sum, keyval_sum, small_sum, grad_input, in_there, out_there,
        attn_part, query_part, keyval_part, pair, full, grad_one, small_mine, small_came, small_all,
        x_sems, *scratch,
    ):
        scatters, gathers = [], []
        parts, sums = (attn_part, query_part, keyval_part), (attn_sum, query_sum, keyval_sum)
        for part, total in zip(parts, sums):
            scatters.append(Scatter(part, scratch[:7]))
            gathers.append(Gather(total, rows, scratch[7:10]))
            scratch = scratch[10:]
        small_out = Gather(small_all, small_came.shape[0], scratch)
        (attn, query_, keyval_), (attn_out, query_out, keyval_out) = scatters, gathers
        partner = {"wa": 1 - lax.axis_index("wa")}
        swaps = [
            remote(source, target, x_sems, (i,), partner)
            for i, (source, target) in enumerate(
                [(small_mine.at[:, side_columns(False)], small_came), (in_ref, in_there),
                 (out_ref, out_there)]
            )
        ]
        steps = range(depth - 1, -1, -1)

        def products(left, left_there, right, right_there, part):
            pair[:tokens] = left[...]
            pair[tokens:] = left_there[...]

            @pl.loop(0, part.shape[1] // 512)
            def _(turn):
                at = pl.ds(pl.multiple_of(turn * 512, 512), 512)
                both = jnp.concatenate([right[:, at], right_there[:, at]], axis=0)
                part[:, at] = columns_by_columns(pair[...], both).astype(jnp.bfloat16)

        products(mixed_ref, mixed_there, middle_ref, middle_there, attn_part)
        greet(across_x=True)
        attn.start()
        products(hidden_ref, hidden_there, query_ref, query_there, query_part)
        for step in steps:
            attn.add_cores(step)
        query_.start()
        products(hidden_ref, hidden_there, keyval_ref, keyval_there, keyval_part)
        keyval_.start()
        for step in steps:
            query_.add_cores(step)
        attn.add_y(depth - 1)
        fill_small(full, small_ref, small_there_ref)
        arrive(0, 1, 5, 6, 7, 8)
        grad_one[:, side_columns(True)] = rows_by_rows(
            query_ref[...], query_own[...]
        ) + rows_by_rows(keyval_ref[...], keyval_own[...])
        attn.add_y(depth - 2)
        grad_one[:, side_columns(False)] = rows_by_rows(
            query_ref[...], query_other[...]
        ) + rows_by_rows(keyval_ref[...], keyval_other[...])
        back, grad_gain = norm_back(
            x_ref[...].astype(jnp.float32), full[experts : experts + 1], grad_one[...]
        )
        grad_input[...] = (grad_middle_ref[...] + back).astype(jnp.bfloat16)
        row = lax.broadcasted_iota(jnp.int32, (small_mine.shape[0], 1), 0)
        small_mine[...] = jnp.where(row == experts, grad_gain, small_grads_ref[...])
        swaps[0].start()
        for step in range(depth - 3, -1, -1):
            attn.add_y(step)
        for step in steps:
            keyval_.add_cores(step)
        attn.last(attn_out.own())
        attn_out.start()
        swaps[1].start()
        swaps[2].start()
        swaps[0].wait()
        small_out.own()[...] = (small_mine[:, side_columns(True)] + small_came[...]).astype(
            jnp.bfloat16
        )
        small_out.start()
        for step in steps:
            query_.add_y(step)
        attn_out.along_z(1)
        query_.last(query_out.own())
        query_out.start()
        attn_out.along_z(2)
        attn_out.along_y(0)
        small_out.along_z(1)
        for step in steps:
            keyval_.add_y(step)
        attn_out.along_z(3)
        attn_out.along_y(1)
        keyval_.last(keyval_out.own())
        keyval_out.start()
        query_out.along_z(1)
        small_out.along_z(2)
        attn_out.along_y(2)
        query_out.along_z(2)
        small_out.along_z(3)
        query_out.along_y(0)
        keyval_out.along_z(1)
        query_out.along_z(3)
        attn_out.along_y(3)
        keyval_out.along_z(2)
        query_out.along_y(1)
        keyval_out.along_z(3)
        query_out.along_y(2)
        small_out.along_y(0)
        keyval_out.along_y(0)
        small_out.along_y(1)
        query_out.along_y(3)
        keyval_out.along_y(1)
        small_out.along_y(2)
        keyval_out.along_y(2)
        small_out.along_y(3)
        keyval_out.along_y(3)
        for one in [small_out] + gathers + scatters:
            one.finish()
        small_rows = small_came.shape[0]
        total = small_all[:small_rows].astype(jnp.float32)
        for device in range(1, count):
            rows_of = slice(device * small_rows, (device + 1) * small_rows)
            total = total + small_all[rows_of].astype(jnp.float32)
        small_sum[...] = total
        swaps[1].wait()
        swaps[2].wait()

    small_shape = (small.shape[0], half)
    out = [jax.ShapeDtypeStruct((half, width), jnp.bfloat16) for width in widths]
    out += [
        jax.ShapeDtypeStruct(small_shape, jnp.float32),
        jax.ShapeDtypeStruct(x.shape, jnp.bfloat16),
        jax.ShapeDtypeStruct(expert_in.shape, expert_in.dtype),
        jax.ShapeDtypeStruct(expert_out.shape, expert_out.dtype),
    ]
    scratch = [pltpu.VMEM((half, width), jnp.bfloat16) for width in widths]
    scratch += [
        pltpu.VMEM((2 * tokens, half), jnp.bfloat16),
        pltpu.VMEM(small_grads.shape, jnp.float32),
        pltpu.VMEM(x.shape, jnp.float32),
        pltpu.VMEM(small_grads.shape, jnp.float32),
        pltpu.VMEM(small_shape, jnp.float32),
        pltpu.VMEM((count * small.shape[0], half), jnp.bfloat16),
        pltpu.SemaphoreType.DMA((2, 3)),
    ]
    for width in widths:
        scratch += Scatter.scratch(depth, rows, width) + Gather.sems(depth)
    scratch += Gather.sems(depth)
    return call(
        kernel, out, scratch, 1, "finish",
        x, grad_middle, small, small_there, small_grads, *matrices, *hidden, *mixed, *middle,
        *query, *keyval, expert_in, expert_out, outside=(19, 20), outside_out=(5, 6),
        late=(0, 1, 5, 6, 7, 8),
    )


def widen(query, keyval, attn, grad_in, in_there, grad_out, out_there):
    quarter, features = grad_out.shape
    steps = 4

    def kernel(*refs):
        query_ref, keyval_ref, attn_ref, in_ref, in_there_ref, out_ref, out_there_ref = refs[:7]
        query_out, keyval_out, attn_out, in_out, out_out = refs[7:]
        query_out[...] = query_ref[...].astype(jnp.float32)
        keyval_out[...] = keyval_ref[...].astype(jnp.float32)
        attn_out[...] = attn_ref[...].astype(jnp.float32)
        both = in_ref[...] + in_there_ref[...].astype(jnp.float32)
        in_out[...] = both
        out_out[0] = out_ref[...] + out_there_ref[...].astype(jnp.float32)

    def rows(values):
        return pl.BlockSpec((values.shape[0] // steps, values.shape[1]), lambda i: (i, 0))

    operands = (query, keyval, attn, grad_in, in_there, grad_out, out_there)
    return pl.pallas_call(
        kernel,
        grid=(steps,),
        out_shape=[
            jax.ShapeDtypeStruct(query.shape, jnp.float32),
            jax.ShapeDtypeStruct(keyval.shape, jnp.float32),
            jax.ShapeDtypeStruct(attn.shape, jnp.float32),
            jax.ShapeDtypeStruct(grad_in.shape, jnp.float32),
            jax.ShapeDtypeStruct((1, quarter, features), jnp.float32),
        ],
        in_specs=[rows(values) for values in operands],
        out_specs=[
            rows(query), rows(keyval), rows(attn),
            rows(grad_in),
            pl.BlockSpec((1, quarter // steps, features), lambda i: (0, i, 0)),
        ],
        compiler_params=pltpu.CompilerParams(vmem_limit_bytes=VMEM_LIMIT),
        name="widen",
    )(*operands)


def gathered_body(
    layer_input, seq_ids, routes, gain_attn, w_query, w_keyval, w_out_attn, gain_ffn, router,
    w_in, w_out, d_out,
):
    me = lax.axis_index("ctx")
    tokens, experts = layer_input.shape[1], router.shape[1]
    x, grad_out = layer_input[0], d_out[0]
    small = jnp.concatenate(
        [router.T, gain_attn[None], gain_ffn[None], jnp.zeros((experts - 2, D // 2), jnp.bfloat16)]
    )
    turns = angle_table(me * tokens + jnp.arange(tokens, dtype=jnp.int32))[:, 0]
    cosine, sine = jnp.cos(turns), jnp.sin(turns)
    angles = (
        jnp.concatenate([cosine, cosine], axis=1), jnp.concatenate([-sine, sine], axis=1)
    )
    in_own = jnp.swapaxes(w_in[0], 1, 2).reshape(-1, D)

    d_out_all, w_query_there, w_keyval_there, small_there = front(
        grad_out, w_query, w_keyval, small
    )
    projections = (w_query, w_query_there, w_keyval, w_keyval_there)
    (
        query, keyval, level, mixed, hidden, mixed_low, middle, send, gates, w_out_attn_there,
        w_out_there,
    ) = attend(
        x, small, small_there, projections, w_out_attn, w_out[0], angles, seq_ids, routes[0].T,
        experts,
    )
    returned, results, grad_in, grad_in_other, grad_out_matrix, grad_out_other = run_experts(
        send, d_out_all, in_own, w_out[0], w_out_there, experts
    )
    (
        output, grad_middle, middle_low, middle_there, grad_query, query_there, grad_keyval,
        keyval_there, small_grads, *halves,
    ) = attend_back(
        returned, gates, small, small_there, middle, grad_out, send, w_out_attn, w_out_attn_there,
        query, keyval, angles, seq_ids, level, mixed, hidden, mixed_low, results, experts,
    )
    attn_sum, query_sum, keyval_sum, small_sum, grad_input, in_there, out_there = finish(
        x, grad_middle, small, small_there, small_grads, projections, halves[:2], halves[2:],
        (middle_low, middle_there), (grad_query, query_there),
        (grad_keyval, keyval_there), grad_in_other, grad_out_other,
    )
    query_sum, keyval_sum, attn_sum, grad_w_in, grad_w_out = widen(
        query_sum, keyval_sum, attn_sum, grad_in, in_there, grad_out_matrix, out_there
    )
    return (
        output[None],
        grad_input[None],
        small_sum[experts],
        query_sum,
        keyval_sum,
        attn_sum,
        small_sum[experts + 1],
        small_sum[:experts].T,
        jnp.swapaxes(grad_w_in.reshape(2, -1, D), 1, 2)[None],
        grad_w_out,
    )


def solution(mesh):
    in_specs = (
        P("wa", "ctx", None),
        P("wa", None),
        P("wa", "ctx", None),
        P("wa"),
        P("wa", None),
        P("wa", None),
        P("wa", None),
        P("wa"),
        P("wa", None),
        P("ctx", None, None, "wa"),
        P("ctx", "wa", None),
        P("wa", "ctx", None),
    )
    out_specs = (
        P("wa", "ctx", None),
        P("wa", "ctx", None),
        P("wa"),
        P("wa", None),
        P("wa", None),
        P("wa", None),
        P("wa"),
        P("wa", None),
        P("ctx", None, None, "wa"),
        P("ctx", "wa", None),
    )
    depth = mesh.shape["ctx"]
    body = gathered_body if depth == 16 else routed_body
    return jax.shard_map(body, mesh=mesh, in_specs=in_specs, out_specs=out_specs, check_vma=False)
```

```python
import functools
import math

import jax
import jax.numpy as jnp
from jax import lax
from jax.experimental import pallas as pl
from jax.experimental.pallas import tpu as pltpu
from jax.sharding import PartitionSpec as P

D = 1536
HEADS = 12
KV_HEADS = 2
HEAD_DIM = 128
TOP = 4
BLOCK = 256


EPSILON = 1e-06
THETA = 1000000.0
NEGATIVE = -1e30


def rms_scale(values, gain_vec):
    return (
        values * lax.rsqrt(jnp.mean(values * values, axis=-1, keepdims=True) + EPSILON) * gain_vec
    )


def rotate(values, angles):
    half_dim = values.shape[-1] // 2
    cosine = jnp.cos(angles)
    sine_part = jnp.sin(angles)
    first_half = values[..., :half_dim]
    second = values[..., half_dim:]
    return jnp.concatenate(
        [first_half * cosine - second * sine_part, second * cosine + first_half * sine_part],
        axis=-1,
    )


def angle_table(positions):
    half_dim = HEAD_DIM // 2
    frequency = THETA ** (-2.0 * jnp.arange(half_dim, dtype=jnp.float32) / HEAD_DIM)
    return (positions.astype(jnp.float32)[:, None] * frequency[None, :])[:, None, :]


def gated(stacked):
    return jax.nn.gelu(stacked[..., 0, :], approximate=True) * stacked[..., 1, :]


def over_keys(key_rows, running, advance):
    key_count = key_rows.shape[0]
    key_width = math.gcd(key_count, 512)

    def one_turn(state_now, block_index):
        key_offset = block_index * key_width
        key_part = lax.dynamic_slice_in_dim(key_rows, key_offset, key_width, 0)
        return (advance(state_now, key_part, key_offset), None)

    running, unused = lax.scan(
        one_turn, running, jnp.arange(key_count // key_width, dtype=jnp.int32)
    )
    return running


def routed_body(
    layer_input,
    seq_ids,
    routes,
    gain_attn,
    w_query,
    w_keyval,
    w_out_attn,
    gain_ffn,
    router,
    w_in,
    w_out,
    d_out,
):
    ctx_count = lax.axis_size("ctx")
    ctx_index = lax.axis_index("ctx")
    tokens = layer_input.shape[1]
    length = tokens * ctx_count
    experts_all = ctx_count // 2
    capacity = 2 * tokens * TOP // experts_all
    group = HEADS // KV_HEADS
    kv_width = KV_HEADS * HEAD_DIM
    row_count = group * tokens
    scale = HEAD_DIM ** (-0.5)
    gain_one, query_matrix, keyvalue_matrix, attention_matrix = (
        lax.all_gather(gain_attn, "wa", axis=0, tiled=True),
        lax.all_gather(w_query, "wa", axis=0, tiled=True),
        lax.all_gather(w_keyval, "wa", axis=0, tiled=True),
        lax.all_gather(w_out_attn, "wa", axis=0, tiled=True),
    )
    residual = layer_input[0].astype(jnp.float32)
    normed_one, norm_one_back = jax.vjp(rms_scale, residual, gain_one.astype(jnp.float32))
    hidden_first_norm = normed_one.astype(jnp.bfloat16)
    positions = ctx_index * tokens + jnp.arange(tokens, dtype=jnp.int32)
    angles = angle_table(positions)
    query_projected = jnp.dot(
        hidden_first_norm, query_matrix, preferred_element_type=jnp.float32
    ).reshape(tokens, HEADS, HEAD_DIM)
    keyvalue_projected = jnp.dot(
        hidden_first_norm, keyvalue_matrix, preferred_element_type=jnp.float32
    )
    key_pre = keyvalue_projected[:, :kv_width].reshape(tokens, KV_HEADS, HEAD_DIM)
    query_low = rotate(query_projected, angles).astype(jnp.bfloat16)
    key_low = rotate(key_pre, angles).astype(jnp.bfloat16)
    value_low = keyvalue_projected[:, kv_width:].astype(jnp.bfloat16)
    keyval_send = jnp.concatenate([key_low.reshape(tokens, kv_width), value_low], axis=1)
    query_rows = (
        query_low.reshape(tokens, KV_HEADS, group, HEAD_DIM)
        .transpose(1, 2, 0, 3)
        .reshape(KV_HEADS, row_count, HEAD_DIM)
    )
    doc_row = seq_ids[0]
    query_docs = lax.dynamic_slice_in_dim(doc_row, ctx_index * tokens, tokens, 0)
    query_blocks = positions // BLOCK

    def block_scores(key_part, first_key):
        key_count = key_part.shape[0]
        split_part = key_part.reshape(key_count, 2, KV_HEADS, HEAD_DIM)
        keys_here = split_part[:, 0]
        values_here = split_part[:, 1]
        scores = (
            jnp.einsum("hrd,nhd->hrn", query_rows, keys_here, preferred_element_type=jnp.float32)
            * scale
        )
        key_docs = lax.dynamic_slice_in_dim(doc_row, first_key, key_count, 0)
        key_blocks = (first_key + jnp.arange(key_count, dtype=jnp.int32)) // BLOCK
        allowed = (query_docs[:, None] == key_docs[None, :]) & (
            key_blocks[None, :] <= query_blocks[:, None]
        )
        allowed = jnp.broadcast_to(allowed[None], (group, tokens, key_count)).reshape(
            1, row_count, key_count
        )
        return (jnp.where(allowed, scores, NEGATIVE), allowed, keys_here, values_here)

    def probs_of(masked, allowed, largest, totals):
        return jnp.where(allowed, jnp.exp(masked - largest[..., None]) / totals[..., None], 0.0)

    def stats_step(running, key_part, first_key):
        largest, totals = running
        masked, allowed, keys_here, values_here = block_scores(key_part, first_key)
        new_largest = jnp.maximum(largest, jnp.max(masked, axis=-1))
        weights = jnp.where(allowed, jnp.exp(masked - new_largest[..., None]), 0.0)
        return (new_largest, totals * jnp.exp(largest - new_largest) + jnp.sum(weights, axis=-1))

    start_stats = (
        jnp.full((KV_HEADS, row_count), NEGATIVE, jnp.float32),
        jnp.zeros((KV_HEADS, row_count), jnp.float32),
    )
    largest, totals = over_keys(
        lax.all_gather(keyval_send, "ctx", axis=0, tiled=True), start_stats, stats_step
    )

    def values_step(running, key_part, first_key):
        masked, allowed, keys_here, values_here = block_scores(key_part, first_key)
        probs_low = probs_of(masked, allowed, largest, totals).astype(jnp.bfloat16)
        return running + jnp.einsum(
            "hrn,nhd->hrd", probs_low, values_here, preferred_element_type=jnp.float32
        )

    start_values = jnp.zeros((KV_HEADS, row_count, HEAD_DIM), jnp.float32)
    mixed_rows = over_keys(
        lax.all_gather(keyval_send, "ctx", axis=0, tiled=True), start_values, values_step
    )
    mixed_low = (
        mixed_rows.reshape(KV_HEADS, group, tokens, HEAD_DIM)
        .transpose(2, 0, 1, 3)
        .reshape(tokens, HEADS * HEAD_DIM)
        .astype(jnp.bfloat16)
    )
    middle_activation = residual + jnp.dot(
        mixed_low, attention_matrix, preferred_element_type=jnp.float32
    )
    gain_two, router_full, w_in_full, w_out_full = (
        lax.all_gather(gain_ffn, "wa", axis=0, tiled=True),
        lax.all_gather(router, "wa", axis=0, tiled=True),
        lax.all_gather(w_in, "wa", axis=3, tiled=True),
        lax.all_gather(w_out, "wa", axis=1, tiled=True),
    )
    in_half = w_in_full[0]
    out_half = w_out_full[0]
    normed_two, norm_two_back = jax.vjp(rms_scale, middle_activation, gain_two.astype(jnp.float32))
    hidden_second_norm = normed_two.astype(jnp.bfloat16)
    router_logits = jnp.dot(hidden_second_norm, router_full, preferred_element_type=jnp.float32)
    route_ids = routes[0]

    def gate_values(logit_rows):
        return jax.nn.softmax(jnp.take_along_axis(logit_rows, route_ids, axis=-1), axis=-1)

    gates, gate_back = jax.vjp(gate_values, router_logits)
    flat_ids = route_ids.reshape(tokens * TOP)
    expert_hits = (flat_ids[:, None] == jnp.arange(experts_all, dtype=jnp.int32)[None, :]).astype(
        jnp.int32
    )
    ranks = jnp.sum(expert_hits * (jnp.cumsum(expert_hits, axis=0) - expert_hits), axis=1)
    slot_first = 2 * flat_ids * capacity + ranks
    slot_second = slot_first + capacity
    slot_total = ctx_count * capacity
    slot_numbers = jnp.arange(slot_total, dtype=jnp.int32)[:, None]
    placed = (
        (slot_first[None, :] == slot_numbers) | (slot_second[None, :] == slot_numbers)
    ).astype(jnp.bfloat16)
    dispatch = jnp.sum(placed.reshape(slot_total, tokens, TOP), axis=2)
    send_rows = (
        jnp.dot(dispatch, hidden_second_norm, preferred_element_type=jnp.float32)
        .astype(jnp.bfloat16)
        .reshape(ctx_count, capacity, D)
    )
    arrived = lax.all_to_all(send_rows, "ctx", split_axis=0, concat_axis=0, tiled=True)
    stacked = jnp.einsum("ncd,gdf->ncgf", arrived, in_half, preferred_element_type=jnp.float32)
    hidden_low = gated(stacked).astype(jnp.bfloat16)
    result = jnp.einsum(
        "ncf,fd->ncd", hidden_low, out_half, preferred_element_type=jnp.float32
    ).astype(jnp.bfloat16)
    returned_rows = lax.all_to_all(result, "ctx", split_axis=0, concat_axis=0, tiled=True)
    returned_flat = returned_rows.reshape(slot_total, D)
    pair_rows = (
        returned_flat[slot_first].astype(jnp.float32)
        + returned_flat[slot_second].astype(jnp.float32)
    ).reshape(tokens, TOP, D)
    output = (middle_activation + jnp.sum(gates[:, :, None] * pair_rows, axis=1)).astype(
        jnp.bfloat16
    )
    grad_out = d_out[0].astype(jnp.float32)
    grad_gates = jnp.sum(pair_rows * grad_out[:, None, :], axis=-1)
    (grad_logits,) = gate_back(grad_gates)
    grad_logits_low = grad_logits.astype(jnp.bfloat16)
    gate_slots = jnp.dot(
        placed.astype(jnp.float32), gates.reshape(tokens * TOP), precision=lax.Precision.HIGHEST
    )
    routed_grad = jnp.dot(dispatch, d_out[0], preferred_element_type=jnp.float32)
    grad_send_rows = (
        (gate_slots[:, None] * routed_grad).astype(jnp.bfloat16).reshape(ctx_count, capacity, D)
    )
    grad_arrived = lax.all_to_all(grad_send_rows, "ctx", split_axis=0, concat_axis=0, tiled=True)
    grad_hidden = jnp.einsum(
        "ncd,fd->ncf", grad_arrived, out_half, preferred_element_type=jnp.float32
    )
    hidden_again, gated_back = jax.vjp(gated, stacked)
    (grad_stacked,) = gated_back(grad_hidden)
    grad_stacked_low = grad_stacked.astype(jnp.bfloat16)
    grad_rows = jnp.einsum(
        "ncgf,gdf->ncd", grad_stacked_low, in_half, preferred_element_type=jnp.float32
    ).astype(jnp.bfloat16)
    grad_returned = lax.all_to_all(grad_rows, "ctx", split_axis=0, concat_axis=0, tiled=True)
    grad_w_in = jnp.einsum(
        "ncd,ncgf->gdf", arrived, grad_stacked_low, preferred_element_type=jnp.float32
    )[None]
    grad_w_out = jnp.einsum(
        "ncf,ncd->fd",
        hidden_again.astype(jnp.bfloat16),
        grad_arrived,
        preferred_element_type=jnp.float32,
    )[None]
    grad_hidden_two = jnp.einsum(
        "st,sd->td",
        dispatch,
        grad_returned.reshape(slot_total, D),
        preferred_element_type=jnp.float32,
    )
    grad_hidden_two = grad_hidden_two + jnp.dot(
        grad_logits_low, router_full.T, preferred_element_type=jnp.float32
    )
    grad_router = jnp.dot(hidden_second_norm.T, grad_logits_low, preferred_element_type=jnp.float32)
    grad_middle_norm, grad_gain_two = norm_two_back(grad_hidden_two)
    grad_middle = grad_out + grad_middle_norm
    grad_middle_low = grad_middle.astype(jnp.bfloat16)
    grad_attn_weight = jnp.dot(mixed_low.T, grad_middle_low, preferred_element_type=jnp.float32)
    grad_mixed = jnp.dot(
        grad_middle_low, attention_matrix.T, preferred_element_type=jnp.float32
    ).astype(jnp.bfloat16)
    grad_rows_out = (
        grad_mixed.reshape(tokens, KV_HEADS, group, HEAD_DIM)
        .transpose(1, 2, 0, 3)
        .reshape(KV_HEADS, row_count, HEAD_DIM)
    )
    delta = jnp.sum(grad_rows_out.astype(jnp.float32) * mixed_rows, axis=-1)

    def score_grads(key_part, first_key):
        masked, allowed, keys_here, values_here = block_scores(key_part, first_key)
        probs = probs_of(masked, allowed, largest, totals)
        grad_probs = jnp.einsum(
            "hrd,nhd->hrn", grad_rows_out, values_here, preferred_element_type=jnp.float32
        )
        grad_scores = (probs * (grad_probs - delta[..., None])).astype(jnp.bfloat16)
        return (grad_scores, probs.astype(jnp.bfloat16), keys_here)

    def key_terms(grad_scores, probs_low, key_count):
        grad_keys = (
            jnp.einsum("hrn,hrd->nhd", grad_scores, query_rows, preferred_element_type=jnp.float32)
            * scale
        )
        grad_values = jnp.einsum(
            "hrn,hrd->nhd", probs_low, grad_rows_out, preferred_element_type=jnp.float32
        )
        return jnp.concatenate(
            [grad_keys.reshape(key_count, kv_width), grad_values.reshape(key_count, kv_width)],
            axis=1,
        )

    start_query = jnp.zeros((KV_HEADS, row_count, HEAD_DIM), jnp.float32)

    def back_step(running, key_part, first_key):
        grad_query_rows, grad_keyvals = running
        grad_scores, probs_low, keys_here = score_grads(key_part, first_key)
        grad_query_rows = (
            grad_query_rows
            + jnp.einsum("hrn,nhd->hrd", grad_scores, keys_here, preferred_element_type=jnp.float32)
            * scale
        )
        fresh = key_terms(grad_scores, probs_low, key_part.shape[0])
        return (grad_query_rows, lax.dynamic_update_slice_in_dim(grad_keyvals, fresh, first_key, 0))

    start_back = (start_query, jnp.zeros((length, 2 * kv_width), jnp.float32))
    grad_query_rows, grad_keyvals = over_keys(
        lax.all_gather(keyval_send, "ctx", axis=0, tiled=True), start_back, back_step
    )
    grad_keyval_mine = lax.psum_scatter(grad_keyvals, "ctx", scatter_dimension=0, tiled=True)
    grad_query = grad_query_rows.reshape(KV_HEADS, group, tokens, HEAD_DIM).transpose(2, 0, 1, 3)
    grad_query_pre = (
        rotate(grad_query.reshape(tokens, HEADS, HEAD_DIM), -angles)
        .reshape(tokens, HEADS * HEAD_DIM)
        .astype(jnp.bfloat16)
    )
    grad_key_pre = rotate(
        grad_keyval_mine[:, :kv_width].reshape(tokens, KV_HEADS, HEAD_DIM), -angles
    ).reshape(tokens, kv_width)
    grad_keyval_pre = jnp.concatenate(
        [grad_key_pre, grad_keyval_mine[:, kv_width:]], axis=1
    ).astype(jnp.bfloat16)
    grad_hidden_one = jnp.dot(
        grad_query_pre, query_matrix.T, preferred_element_type=jnp.float32
    ) + jnp.dot(grad_keyval_pre, keyvalue_matrix.T, preferred_element_type=jnp.float32)
    grad_query_weight = jnp.dot(
        hidden_first_norm.T, grad_query_pre, preferred_element_type=jnp.float32
    )
    grad_keyval_weight = jnp.dot(
        hidden_first_norm.T, grad_keyval_pre, preferred_element_type=jnp.float32
    )
    grad_residual_norm, grad_gain_one = norm_one_back(grad_hidden_one)
    grad_input = (grad_middle + grad_residual_norm).astype(jnp.bfloat16)
    shares = (
        lax.psum_scatter(
            grad_gain_one.astype(jnp.bfloat16), "wa", scatter_dimension=0, tiled=True
        ).astype(jnp.float32),
        lax.psum_scatter(
            grad_query_weight.astype(jnp.bfloat16), "wa", scatter_dimension=0, tiled=True
        ).astype(jnp.float32),
        lax.psum_scatter(
            grad_keyval_weight.astype(jnp.bfloat16), "wa", scatter_dimension=0, tiled=True
        ).astype(jnp.float32),
        lax.psum_scatter(
            grad_attn_weight.astype(jnp.bfloat16), "wa", scatter_dimension=0, tiled=True
        ).astype(jnp.float32),
        lax.psum_scatter(
            grad_gain_two.astype(jnp.bfloat16), "wa", scatter_dimension=0, tiled=True
        ).astype(jnp.float32),
        lax.psum_scatter(
            grad_router.astype(jnp.bfloat16), "wa", scatter_dimension=0, tiled=True
        ).astype(jnp.float32),
        lax.psum_scatter(
            grad_w_in.astype(jnp.bfloat16), "wa", scatter_dimension=3, tiled=True
        ).astype(jnp.float32),
        lax.psum_scatter(
            grad_w_out.astype(jnp.bfloat16), "wa", scatter_dimension=1, tiled=True
        ).astype(jnp.float32),
    )
    summed = lax.psum((shares[0], shares[1], shares[2], shares[3], shares[4], shares[5]), "ctx")
    return (
        output[None],
        grad_input[None],
        summed[0],
        summed[1],
        summed[2],
        summed[3],
        summed[4],
        summed[5],
        shares[6],
        shares[7],
    )

MESH = pl.DeviceIdType.MESH
VMEM_LIMIT = 60 * 1024 * 1024


def chip_place():
    count = lax.axis_size("ctx")
    me = lax.axis_index("ctx")
    return me // 4, lax.rem(me // 2, 2), lax.rem(me, 2), count // 4


def ctx_of(z, y, c):
    return (z * 2 + y) * 2 + c


def greet(across_x=False):
    z, y, c, depth = chip_place()
    barrier = pltpu.get_barrier_semaphore()

    def signal(device):
        pl.semaphore_signal(barrier, 1, device_id=device, device_id_type=MESH)

    signal({"ctx": ctx_of(z, y, 1 - c)})
    signal({"ctx": ctx_of(z, 1 - y, c)})
    if across_x:
        signal({"wa": 1 - lax.axis_index("wa")})
    pl.when(z > 0)(lambda: signal({"ctx": ctx_of(z - 1, y, c)}))
    pl.when(z < depth - 1)(lambda: signal({"ctx": ctx_of(z + 1, y, c)}))
    ends = (z > 0).astype(jnp.int32) + (z < depth - 1).astype(jnp.int32)
    pl.semaphore_wait(barrier, (3 if across_x else 2) + ends)


def remote(source, target_ref, sems, at, device):
    return pltpu.make_async_remote_copy(
        src_ref=source,
        dst_ref=target_ref,
        send_sem=sems.at[(0,) + at],
        recv_sem=sems.at[(1,) + at],
        device_id=device,
        device_id_type=MESH,
    )


def each(step, act):
    z, _, _, depth = chip_place()
    if step == 0:
        act(z)
    else:
        pl.when(z + step < depth)(lambda: act(z + step))
        pl.when(z - step >= 0)(lambda: act(z - step))


def nearest(k):
    z, _, _, depth = chip_place()
    low = jnp.minimum(z, depth - 1 - z)
    step = (k + 1) // 2
    place = jnp.where(k > 2 * low, k, jnp.where(lax.rem(k, 2) == 1, low - step, low + step))
    return jnp.where(z == low, place, depth - 1 - place)


class Gather:
    def __init__(self, out, rows, sems, part=0, parts=1):
        self.out, self.block, self.rows = out, rows, rows // parts
        self.first = part * self.rows
        self.z_sems, self.y_sems, self.c_sems = sems
        self.z, self.y, self.c, self.depth = chip_place()

    @staticmethod
    def sems(depth):
        return [
            pltpu.SemaphoreType.DMA((2, 2, depth)),
            pltpu.SemaphoreType.DMA((2, depth)),
            pltpu.SemaphoreType.DMA((2, 2 * depth)),
        ]

    def slot(self, z, y, c):
        start = ctx_of(z, y, c) * self.block + self.first
        return self.out.at[pl.ds(pl.multiple_of(start, 16), self.rows)]

    def own(self):
        return self.slot(self.z, self.y, self.c)

    def on_z(self, way, of_z, source=None):
        goal = jnp.minimum(self.z + 1, self.depth - 1) if way == 0 else jnp.maximum(self.z - 1, 0)
        block = self.slot(of_z, self.y, self.c)
        target = {"ctx": ctx_of(goal, self.y, self.c)}
        return remote(block if source is None else source, block, self.z_sems, (way, of_z), target)

    def on_y(self, of_z, mine=True, source=None):
        block = self.slot(of_z, self.y if mine else 1 - self.y, self.c)
        target = {"ctx": ctx_of(self.z, 1 - self.y, self.c)}
        return remote(block if source is None else source, block, self.y_sems, (of_z,), target)

    def on_core(self, of_z, of_y, mine=True, source=None):
        block = self.slot(of_z, of_y, self.c if mine else 1 - self.c)
        target = {"ctx": ctx_of(self.z, self.y, 1 - self.c)}
        at = (of_z * 2 + of_y,)
        return remote(block if source is None else source, block, self.c_sems, at, target)

    def start(self, source=None):
        z, depth = self.z, self.depth
        if source is not None:
            source = source.at[pl.ds(self.first, self.rows)]
        pl.when(z < depth - 1)(lambda: self.on_z(0, z, source).start())
        pl.when(z > 0)(lambda: self.on_z(1, z, source).start())
        self.on_y(z, source=source).start()
        self.on_core(z, self.y, source=source).start()

    def along_z(self, step):
        z, depth = self.z, self.depth

        def from_side(way, of_z, more):
            self.on_z(way, of_z).wait_recv()
            pl.when(more)(lambda: self.on_z(way, of_z).start())
            self.on_y(of_z).start()
            self.on_core(of_z, self.y).start()

        pl.when(z - step >= 0)(lambda: from_side(0, z - step, z < depth - 1))
        pl.when(z + step < depth)(lambda: from_side(1, z + step, z > 0))

    def along_y(self, step):
        def across(of_z):
            self.on_y(of_z, mine=False).wait_recv()
            self.on_core(of_z, 1 - self.y).start()

        each(step, across)

    def take_core(self, of_z):
        for of_y in range(2):
            self.on_core(of_z, of_y, mine=False).wait_recv()

    def finish(self, *taken):
        z, depth = self.z, self.depth
        for of_z in range(depth):
            pl.when((z < depth - 1) & (of_z <= z))(lambda: self.on_z(0, of_z).wait_send())
            pl.when((z > 0) & (of_z >= z))(lambda: self.on_z(1, of_z).wait_send())
            self.on_y(of_z).wait_send()
            for of_y in range(2):
                self.on_core(of_z, of_y).wait_send()
            open_still = of_z >= 0
            for one in taken:
                open_still = (of_z != one) & open_still
            pl.when(open_still)(lambda: self.take_core(of_z))


class Several:
    def __init__(self, members):
        self.members = members

    def __getattr__(self, name):
        def every(*given, **named):
            for member in self.members:
                getattr(member, name)(*given, **named)

        return every


def gather_parts(out, rows, sems, parts):
    return Several(
        [Gather(out, rows, sems[3 * i : 3 * i + 3], i, parts) for i in range(parts)]
    )


def follow(gather):
    depth = chip_place()[3]
    gather.along_z(1)
    for step in range(depth):
        if step >= 1 and step + 1 < depth:
            gather.along_z(step + 1)
        gather.along_y(step)
    gather.finish()


def add_into(target, terms, rows):
    some = 32 if rows % 32 == 0 else 48 if rows % 48 == 0 else 16

    @pl.loop(0, rows // some)
    def _(turn):
        at = pl.ds(pl.multiple_of(turn * some, 16), some)
        total = terms[0][at, :].astype(jnp.float32)
        for term in terms[1:]:
            total = total + term[at, :].astype(jnp.float32)
        target[at, :] = total.astype(target.dtype)


class Scatter:
    def __init__(self, part, scratch, sums=None, piece=0, pieces=1):
        self.part = part
        self.from_core, self.totals, self.from_y, self.from_z = scratch[:4]
        self.sums = self.totals if sums is None else sums
        self.c_sems, self.y_sems, self.z_sems = scratch[4:]
        self.block = self.totals.shape[1]
        self.rows = self.block // pieces
        self.first = piece * self.rows
        self.z, self.y, self.c, self.depth = chip_place()

    @staticmethod
    def sems(depth):
        return [
            pltpu.SemaphoreType.DMA((2, 2 * depth)),
            pltpu.SemaphoreType.DMA((2, depth)),
            pltpu.SemaphoreType.DMA((2, 2, depth)),
        ]

    @staticmethod
    def scratch(depth, rows, columns, pieces=1):
        return [
            pltpu.VMEM((2 * depth, rows, columns), jnp.bfloat16),
            pltpu.VMEM((2 * depth, rows, columns), jnp.bfloat16),
            pltpu.VMEM((depth, rows, columns), jnp.bfloat16),
            pltpu.VMEM((depth + 1, rows, columns), jnp.bfloat16),
        ] + Scatter.sems(depth) * pieces

    def of(self, ref, place):
        return ref.at[place, pl.ds(self.first, self.rows)]

    def split(self):
        return len(self.part.shape) == 3

    def share(self, chip, c):
        start = (chip * 2 + c) * self.block + self.first
        return self.part.at[pl.ds(pl.multiple_of(start, 16), self.rows)]

    def on_core(self, chip):
        target = {"ctx": ctx_of(self.z, self.y, 1 - self.c)}
        source = self.of(self.part, chip) if self.split() else self.share(chip, 1 - self.c)
        return remote(source, self.of(self.from_core, chip), self.c_sems, (chip,), target)

    def send_core(self, chip):
        self.on_core(chip).start()

    def send_y(self, of_z):
        self.on_y(of_z).start()

    def on_y(self, of_z):
        target = {"ctx": ctx_of(self.z, 1 - self.y, self.c)}
        source = self.of(self.sums, of_z * 2 + 1 - self.y)
        return remote(source, self.of(self.from_y, of_z), self.y_sems, (of_z,), target)

    def on_z(self, way, of_z):
        goal = jnp.minimum(self.z + 1, self.depth - 1) if way == 0 else jnp.maximum(self.z - 1, 0)
        place = of_z if way == 0 else jnp.where(of_z == goal, self.depth, of_z)
        source = self.of(self.totals, of_z * 2 + self.y)
        target = {"ctx": ctx_of(goal, self.y, self.c)}
        return remote(source, self.of(self.from_z, place), self.z_sems, (way, of_z), target)

    def start(self):
        def send(of_z):
            self.on_core(of_z * 2 + 1 - self.y).start()
            self.on_core(of_z * 2 + self.y).start()

        for step in range(self.depth - 1, -1, -1):
            each(step, send)

    def add_chip(self, of_z, other, send=True):
        chip = of_z * 2 + (1 - self.y if other else self.y)
        self.on_core(chip).wait_recv()
        total = self.of(self.sums, chip)
        own = total if self.split() else self.share(chip, self.c)
        add_into(total, (own, self.of(self.from_core, chip)), self.rows)
        if other and send:
            self.on_y(of_z).start()

    def add_cores(self, step):
        def add(of_z):
            self.add_chip(of_z, True)
            self.add_chip(of_z, False)

        each(step, add)

    def add_y_of(self, of_z):
        z, depth = self.z, self.depth
        self.on_y(of_z).wait_recv()
        place = of_z * 2 + self.y
        total, own = self.of(self.totals, place), self.of(self.sums, place)
        other = self.of(self.from_y, of_z)
        upward, downward = (of_z > z) & (z > 0), (of_z < z) & (z < depth - 1)
        pl.when(upward)(lambda: self.on_z(0, of_z).wait_recv())
        pl.when(downward)(lambda: self.on_z(1, of_z).wait_recv())

        @pl.when(upward | downward)
        def _():
            add_into(total, (own, other, self.of(self.from_z, of_z)), self.rows)

        @pl.when(jnp.logical_not(upward | downward))
        def _():
            add_into(total, (own, other), self.rows)

        pl.when(of_z > z)(lambda: self.on_z(0, of_z).start())
        pl.when(of_z < z)(lambda: self.on_z(1, of_z).start())

    def add_y(self, step):
        each(step, self.add_y_of)

    def last(self, result):
        z, depth = self.z, self.depth
        own = self.of(self.totals, z * 2 + self.y)
        low, high = self.of(self.from_z, z), self.of(self.from_z, depth)
        result = result.at[pl.ds(self.first, self.rows)]
        pl.when(z > 0)(lambda: self.on_z(0, z).wait_recv())
        pl.when(z < depth - 1)(lambda: self.on_z(1, z).wait_recv())
        inside = (z > 0) & (z < depth - 1)
        pl.when(inside)(lambda: add_into(result, (own, low, high), self.rows))
        pl.when(z == 0)(lambda: add_into(result, (own, high), self.rows))
        pl.when(z == depth - 1)(lambda: add_into(result, (own, low), self.rows))

    def finish(self, cores=True):
        for of_z in range(self.depth):
            self.on_y(of_z).wait_send()
            if cores:
                self.on_core(of_z * 2).wait_send()
                self.on_core(of_z * 2 + 1).wait_send()
            pl.when(of_z > self.z)(lambda: self.on_z(0, of_z).wait_send())
            pl.when(of_z < self.z)(lambda: self.on_z(1, of_z).wait_send())


def scatter_parts(part, scratch, pieces, sums=None):
    arrays, sems = tuple(scratch[:4]), tuple(scratch[4:])
    return Several(
        [
            Scatter(part, arrays + sems[3 * i : 3 * i + 3], sums, i, pieces)
            for i in range(pieces)
        ]
    )


def call(kernel, out, scratch, number, name, *operands, outside=(), outside_out=(), late=()):
    many = isinstance(out, (tuple, list))
    count, results = len(operands), len(out) if many else 1
    late = tuple(late)

    def spec(position, far):
        return pl.BlockSpec(memory_space=pl.ANY if position in far else pltpu.VMEM)

    def with_late(*refs):
        near, sems = refs[-len(late) - 1 : -1], refs[-1]
        copies = {
            i: pltpu.make_async_copy(refs[i], near[k], sems.at[k]) for k, i in enumerate(late)
        }
        for copy in copies.values():
            copy.start()
        held = [near[late.index(i)] if i in late else refs[i] for i in range(count)]

        def arrive(*which):
            for i in which:
                copies[i].wait()

        kernel(arrive, *held, *refs[count : -len(late) - 1])

    if late:
        scratch = list(scratch) + [pltpu.VMEM(operands[i].shape, operands[i].dtype) for i in late]
        scratch.append(pltpu.SemaphoreType.DMA((len(late),)))
    far = tuple(outside) + late
    out_specs = [spec(i, outside_out) for i in range(results)]
    return pl.pallas_call(
        with_late if late else kernel,
        out_shape=out,
        in_specs=[spec(i, far) for i in range(count)],
        out_specs=out_specs if many else out_specs[0],
        scratch_shapes=scratch,
        compiler_params=pltpu.CompilerParams(
            collective_id=number,
            has_side_effects=number is not None,
            vmem_limit_bytes=VMEM_LIMIT,
        ),
        name=name,
    )(*operands)


class Relay:
    def __init__(self, source, out, sems, parts=1, paired=False):
        self.source, self.out, self.sems, self.parts = source, out, sems, parts
        self.paired = paired
        self.z, self.y, self.c, _ = chip_place()
        self.odd = lax.rem(self.z, 2)
        self.rows = source.shape[0] // ((4 if paired else 2) * parts)

    @staticmethod
    def semaphores():
        return pltpu.SemaphoreType.DMA((2, 8))

    def block(self, ref, part, c, odd):
        place = (c * 2 + odd if self.paired else c) * self.parts + part
        return ref.at[pl.ds(pl.multiple_of(place * self.rows, 16), self.rows)]

    def on_x(self, part):
        source = self.block(self.source, part, self.c, self.odd)
        target = self.block(self.out, part, self.c, self.odd)
        return remote(source, target, self.sems, (part,), {"wa": 1 - lax.axis_index("wa")})

    def on_core(self, part, c, other_z=False):
        block = self.block(self.out, part, c, 1 - self.odd if other_z else self.odd)
        at = ((4 if other_z else 2) + part,)
        return remote(block, block, self.sems, at, {"ctx": ctx_of(self.z, self.y, 1 - self.c)})

    def on_pair(self, part, mine=True):
        block = self.block(self.out, part, self.c, self.odd if mine else 1 - self.odd)
        target = {"ctx": ctx_of(self.z + 1 - 2 * self.odd, self.y, self.c)}
        return remote(block, block, self.sems, (6 + part,), target)

    def start(self):
        for part in range(self.parts):
            self.on_x(part).start()

    def pass_on(self, part=0):
        self.on_x(part).wait_recv()
        if self.paired:
            self.on_pair(part).start()
        self.on_core(part, self.c).start()

    def pass_on_pair(self, part):
        self.on_pair(part, mine=False).wait_recv()
        self.on_core(part, self.c, other_z=True).start()

    def finish(self):
        for part in range(self.parts):
            self.on_x(part).wait_send()
            self.on_core(part, self.c).wait_send()
            self.on_core(part, 1 - self.c).wait_recv()
            if self.paired:
                self.on_pair(part).wait_send()
                self.on_core(part, self.c, other_z=True).wait_send()
                self.on_core(part, 1 - self.c, other_z=True).wait_recv()


def rows_by_rows(left, right):
    return lax.dot_general(
        left, right, (((1,), (1,)), ((), ())), preferred_element_type=jnp.float32
    )


def columns_by_columns(left, right):
    return lax.dot_general(
        left, right, (((0,), (0,)), ((), ())), preferred_element_type=jnp.float32
    )


def down(row):
    return jnp.transpose(jnp.broadcast_to(row.astype(jnp.float32), (128, 128)))


def allowed_bias(doc_row, tokens):
    keys, me = doc_row.shape[1], lax.axis_index("ctx")
    own = down(doc_row[:, pl.ds(pl.multiple_of(me * tokens, 128), tokens)])[:, :1]
    key_block = lax.broadcasted_iota(jnp.int32, (tokens, keys), 1) // BLOCK
    same = doc_row[...].astype(jnp.float32) == own
    return jnp.where(same & (key_block <= me * tokens // BLOCK), 0.0, NEGATIVE)


def chosen_by(routes, lanes, experts):
    numbers = lax.rem(lanes, experts).astype(jnp.float32)
    found = down(routes[:1]) == numbers
    for k in range(1, routes.shape[0]):
        found = found | (down(routes[k : k + 1]) == numbers)
    return found & (lanes < 2 * experts)


def side_columns(own):
    side = lax.axis_index("wa")
    return pl.ds(pl.multiple_of((side if own else 1 - side) * (D // 2), 128), D // 2)


def turned(values, cosine, sine):
    heads = []
    for head in range(values.shape[1] // HEAD_DIM):
        one = values[:, head * HEAD_DIM : (head + 1) * HEAD_DIM]
        heads.append(one * cosine + pltpu.roll(one, HEAD_DIM // 2, axis=1) * sine)
    return jnp.concatenate(heads, axis=1)


def normed(values, gain_vec):
    return values * lax.rsqrt(jnp.mean(values * values, axis=-1, keepdims=True) + EPSILON) * gain_vec


def fill_small(full, small, small_there):
    full[:, side_columns(True)] = small[...].astype(jnp.float32)
    full[:, side_columns(False)] = small_there[...].astype(jnp.float32)


def router_block(full, experts):
    rows = full[:experts]
    spare = jnp.zeros((128 - 2 * experts, rows.shape[1]), jnp.float32)
    return jnp.concatenate([rows, rows, spare], axis=0).astype(jnp.bfloat16)


def attend(
    x, d_out, small, w_query, w_keyval, w_out_attn, w_out, angles, doc_row, routes, experts
):
    count, tokens, features = lax.axis_size("ctx"), x.shape[0], x.shape[1]
    depth, length = count // 4, count * tokens
    kv_columns = w_keyval.shape[1]

    def kernel(
        arrive, x_ref, small_ref, query_own, keyval_own, attn_own, d_out_far, query_far,
        keyval_far, attn_far, out_far, cosine_ref, sine_ref, doc_row_ref, routes_ref,
        query, keyval, level, mixed, hidden, mixed_low, middle, send, gates_out, query_other,
        keyval_other, attn_other, small_there, d_out_all, out_other,
        full, stacked, bias, query_sems, keyval_sems, attn_sems, small_sems, own_sem, *sems,
    ):
        gather = gather_parts(keyval, tokens, sems[:6], 2)
        spread = gather_parts(d_out_all, tokens, sems[6:], 2)
        query_relay = Relay(query_far, query_other, query_sems, parts=2)
        keyval_relay = Relay(keyval_far, keyval_other, keyval_sems)
        attn = Relay(attn_far, attn_other, attn_sems, parts=2, paired=True)
        partner = {"wa": 1 - lax.axis_index("wa")}
        swap = remote(small_ref, small_there, small_sems, (0,), partner)
        swap_out = remote(out_far, out_other, small_sems, (1,), partner)
        keep = pltpu.make_async_copy(
            d_out_far, Gather(d_out_all, tokens, sems[6:9]).own(), own_sem.at[0]
        )
        keep.start()
        greet(across_x=True)
        swap.start()
        keyval_relay.start()
        query_relay.start()
        attn.start()
        swap_out.start()
        spread.start(d_out_far)
        swap.wait()
        fill_small(full, small_ref, small_there)
        residual = x_ref[...].astype(jnp.float32)
        hidden[...] = normed(residual, full[experts : experts + 1]).astype(jnp.bfloat16)
        own, other = hidden[:, side_columns(True)], hidden[:, side_columns(False)]
        cosine, sine = cosine_ref[...], sine_ref[...]

        def onto(matrix, matrix_other):
            return jnp.dot(own, matrix[...], preferred_element_type=jnp.float32) + jnp.dot(
                other, matrix_other[...], preferred_element_type=jnp.float32
            )

        bias[...] = allowed_bias(doc_row_ref, tokens)
        spread.along_z(1)
        spread.along_y(0)
        keyval_relay.pass_on()
        keyval_relay.finish()
        arrive(3)
        pre = onto(keyval_own, keyval_other)
        keys = turned(pre[:, : kv_columns // 2], cosine, sine)
        block = jnp.concatenate([keys, pre[:, kv_columns // 2 :]], axis=1)
        Gather(keyval, tokens, sems[:3]).own()[...] = block.astype(jnp.bfloat16)
        spread.along_z(2)
        spread.along_y(1)
        query_relay.pass_on(0)
        spread.along_z(3)
        gather.start()
        gather.along_z(1)
        spread.along_y(2)
        gather.along_y(0)
        gather.along_z(2)
        query_relay.pass_on(1)
        spread.along_y(3)
        gather.along_y(1)
        gather.along_z(3)
        query_relay.finish()
        arrive(2)
        query[...] = turned(onto(query_own, query_other), cosine, sine).astype(jnp.bfloat16)
        for head in range(HEADS):
            rows = slice(head * tokens, (head + 1) * tokens)
            stacked[rows, :] = query[:, head * 128 : (head + 1) * 128]
        attn.pass_on(0)
        gather.along_y(2)
        gather.along_y(3)
        gather.finish()

        @pl.loop(0, HEADS // 2)
        def _(pair):
            rows = pl.ds(pl.multiple_of(pair * 2 * tokens, 128), 2 * tokens)
            kind = pair // (HEADS // KV_HEADS // 2)
            key_part = keyval[:, pl.ds(pl.multiple_of(kind * 128, 128), 128)]
            val_part = keyval[:, pl.ds(pl.multiple_of(kind * 128 + 256, 128), 128)]
            scores = rows_by_rows(stacked[rows, :], key_part) * HEAD_DIM**-0.5
            scores = (scores.reshape(2, tokens, -1) + bias[...][None]).reshape(scores.shape)
            top = jnp.max(scores, axis=-1, keepdims=True)
            weights = jnp.exp(scores - top)
            total = jnp.sum(weights, axis=-1, keepdims=True)
            probs = (weights * (1 / total)).astype(jnp.bfloat16)
            mixture = jnp.dot(probs, val_part, preferred_element_type=jnp.float32)
            for part in range(2):
                columns = pl.ds(pl.multiple_of((pair * 2 + part) * 128, 128), 128)
                mixed[:, columns] = mixture[part * tokens : (part + 1) * tokens]
            column = jnp.broadcast_to(top + jnp.log(total), (2 * tokens, 128))
            level[pl.ds(pair, 1), :] = jnp.transpose(column)[:1]
            pl.when(pair == 1)(lambda: attn.pass_on(1))
            pl.when(pair == 4)(lambda: attn.pass_on_pair(0))

        mixed_low[...] = mixed[...].astype(jnp.bfloat16)
        attn.pass_on_pair(1)
        own, other = mixed_low[:, side_columns(True)], mixed_low[:, side_columns(False)]
        arrive(4)
        attn.finish()
        middle[...] = residual + onto(attn_own, attn_other)
        hidden_two = normed(middle[...], full[experts + 1 : experts + 2]).astype(jnp.bfloat16)
        send[:, :features] = hidden_two
        logits = rows_by_rows(hidden_two, router_block(full, experts))
        lane = lax.broadcasted_iota(jnp.int32, logits.shape, 1)
        masked = jnp.where(chosen_by(routes_ref[...], lane, experts), logits, NEGATIVE)
        weights = jnp.exp(masked - jnp.max(masked, axis=1, keepdims=True))
        total = jnp.sum(jnp.where(lane < experts, weights, 0.0), axis=1, keepdims=True)
        gates = weights / total
        high = gates.astype(jnp.bfloat16).astype(jnp.float32)
        carried = jnp.where(lane < experts, high, jnp.where(lane < 2 * experts, gates - high, 0.0))
        send[:, features:] = carried.astype(jnp.bfloat16)
        gates_out[...] = jnp.where(lane < experts, gates, 0.0)
        spread.finish()
        keep.wait()
        swap_out.wait()

    def shape(rows, columns, kind=jnp.bfloat16):
        return jax.ShapeDtypeStruct((rows, columns), kind)

    wide = features + 128
    out = [
        shape(tokens, features), shape(length, kv_columns), shape(8, 2 * tokens, jnp.float32),
        shape(tokens, features, jnp.float32), shape(tokens, features), shape(tokens, features),
        shape(tokens, features, jnp.float32), shape(tokens, wide), shape(tokens, 128, jnp.float32),
        shape(*w_query.shape), shape(*w_keyval.shape), shape(*w_out_attn.shape),
        shape(*small.shape), shape(length, features), shape(*w_out.shape),
    ]
    scratch = [
        pltpu.VMEM((small.shape[0], features), jnp.float32),
        pltpu.VMEM((HEADS * tokens, HEAD_DIM), jnp.bfloat16),
        pltpu.VMEM((tokens, length), jnp.float32),
        Relay.semaphores(),
        Relay.semaphores(),
        Relay.semaphores(),
        pltpu.SemaphoreType.DMA((2, 2)),
        pltpu.SemaphoreType.DMA((1,)),
    ] + Gather.sems(depth) * 4
    return call(
        kernel, out, scratch, 2, "attend",
        x, small, w_query, w_keyval, w_out_attn, d_out, w_query, w_keyval, w_out_attn, w_out,
        *angles, doc_row, routes, outside=(5, 6, 7, 8, 9), outside_out=(13, 14), late=(3, 2, 4),
    )


def norm_back(values, gain_vec, grad):
    scale = lax.rsqrt(jnp.mean(values * values, axis=-1, keepdims=True) + EPSILON)
    through = jnp.mean(gain_vec * grad * values, axis=-1, keepdims=True)
    back = scale * gain_vec * grad - values * (scale * scale * scale * through)
    return back, jnp.sum(grad * values * scale, axis=0, keepdims=True)


def attend_back(
    returned, gates, small, small_there, middle, d_out, send, attn_own, attn_other, query, keyval,
    angles, doc_row, level, mixed, hidden, mixed_low, results, experts,
):
    count, tokens, features = lax.axis_size("ctx"), query.shape[0], query.shape[1]
    depth, length, kv_columns = count // 4, keyval.shape[0], keyval.shape[1]

    def kernel(
        arrive, returned_ref, gates_ref, small_ref, small_there_ref, middle_ref, d_out_ref, send_ref,
        attn_own_ref, attn_other_ref, query_ref, keyval_ref, cosine_ref, sine_ref, doc_row_ref,
        level_ref, mixed_ref, hidden_ref, mixed_low_ref, results_ref,
        output, grad_middle, grad_middle_low, grad_middle_there, grad_query, grad_query_there,
        grad_keyval, grad_keyval_there, small_grads, hidden_own, hidden_there, mixed_own,
        mixed_there,
        full, grad_mixed, turned_query, own_keyval, result_sum, stacked, grads, bias, delta, total,
        part, x_sems, *scratch,
    ):
        result = scatter_parts(
            None, (None,) + tuple(scratch[:3]) + tuple(scratch[3:9]), 2, results_ref
        )
        keyval_sum = scatter_parts(part, scratch[9:], 2)
        partner = {"wa": 1 - lax.axis_index("wa")}
        swaps = [
            remote(source, target, x_sems, (i,), partner)
            for i, (source, target) in enumerate(
                [(grad_middle_low, grad_middle_there), (grad_query, grad_query_there),
                 (grad_keyval, grad_keyval_there),
                 (hidden_ref.at[:, side_columns(False)], hidden_there),
                 (mixed_low_ref.at[:, side_columns(False)], mixed_there)]
            )
        ]
        greet(across_x=True)
        arrive(18)
        for k in range(depth - 1, 0, -1):
            result.send_y(nearest(k))
        swaps[3].start()
        swaps[4].start()
        hidden_own[...] = hidden_ref[:, side_columns(True)]
        mixed_own[...] = mixed_low_ref[:, side_columns(True)]
        fill_small(full, small_ref, small_there_ref)
        arrive(0, 4, 5, 6)
        lane = lax.broadcasted_iota(jnp.int32, (tokens, 128), 1)
        gates = gates_ref[...]
        grad_gates = jnp.where(lane < experts, returned_ref[:, features:], 0.0)
        inner = jnp.sum(gates * grad_gates, axis=1, keepdims=True)
        grad_logits = (gates * (grad_gates - inner)).astype(jnp.bfloat16)
        z = chip_place()[0]
        at_end = (z == 0) | (z == depth - 1)
        within = jnp.logical_not(at_end)
        grad_two = returned_ref[:, :features] + jnp.dot(
            grad_logits, router_block(full, experts), preferred_element_type=jnp.float32
        )
        grad_router = columns_by_columns(grad_logits, send_ref[:, :features])
        back, grad_gain = norm_back(middle_ref[...], full[experts + 1 : experts + 2], grad_two)
        grad_middle[...] = d_out_ref[...].astype(jnp.float32) + back
        grad_middle_low[...] = grad_middle[...].astype(jnp.bfloat16)
        swaps[0].start()
        small_grads[:experts] = grad_router[:experts]
        row = lax.broadcasted_iota(jnp.int32, (small_grads.shape[0] - experts, 1), 0)
        small_grads[experts:] = jnp.where(row == 1, grad_gain, 0.0)
        arrive(7, 8)
        grad_mixed[:, side_columns(True)] = rows_by_rows(
            grad_middle_low[...], attn_own_ref[...]
        ).astype(jnp.bfloat16)
        grad_mixed[:, side_columns(False)] = rows_by_rows(
            grad_middle_low[...], attn_other_ref[...]
        ).astype(jnp.bfloat16)
        allowed = jnp.transpose(allowed_bias(doc_row_ref, tokens))
        bias[:, :tokens] = allowed
        bias[:, tokens:] = allowed
        total[...] = jnp.zeros_like(total)
        arrive(9, 10, 15)
        for head in range(HEADS):
            rows = slice(head * tokens, (head + 1) * tokens)
            columns = slice(head * 128, head * 128 + 128)
            stacked[rows, :] = query_ref[:, columns]
            grads[rows, :] = grad_mixed[:, columns]
            product = grad_mixed[:, columns].astype(jnp.float32) * mixed_ref[:, columns]
            delta[head // 2 : head // 2 + 1, (head % 2) * tokens : (head % 2 + 1) * tokens] = (
                jnp.sum(jnp.transpose(product), axis=0, keepdims=True)
            )

        @pl.loop(0, HEADS // 2)
        def _(pair):
            rows = pl.ds(pl.multiple_of(pair * 2 * tokens, 128), 2 * tokens)
            kind = pair // (HEADS // KV_HEADS // 2)
            key_columns = pl.ds(pl.multiple_of(kind * 128, 128), 128)
            val_columns = pl.ds(pl.multiple_of(kind * 128 + 256, 128), 128)
            key_part, val_part = keyval_ref[:, key_columns], keyval_ref[:, val_columns]
            own, grad = stacked[rows, :], grads[rows, :]
            pair_row = pl.ds(pair, 1)
            scores = rows_by_rows(key_part, own) * HEAD_DIM**-0.5 + bias[...]
            probs = jnp.exp(scores - level_ref[pair_row, :])
            grad_probs = rows_by_rows(val_part, grad)
            grad_scores = (probs * (grad_probs - delta[pair_row, :])).astype(jnp.bfloat16)
            own_grad = jnp.transpose(columns_by_columns(key_part, grad_scores))
            for half in range(2):
                columns = pl.ds(pl.multiple_of((pair * 2 + half) * 128, 128), 128)
                turned_query[:, columns] = (
                    own_grad[half * tokens : (half + 1) * tokens] * HEAD_DIM**-0.5
                )
            total[:, key_columns] += (
                jnp.dot(grad_scores, own, preferred_element_type=jnp.float32) * HEAD_DIM**-0.5
            )
            total[:, val_columns] += jnp.dot(
                probs.astype(jnp.bfloat16), grad, preferred_element_type=jnp.float32
            )
            pl.when((pair == HEADS // 4) & at_end)(lambda: result.add_y_of(nearest(depth - 1)))

        part[...] = total[...].astype(jnp.bfloat16)
        keyval_sum.start()
        cosine, sine = cosine_ref[...], -sine_ref[...]
        grad_query[...] = turned(turned_query[...], cosine, sine).astype(jnp.bfloat16)
        swaps[1].start()
        steps = range(depth - 1, -1, -1)
        for step in steps:
            keyval_sum.add_cores(step)
        result.send_y(nearest(0))
        pl.when(within)(lambda: result.add_y_of(nearest(depth - 1)))
        for k in range(depth - 2, 0, -1):
            result.add_y_of(nearest(k))
        for step in steps:
            keyval_sum.add_y(step)
        keyval_sum.last(own_keyval)
        keys = turned(own_keyval[:, : kv_columns // 2], cosine, sine)
        grad_keyval[...] = jnp.concatenate(
            [keys, own_keyval[:, kv_columns // 2 :]], axis=1
        ).astype(jnp.bfloat16)
        swaps[2].start()
        result.add_y_of(nearest(0))
        result.last(result_sum)
        output[...] = (middle_ref[...] + result_sum[...]).astype(jnp.bfloat16)
        keyval_sum.finish()
        result.finish(cores=False)
        for swap in swaps:
            swap.wait()

    def shape(like, kind=jnp.bfloat16):
        return jax.ShapeDtypeStruct(like, kind)

    rows, narrow = (tokens, features), (tokens, kv_columns)
    small_shape = (small.shape[0], features)
    out = [
        shape(rows), shape(rows, jnp.float32), shape(rows), shape(rows), shape(rows), shape(rows),
        shape(narrow), shape(narrow), shape(small_shape, jnp.float32),
    ] + [shape((tokens, features // 2))] * 4
    scratch = [
        pltpu.VMEM(small_shape, jnp.float32),
        pltpu.VMEM(rows, jnp.bfloat16),
        pltpu.VMEM(rows, jnp.float32),
        pltpu.VMEM(narrow, jnp.float32),
        pltpu.VMEM(rows, jnp.float32),
        pltpu.VMEM((HEADS * tokens, HEAD_DIM), jnp.bfloat16),
        pltpu.VMEM((HEADS * tokens, HEAD_DIM), jnp.bfloat16),
        pltpu.VMEM((length, 2 * tokens), jnp.float32),
        pltpu.VMEM((8, 2 * tokens), jnp.float32),
        pltpu.VMEM(keyval.shape, jnp.float32),
        pltpu.VMEM(keyval.shape, jnp.bfloat16),
        pltpu.SemaphoreType.DMA((2, 5)),
    ]
    wide = Scatter.scratch(depth, tokens, features)
    scratch += wide[1:4] + Scatter.sems(depth) * 2 + Scatter.scratch(depth, tokens, kv_columns, 2)
    return call(
        kernel, out, scratch, 4, "attend_back",
        returned, gates, small, small_there, middle, d_out, send, attn_own, attn_other, query,
        keyval, *angles, doc_row, level, mixed, hidden, mixed_low, results,
        late=(18, 0, 4, 5, 6, 7, 8, 9, 10, 15),
    )


def gate_unit(first, second):
    root, cube = math.sqrt(2 / math.pi), 0.044715
    square = first * first
    bend = jnp.tanh(root * first * (1 + cube * square))
    lift = 0.5 * (1 + bend)
    slope = lift + 0.5 * first * (1 - bend * bend) * root * (1 + 3 * cube * square)
    gelu = first * lift
    return gelu * second, slope * second, gelu


def run_experts(send, d_out_all, in_own, out_own, out_other, experts):
    count, tokens = lax.axis_size("ctx"), send.shape[0]
    depth, chips, length = count // 4, count // 2, count * tokens
    wide, features = send.shape[1], d_out_all.shape[1]
    quarter = out_own.shape[0]
    width = 2 * quarter

    def kernel(
        send_ref, d_out_far, in_own_ref, out_own_ref, out_other_ref,
        returned, results_far, grad_in_far, grad_in_other_far, grad_out_far, grad_out_other_far,
        hidden_all, grad_both, gated_hidden, other_part, other_result, result_from, result_sems,
        in_ref, out_ref, d_out_ref, x_sems, near_sem, results, grad_in, grad_in_other, grad_out,
        grad_out_other, far_sems, *scratch,
    ):
        gather = gather_parts(hidden_all, tokens, scratch[:6], 2)
        scatter = scatter_parts(other_part, scratch[6:], 2)
        chip_sums = scratch[7]
        z, y, c, _ = chip_place()
        expert = lax.axis_index("ctx") // 2
        lane = lax.broadcasted_iota(jnp.int32, (1, 128), 1)
        Gather(hidden_all, tokens, scratch[:3]).own()[...] = send_ref[...]
        partner = {"wa": 1 - lax.axis_index("wa")}
        stores = [
            pltpu.make_async_copy(source, target, far_sems.at[i])
            for i, (source, target) in enumerate(
                [(results, results_far), (grad_in, grad_in_far),
                 (grad_in_other, grad_in_other_far), (grad_out, grad_out_far),
                 (grad_out_other, grad_out_other_far)]
            )
        ]
        near = pltpu.make_async_copy(d_out_far, d_out_ref, near_sem.at[0])
        near.start()
        swaps = [
            remote(
                in_own_ref.at[pl.ds(part * quarter, quarter)],
                in_ref.at[pl.ds((2 * part + 1) * quarter, quarter)],
                x_sems,
                (part,),
                partner,
            )
            for part in range(2)
        ]
        greet(across_x=True)
        gather.start()
        for swap in swaps:
            swap.start()
        out_ref[:quarter] = out_own_ref[...]
        out_ref[quarter:] = out_other_ref[...]
        in_ref[:quarter] = in_own_ref[:quarter]
        in_ref[width : width + quarter] = in_own_ref[quarter:]
        def chip_rows(chip):
            return pl.ds(pl.multiple_of(chip * 2 * tokens, 16), 2 * tokens)

        def parted(values):
            low, high = values[:tokens], values[tokens:]
            return jnp.where(c == 0, low, high), jnp.where(c == 0, high, low)

        def backward(chip):
            rows = chip_rows(chip)
            carried = hidden_all[rows, features:].astype(jnp.float32)
            mine = (lane == expert) | (lane == expert + experts)
            gate = jnp.sum(jnp.where(mine, carried, 0.0), axis=1, keepdims=True)
            both = rows_by_rows(hidden_all[rows, :features], in_ref[...])
            hidden, by_first, by_second = gate_unit(both[:, :width], both[:, width:])
            gated_hidden[rows, :] = (hidden * gate).astype(jnp.bfloat16)
            grad_hidden = rows_by_rows(d_out_ref[rows, :], out_ref[...])
            grad_gate = jnp.sum(grad_hidden * hidden, axis=1, keepdims=True)
            grad_hidden = grad_hidden * gate
            grad_both[rows, :width] = (grad_hidden * by_first).astype(jnp.bfloat16)
            grad_both[rows, width:] = (grad_hidden * by_second).astype(jnp.bfloat16)
            own, other = parted(
                jnp.dot(grad_both[rows, :], in_ref[...], preferred_element_type=jnp.float32)
            )
            chip_sums[chip, :, :features] = own.astype(jnp.bfloat16)
            other_part[chip, :, :features] = other.astype(jnp.bfloat16)
            own, other = parted(jnp.where(lane == expert, grad_gate, 0.0))
            chip_sums[chip, :, features:] = own.astype(jnp.bfloat16)
            other_part[chip, :, features:] = other.astype(jnp.bfloat16)
            scatter.send_core(chip)

        gather.along_z(1)
        for step in range(2, depth):
            gather.along_y(step - 2)
            gather.along_z(step)
        near.wait()
        for swap in swaps:
            swap.wait()
        for of_z in (nearest(1), z):
            gather.take_core(of_z)
        backward(nearest(1) * 2 + 1 - y)
        backward(nearest(1) * 2 + y)
        scatter.add_chip(nearest(1), True)
        gather.along_y(depth - 2)
        backward(z * 2 + 1 - y)
        gather.along_y(depth - 1)
        backward(z * 2 + y)
        gather.finish(nearest(1), z)
        scatter.add_chip(nearest(1), False)

        @pl.loop(0, depth - 2)
        def _(turn):
            of_z = nearest(depth - 1 - turn)
            backward(of_z * 2 + 1 - y)
            pl.when(turn > 0)(lambda: scatter.add_chip(nearest(depth - turn), False))
            backward(of_z * 2 + y)
            scatter.add_chip(of_z, True)

        scatter.add_chip(nearest(2), False)
        scatter.add_chip(z, True)
        scatter.add_chip(nearest(0), False)
        scatter.add_y_of(nearest(depth - 1))

        def result_copy(chip):
            target = {"ctx": ctx_of(z, y, 1 - c)}
            return remote(
                other_result.at[chip], result_from.at[chip], result_sems, (chip,), target
            )

        @pl.loop(0, chips)
        def _(chip):
            result = jnp.dot(
                gated_hidden[chip_rows(chip), :], out_ref[...], preferred_element_type=jnp.float32
            )
            own, other = parted(result)
            results[chip] = own.astype(jnp.bfloat16)
            other_result[chip] = other.astype(jnp.bfloat16)
            result_copy(chip).start()

        scatter.add_y_of(nearest(depth - 2))

        @pl.loop(0, features // 512)
        def _(turn):
            at = pl.ds(pl.multiple_of(turn * 512, 512), 512)
            grad = columns_by_columns(gated_hidden[...], d_out_ref[:, at])
            grad_out[:, at] = grad[:quarter]
            grad_out_other[:, at] = grad[quarter:].astype(jnp.bfloat16)

        stores[3].start()
        stores[4].start()
        for k in range(depth - 3, 0, -1):
            scatter.add_y_of(nearest(k))

        @pl.loop(0, features // 512)
        def _(turn):
            at = pl.ds(pl.multiple_of(turn * 512, 512), 512)
            grad = columns_by_columns(grad_both[...], hidden_all[:, at])
            for part in range(2):
                rows = slice(part * quarter, (part + 1) * quarter)
                first = part * width
                grad_in[rows, at] = grad[first : first + quarter]
                grad_in_other[rows, at] = grad[first + quarter : first + width].astype(jnp.bfloat16)

        stores[1].start()
        stores[2].start()

        @pl.loop(0, chips)
        def _(chip):
            result_copy(chip).wait_recv()
            add_into(results.at[chip], (results.at[chip], result_from.at[chip]), tokens)

        stores[0].start()
        scatter.add_y_of(nearest(0))
        scatter.last(returned)
        scatter.finish()
        for chip in range(chips):
            result_copy(chip).wait_send()
        for store in stores:
            store.wait()

    block = (chips, tokens, features)
    out = [
        jax.ShapeDtypeStruct((tokens, wide), jnp.float32),
        jax.ShapeDtypeStruct(block, jnp.bfloat16),
        jax.ShapeDtypeStruct(in_own.shape, jnp.float32),
        jax.ShapeDtypeStruct(in_own.shape, jnp.bfloat16),
        jax.ShapeDtypeStruct(out_own.shape, jnp.float32),
        jax.ShapeDtypeStruct(out_own.shape, jnp.bfloat16),
    ]
    scratch = [
        pltpu.VMEM((length, wide), jnp.bfloat16),
        pltpu.VMEM((length, 2 * width), jnp.bfloat16),
        pltpu.VMEM((length, width), jnp.bfloat16),
        pltpu.VMEM((chips, tokens, wide), jnp.bfloat16),
        pltpu.VMEM(block, jnp.bfloat16),
        pltpu.VMEM(block, jnp.bfloat16),
        pltpu.SemaphoreType.DMA((2, chips)),
        pltpu.VMEM((2 * width, features), jnp.bfloat16),
        pltpu.VMEM((width, features), jnp.bfloat16),
        pltpu.VMEM(d_out_all.shape, jnp.bfloat16),
        pltpu.SemaphoreType.DMA((2, 2)),
        pltpu.SemaphoreType.DMA((1,)),
    ]
    scratch += [pltpu.VMEM(one.shape, one.dtype) for one in out[1:]]
    scratch.append(pltpu.SemaphoreType.DMA((5,)))
    scratch += Gather.sems(depth) * 2 + Scatter.scratch(depth, tokens, wide, 2)
    return call(
        kernel, out, scratch, 3, "experts", send, d_out_all, in_own, out_own, out_other, outside=(1,),
        outside_out=range(1, 6),
    )


def finish(
    x, grad_middle, small, small_there, small_grads, matrices, hidden, mixed, middle, query, keyval,
    expert_in, expert_out,
):
    count, tokens, half = lax.axis_size("ctx"), x.shape[0], x.shape[1] // 2
    depth, rows = count // 4, half // count
    widths = (middle[0].shape[1], query[0].shape[1], keyval[0].shape[1])
    experts = small.shape[0] // 2

    def kernel(
        arrive, x_ref, grad_middle_ref, small_ref, small_there_ref, small_grads_ref,
        query_own, query_other, keyval_own, keyval_other,
        hidden_ref, hidden_there, mixed_ref, mixed_there, middle_ref, middle_there,
        query_ref, query_there, keyval_ref, keyval_there, in_ref, out_ref,
        attn_sum, query_sum, keyval_sum, small_sum, grad_input, in_there, out_there,
        attn_part, query_part, keyval_part, pair, full, grad_one, small_mine, small_came, small_all,
        x_sems, *scratch,
    ):
        scatters, gathers = [], []
        parts, sums = (attn_part, query_part, keyval_part), (attn_sum, query_sum, keyval_sum)
        for part, total in zip(parts, sums):
            scatters.append(Scatter(part, scratch[:7]))
            gathers.append(Gather(total, rows, scratch[7:10]))
            scratch = scratch[10:]
        small_out = Gather(small_all, small_came.shape[0], scratch)
        (attn, query_, keyval_), (attn_out, query_out, keyval_out) = scatters, gathers
        partner = {"wa": 1 - lax.axis_index("wa")}
        swaps = [
            remote(source, target, x_sems, (i,), partner)
            for i, (source, target) in enumerate(
                [(small_mine.at[:, side_columns(False)], small_came), (in_ref, in_there),
                 (out_ref, out_there)]
            )
        ]
        steps = range(depth - 1, -1, -1)

        def products(left, left_there, right, right_there, part):
            pair[:tokens] = left[...]
            pair[tokens:] = left_there[...]

            @pl.loop(0, part.shape[1] // 512)
            def _(turn):
                at = pl.ds(pl.multiple_of(turn * 512, 512), 512)
                both = jnp.concatenate([right[:, at], right_there[:, at]], axis=0)
                part[:, at] = columns_by_columns(pair[...], both).astype(jnp.bfloat16)

        products(mixed_ref, mixed_there, middle_ref, middle_there, attn_part)
        greet(across_x=True)
        attn.start()
        products(hidden_ref, hidden_there, query_ref, query_there, query_part)
        for step in steps:
            attn.add_cores(step)
        query_.start()
        products(hidden_ref, hidden_there, keyval_ref, keyval_there, keyval_part)
        keyval_.start()
        for step in steps:
            query_.add_cores(step)
        attn.add_y(depth - 1)
        fill_small(full, small_ref, small_there_ref)
        arrive(0, 1, 5, 6, 7, 8)
        grad_one[:, side_columns(True)] = rows_by_rows(
            query_ref[...], query_own[...]
        ) + rows_by_rows(keyval_ref[...], keyval_own[...])
        attn.add_y(depth - 2)
        grad_one[:, side_columns(False)] = rows_by_rows(
            query_ref[...], query_other[...]
        ) + rows_by_rows(keyval_ref[...], keyval_other[...])
        back, grad_gain = norm_back(
            x_ref[...].astype(jnp.float32), full[experts : experts + 1], grad_one[...]
        )
        grad_input[...] = (grad_middle_ref[...] + back).astype(jnp.bfloat16)
        row = lax.broadcasted_iota(jnp.int32, (small_mine.shape[0], 1), 0)
        small_mine[...] = jnp.where(row == experts, grad_gain, small_grads_ref[...])
        swaps[0].start()
        for step in range(depth - 3, -1, -1):
            attn.add_y(step)
        for step in steps:
            keyval_.add_cores(step)
        attn.last(attn_out.own())
        attn_out.start()
        swaps[1].start()
        swaps[2].start()
        swaps[0].wait()
        small_out.own()[...] = (small_mine[:, side_columns(True)] + small_came[...]).astype(
            jnp.bfloat16
        )
        small_out.start()
        for step in steps:
            query_.add_y(step)
        attn_out.along_z(1)
        query_.last(query_out.own())
        query_out.start()
        attn_out.along_z(2)
        attn_out.along_y(0)
        small_out.along_z(1)
        for step in steps:
            keyval_.add_y(step)
        attn_out.along_z(3)
        attn_out.along_y(1)
        keyval_.last(keyval_out.own())
        keyval_out.start()
        query_out.along_z(1)
        small_out.along_z(2)
        attn_out.along_y(2)
        query_out.along_z(2)
        small_out.along_z(3)
        query_out.along_y(0)
        keyval_out.along_z(1)
        query_out.along_z(3)
        attn_out.along_y(3)
        keyval_out.along_z(2)
        query_out.along_y(1)
        keyval_out.along_z(3)
        query_out.along_y(2)
        small_out.along_y(0)
        keyval_out.along_y(0)
        small_out.along_y(1)
        query_out.along_y(3)
        keyval_out.along_y(1)
        small_out.along_y(2)
        keyval_out.along_y(2)
        small_out.along_y(3)
        keyval_out.along_y(3)
        for one in [small_out] + gathers + scatters:
            one.finish()
        small_rows = small_came.shape[0]
        total = small_all[:small_rows].astype(jnp.float32)
        for device in range(1, count):
            rows_of = slice(device * small_rows, (device + 1) * small_rows)
            total = total + small_all[rows_of].astype(jnp.float32)
        small_sum[...] = total
        swaps[1].wait()
        swaps[2].wait()

    small_shape = (small.shape[0], half)
    out = [jax.ShapeDtypeStruct((half, width), jnp.bfloat16) for width in widths]
    out += [
        jax.ShapeDtypeStruct(small_shape, jnp.float32),
        jax.ShapeDtypeStruct(x.shape, jnp.bfloat16),
        jax.ShapeDtypeStruct(expert_in.shape, expert_in.dtype),
        jax.ShapeDtypeStruct(expert_out.shape, expert_out.dtype),
    ]
    scratch = [pltpu.VMEM((half, width), jnp.bfloat16) for width in widths]
    scratch += [
        pltpu.VMEM((2 * tokens, half), jnp.bfloat16),
        pltpu.VMEM(small_grads.shape, jnp.float32),
        pltpu.VMEM(x.shape, jnp.float32),
        pltpu.VMEM(small_grads.shape, jnp.float32),
        pltpu.VMEM(small_shape, jnp.float32),
        pltpu.VMEM((count * small.shape[0], half), jnp.bfloat16),
        pltpu.SemaphoreType.DMA((2, 3)),
    ]
    for width in widths:
        scratch += Scatter.scratch(depth, rows, width) + Gather.sems(depth)
    scratch += Gather.sems(depth)
    return call(
        kernel, out, scratch, 1, "finish",
        x, grad_middle, small, small_there, small_grads, *matrices, *hidden, *mixed, *middle,
        *query, *keyval, expert_in, expert_out, outside=(19, 20), outside_out=(5, 6),
        late=(0, 1, 5, 6, 7, 8),
    )


def widen(query, keyval, attn, grad_in, in_there, grad_out, out_there):
    quarter, features = grad_out.shape
    steps = 4

    def kernel(*refs):
        query_ref, keyval_ref, attn_ref, in_ref, in_there_ref, out_ref, out_there_ref = refs[:7]
        query_out, keyval_out, attn_out, in_out, out_out = refs[7:]
        query_out[...] = query_ref[...].astype(jnp.float32)
        keyval_out[...] = keyval_ref[...].astype(jnp.float32)
        attn_out[...] = attn_ref[...].astype(jnp.float32)
        both = in_ref[...] + in_there_ref[...].astype(jnp.float32)
        in_out[...] = both
        out_out[0] = out_ref[...] + out_there_ref[...].astype(jnp.float32)

    def rows(values):
        return pl.BlockSpec((values.shape[0] // steps, values.shape[1]), lambda i: (i, 0))

    operands = (query, keyval, attn, grad_in, in_there, grad_out, out_there)
    return pl.pallas_call(
        kernel,
        grid=(steps,),
        out_shape=[
            jax.ShapeDtypeStruct(query.shape, jnp.float32),
            jax.ShapeDtypeStruct(keyval.shape, jnp.float32),
            jax.ShapeDtypeStruct(attn.shape, jnp.float32),
            jax.ShapeDtypeStruct(grad_in.shape, jnp.float32),
            jax.ShapeDtypeStruct((1, quarter, features), jnp.float32),
        ],
        in_specs=[rows(values) for values in operands],
        out_specs=[
            rows(query), rows(keyval), rows(attn),
            rows(grad_in),
            pl.BlockSpec((1, quarter // steps, features), lambda i: (0, i, 0)),
        ],
        compiler_params=pltpu.CompilerParams(vmem_limit_bytes=VMEM_LIMIT),
        name="widen",
    )(*operands)


def gathered_body(
    layer_input, seq_ids, routes, gain_attn, w_query, w_keyval, w_out_attn, gain_ffn, router,
    w_in, w_out, d_out,
):
    me = lax.axis_index("ctx")
    tokens, experts = layer_input.shape[1], router.shape[1]
    x, grad_out = layer_input[0], d_out[0]
    small = jnp.concatenate(
        [router.T, gain_attn[None], gain_ffn[None], jnp.zeros((experts - 2, D // 2), jnp.bfloat16)]
    )
    turns = angle_table(me * tokens + jnp.arange(tokens, dtype=jnp.int32))[:, 0]
    cosine, sine = jnp.cos(turns), jnp.sin(turns)
    angles = (
        jnp.concatenate([cosine, cosine], axis=1), jnp.concatenate([-sine, sine], axis=1)
    )
    in_own = jnp.swapaxes(w_in[0], 1, 2).reshape(-1, D)

    (
        query, keyval, level, mixed, hidden, mixed_low, middle, send, gates, w_query_there,
        w_keyval_there, w_out_attn_there, small_there, d_out_all, w_out_there,
    ) = attend(
        x, grad_out, small, w_query, w_keyval, w_out_attn, w_out[0], angles, seq_ids,
        routes[0].T, experts,
    )
    projections = (w_query, w_query_there, w_keyval, w_keyval_there)
    returned, results, grad_in, grad_in_other, grad_out_matrix, grad_out_other = run_experts(
        send, d_out_all, in_own, w_out[0], w_out_there, experts
    )
    (
        output, grad_middle, middle_low, middle_there, grad_query, query_there, grad_keyval,
        keyval_there, small_grads, *halves,
    ) = attend_back(
        returned, gates, small, small_there, middle, grad_out, send, w_out_attn, w_out_attn_there,
        query, keyval, angles, seq_ids, level, mixed, hidden, mixed_low, results, experts,
    )
    attn_sum, query_sum, keyval_sum, small_sum, grad_input, in_there, out_there = finish(
        x, grad_middle, small, small_there, small_grads, projections, halves[:2], halves[2:],
        (middle_low, middle_there), (grad_query, query_there),
        (grad_keyval, keyval_there), grad_in_other, grad_out_other,
    )
    query_sum, keyval_sum, attn_sum, grad_w_in, grad_w_out = widen(
        query_sum, keyval_sum, attn_sum, grad_in, in_there, grad_out_matrix, out_there
    )
    return (
        output[None],
        grad_input[None],
        small_sum[experts],
        query_sum,
        keyval_sum,
        attn_sum,
        small_sum[experts + 1],
        small_sum[:experts].T,
        jnp.swapaxes(grad_w_in.reshape(2, -1, D), 1, 2)[None],
        grad_w_out,
    )


def solution(mesh):
    in_specs = (
        P("wa", "ctx", None),
        P("wa", None),
        P("wa", "ctx", None),
        P("wa"),
        P("wa", None),
        P("wa", None),
        P("wa", None),
        P("wa"),
        P("wa", None),
        P("ctx", None, None, "wa"),
        P("ctx", "wa", None),
        P("wa", "ctx", None),
    )
    out_specs = (
        P("wa", "ctx", None),
        P("wa", "ctx", None),
        P("wa"),
        P("wa", None),
        P("wa", None),
        P("wa", None),
        P("wa"),
        P("wa", None),
        P("ctx", None, None, "wa"),
        P("ctx", "wa", None),
    )
    depth = mesh.shape["ctx"]
    body = gathered_body if depth == 16 else routed_body
    return jax.shard_map(body, mesh=mesh, in_specs=in_specs, out_specs=out_specs, check_vma=False)
```

```python
import functools
import math

import jax
import jax.numpy as jnp
from jax import lax
from jax.experimental import pallas as pl
from jax.experimental.pallas import tpu as pltpu
from jax.sharding import PartitionSpec as P

D = 1536
HEADS = 12
KV_HEADS = 2
HEAD_DIM = 128
TOP = 4
BLOCK = 256


EPSILON = 1e-06
THETA = 1000000.0
NEGATIVE = -1e30


def rms_scale(values, gain_vec):
    return (
        values * lax.rsqrt(jnp.mean(values * values, axis=-1, keepdims=True) + EPSILON) * gain_vec
    )


def rotate(values, angles):
    half_dim = values.shape[-1] // 2
    cosine = jnp.cos(angles)
    sine_part = jnp.sin(angles)
    first_half = values[..., :half_dim]
    second = values[..., half_dim:]
    return jnp.concatenate(
        [first_half * cosine - second * sine_part, second * cosine + first_half * sine_part],
        axis=-1,
    )


def angle_table(positions):
    half_dim = HEAD_DIM // 2
    frequency = THETA ** (-2.0 * jnp.arange(half_dim, dtype=jnp.float32) / HEAD_DIM)
    return (positions.astype(jnp.float32)[:, None] * frequency[None, :])[:, None, :]


def gated(stacked):
    return jax.nn.gelu(stacked[..., 0, :], approximate=True) * stacked[..., 1, :]


def over_keys(key_rows, running, advance):
    key_count = key_rows.shape[0]
    key_width = math.gcd(key_count, 512)

    def one_turn(state_now, block_index):
        key_offset = block_index * key_width
        key_part = lax.dynamic_slice_in_dim(key_rows, key_offset, key_width, 0)
        return (advance(state_now, key_part, key_offset), None)

    running, unused = lax.scan(
        one_turn, running, jnp.arange(key_count // key_width, dtype=jnp.int32)
    )
    return running


def routed_body(
    layer_input,
    seq_ids,
    routes,
    gain_attn,
    w_query,
    w_keyval,
    w_out_attn,
    gain_ffn,
    router,
    w_in,
    w_out,
    d_out,
):
    ctx_count = lax.axis_size("ctx")
    ctx_index = lax.axis_index("ctx")
    tokens = layer_input.shape[1]
    length = tokens * ctx_count
    experts_all = ctx_count // 2
    capacity = 2 * tokens * TOP // experts_all
    group = HEADS // KV_HEADS
    kv_width = KV_HEADS * HEAD_DIM
    row_count = group * tokens
    scale = HEAD_DIM ** (-0.5)
    gain_one, query_matrix, keyvalue_matrix, attention_matrix = (
        lax.all_gather(gain_attn, "wa", axis=0, tiled=True),
        lax.all_gather(w_query, "wa", axis=0, tiled=True),
        lax.all_gather(w_keyval, "wa", axis=0, tiled=True),
        lax.all_gather(w_out_attn, "wa", axis=0, tiled=True),
    )
    residual = layer_input[0].astype(jnp.float32)
    normed_one, norm_one_back = jax.vjp(rms_scale, residual, gain_one.astype(jnp.float32))
    hidden_first_norm = normed_one.astype(jnp.bfloat16)
    positions = ctx_index * tokens + jnp.arange(tokens, dtype=jnp.int32)
    angles = angle_table(positions)
    query_projected = jnp.dot(
        hidden_first_norm, query_matrix, preferred_element_type=jnp.float32
    ).reshape(tokens, HEADS, HEAD_DIM)
    keyvalue_projected = jnp.dot(
        hidden_first_norm, keyvalue_matrix, preferred_element_type=jnp.float32
    )
    key_pre = keyvalue_projected[:, :kv_width].reshape(tokens, KV_HEADS, HEAD_DIM)
    query_low = rotate(query_projected, angles).astype(jnp.bfloat16)
    key_low = rotate(key_pre, angles).astype(jnp.bfloat16)
    value_low = keyvalue_projected[:, kv_width:].astype(jnp.bfloat16)
    keyval_send = jnp.concatenate([key_low.reshape(tokens, kv_width), value_low], axis=1)
    query_rows = (
        query_low.reshape(tokens, KV_HEADS, group, HEAD_DIM)
        .transpose(1, 2, 0, 3)
        .reshape(KV_HEADS, row_count, HEAD_DIM)
    )
    doc_row = seq_ids[0]
    query_docs = lax.dynamic_slice_in_dim(doc_row, ctx_index * tokens, tokens, 0)
    query_blocks = positions // BLOCK

    def block_scores(key_part, first_key):
        key_count = key_part.shape[0]
        split_part = key_part.reshape(key_count, 2, KV_HEADS, HEAD_DIM)
        keys_here = split_part[:, 0]
        values_here = split_part[:, 1]
        scores = (
            jnp.einsum("hrd,nhd->hrn", query_rows, keys_here, preferred_element_type=jnp.float32)
            * scale
        )
        key_docs = lax.dynamic_slice_in_dim(doc_row, first_key, key_count, 0)
        key_blocks = (first_key + jnp.arange(key_count, dtype=jnp.int32)) // BLOCK
        allowed = (query_docs[:, None] == key_docs[None, :]) & (
            key_blocks[None, :] <= query_blocks[:, None]
        )
        allowed = jnp.broadcast_to(allowed[None], (group, tokens, key_count)).reshape(
            1, row_count, key_count
        )
        return (jnp.where(allowed, scores, NEGATIVE), allowed, keys_here, values_here)

    def probs_of(masked, allowed, largest, totals):
        return jnp.where(allowed, jnp.exp(masked - largest[..., None]) / totals[..., None], 0.0)

    def stats_step(running, key_part, first_key):
        largest, totals = running
        masked, allowed, keys_here, values_here = block_scores(key_part, first_key)
        new_largest = jnp.maximum(largest, jnp.max(masked, axis=-1))
        weights = jnp.where(allowed, jnp.exp(masked - new_largest[..., None]), 0.0)
        return (new_largest, totals * jnp.exp(largest - new_largest) + jnp.sum(weights, axis=-1))

    start_stats = (
        jnp.full((KV_HEADS, row_count), NEGATIVE, jnp.float32),
        jnp.zeros((KV_HEADS, row_count), jnp.float32),
    )
    largest, totals = over_keys(
        lax.all_gather(keyval_send, "ctx", axis=0, tiled=True), start_stats, stats_step
    )

    def values_step(running, key_part, first_key):
        masked, allowed, keys_here, values_here = block_scores(key_part, first_key)
        probs_low = probs_of(masked, allowed, largest, totals).astype(jnp.bfloat16)
        return running + jnp.einsum(
            "hrn,nhd->hrd", probs_low, values_here, preferred_element_type=jnp.float32
        )

    start_values = jnp.zeros((KV_HEADS, row_count, HEAD_DIM), jnp.float32)
    mixed_rows = over_keys(
        lax.all_gather(keyval_send, "ctx", axis=0, tiled=True), start_values, values_step
    )
    mixed_low = (
        mixed_rows.reshape(KV_HEADS, group, tokens, HEAD_DIM)
        .transpose(2, 0, 1, 3)
        .reshape(tokens, HEADS * HEAD_DIM)
        .astype(jnp.bfloat16)
    )
    middle_activation = residual + jnp.dot(
        mixed_low, attention_matrix, preferred_element_type=jnp.float32
    )
    gain_two, router_full, w_in_full, w_out_full = (
        lax.all_gather(gain_ffn, "wa", axis=0, tiled=True),
        lax.all_gather(router, "wa", axis=0, tiled=True),
        lax.all_gather(w_in, "wa", axis=3, tiled=True),
        lax.all_gather(w_out, "wa", axis=1, tiled=True),
    )
    in_half = w_in_full[0]
    out_half = w_out_full[0]
    normed_two, norm_two_back = jax.vjp(rms_scale, middle_activation, gain_two.astype(jnp.float32))
    hidden_second_norm = normed_two.astype(jnp.bfloat16)
    router_logits = jnp.dot(hidden_second_norm, router_full, preferred_element_type=jnp.float32)
    route_ids = routes[0]

    def gate_values(logit_rows):
        return jax.nn.softmax(jnp.take_along_axis(logit_rows, route_ids, axis=-1), axis=-1)

    gates, gate_back = jax.vjp(gate_values, router_logits)
    flat_ids = route_ids.reshape(tokens * TOP)
    expert_hits = (flat_ids[:, None] == jnp.arange(experts_all, dtype=jnp.int32)[None, :]).astype(
        jnp.int32
    )
    ranks = jnp.sum(expert_hits * (jnp.cumsum(expert_hits, axis=0) - expert_hits), axis=1)
    slot_first = 2 * flat_ids * capacity + ranks
    slot_second = slot_first + capacity
    slot_total = ctx_count * capacity
    slot_numbers = jnp.arange(slot_total, dtype=jnp.int32)[:, None]
    placed = (
        (slot_first[None, :] == slot_numbers) | (slot_second[None, :] == slot_numbers)
    ).astype(jnp.bfloat16)
    dispatch = jnp.sum(placed.reshape(slot_total, tokens, TOP), axis=2)
    send_rows = (
        jnp.dot(dispatch, hidden_second_norm, preferred_element_type=jnp.float32)
        .astype(jnp.bfloat16)
        .reshape(ctx_count, capacity, D)
    )
    arrived = lax.all_to_all(send_rows, "ctx", split_axis=0, concat_axis=0, tiled=True)
    stacked = jnp.einsum("ncd,gdf->ncgf", arrived, in_half, preferred_element_type=jnp.float32)
    hidden_low = gated(stacked).astype(jnp.bfloat16)
    result = jnp.einsum(
        "ncf,fd->ncd", hidden_low, out_half, preferred_element_type=jnp.float32
    ).astype(jnp.bfloat16)
    returned_rows = lax.all_to_all(result, "ctx", split_axis=0, concat_axis=0, tiled=True)
    returned_flat = returned_rows.reshape(slot_total, D)
    pair_rows = (
        returned_flat[slot_first].astype(jnp.float32)
        + returned_flat[slot_second].astype(jnp.float32)
    ).reshape(tokens, TOP, D)
    output = (middle_activation + jnp.sum(gates[:, :, None] * pair_rows, axis=1)).astype(
        jnp.bfloat16
    )
    grad_out = d_out[0].astype(jnp.float32)
    grad_gates = jnp.sum(pair_rows * grad_out[:, None, :], axis=-1)
    (grad_logits,) = gate_back(grad_gates)
    grad_logits_low = grad_logits.astype(jnp.bfloat16)
    gate_slots = jnp.dot(
        placed.astype(jnp.float32), gates.reshape(tokens * TOP), precision=lax.Precision.HIGHEST
    )
    routed_grad = jnp.dot(dispatch, d_out[0], preferred_element_type=jnp.float32)
    grad_send_rows = (
        (gate_slots[:, None] * routed_grad).astype(jnp.bfloat16).reshape(ctx_count, capacity, D)
    )
    grad_arrived = lax.all_to_all(grad_send_rows, "ctx", split_axis=0, concat_axis=0, tiled=True)
    grad_hidden = jnp.einsum(
        "ncd,fd->ncf", grad_arrived, out_half, preferred_element_type=jnp.float32
    )
    hidden_again, gated_back = jax.vjp(gated, stacked)
    (grad_stacked,) = gated_back(grad_hidden)
    grad_stacked_low = grad_stacked.astype(jnp.bfloat16)
    grad_rows = jnp.einsum(
        "ncgf,gdf->ncd", grad_stacked_low, in_half, preferred_element_type=jnp.float32
    ).astype(jnp.bfloat16)
    grad_returned = lax.all_to_all(grad_rows, "ctx", split_axis=0, concat_axis=0, tiled=True)
    grad_w_in = jnp.einsum(
        "ncd,ncgf->gdf", arrived, grad_stacked_low, preferred_element_type=jnp.float32
    )[None]
    grad_w_out = jnp.einsum(
        "ncf,ncd->fd",
        hidden_again.astype(jnp.bfloat16),
        grad_arrived,
        preferred_element_type=jnp.float32,
    )[None]
    grad_hidden_two = jnp.einsum(
        "st,sd->td",
        dispatch,
        grad_returned.reshape(slot_total, D),
        preferred_element_type=jnp.float32,
    )
    grad_hidden_two = grad_hidden_two + jnp.dot(
        grad_logits_low, router_full.T, preferred_element_type=jnp.float32
    )
    grad_router = jnp.dot(hidden_second_norm.T, grad_logits_low, preferred_element_type=jnp.float32)
    grad_middle_norm, grad_gain_two = norm_two_back(grad_hidden_two)
    grad_middle = grad_out + grad_middle_norm
    grad_middle_low = grad_middle.astype(jnp.bfloat16)
    grad_attn_weight = jnp.dot(mixed_low.T, grad_middle_low, preferred_element_type=jnp.float32)
    grad_mixed = jnp.dot(
        grad_middle_low, attention_matrix.T, preferred_element_type=jnp.float32
    ).astype(jnp.bfloat16)
    grad_rows_out = (
        grad_mixed.reshape(tokens, KV_HEADS, group, HEAD_DIM)
        .transpose(1, 2, 0, 3)
        .reshape(KV_HEADS, row_count, HEAD_DIM)
    )
    delta = jnp.sum(grad_rows_out.astype(jnp.float32) * mixed_rows, axis=-1)

    def score_grads(key_part, first_key):
        masked, allowed, keys_here, values_here = block_scores(key_part, first_key)
        probs = probs_of(masked, allowed, largest, totals)
        grad_probs = jnp.einsum(
            "hrd,nhd->hrn", grad_rows_out, values_here, preferred_element_type=jnp.float32
        )
        grad_scores = (probs * (grad_probs - delta[..., None])).astype(jnp.bfloat16)
        return (grad_scores, probs.astype(jnp.bfloat16), keys_here)

    def key_terms(grad_scores, probs_low, key_count):
        grad_keys = (
            jnp.einsum("hrn,hrd->nhd", grad_scores, query_rows, preferred_element_type=jnp.float32)
            * scale
        )
        grad_values = jnp.einsum(
            "hrn,hrd->nhd", probs_low, grad_rows_out, preferred_element_type=jnp.float32
        )
        return jnp.concatenate(
            [grad_keys.reshape(key_count, kv_width), grad_values.reshape(key_count, kv_width)],
            axis=1,
        )

    start_query = jnp.zeros((KV_HEADS, row_count, HEAD_DIM), jnp.float32)

    def back_step(running, key_part, first_key):
        grad_query_rows, grad_keyvals = running
        grad_scores, probs_low, keys_here = score_grads(key_part, first_key)
        grad_query_rows = (
            grad_query_rows
            + jnp.einsum("hrn,nhd->hrd", grad_scores, keys_here, preferred_element_type=jnp.float32)
            * scale
        )
        fresh = key_terms(grad_scores, probs_low, key_part.shape[0])
        return (grad_query_rows, lax.dynamic_update_slice_in_dim(grad_keyvals, fresh, first_key, 0))

    start_back = (start_query, jnp.zeros((length, 2 * kv_width), jnp.float32))
    grad_query_rows, grad_keyvals = over_keys(
        lax.all_gather(keyval_send, "ctx", axis=0, tiled=True), start_back, back_step
    )
    grad_keyval_mine = lax.psum_scatter(grad_keyvals, "ctx", scatter_dimension=0, tiled=True)
    grad_query = grad_query_rows.reshape(KV_HEADS, group, tokens, HEAD_DIM).transpose(2, 0, 1, 3)
    grad_query_pre = (
        rotate(grad_query.reshape(tokens, HEADS, HEAD_DIM), -angles)
        .reshape(tokens, HEADS * HEAD_DIM)
        .astype(jnp.bfloat16)
    )
    grad_key_pre = rotate(
        grad_keyval_mine[:, :kv_width].reshape(tokens, KV_HEADS, HEAD_DIM), -angles
    ).reshape(tokens, kv_width)
    grad_keyval_pre = jnp.concatenate(
        [grad_key_pre, grad_keyval_mine[:, kv_width:]], axis=1
    ).astype(jnp.bfloat16)
    grad_hidden_one = jnp.dot(
        grad_query_pre, query_matrix.T, preferred_element_type=jnp.float32
    ) + jnp.dot(grad_keyval_pre, keyvalue_matrix.T, preferred_element_type=jnp.float32)
    grad_query_weight = jnp.dot(
        hidden_first_norm.T, grad_query_pre, preferred_element_type=jnp.float32
    )
    grad_keyval_weight = jnp.dot(
        hidden_first_norm.T, grad_keyval_pre, preferred_element_type=jnp.float32
    )
    grad_residual_norm, grad_gain_one = norm_one_back(grad_hidden_one)
    grad_input = (grad_middle + grad_residual_norm).astype(jnp.bfloat16)
    shares = (
        lax.psum_scatter(
            grad_gain_one.astype(jnp.bfloat16), "wa", scatter_dimension=0, tiled=True
        ).astype(jnp.float32),
        lax.psum_scatter(
            grad_query_weight.astype(jnp.bfloat16), "wa", scatter_dimension=0, tiled=True
        ).astype(jnp.float32),
        lax.psum_scatter(
            grad_keyval_weight.astype(jnp.bfloat16), "wa", scatter_dimension=0, tiled=True
        ).astype(jnp.float32),
        lax.psum_scatter(
            grad_attn_weight.astype(jnp.bfloat16), "wa", scatter_dimension=0, tiled=True
        ).astype(jnp.float32),
        lax.psum_scatter(
            grad_gain_two.astype(jnp.bfloat16), "wa", scatter_dimension=0, tiled=True
        ).astype(jnp.float32),
        lax.psum_scatter(
            grad_router.astype(jnp.bfloat16), "wa", scatter_dimension=0, tiled=True
        ).astype(jnp.float32),
        lax.psum_scatter(
            grad_w_in.astype(jnp.bfloat16), "wa", scatter_dimension=3, tiled=True
        ).astype(jnp.float32),
        lax.psum_scatter(
            grad_w_out.astype(jnp.bfloat16), "wa", scatter_dimension=1, tiled=True
        ).astype(jnp.float32),
    )
    summed = lax.psum((shares[0], shares[1], shares[2], shares[3], shares[4], shares[5]), "ctx")
    return (
        output[None],
        grad_input[None],
        summed[0],
        summed[1],
        summed[2],
        summed[3],
        summed[4],
        summed[5],
        shares[6],
        shares[7],
    )

MESH = pl.DeviceIdType.MESH
VMEM_LIMIT = 60 * 1024 * 1024


def chip_place():
    count = lax.axis_size("ctx")
    me = lax.axis_index("ctx")
    return me // 4, lax.rem(me // 2, 2), lax.rem(me, 2), count // 4


def ctx_of(z, y, c):
    return (z * 2 + y) * 2 + c


def greet(across_x=False):
    z, y, c, depth = chip_place()
    barrier = pltpu.get_barrier_semaphore()

    def signal(device):
        pl.semaphore_signal(barrier, 1, device_id=device, device_id_type=MESH)

    signal({"ctx": ctx_of(z, y, 1 - c)})
    signal({"ctx": ctx_of(z, 1 - y, c)})
    if across_x:
        signal({"wa": 1 - lax.axis_index("wa")})
    pl.when(z > 0)(lambda: signal({"ctx": ctx_of(z - 1, y, c)}))
    pl.when(z < depth - 1)(lambda: signal({"ctx": ctx_of(z + 1, y, c)}))
    ends = (z > 0).astype(jnp.int32) + (z < depth - 1).astype(jnp.int32)
    pl.semaphore_wait(barrier, (3 if across_x else 2) + ends)


def remote(source, target_ref, sems, at, device):
    return pltpu.make_async_remote_copy(
        src_ref=source,
        dst_ref=target_ref,
        send_sem=sems.at[(0,) + at],
        recv_sem=sems.at[(1,) + at],
        device_id=device,
        device_id_type=MESH,
    )


def each(step, act):
    z, _, _, depth = chip_place()
    if step == 0:
        act(z)
    else:
        pl.when(z + step < depth)(lambda: act(z + step))
        pl.when(z - step >= 0)(lambda: act(z - step))


def nearest(k):
    z, _, _, depth = chip_place()
    low = jnp.minimum(z, depth - 1 - z)
    step = (k + 1) // 2
    place = jnp.where(k > 2 * low, k, jnp.where(lax.rem(k, 2) == 1, low - step, low + step))
    return jnp.where(z == low, place, depth - 1 - place)


class Gather:
    def __init__(self, out, rows, sems, part=0, parts=1):
        self.out, self.block, self.rows = out, rows, rows // parts
        self.first = part * self.rows
        self.z_sems, self.y_sems, self.c_sems = sems
        self.z, self.y, self.c, self.depth = chip_place()

    @staticmethod
    def sems(depth):
        return [
            pltpu.SemaphoreType.DMA((2, 2, depth)),
            pltpu.SemaphoreType.DMA((2, depth)),
            pltpu.SemaphoreType.DMA((2, 2 * depth)),
        ]

    def slot(self, z, y, c):
        start = ctx_of(z, y, c) * self.block + self.first
        return self.out.at[pl.ds(pl.multiple_of(start, 16), self.rows)]

    def own(self):
        return self.slot(self.z, self.y, self.c)

    def on_z(self, way, of_z, source=None):
        goal = jnp.minimum(self.z + 1, self.depth - 1) if way == 0 else jnp.maximum(self.z - 1, 0)
        block = self.slot(of_z, self.y, self.c)
        target = {"ctx": ctx_of(goal, self.y, self.c)}
        return remote(block if source is None else source, block, self.z_sems, (way, of_z), target)

    def on_y(self, of_z, mine=True, source=None):
        block = self.slot(of_z, self.y if mine else 1 - self.y, self.c)
        target = {"ctx": ctx_of(self.z, 1 - self.y, self.c)}
        return remote(block if source is None else source, block, self.y_sems, (of_z,), target)

    def on_core(self, of_z, of_y, mine=True, source=None):
        block = self.slot(of_z, of_y, self.c if mine else 1 - self.c)
        target = {"ctx": ctx_of(self.z, self.y, 1 - self.c)}
        at = (of_z * 2 + of_y,)
        return remote(block if source is None else source, block, self.c_sems, at, target)

    def start(self, source=None):
        z, depth = self.z, self.depth
        if source is not None:
            source = source.at[pl.ds(self.first, self.rows)]
        pl.when(z < depth - 1)(lambda: self.on_z(0, z, source).start())
        pl.when(z > 0)(lambda: self.on_z(1, z, source).start())
        self.on_y(z, source=source).start()
        self.on_core(z, self.y, source=source).start()

    def along_z(self, step):
        z, depth = self.z, self.depth

        def from_side(way, of_z, more):
            self.on_z(way, of_z).wait_recv()
            pl.when(more)(lambda: self.on_z(way, of_z).start())
            self.on_y(of_z).start()
            self.on_core(of_z, self.y).start()

        pl.when(z - step >= 0)(lambda: from_side(0, z - step, z < depth - 1))
        pl.when(z + step < depth)(lambda: from_side(1, z + step, z > 0))

    def along_y(self, step):
        def across(of_z):
            self.on_y(of_z, mine=False).wait_recv()
            self.on_core(of_z, 1 - self.y).start()

        each(step, across)

    def take_core(self, of_z):
        for of_y in range(2):
            self.on_core(of_z, of_y, mine=False).wait_recv()

    def finish(self, *taken):
        z, depth = self.z, self.depth
        for of_z in range(depth):
            pl.when((z < depth - 1) & (of_z <= z))(lambda: self.on_z(0, of_z).wait_send())
            pl.when((z > 0) & (of_z >= z))(lambda: self.on_z(1, of_z).wait_send())
            self.on_y(of_z).wait_send()
            for of_y in range(2):
                self.on_core(of_z, of_y).wait_send()
            open_still = of_z >= 0
            for one in taken:
                open_still = (of_z != one) & open_still
            pl.when(open_still)(lambda: self.take_core(of_z))


class Several:
    def __init__(self, members):
        self.members = members

    def __getattr__(self, name):
        def every(*given, **named):
            for member in self.members:
                getattr(member, name)(*given, **named)

        return every


def gather_parts(out, rows, sems, parts):
    return Several(
        [Gather(out, rows, sems[3 * i : 3 * i + 3], i, parts) for i in range(parts)]
    )


def follow(gather):
    depth = chip_place()[3]
    gather.along_z(1)
    for step in range(depth):
        if step >= 1 and step + 1 < depth:
            gather.along_z(step + 1)
        gather.along_y(step)
    gather.finish()


def add_into(target, terms, rows):
    some = 32 if rows % 32 == 0 else 48 if rows % 48 == 0 else 16

    @pl.loop(0, rows // some)
    def _(turn):
        at = pl.ds(pl.multiple_of(turn * some, 16), some)
        total = terms[0][at, :].astype(jnp.float32)
        for term in terms[1:]:
            total = total + term[at, :].astype(jnp.float32)
        target[at, :] = total.astype(target.dtype)


class Scatter:
    def __init__(self, part, scratch, sums=None, piece=0, pieces=1):
        self.part = part
        self.from_core, self.totals, self.from_y, self.from_z = scratch[:4]
        self.sums = self.totals if sums is None else sums
        self.c_sems, self.y_sems, self.z_sems = scratch[4:]
        self.block = self.totals.shape[1]
        self.rows = self.block // pieces
        self.first = piece * self.rows
        self.z, self.y, self.c, self.depth = chip_place()

    @staticmethod
    def sems(depth):
        return [
            pltpu.SemaphoreType.DMA((2, 2 * depth)),
            pltpu.SemaphoreType.DMA((2, depth)),
            pltpu.SemaphoreType.DMA((2, 2, depth)),
        ]

    @staticmethod
    def scratch(depth, rows, columns, pieces=1):
        return [
            pltpu.VMEM((2 * depth, rows, columns), jnp.bfloat16),
            pltpu.VMEM((2 * depth, rows, columns), jnp.bfloat16),
            pltpu.VMEM((depth, rows, columns), jnp.bfloat16),
            pltpu.VMEM((depth + 1, rows, columns), jnp.bfloat16),
        ] + Scatter.sems(depth) * pieces

    def of(self, ref, place):
        return ref.at[place, pl.ds(self.first, self.rows)]

    def split(self):
        return len(self.part.shape) == 3

    def share(self, chip, c):
        start = (chip * 2 + c) * self.block + self.first
        return self.part.at[pl.ds(pl.multiple_of(start, 16), self.rows)]

    def on_core(self, chip):
        target = {"ctx": ctx_of(self.z, self.y, 1 - self.c)}
        source = self.of(self.part, chip) if self.split() else self.share(chip, 1 - self.c)
        return remote(source, self.of(self.from_core, chip), self.c_sems, (chip,), target)

    def send_core(self, chip):
        self.on_core(chip).start()

    def send_y(self, of_z):
        self.on_y(of_z).start()

    def on_y(self, of_z):
        target = {"ctx": ctx_of(self.z, 1 - self.y, self.c)}
        source = self.of(self.sums, of_z * 2 + 1 - self.y)
        return remote(source, self.of(self.from_y, of_z), self.y_sems, (of_z,), target)

    def on_z(self, way, of_z):
        goal = jnp.minimum(self.z + 1, self.depth - 1) if way == 0 else jnp.maximum(self.z - 1, 0)
        place = of_z if way == 0 else jnp.where(of_z == goal, self.depth, of_z)
        source = self.of(self.totals, of_z * 2 + self.y)
        target = {"ctx": ctx_of(goal, self.y, self.c)}
        return remote(source, self.of(self.from_z, place), self.z_sems, (way, of_z), target)

    def start(self):
        def send(of_z):
            self.on_core(of_z * 2 + 1 - self.y).start()
            self.on_core(of_z * 2 + self.y).start()

        for step in range(self.depth - 1, -1, -1):
            each(step, send)

    def add_chip(self, of_z, other, send=True):
        chip = of_z * 2 + (1 - self.y if other else self.y)
        self.on_core(chip).wait_recv()
        total = self.of(self.sums, chip)
        own = total if self.split() else self.share(chip, self.c)
        add_into(total, (own, self.of(self.from_core, chip)), self.rows)
        if other and send:
            self.on_y(of_z).start()

    def add_cores(self, step):
        def add(of_z):
            self.add_chip(of_z, True)
            self.add_chip(of_z, False)

        each(step, add)

    def add_y_of(self, of_z):
        z, depth = self.z, self.depth
        self.on_y(of_z).wait_recv()
        place = of_z * 2 + self.y
        total, own = self.of(self.totals, place), self.of(self.sums, place)
        other = self.of(self.from_y, of_z)
        upward, downward = (of_z > z) & (z > 0), (of_z < z) & (z < depth - 1)
        pl.when(upward)(lambda: self.on_z(0, of_z).wait_recv())
        pl.when(downward)(lambda: self.on_z(1, of_z).wait_recv())

        @pl.when(upward | downward)
        def _():
            add_into(total, (own, other, self.of(self.from_z, of_z)), self.rows)

        @pl.when(jnp.logical_not(upward | downward))
        def _():
            add_into(total, (own, other), self.rows)

        pl.when(of_z > z)(lambda: self.on_z(0, of_z).start())
        pl.when(of_z < z)(lambda: self.on_z(1, of_z).start())

    def add_y(self, step):
        each(step, self.add_y_of)

    def last(self, result):
        z, depth = self.z, self.depth
        own = self.of(self.totals, z * 2 + self.y)
        low, high = self.of(self.from_z, z), self.of(self.from_z, depth)
        result = result.at[pl.ds(self.first, self.rows)]
        pl.when(z > 0)(lambda: self.on_z(0, z).wait_recv())
        pl.when(z < depth - 1)(lambda: self.on_z(1, z).wait_recv())
        inside = (z > 0) & (z < depth - 1)
        pl.when(inside)(lambda: add_into(result, (own, low, high), self.rows))
        pl.when(z == 0)(lambda: add_into(result, (own, high), self.rows))
        pl.when(z == depth - 1)(lambda: add_into(result, (own, low), self.rows))

    def finish(self, cores=True):
        for of_z in range(self.depth):
            self.on_y(of_z).wait_send()
            if cores:
                self.on_core(of_z * 2).wait_send()
                self.on_core(of_z * 2 + 1).wait_send()
            pl.when(of_z > self.z)(lambda: self.on_z(0, of_z).wait_send())
            pl.when(of_z < self.z)(lambda: self.on_z(1, of_z).wait_send())


def scatter_parts(part, scratch, pieces, sums=None):
    arrays, sems = tuple(scratch[:4]), tuple(scratch[4:])
    return Several(
        [
            Scatter(part, arrays + sems[3 * i : 3 * i + 3], sums, i, pieces)
            for i in range(pieces)
        ]
    )


def call(
    kernel, out, scratch, number, name, *operands, outside=(), outside_out=(), late=(), early=()
):
    many = isinstance(out, (tuple, list))
    count, results = len(operands), len(out) if many else 1
    late, early = tuple(late), tuple(early)
    more = len(late) + len(early) + 1

    def spec(position, far):
        return pl.BlockSpec(memory_space=pl.ANY if position in far else pltpu.VMEM)

    def moving(*refs):
        near, sems = refs[-more:-1], refs[-1]
        loads = {
            i: pltpu.make_async_copy(refs[i], near[k], sems.at[k]) for k, i in enumerate(late)
        }
        stores = {
            i: pltpu.make_async_copy(near[k], refs[count + i], sems.at[k])
            for k, i in enumerate(early, len(late))
        }
        for copy in loads.values():
            copy.start()
        held = [near[late.index(i)] if i in late else refs[i] for i in range(count)]
        given = [
            near[len(late) + early.index(i)] if i in early else refs[count + i]
            for i in range(results)
        ]

        def arrive(*which):
            for i in which:
                loads[i].wait()

        def leave(*which):
            for i in which:
                stores[i].start()

        helpers = (arrive, leave) if early else (arrive,)
        kernel(*helpers, *held, *given, *refs[count + results : -more])
        for copy in stores.values():
            copy.wait()

    if late or early:
        scratch = list(scratch) + [pltpu.VMEM(operands[i].shape, operands[i].dtype) for i in late]
        scratch += [pltpu.VMEM(out[i].shape, out[i].dtype) for i in early]
        scratch.append(pltpu.SemaphoreType.DMA((more - 1,)))
    far, far_out = tuple(outside) + late, tuple(outside_out) + early
    out_specs = [spec(i, far_out) for i in range(results)]
    return pl.pallas_call(
        moving if late or early else kernel,
        out_shape=out,
        in_specs=[spec(i, far) for i in range(count)],
        out_specs=out_specs if many else out_specs[0],
        scratch_shapes=scratch,
        compiler_params=pltpu.CompilerParams(
            collective_id=number,
            has_side_effects=number is not None,
            vmem_limit_bytes=VMEM_LIMIT,
        ),
        name=name,
    )(*operands)


class Relay:
    def __init__(self, source, out, sems, parts=1, paired=False):
        self.source, self.out, self.sems, self.parts = source, out, sems, parts
        self.paired = paired
        self.z, self.y, self.c, _ = chip_place()
        self.odd = lax.rem(self.z, 2)
        self.rows = source.shape[0] // ((4 if paired else 2) * parts)

    @staticmethod
    def semaphores():
        return pltpu.SemaphoreType.DMA((2, 8))

    def block(self, ref, part, c, odd):
        place = (c * 2 + odd if self.paired else c) * self.parts + part
        return ref.at[pl.ds(pl.multiple_of(place * self.rows, 16), self.rows)]

    def on_x(self, part):
        source = self.block(self.source, part, self.c, self.odd)
        target = self.block(self.out, part, self.c, self.odd)
        return remote(source, target, self.sems, (part,), {"wa": 1 - lax.axis_index("wa")})

    def on_core(self, part, c, other_z=False):
        block = self.block(self.out, part, c, 1 - self.odd if other_z else self.odd)
        at = ((4 if other_z else 2) + part,)
        return remote(block, block, self.sems, at, {"ctx": ctx_of(self.z, self.y, 1 - self.c)})

    def on_pair(self, part, mine=True):
        block = self.block(self.out, part, self.c, self.odd if mine else 1 - self.odd)
        target = {"ctx": ctx_of(self.z + 1 - 2 * self.odd, self.y, self.c)}
        return remote(block, block, self.sems, (6 + part,), target)

    def start(self):
        for part in range(self.parts):
            self.on_x(part).start()

    def pass_on(self, part=0):
        self.on_x(part).wait_recv()
        if self.paired:
            self.on_pair(part).start()
        self.on_core(part, self.c).start()

    def pass_on_pair(self, part):
        self.on_pair(part, mine=False).wait_recv()
        self.on_core(part, self.c, other_z=True).start()

    def finish(self):
        for part in range(self.parts):
            self.on_x(part).wait_send()
            self.on_core(part, self.c).wait_send()
            self.on_core(part, 1 - self.c).wait_recv()
            if self.paired:
                self.on_pair(part).wait_send()
                self.on_core(part, self.c, other_z=True).wait_send()
                self.on_core(part, 1 - self.c, other_z=True).wait_recv()


def rows_by_rows(left, right):
    return lax.dot_general(
        left, right, (((1,), (1,)), ((), ())), preferred_element_type=jnp.float32
    )


def columns_by_columns(left, right):
    return lax.dot_general(
        left, right, (((0,), (0,)), ((), ())), preferred_element_type=jnp.float32
    )


def down(row):
    return jnp.transpose(jnp.broadcast_to(row.astype(jnp.float32), (128, 128)))


def allowed_bias(doc_row, tokens):
    keys, me = doc_row.shape[1], lax.axis_index("ctx")
    own = down(doc_row[:, pl.ds(pl.multiple_of(me * tokens, 128), tokens)])[:, :1]
    key_block = lax.broadcasted_iota(jnp.int32, (tokens, keys), 1) // BLOCK
    same = doc_row[...].astype(jnp.float32) == own
    return jnp.where(same & (key_block <= me * tokens // BLOCK), 0.0, NEGATIVE)


def chosen_by(routes, lanes, experts):
    numbers = lax.rem(lanes, experts).astype(jnp.float32)
    found = down(routes[:1]) == numbers
    for k in range(1, routes.shape[0]):
        found = found | (down(routes[k : k + 1]) == numbers)
    return found & (lanes < 2 * experts)


def side_columns(own):
    side = lax.axis_index("wa")
    return pl.ds(pl.multiple_of((side if own else 1 - side) * (D // 2), 128), D // 2)


def turned(values, cosine, sine):
    heads = []
    for head in range(values.shape[1] // HEAD_DIM):
        one = values[:, head * HEAD_DIM : (head + 1) * HEAD_DIM]
        heads.append(one * cosine + pltpu.roll(one, HEAD_DIM // 2, axis=1) * sine)
    return jnp.concatenate(heads, axis=1)


def normed(values, gain_vec):
    return values * lax.rsqrt(jnp.mean(values * values, axis=-1, keepdims=True) + EPSILON) * gain_vec


def fill_small(full, small, small_there):
    full[:, side_columns(True)] = small[...].astype(jnp.float32)
    full[:, side_columns(False)] = small_there[...].astype(jnp.float32)


def router_block(full, experts):
    rows = full[:experts]
    spare = jnp.zeros((128 - 2 * experts, rows.shape[1]), jnp.float32)
    return jnp.concatenate([rows, rows, spare], axis=0).astype(jnp.bfloat16)


def attend(
    x, d_out, router, gains, w_query, w_keyval, w_out_attn, w_out, angles, doc_row, routes
):
    count, tokens, features = lax.axis_size("ctx"), x.shape[0], x.shape[1]
    depth, length = count // 4, count * tokens
    kv_columns, experts = w_keyval.shape[1], router.shape[0]
    small_shape = (2 * experts, router.shape[1])

    def kernel(
        arrive, leave, x_ref, router_ref, query_own, keyval_own, attn_own, d_out_far, query_far,
        keyval_far, attn_far, out_far, cosine_ref, sine_ref, doc_row_ref, routes_ref, gain_one, gain_two,
        query, keyval, level, mixed, hidden, mixed_low, middle, send, gates_out, query_other,
        keyval_other, attn_other, small_there, d_out_all, out_other,
        small_ref,
        filled, full, stacked, bias, query_sems, keyval_sems, attn_sems, small_sems, own_sem, *sems,
    ):
        gather = gather_parts(keyval, tokens, sems[:6], 2)
        spread = gather_parts(d_out_all, tokens, sems[6:], 2)
        query_relay = Relay(query_far, query_other, query_sems, parts=2)
        keyval_relay = Relay(keyval_far, keyval_other, keyval_sems)
        attn = Relay(attn_far, attn_other, attn_sems, parts=2, paired=True)
        partner = {"wa": 1 - lax.axis_index("wa")}
        swap = remote(small_ref, small_there, small_sems, (0,), partner)
        swap_out = remote(out_far, out_other, small_sems, (1,), partner)
        keep = pltpu.make_async_copy(
            d_out_far, Gather(d_out_all, tokens, sems[6:9]).own(), own_sem.at[0]
        )
        keep.start()
        filled[...] = jnp.zeros_like(filled)
        filled[:experts] = router_ref[...].astype(jnp.float32)
        filled[experts : experts + 1] = gain_one[...].astype(jnp.float32)
        filled[experts + 1 : experts + 2] = gain_two[...].astype(jnp.float32)
        small_ref[...] = filled[...].astype(jnp.bfloat16)
        greet(across_x=True)
        swap.start()
        keyval_relay.start()
        query_relay.start()
        attn.start()
        swap_out.start()
        spread.start(d_out_far)
        swap.wait()
        fill_small(full, small_ref, small_there)
        residual = x_ref[...].astype(jnp.float32)
        hidden[...] = normed(residual, full[experts : experts + 1]).astype(jnp.bfloat16)
        own, other = hidden[:, side_columns(True)], hidden[:, side_columns(False)]
        cosine, sine = cosine_ref[...], sine_ref[...]

        def onto(matrix, matrix_other):
            return jnp.dot(own, matrix[...], preferred_element_type=jnp.float32) + jnp.dot(
                other, matrix_other[...], preferred_element_type=jnp.float32
            )

        bias[...] = allowed_bias(doc_row_ref, tokens)
        spread.along_z(1)
        spread.along_y(0)
        keyval_relay.pass_on()
        keyval_relay.finish()
        arrive(3)
        pre = onto(keyval_own, keyval_other)
        keys = turned(pre[:, : kv_columns // 2], cosine, sine)
        block = jnp.concatenate([keys, pre[:, kv_columns // 2 :]], axis=1)
        Gather(keyval, tokens, sems[:3]).own()[...] = block.astype(jnp.bfloat16)
        leave(4, 10)
        spread.along_z(2)
        spread.along_y(1)
        query_relay.pass_on(0)
        spread.along_z(3)
        gather.start()
        gather.along_z(1)
        spread.along_y(2)
        gather.along_y(0)
        gather.along_z(2)
        query_relay.pass_on(1)
        spread.along_y(3)
        gather.along_y(1)
        gather.along_z(3)
        query_relay.finish()
        arrive(2)
        query[...] = turned(onto(query_own, query_other), cosine, sine).astype(jnp.bfloat16)
        for head in range(HEADS):
            rows = slice(head * tokens, (head + 1) * tokens)
            stacked[rows, :] = query[:, head * 128 : (head + 1) * 128]
        leave(0, 9)
        attn.pass_on(0)
        gather.along_y(2)
        gather.along_y(3)
        gather.finish()
        leave(1)

        @pl.loop(0, HEADS // 2)
        def _(pair):
            rows = pl.ds(pl.multiple_of(pair * 2 * tokens, 128), 2 * tokens)
            kind = pair // (HEADS // KV_HEADS // 2)
            key_part = keyval[:, pl.ds(pl.multiple_of(kind * 128, 128), 128)]
            val_part = keyval[:, pl.ds(pl.multiple_of(kind * 128 + 256, 128), 128)]
            scores = rows_by_rows(stacked[rows, :], key_part) * HEAD_DIM**-0.5
            scores = (scores.reshape(2, tokens, -1) + bias[...][None]).reshape(scores.shape)
            top = jnp.max(scores, axis=-1, keepdims=True)
            weights = jnp.exp(scores - top)
            total = jnp.sum(weights, axis=-1, keepdims=True)
            probs = (weights * (1 / total)).astype(jnp.bfloat16)
            mixture = jnp.dot(probs, val_part, preferred_element_type=jnp.float32)
            for part in range(2):
                columns = pl.ds(pl.multiple_of((pair * 2 + part) * 128, 128), 128)
                mixed[:, columns] = mixture[part * tokens : (part + 1) * tokens]
            column = jnp.broadcast_to(top + jnp.log(total), (2 * tokens, 128))
            level[pl.ds(pair, 1), :] = jnp.transpose(column)[:1]
            pl.when(pair == 1)(lambda: attn.pass_on(1))
            pl.when(pair == 4)(lambda: attn.pass_on_pair(0))

        mixed_low[...] = mixed[...].astype(jnp.bfloat16)
        leave(3, 5)
        attn.pass_on_pair(1)
        own, other = mixed_low[:, side_columns(True)], mixed_low[:, side_columns(False)]
        arrive(4)
        attn.finish()
        leave(11)
        middle[...] = residual + onto(attn_own, attn_other)
        hidden_two = normed(middle[...], full[experts + 1 : experts + 2]).astype(jnp.bfloat16)
        send[:, :features] = hidden_two
        logits = rows_by_rows(hidden_two, router_block(full, experts))
        lane = lax.broadcasted_iota(jnp.int32, logits.shape, 1)
        masked = jnp.where(chosen_by(routes_ref[...], lane, experts), logits, NEGATIVE)
        weights = jnp.exp(masked - jnp.max(masked, axis=1, keepdims=True))
        total = jnp.sum(jnp.where(lane < experts, weights, 0.0), axis=1, keepdims=True)
        gates = weights / total
        high = gates.astype(jnp.bfloat16).astype(jnp.float32)
        carried = jnp.where(lane < experts, high, jnp.where(lane < 2 * experts, gates - high, 0.0))
        send[:, features:] = carried.astype(jnp.bfloat16)
        gates_out[...] = jnp.where(lane < experts, gates, 0.0)
        spread.finish()
        keep.wait()
        swap_out.wait()

    def shape(rows, columns, kind=jnp.bfloat16):
        return jax.ShapeDtypeStruct((rows, columns), kind)

    wide = features + 128
    out = [
        shape(tokens, features), shape(length, kv_columns), shape(8, 2 * tokens, jnp.float32),
        shape(tokens, features, jnp.float32), shape(tokens, features), shape(tokens, features),
        shape(tokens, features, jnp.float32), shape(tokens, wide), shape(tokens, 128, jnp.float32),
        shape(*w_query.shape), shape(*w_keyval.shape), shape(*w_out_attn.shape),
        shape(*small_shape), shape(length, features), shape(*w_out.shape), shape(*small_shape),
    ]
    scratch = [
        pltpu.VMEM(small_shape, jnp.float32),
        pltpu.VMEM((small_shape[0], features), jnp.float32),
        pltpu.VMEM((HEADS * tokens, HEAD_DIM), jnp.bfloat16),
        pltpu.VMEM((tokens, length), jnp.float32),
        Relay.semaphores(),
        Relay.semaphores(),
        Relay.semaphores(),
        pltpu.SemaphoreType.DMA((2, 2)),
        pltpu.SemaphoreType.DMA((1,)),
    ] + Gather.sems(depth) * 4
    return call(
        kernel, out, scratch, 2, "attend",
        x, router, w_query, w_keyval, w_out_attn, d_out, w_query, w_keyval, w_out_attn, w_out,
        *angles, doc_row, routes, *gains, outside=(5, 6, 7, 8, 9), outside_out=(13, 14), late=(3, 2, 4),
        early=(0, 1, 3, 4, 5, 9, 10, 11),
    )


def norm_back(values, gain_vec, grad):
    scale = lax.rsqrt(jnp.mean(values * values, axis=-1, keepdims=True) + EPSILON)
    through = jnp.mean(gain_vec * grad * values, axis=-1, keepdims=True)
    back = scale * gain_vec * grad - values * (scale * scale * scale * through)
    return back, jnp.sum(grad * values * scale, axis=0, keepdims=True)


def attend_back(
    returned, gates, small, small_there, middle, d_out, send, attn_own, attn_other, query, keyval,
    angles, doc_row, level, mixed, hidden, mixed_low, results, experts,
):
    count, tokens, features = lax.axis_size("ctx"), query.shape[0], query.shape[1]
    depth, length, kv_columns = count // 4, keyval.shape[0], keyval.shape[1]

    def kernel(
        arrive, leave, returned_ref, gates_ref, small_ref, small_there_ref, middle_ref, d_out_ref, send_ref,
        attn_own_ref, attn_other_ref, query_ref, keyval_ref, cosine_ref, sine_ref, doc_row_ref,
        level_ref, mixed_ref, hidden_ref, mixed_low_ref, results_ref,
        output, grad_middle, grad_middle_low, grad_middle_there, grad_query, grad_query_there,
        grad_keyval, grad_keyval_there, small_grads, hidden_own, hidden_there, mixed_own,
        mixed_there,
        full, grad_mixed, turned_query, own_keyval, result_sum, stacked, grads, bias, delta, total,
        part, x_sems, *scratch,
    ):
        result = scatter_parts(
            None, (None,) + tuple(scratch[:3]) + tuple(scratch[3:9]), 2, results_ref
        )
        keyval_sum = scatter_parts(part, scratch[9:], 2)
        partner = {"wa": 1 - lax.axis_index("wa")}
        swaps = [
            remote(source, target, x_sems, (i,), partner)
            for i, (source, target) in enumerate(
                [(grad_middle_low, grad_middle_there), (grad_query, grad_query_there),
                 (grad_keyval, grad_keyval_there),
                 (hidden_ref.at[:, side_columns(False)], hidden_there),
                 (mixed_low_ref.at[:, side_columns(False)], mixed_there)]
            )
        ]
        greet(across_x=True)
        arrive(18)
        for k in range(depth - 1, 0, -1):
            result.send_y(nearest(k))
        swaps[3].start()
        swaps[4].start()
        hidden_own[...] = hidden_ref[:, side_columns(True)]
        mixed_own[...] = mixed_low_ref[:, side_columns(True)]
        leave(9, 11)
        fill_small(full, small_ref, small_there_ref)
        arrive(0, 4, 5, 6)
        lane = lax.broadcasted_iota(jnp.int32, (tokens, 128), 1)
        gates = gates_ref[...]
        grad_gates = jnp.where(lane < experts, returned_ref[:, features:], 0.0)
        inner = jnp.sum(gates * grad_gates, axis=1, keepdims=True)
        grad_logits = (gates * (grad_gates - inner)).astype(jnp.bfloat16)
        z = chip_place()[0]
        at_end = (z == 0) | (z == depth - 1)
        within = jnp.logical_not(at_end)
        grad_two = returned_ref[:, :features] + jnp.dot(
            grad_logits, router_block(full, experts), preferred_element_type=jnp.float32
        )
        grad_router = columns_by_columns(grad_logits, send_ref[:, :features])
        back, grad_gain = norm_back(middle_ref[...], full[experts + 1 : experts + 2], grad_two)
        grad_middle[...] = d_out_ref[...].astype(jnp.float32) + back
        grad_middle_low[...] = grad_middle[...].astype(jnp.bfloat16)
        swaps[0].start()
        leave(1, 2)
        small_grads[:experts] = grad_router[:experts]
        row = lax.broadcasted_iota(jnp.int32, (small_grads.shape[0] - experts, 1), 0)
        small_grads[experts:] = jnp.where(row == 1, grad_gain, 0.0)
        arrive(7, 8)
        grad_mixed[:, side_columns(True)] = rows_by_rows(
            grad_middle_low[...], attn_own_ref[...]
        ).astype(jnp.bfloat16)
        grad_mixed[:, side_columns(False)] = rows_by_rows(
            grad_middle_low[...], attn_other_ref[...]
        ).astype(jnp.bfloat16)
        allowed = jnp.transpose(allowed_bias(doc_row_ref, tokens))
        bias[:, :tokens] = allowed
        bias[:, tokens:] = allowed
        total[...] = jnp.zeros_like(total)
        arrive(9, 10, 15)
        for head in range(HEADS):
            rows = slice(head * tokens, (head + 1) * tokens)
            columns = slice(head * 128, head * 128 + 128)
            stacked[rows, :] = query_ref[:, columns]
            grads[rows, :] = grad_mixed[:, columns]
            product = grad_mixed[:, columns].astype(jnp.float32) * mixed_ref[:, columns]
            delta[head // 2 : head // 2 + 1, (head % 2) * tokens : (head % 2 + 1) * tokens] = (
                jnp.sum(jnp.transpose(product), axis=0, keepdims=True)
            )

        @pl.loop(0, HEADS // 2)
        def _(pair):
            rows = pl.ds(pl.multiple_of(pair * 2 * tokens, 128), 2 * tokens)
            kind = pair // (HEADS // KV_HEADS // 2)
            key_columns = pl.ds(pl.multiple_of(kind * 128, 128), 128)
            val_columns = pl.ds(pl.multiple_of(kind * 128 + 256, 128), 128)
            key_part, val_part = keyval_ref[:, key_columns], keyval_ref[:, val_columns]
            own, grad = stacked[rows, :], grads[rows, :]
            pair_row = pl.ds(pair, 1)
            scores = rows_by_rows(key_part, own) * HEAD_DIM**-0.5 + bias[...]
            probs = jnp.exp(scores - level_ref[pair_row, :])
            grad_probs = rows_by_rows(val_part, grad)
            grad_scores = (probs * (grad_probs - delta[pair_row, :])).astype(jnp.bfloat16)
            own_grad = jnp.transpose(columns_by_columns(key_part, grad_scores))
            for half in range(2):
                columns = pl.ds(pl.multiple_of((pair * 2 + half) * 128, 128), 128)
                turned_query[:, columns] = (
                    own_grad[half * tokens : (half + 1) * tokens] * HEAD_DIM**-0.5
                )
            total[:, key_columns] += (
                jnp.dot(grad_scores, own, preferred_element_type=jnp.float32) * HEAD_DIM**-0.5
            )
            total[:, val_columns] += jnp.dot(
                probs.astype(jnp.bfloat16), grad, preferred_element_type=jnp.float32
            )
            pl.when((pair == HEADS // 4) & at_end)(lambda: result.add_y_of(nearest(depth - 1)))

        part[...] = total[...].astype(jnp.bfloat16)
        keyval_sum.start()
        cosine, sine = cosine_ref[...], -sine_ref[...]
        grad_query[...] = turned(turned_query[...], cosine, sine).astype(jnp.bfloat16)
        swaps[1].start()
        leave(4)
        steps = range(depth - 1, -1, -1)
        for step in steps:
            keyval_sum.add_cores(step)
        result.send_y(nearest(0))
        pl.when(within)(lambda: result.add_y_of(nearest(depth - 1)))
        for k in range(depth - 2, 0, -1):
            result.add_y_of(nearest(k))
        for step in steps:
            keyval_sum.add_y(step)
        keyval_sum.last(own_keyval)
        keys = turned(own_keyval[:, : kv_columns // 2], cosine, sine)
        grad_keyval[...] = jnp.concatenate(
            [keys, own_keyval[:, kv_columns // 2 :]], axis=1
        ).astype(jnp.bfloat16)
        swaps[2].start()
        result.add_y_of(nearest(0))
        result.last(result_sum)
        output[...] = (middle_ref[...] + result_sum[...]).astype(jnp.bfloat16)
        keyval_sum.finish()
        result.finish(cores=False)
        for swap in swaps:
            swap.wait()

    def shape(like, kind=jnp.bfloat16):
        return jax.ShapeDtypeStruct(like, kind)

    rows, narrow = (tokens, features), (tokens, kv_columns)
    small_shape = (small.shape[0], features)
    out = [
        shape(rows), shape(rows, jnp.float32), shape(rows), shape(rows), shape(rows), shape(rows),
        shape(narrow), shape(narrow), shape(small_shape, jnp.float32),
    ] + [shape((tokens, features // 2))] * 4
    scratch = [
        pltpu.VMEM(small_shape, jnp.float32),
        pltpu.VMEM(rows, jnp.bfloat16),
        pltpu.VMEM(rows, jnp.float32),
        pltpu.VMEM(narrow, jnp.float32),
        pltpu.VMEM(rows, jnp.float32),
        pltpu.VMEM((HEADS * tokens, HEAD_DIM), jnp.bfloat16),
        pltpu.VMEM((HEADS * tokens, HEAD_DIM), jnp.bfloat16),
        pltpu.VMEM((length, 2 * tokens), jnp.float32),
        pltpu.VMEM((8, 2 * tokens), jnp.float32),
        pltpu.VMEM(keyval.shape, jnp.float32),
        pltpu.VMEM(keyval.shape, jnp.bfloat16),
        pltpu.SemaphoreType.DMA((2, 5)),
    ]
    wide = Scatter.scratch(depth, tokens, features)
    scratch += wide[1:4] + Scatter.sems(depth) * 2 + Scatter.scratch(depth, tokens, kv_columns, 2)
    return call(
        kernel, out, scratch, 4, "attend_back",
        returned, gates, small, small_there, middle, d_out, send, attn_own, attn_other, query,
        keyval, *angles, doc_row, level, mixed, hidden, mixed_low, results,
        late=(18, 0, 4, 5, 6, 7, 8, 9, 10, 15), early=(1, 2, 4, 9, 11),
    )


def gate_unit(first, second):
    root, cube = math.sqrt(2 / math.pi), 0.044715
    square = first * first
    bend = jnp.tanh(root * first * (1 + cube * square))
    lift = 0.5 * (1 + bend)
    slope = lift + 0.5 * first * (1 - bend * bend) * root * (1 + 3 * cube * square)
    gelu = first * lift
    return gelu * second, slope * second, gelu


def run_experts(send, d_out_all, in_own, out_own, out_other, experts):
    count, tokens = lax.axis_size("ctx"), send.shape[0]
    depth, chips, length = count // 4, count // 2, count * tokens
    wide, features = send.shape[1], d_out_all.shape[1]
    quarter = out_own.shape[0]
    width = 2 * quarter

    def kernel(
        send_ref, d_out_far, in_own_ref, out_own_ref, out_other_ref,
        returned, results_far, grad_in_far, grad_in_other_far, grad_out_far, grad_out_other_far,
        hidden_all, grad_both, gated_hidden, other_part, other_result, result_from, result_sems,
        in_ref, out_ref, d_out_ref, x_sems, near_sem, results, grad_in, grad_in_other, grad_out,
        grad_out_other, far_sems, *scratch,
    ):
        gather = gather_parts(hidden_all, tokens, scratch[:6], 2)
        scatter = scatter_parts(other_part, scratch[6:], 2)
        chip_sums = scratch[7]
        z, y, c, _ = chip_place()
        expert = lax.axis_index("ctx") // 2
        lane = lax.broadcasted_iota(jnp.int32, (1, 128), 1)
        Gather(hidden_all, tokens, scratch[:3]).own()[...] = send_ref[...]
        partner = {"wa": 1 - lax.axis_index("wa")}
        stores = [
            pltpu.make_async_copy(source, target, far_sems.at[i])
            for i, (source, target) in enumerate(
                [(results, results_far), (grad_in, grad_in_far),
                 (grad_in_other, grad_in_other_far), (grad_out, grad_out_far),
                 (grad_out_other, grad_out_other_far)]
            )
        ]
        near = pltpu.make_async_copy(d_out_far, d_out_ref, near_sem.at[0])
        near.start()
        swaps = [
            remote(
                in_own_ref.at[pl.ds(part * quarter, quarter)],
                in_ref.at[pl.ds((2 * part + 1) * quarter, quarter)],
                x_sems,
                (part,),
                partner,
            )
            for part in range(2)
        ]
        greet(across_x=True)
        gather.start()
        for swap in swaps:
            swap.start()
        out_ref[:quarter] = out_own_ref[...]
        out_ref[quarter:] = out_other_ref[...]
        in_ref[:quarter] = in_own_ref[:quarter]
        in_ref[width : width + quarter] = in_own_ref[quarter:]
        def chip_rows(chip):
            return pl.ds(pl.multiple_of(chip * 2 * tokens, 16), 2 * tokens)

        def parted(values):
            low, high = values[:tokens], values[tokens:]
            return jnp.where(c == 0, low, high), jnp.where(c == 0, high, low)

        def backward(chip):
            rows = chip_rows(chip)
            carried = hidden_all[rows, features:].astype(jnp.float32)
            mine = (lane == expert) | (lane == expert + experts)
            gate = jnp.sum(jnp.where(mine, carried, 0.0), axis=1, keepdims=True)
            both = rows_by_rows(hidden_all[rows, :features], in_ref[...])
            hidden, by_first, by_second = gate_unit(both[:, :width], both[:, width:])
            gated_hidden[rows, :] = (hidden * gate).astype(jnp.bfloat16)
            grad_hidden = rows_by_rows(d_out_ref[rows, :], out_ref[...])
            grad_gate = jnp.sum(grad_hidden * hidden, axis=1, keepdims=True)
            grad_hidden = grad_hidden * gate
            grad_both[rows, :width] = (grad_hidden * by_first).astype(jnp.bfloat16)
            grad_both[rows, width:] = (grad_hidden * by_second).astype(jnp.bfloat16)
            own, other = parted(
                jnp.dot(grad_both[rows, :], in_ref[...], preferred_element_type=jnp.float32)
            )
            chip_sums[chip, :, :features] = own.astype(jnp.bfloat16)
            other_part[chip, :, :features] = other.astype(jnp.bfloat16)
            own, other = parted(jnp.where(lane == expert, grad_gate, 0.0))
            chip_sums[chip, :, features:] = own.astype(jnp.bfloat16)
            other_part[chip, :, features:] = other.astype(jnp.bfloat16)
            scatter.send_core(chip)

        gather.along_z(1)
        for step in range(2, depth):
            gather.along_y(step - 2)
            gather.along_z(step)
        near.wait()
        for swap in swaps:
            swap.wait()
        for of_z in (nearest(1), z):
            gather.take_core(of_z)
        backward(nearest(1) * 2 + 1 - y)
        backward(nearest(1) * 2 + y)
        scatter.add_chip(nearest(1), True)
        gather.along_y(depth - 2)
        backward(z * 2 + 1 - y)
        gather.along_y(depth - 1)
        backward(z * 2 + y)
        gather.finish(nearest(1), z)
        scatter.add_chip(nearest(1), False)

        @pl.loop(0, depth - 2)
        def _(turn):
            of_z = nearest(depth - 1 - turn)
            backward(of_z * 2 + 1 - y)
            pl.when(turn > 0)(lambda: scatter.add_chip(nearest(depth - turn), False))
            backward(of_z * 2 + y)
            scatter.add_chip(of_z, True)

        scatter.add_chip(nearest(2), False)
        scatter.add_chip(z, True)
        scatter.add_chip(nearest(0), False)
        scatter.add_y_of(nearest(depth - 1))

        def result_copy(chip):
            target = {"ctx": ctx_of(z, y, 1 - c)}
            return remote(
                other_result.at[chip], result_from.at[chip], result_sems, (chip,), target
            )

        @pl.loop(0, chips)
        def _(chip):
            result = jnp.dot(
                gated_hidden[chip_rows(chip), :], out_ref[...], preferred_element_type=jnp.float32
            )
            own, other = parted(result)
            results[chip] = own.astype(jnp.bfloat16)
            other_result[chip] = other.astype(jnp.bfloat16)
            result_copy(chip).start()

        scatter.add_y_of(nearest(depth - 2))

        @pl.loop(0, features // 512)
        def _(turn):
            at = pl.ds(pl.multiple_of(turn * 512, 512), 512)
            grad = columns_by_columns(gated_hidden[...], d_out_ref[:, at])
            grad_out[:, at] = grad[:quarter]
            grad_out_other[:, at] = grad[quarter:].astype(jnp.bfloat16)

        stores[3].start()
        stores[4].start()
        for k in range(depth - 3, 0, -1):
            scatter.add_y_of(nearest(k))

        @pl.loop(0, features // 512)
        def _(turn):
            at = pl.ds(pl.multiple_of(turn * 512, 512), 512)
            grad = columns_by_columns(grad_both[...], hidden_all[:, at])
            for part in range(2):
                rows = slice(part * quarter, (part + 1) * quarter)
                first = part * width
                grad_in[rows, at] = grad[first : first + quarter]
                grad_in_other[rows, at] = grad[first + quarter : first + width].astype(jnp.bfloat16)

        stores[1].start()
        stores[2].start()

        @pl.loop(0, chips)
        def _(chip):
            result_copy(chip).wait_recv()
            add_into(results.at[chip], (results.at[chip], result_from.at[chip]), tokens)

        stores[0].start()
        scatter.add_y_of(nearest(0))
        scatter.last(returned)
        scatter.finish()
        for chip in range(chips):
            result_copy(chip).wait_send()
        for store in stores:
            store.wait()

    block = (chips, tokens, features)
    out = [
        jax.ShapeDtypeStruct((tokens, wide), jnp.float32),
        jax.ShapeDtypeStruct(block, jnp.bfloat16),
        jax.ShapeDtypeStruct(in_own.shape, jnp.float32),
        jax.ShapeDtypeStruct(in_own.shape, jnp.bfloat16),
        jax.ShapeDtypeStruct(out_own.shape, jnp.float32),
        jax.ShapeDtypeStruct(out_own.shape, jnp.bfloat16),
    ]
    scratch = [
        pltpu.VMEM((length, wide), jnp.bfloat16),
        pltpu.VMEM((length, 2 * width), jnp.bfloat16),
        pltpu.VMEM((length, width), jnp.bfloat16),
        pltpu.VMEM((chips, tokens, wide), jnp.bfloat16),
        pltpu.VMEM(block, jnp.bfloat16),
        pltpu.VMEM(block, jnp.bfloat16),
        pltpu.SemaphoreType.DMA((2, chips)),
        pltpu.VMEM((2 * width, features), jnp.bfloat16),
        pltpu.VMEM((width, features), jnp.bfloat16),
        pltpu.VMEM(d_out_all.shape, jnp.bfloat16),
        pltpu.SemaphoreType.DMA((2, 2)),
        pltpu.SemaphoreType.DMA((1,)),
    ]
    scratch += [pltpu.VMEM(one.shape, one.dtype) for one in out[1:]]
    scratch.append(pltpu.SemaphoreType.DMA((5,)))
    scratch += Gather.sems(depth) * 2 + Scatter.scratch(depth, tokens, wide, 2)
    return call(
        kernel, out, scratch, 3, "experts", send, d_out_all, in_own, out_own, out_other, outside=(1,),
        outside_out=range(1, 6),
    )


def finish(
    x, grad_middle, small, small_there, small_grads, matrices, hidden, mixed, middle, query, keyval,
    expert_in, expert_out,
):
    count, tokens, half = lax.axis_size("ctx"), x.shape[0], x.shape[1] // 2
    depth, rows = count // 4, half // count
    widths = (middle[0].shape[1], query[0].shape[1], keyval[0].shape[1])
    experts = small.shape[0] // 2

    def kernel(
        arrive, leave, x_ref, grad_middle_ref, small_ref, small_there_ref, small_grads_ref,
        query_own, query_other, keyval_own, keyval_other,
        hidden_ref, hidden_there, mixed_ref, mixed_there, middle_ref, middle_there,
        query_ref, query_there, keyval_ref, keyval_there, in_ref, out_ref,
        attn_sum, query_sum, keyval_sum, small_sum, grad_input, in_there, out_there,
        attn_part, query_part, keyval_part, pair, full, grad_one, small_mine, small_came, small_all,
        x_sems, *scratch,
    ):
        scatters, gathers = [], []
        parts, sums = (attn_part, query_part, keyval_part), (attn_sum, query_sum, keyval_sum)
        for part, total in zip(parts, sums):
            scatters.append(Scatter(part, scratch[:7]))
            gathers.append(Gather(total, rows, scratch[7:10]))
            scratch = scratch[10:]
        small_out = Gather(small_all, small_came.shape[0], scratch)
        (attn, query_, keyval_), (attn_out, query_out, keyval_out) = scatters, gathers
        partner = {"wa": 1 - lax.axis_index("wa")}
        swaps = [
            remote(source, target, x_sems, (i,), partner)
            for i, (source, target) in enumerate(
                [(small_mine.at[:, side_columns(False)], small_came), (in_ref, in_there),
                 (out_ref, out_there)]
            )
        ]
        steps = range(depth - 1, -1, -1)

        def products(left, left_there, right, right_there, part):
            pair[:tokens] = left[...]
            pair[tokens:] = left_there[...]

            @pl.loop(0, part.shape[1] // 512)
            def _(turn):
                at = pl.ds(pl.multiple_of(turn * 512, 512), 512)
                both = jnp.concatenate([right[:, at], right_there[:, at]], axis=0)
                part[:, at] = columns_by_columns(pair[...], both).astype(jnp.bfloat16)

        products(mixed_ref, mixed_there, middle_ref, middle_there, attn_part)
        greet(across_x=True)
        attn.start()
        arrive(9, 10, 15, 16)
        products(hidden_ref, hidden_there, query_ref, query_there, query_part)
        for step in steps:
            attn.add_cores(step)
        query_.start()
        arrive(17, 18)
        products(hidden_ref, hidden_there, keyval_ref, keyval_there, keyval_part)
        keyval_.start()
        for step in steps:
            query_.add_cores(step)
        attn.add_y(depth - 1)
        fill_small(full, small_ref, small_there_ref)
        arrive(0, 1, 5, 6, 7, 8)
        grad_one[:, side_columns(True)] = rows_by_rows(
            query_ref[...], query_own[...]
        ) + rows_by_rows(keyval_ref[...], keyval_own[...])
        attn.add_y(depth - 2)
        grad_one[:, side_columns(False)] = rows_by_rows(
            query_ref[...], query_other[...]
        ) + rows_by_rows(keyval_ref[...], keyval_other[...])
        back, grad_gain = norm_back(
            x_ref[...].astype(jnp.float32), full[experts : experts + 1], grad_one[...]
        )
        grad_input[...] = (grad_middle_ref[...] + back).astype(jnp.bfloat16)
        leave(4)
        row = lax.broadcasted_iota(jnp.int32, (small_mine.shape[0], 1), 0)
        small_mine[...] = jnp.where(row == experts, grad_gain, small_grads_ref[...])
        swaps[0].start()
        for step in range(depth - 3, -1, -1):
            attn.add_y(step)
        for step in steps:
            keyval_.add_cores(step)
        attn.last(attn_out.own())
        attn_out.start()
        swaps[1].start()
        swaps[2].start()
        swaps[0].wait()
        small_out.own()[...] = (small_mine[:, side_columns(True)] + small_came[...]).astype(
            jnp.bfloat16
        )
        small_out.start()
        for step in steps:
            query_.add_y(step)
        attn_out.along_z(1)
        query_.last(query_out.own())
        query_out.start()
        attn_out.along_z(2)
        attn_out.along_y(0)
        small_out.along_z(1)
        for step in steps:
            keyval_.add_y(step)
        attn_out.along_z(3)
        attn_out.along_y(1)
        keyval_.last(keyval_out.own())
        keyval_out.start()
        query_out.along_z(1)
        small_out.along_z(2)
        attn_out.along_y(2)
        query_out.along_z(2)
        small_out.along_z(3)
        query_out.along_y(0)
        keyval_out.along_z(1)
        query_out.along_z(3)
        attn_out.along_y(3)
        keyval_out.along_z(2)
        query_out.along_y(1)
        keyval_out.along_z(3)
        query_out.along_y(2)
        attn_out.finish()
        leave(0)
        small_out.along_y(0)
        keyval_out.along_y(0)
        small_out.along_y(1)
        query_out.along_y(3)
        keyval_out.along_y(1)
        small_out.along_y(2)
        keyval_out.along_y(2)
        small_out.along_y(3)
        keyval_out.along_y(3)
        query_out.finish()
        leave(1)
        keyval_out.finish()
        leave(2)
        for one in [small_out] + scatters:
            one.finish()
        small_rows = small_came.shape[0]
        total = small_all[:small_rows].astype(jnp.float32)
        for device in range(1, count):
            rows_of = slice(device * small_rows, (device + 1) * small_rows)
            total = total + small_all[rows_of].astype(jnp.float32)
        small_sum[...] = total
        swaps[1].wait()
        swaps[2].wait()

    small_shape = (small.shape[0], half)
    out = [jax.ShapeDtypeStruct((half, width), jnp.bfloat16) for width in widths]
    out += [
        jax.ShapeDtypeStruct(small_shape, jnp.float32),
        jax.ShapeDtypeStruct(x.shape, jnp.bfloat16),
        jax.ShapeDtypeStruct(expert_in.shape, expert_in.dtype),
        jax.ShapeDtypeStruct(expert_out.shape, expert_out.dtype),
    ]
    scratch = [pltpu.VMEM((half, width), jnp.bfloat16) for width in widths]
    scratch += [
        pltpu.VMEM((2 * tokens, half), jnp.bfloat16),
        pltpu.VMEM(small_grads.shape, jnp.float32),
        pltpu.VMEM(x.shape, jnp.float32),
        pltpu.VMEM(small_grads.shape, jnp.float32),
        pltpu.VMEM(small_shape, jnp.float32),
        pltpu.VMEM((count * small.shape[0], half), jnp.bfloat16),
        pltpu.SemaphoreType.DMA((2, 3)),
    ]
    for width in widths:
        scratch += Scatter.scratch(depth, rows, width) + Gather.sems(depth)
    scratch += Gather.sems(depth)
    return call(
        kernel, out, scratch, 1, "finish",
        x, grad_middle, small, small_there, small_grads, *matrices, *hidden, *mixed, *middle,
        *query, *keyval, expert_in, expert_out, outside=(19, 20), outside_out=(5, 6),
        late=(9, 10, 15, 16, 17, 18, 5, 6, 7, 8, 0, 1), early=(0, 1, 2, 4),
    )


def widen(query, keyval, attn, grad_in, in_there, grad_out, out_there, small):
    quarter, features = grad_out.shape
    steps, experts = 4, small.shape[0] // 2

    def kernel(*refs):
        query_ref, keyval_ref, attn_ref, in_ref, in_there_ref, out_ref, out_there_ref = refs[:7]
        small_ref, query_out, keyval_out, attn_out, in_out, out_out, router_out = refs[7:]
        router_out[...] = small_ref[:experts]
        query_out[...] = query_ref[...].astype(jnp.float32)
        keyval_out[...] = keyval_ref[...].astype(jnp.float32)
        attn_out[...] = attn_ref[...].astype(jnp.float32)
        both = in_ref[...] + in_there_ref[...].astype(jnp.float32)
        in_out[...] = both
        out_out[0] = out_ref[...] + out_there_ref[...].astype(jnp.float32)

    def rows(values):
        return pl.BlockSpec((values.shape[0] // steps, values.shape[1]), lambda i: (i, 0))

    operands = (query, keyval, attn, grad_in, in_there, grad_out, out_there)
    return pl.pallas_call(
        kernel,
        grid=(steps,),
        out_shape=[
            jax.ShapeDtypeStruct(query.shape, jnp.float32),
            jax.ShapeDtypeStruct(keyval.shape, jnp.float32),
            jax.ShapeDtypeStruct(attn.shape, jnp.float32),
            jax.ShapeDtypeStruct(grad_in.shape, jnp.float32),
            jax.ShapeDtypeStruct((1, quarter, features), jnp.float32),
            jax.ShapeDtypeStruct((experts, small.shape[1]), jnp.float32),
        ],
        in_specs=[rows(values) for values in operands]
        + [pl.BlockSpec(small.shape, lambda i: (0, 0))],
        out_specs=[
            rows(query), rows(keyval), rows(attn),
            rows(grad_in),
            pl.BlockSpec((1, quarter // steps, features), lambda i: (0, i, 0)),
            pl.BlockSpec((experts, small.shape[1]), lambda i: (0, 0)),
        ],
        compiler_params=pltpu.CompilerParams(vmem_limit_bytes=VMEM_LIMIT),
        name="widen",
    )(*operands, small)


def gathered_body(
    layer_input, seq_ids, routes, gain_attn, w_query, w_keyval, w_out_attn, gain_ffn, router,
    w_in, w_out, d_out,
):
    me = lax.axis_index("ctx")
    tokens, experts = layer_input.shape[1], router.shape[1]
    x, grad_out = layer_input[0], d_out[0]
    turns = angle_table(me * tokens + jnp.arange(tokens, dtype=jnp.int32))[:, 0]
    cosine, sine = jnp.cos(turns), jnp.sin(turns)
    angles = (
        jnp.concatenate([cosine, cosine], axis=1), jnp.concatenate([-sine, sine], axis=1)
    )
    in_own = jnp.swapaxes(w_in[0], 1, 2).reshape(-1, D)

    (
        query, keyval, level, mixed, hidden, mixed_low, middle, send, gates, w_query_there,
        w_keyval_there, w_out_attn_there, small_there, d_out_all, w_out_there, small,
    ) = attend(
        x, grad_out, router.T, (gain_attn[None], gain_ffn[None]), w_query, w_keyval, w_out_attn,
        w_out[0], angles, seq_ids, routes[0].T,
    )
    projections = (w_query, w_query_there, w_keyval, w_keyval_there)
    returned, results, grad_in, grad_in_other, grad_out_matrix, grad_out_other = run_experts(
        send, d_out_all, in_own, w_out[0], w_out_there, experts
    )
    (
        output, grad_middle, middle_low, middle_there, grad_query, query_there, grad_keyval,
        keyval_there, small_grads, *halves,
    ) = attend_back(
        returned, gates, small, small_there, middle, grad_out, send, w_out_attn, w_out_attn_there,
        query, keyval, angles, seq_ids, level, mixed, hidden, mixed_low, results, experts,
    )
    attn_sum, query_sum, keyval_sum, small_sum, grad_input, in_there, out_there = finish(
        x, grad_middle, small, small_there, small_grads, projections, halves[:2], halves[2:],
        (middle_low, middle_there), (grad_query, query_there),
        (grad_keyval, keyval_there), grad_in_other, grad_out_other,
    )
    query_sum, keyval_sum, attn_sum, grad_w_in, grad_w_out, grad_router = widen(
        query_sum, keyval_sum, attn_sum, grad_in, in_there, grad_out_matrix, out_there, small_sum
    )
    return (
        output[None],
        grad_input[None],
        small_sum[experts],
        query_sum,
        keyval_sum,
        attn_sum,
        small_sum[experts + 1],
        grad_router.T,
        jnp.swapaxes(grad_w_in.reshape(2, -1, D), 1, 2)[None],
        grad_w_out,
    )


def solution(mesh):
    in_specs = (
        P("wa", "ctx", None),
        P("wa", None),
        P("wa", "ctx", None),
        P("wa"),
        P("wa", None),
        P("wa", None),
        P("wa", None),
        P("wa"),
        P("wa", None),
        P("ctx", None, None, "wa"),
        P("ctx", "wa", None),
        P("wa", "ctx", None),
    )
    out_specs = (
        P("wa", "ctx", None),
        P("wa", "ctx", None),
        P("wa"),
        P("wa", None),
        P("wa", None),
        P("wa", None),
        P("wa"),
        P("wa", None),
        P("ctx", None, None, "wa"),
        P("ctx", "wa", None),
    )
    depth = mesh.shape["ctx"]
    body = gathered_body if depth == 16 else routed_body
    return jax.shard_map(body, mesh=mesh, in_specs=in_specs, out_specs=out_specs, check_vma=False)
```

```python
import functools
import math

import jax
import jax.numpy as jnp
from jax import lax
from jax.experimental import pallas as pl
from jax.experimental.pallas import tpu as pltpu
from jax.sharding import PartitionSpec as P

D = 1536
HEADS = 12
KV_HEADS = 2
HEAD_DIM = 128
TOP = 4
BLOCK = 256


EPSILON = 1e-06
THETA = 1000000.0
NEGATIVE = -1e30


def rms_scale(values, gain_vec):
    return (
        values * lax.rsqrt(jnp.mean(values * values, axis=-1, keepdims=True) + EPSILON) * gain_vec
    )


def rotate(values, angles):
    half_dim = values.shape[-1] // 2
    cosine = jnp.cos(angles)
    sine_part = jnp.sin(angles)
    first_half = values[..., :half_dim]
    second = values[..., half_dim:]
    return jnp.concatenate(
        [first_half * cosine - second * sine_part, second * cosine + first_half * sine_part],
        axis=-1,
    )


def angle_table(positions):
    half_dim = HEAD_DIM // 2
    frequency = THETA ** (-2.0 * jnp.arange(half_dim, dtype=jnp.float32) / HEAD_DIM)
    return (positions.astype(jnp.float32)[:, None] * frequency[None, :])[:, None, :]


def gated(stacked):
    return jax.nn.gelu(stacked[..., 0, :], approximate=True) * stacked[..., 1, :]


def over_keys(key_rows, running, advance):
    key_count = key_rows.shape[0]
    key_width = math.gcd(key_count, 512)

    def one_turn(state_now, block_index):
        key_offset = block_index * key_width
        key_part = lax.dynamic_slice_in_dim(key_rows, key_offset, key_width, 0)
        return (advance(state_now, key_part, key_offset), None)

    running, unused = lax.scan(
        one_turn, running, jnp.arange(key_count // key_width, dtype=jnp.int32)
    )
    return running


def routed_body(
    layer_input,
    seq_ids,
    routes,
    gain_attn,
    w_query,
    w_keyval,
    w_out_attn,
    gain_ffn,
    router,
    w_in,
    w_out,
    d_out,
):
    ctx_count = lax.axis_size("ctx")
    ctx_index = lax.axis_index("ctx")
    tokens = layer_input.shape[1]
    length = tokens * ctx_count
    experts_all = ctx_count // 2
    capacity = 2 * tokens * TOP // experts_all
    group = HEADS // KV_HEADS
    kv_width = KV_HEADS * HEAD_DIM
    row_count = group * tokens
    scale = HEAD_DIM ** (-0.5)
    gain_one, query_matrix, keyvalue_matrix, attention_matrix = (
        lax.all_gather(gain_attn, "wa", axis=0, tiled=True),
        lax.all_gather(w_query, "wa", axis=0, tiled=True),
        lax.all_gather(w_keyval, "wa", axis=0, tiled=True),
        lax.all_gather(w_out_attn, "wa", axis=0, tiled=True),
    )
    residual = layer_input[0].astype(jnp.float32)
    normed_one, norm_one_back = jax.vjp(rms_scale, residual, gain_one.astype(jnp.float32))
    hidden_first_norm = normed_one.astype(jnp.bfloat16)
    positions = ctx_index * tokens + jnp.arange(tokens, dtype=jnp.int32)
    angles = angle_table(positions)
    query_projected = jnp.dot(
        hidden_first_norm, query_matrix, preferred_element_type=jnp.float32
    ).reshape(tokens, HEADS, HEAD_DIM)
    keyvalue_projected = jnp.dot(
        hidden_first_norm, keyvalue_matrix, preferred_element_type=jnp.float32
    )
    key_pre = keyvalue_projected[:, :kv_width].reshape(tokens, KV_HEADS, HEAD_DIM)
    query_low = rotate(query_projected, angles).astype(jnp.bfloat16)
    key_low = rotate(key_pre, angles).astype(jnp.bfloat16)
    value_low = keyvalue_projected[:, kv_width:].astype(jnp.bfloat16)
    keyval_send = jnp.concatenate([key_low.reshape(tokens, kv_width), value_low], axis=1)
    query_rows = (
        query_low.reshape(tokens, KV_HEADS, group, HEAD_DIM)
        .transpose(1, 2, 0, 3)
        .reshape(KV_HEADS, row_count, HEAD_DIM)
    )
    doc_row = seq_ids[0]
    query_docs = lax.dynamic_slice_in_dim(doc_row, ctx_index * tokens, tokens, 0)
    query_blocks = positions // BLOCK

    def block_scores(key_part, first_key):
        key_count = key_part.shape[0]
        split_part = key_part.reshape(key_count, 2, KV_HEADS, HEAD_DIM)
        keys_here = split_part[:, 0]
        values_here = split_part[:, 1]
        scores = (
            jnp.einsum("hrd,nhd->hrn", query_rows, keys_here, preferred_element_type=jnp.float32)
            * scale
        )
        key_docs = lax.dynamic_slice_in_dim(doc_row, first_key, key_count, 0)
        key_blocks = (first_key + jnp.arange(key_count, dtype=jnp.int32)) // BLOCK
        allowed = (query_docs[:, None] == key_docs[None, :]) & (
            key_blocks[None, :] <= query_blocks[:, None]
        )
        allowed = jnp.broadcast_to(allowed[None], (group, tokens, key_count)).reshape(
            1, row_count, key_count
        )
        return (jnp.where(allowed, scores, NEGATIVE), allowed, keys_here, values_here)

    def probs_of(masked, allowed, largest, totals):
        return jnp.where(allowed, jnp.exp(masked - largest[..., None]) / totals[..., None], 0.0)

    def stats_step(running, key_part, first_key):
        largest, totals = running
        masked, allowed, keys_here, values_here = block_scores(key_part, first_key)
        new_largest = jnp.maximum(largest, jnp.max(masked, axis=-1))
        weights = jnp.where(allowed, jnp.exp(masked - new_largest[..., None]), 0.0)
        return (new_largest, totals * jnp.exp(largest - new_largest) + jnp.sum(weights, axis=-1))

    start_stats = (
        jnp.full((KV_HEADS, row_count), NEGATIVE, jnp.float32),
        jnp.zeros((KV_HEADS, row_count), jnp.float32),
    )
    largest, totals = over_keys(
        lax.all_gather(keyval_send, "ctx", axis=0, tiled=True), start_stats, stats_step
    )

    def values_step(running, key_part, first_key):
        masked, allowed, keys_here, values_here = block_scores(key_part, first_key)
        probs_low = probs_of(masked, allowed, largest, totals).astype(jnp.bfloat16)
        return running + jnp.einsum(
            "hrn,nhd->hrd", probs_low, values_here, preferred_element_type=jnp.float32
        )

    start_values = jnp.zeros((KV_HEADS, row_count, HEAD_DIM), jnp.float32)
    mixed_rows = over_keys(
        lax.all_gather(keyval_send, "ctx", axis=0, tiled=True), start_values, values_step
    )
    mixed_low = (
        mixed_rows.reshape(KV_HEADS, group, tokens, HEAD_DIM)
        .transpose(2, 0, 1, 3)
        .reshape(tokens, HEADS * HEAD_DIM)
        .astype(jnp.bfloat16)
    )
    middle_activation = residual + jnp.dot(
        mixed_low, attention_matrix, preferred_element_type=jnp.float32
    )
    gain_two, router_full, w_in_full, w_out_full = (
        lax.all_gather(gain_ffn, "wa", axis=0, tiled=True),
        lax.all_gather(router, "wa", axis=0, tiled=True),
        lax.all_gather(w_in, "wa", axis=3, tiled=True),
        lax.all_gather(w_out, "wa", axis=1, tiled=True),
    )
    in_half = w_in_full[0]
    out_half = w_out_full[0]
    normed_two, norm_two_back = jax.vjp(rms_scale, middle_activation, gain_two.astype(jnp.float32))
    hidden_second_norm = normed_two.astype(jnp.bfloat16)
    router_logits = jnp.dot(hidden_second_norm, router_full, preferred_element_type=jnp.float32)
    route_ids = routes[0]

    def gate_values(logit_rows):
        return jax.nn.softmax(jnp.take_along_axis(logit_rows, route_ids, axis=-1), axis=-1)

    gates, gate_back = jax.vjp(gate_values, router_logits)
    flat_ids = route_ids.reshape(tokens * TOP)
    expert_hits = (flat_ids[:, None] == jnp.arange(experts_all, dtype=jnp.int32)[None, :]).astype(
        jnp.int32
    )
    ranks = jnp.sum(expert_hits * (jnp.cumsum(expert_hits, axis=0) - expert_hits), axis=1)
    slot_first = 2 * flat_ids * capacity + ranks
    slot_second = slot_first + capacity
    slot_total = ctx_count * capacity
    slot_numbers = jnp.arange(slot_total, dtype=jnp.int32)[:, None]
    placed = (
        (slot_first[None, :] == slot_numbers) | (slot_second[None, :] == slot_numbers)
    ).astype(jnp.bfloat16)
    dispatch = jnp.sum(placed.reshape(slot_total, tokens, TOP), axis=2)
    send_rows = (
        jnp.dot(dispatch, hidden_second_norm, preferred_element_type=jnp.float32)
        .astype(jnp.bfloat16)
        .reshape(ctx_count, capacity, D)
    )
    arrived = lax.all_to_all(send_rows, "ctx", split_axis=0, concat_axis=0, tiled=True)
    stacked = jnp.einsum("ncd,gdf->ncgf", arrived, in_half, preferred_element_type=jnp.float32)
    hidden_low = gated(stacked).astype(jnp.bfloat16)
    result = jnp.einsum(
        "ncf,fd->ncd", hidden_low, out_half, preferred_element_type=jnp.float32
    ).astype(jnp.bfloat16)
    returned_rows = lax.all_to_all(result, "ctx", split_axis=0, concat_axis=0, tiled=True)
    returned_flat = returned_rows.reshape(slot_total, D)
    pair_rows = (
        returned_flat[slot_first].astype(jnp.float32)
        + returned_flat[slot_second].astype(jnp.float32)
    ).reshape(tokens, TOP, D)
    output = (middle_activation + jnp.sum(gates[:, :, None] * pair_rows, axis=1)).astype(
        jnp.bfloat16
    )
    grad_out = d_out[0].astype(jnp.float32)
    grad_gates = jnp.sum(pair_rows * grad_out[:, None, :], axis=-1)
    (grad_logits,) = gate_back(grad_gates)
    grad_logits_low = grad_logits.astype(jnp.bfloat16)
    gate_slots = jnp.dot(
        placed.astype(jnp.float32), gates.reshape(tokens * TOP), precision=lax.Precision.HIGHEST
    )
    routed_grad = jnp.dot(dispatch, d_out[0], preferred_element_type=jnp.float32)
    grad_send_rows = (
        (gate_slots[:, None] * routed_grad).astype(jnp.bfloat16).reshape(ctx_count, capacity, D)
    )
    grad_arrived = lax.all_to_all(grad_send_rows, "ctx", split_axis=0, concat_axis=0, tiled=True)
    grad_hidden = jnp.einsum(
        "ncd,fd->ncf", grad_arrived, out_half, preferred_element_type=jnp.float32
    )
    hidden_again, gated_back = jax.vjp(gated, stacked)
    (grad_stacked,) = gated_back(grad_hidden)
    grad_stacked_low = grad_stacked.astype(jnp.bfloat16)
    grad_rows = jnp.einsum(
        "ncgf,gdf->ncd", grad_stacked_low, in_half, preferred_element_type=jnp.float32
    ).astype(jnp.bfloat16)
    grad_returned = lax.all_to_all(grad_rows, "ctx", split_axis=0, concat_axis=0, tiled=True)
    grad_w_in = jnp.einsum(
        "ncd,ncgf->gdf", arrived, grad_stacked_low, preferred_element_type=jnp.float32
    )[None]
    grad_w_out = jnp.einsum(
        "ncf,ncd->fd",
        hidden_again.astype(jnp.bfloat16),
        grad_arrived,
        preferred_element_type=jnp.float32,
    )[None]
    grad_hidden_two = jnp.einsum(
        "st,sd->td",
        dispatch,
        grad_returned.reshape(slot_total, D),
        preferred_element_type=jnp.float32,
    )
    grad_hidden_two = grad_hidden_two + jnp.dot(
        grad_logits_low, router_full.T, preferred_element_type=jnp.float32
    )
    grad_router = jnp.dot(hidden_second_norm.T, grad_logits_low, preferred_element_type=jnp.float32)
    grad_middle_norm, grad_gain_two = norm_two_back(grad_hidden_two)
    grad_middle = grad_out + grad_middle_norm
    grad_middle_low = grad_middle.astype(jnp.bfloat16)
    grad_attn_weight = jnp.dot(mixed_low.T, grad_middle_low, preferred_element_type=jnp.float32)
    grad_mixed = jnp.dot(
        grad_middle_low, attention_matrix.T, preferred_element_type=jnp.float32
    ).astype(jnp.bfloat16)
    grad_rows_out = (
        grad_mixed.reshape(tokens, KV_HEADS, group, HEAD_DIM)
        .transpose(1, 2, 0, 3)
        .reshape(KV_HEADS, row_count, HEAD_DIM)
    )
    delta = jnp.sum(grad_rows_out.astype(jnp.float32) * mixed_rows, axis=-1)

    def score_grads(key_part, first_key):
        masked, allowed, keys_here, values_here = block_scores(key_part, first_key)
        probs = probs_of(masked, allowed, largest, totals)
        grad_probs = jnp.einsum(
            "hrd,nhd->hrn", grad_rows_out, values_here, preferred_element_type=jnp.float32
        )
        grad_scores = (probs * (grad_probs - delta[..., None])).astype(jnp.bfloat16)
        return (grad_scores, probs.astype(jnp.bfloat16), keys_here)

    def key_terms(grad_scores, probs_low, key_count):
        grad_keys = (
            jnp.einsum("hrn,hrd->nhd", grad_scores, query_rows, preferred_element_type=jnp.float32)
            * scale
        )
        grad_values = jnp.einsum(
            "hrn,hrd->nhd", probs_low, grad_rows_out, preferred_element_type=jnp.float32
        )
        return jnp.concatenate(
            [grad_keys.reshape(key_count, kv_width), grad_values.reshape(key_count, kv_width)],
            axis=1,
        )

    start_query = jnp.zeros((KV_HEADS, row_count, HEAD_DIM), jnp.float32)

    def back_step(running, key_part, first_key):
        grad_query_rows, grad_keyvals = running
        grad_scores, probs_low, keys_here = score_grads(key_part, first_key)
        grad_query_rows = (
            grad_query_rows
            + jnp.einsum("hrn,nhd->hrd", grad_scores, keys_here, preferred_element_type=jnp.float32)
            * scale
        )
        fresh = key_terms(grad_scores, probs_low, key_part.shape[0])
        return (grad_query_rows, lax.dynamic_update_slice_in_dim(grad_keyvals, fresh, first_key, 0))

    start_back = (start_query, jnp.zeros((length, 2 * kv_width), jnp.float32))
    grad_query_rows, grad_keyvals = over_keys(
        lax.all_gather(keyval_send, "ctx", axis=0, tiled=True), start_back, back_step
    )
    grad_keyval_mine = lax.psum_scatter(grad_keyvals, "ctx", scatter_dimension=0, tiled=True)
    grad_query = grad_query_rows.reshape(KV_HEADS, group, tokens, HEAD_DIM).transpose(2, 0, 1, 3)
    grad_query_pre = (
        rotate(grad_query.reshape(tokens, HEADS, HEAD_DIM), -angles)
        .reshape(tokens, HEADS * HEAD_DIM)
        .astype(jnp.bfloat16)
    )
    grad_key_pre = rotate(
        grad_keyval_mine[:, :kv_width].reshape(tokens, KV_HEADS, HEAD_DIM), -angles
    ).reshape(tokens, kv_width)
    grad_keyval_pre = jnp.concatenate(
        [grad_key_pre, grad_keyval_mine[:, kv_width:]], axis=1
    ).astype(jnp.bfloat16)
    grad_hidden_one = jnp.dot(
        grad_query_pre, query_matrix.T, preferred_element_type=jnp.float32
    ) + jnp.dot(grad_keyval_pre, keyvalue_matrix.T, preferred_element_type=jnp.float32)
    grad_query_weight = jnp.dot(
        hidden_first_norm.T, grad_query_pre, preferred_element_type=jnp.float32
    )
    grad_keyval_weight = jnp.dot(
        hidden_first_norm.T, grad_keyval_pre, preferred_element_type=jnp.float32
    )
    grad_residual_norm, grad_gain_one = norm_one_back(grad_hidden_one)
    grad_input = (grad_middle + grad_residual_norm).astype(jnp.bfloat16)
    shares = (
        lax.psum_scatter(
            grad_gain_one.astype(jnp.bfloat16), "wa", scatter_dimension=0, tiled=True
        ).astype(jnp.float32),
        lax.psum_scatter(
            grad_query_weight.astype(jnp.bfloat16), "wa", scatter_dimension=0, tiled=True
        ).astype(jnp.float32),
        lax.psum_scatter(
            grad_keyval_weight.astype(jnp.bfloat16), "wa", scatter_dimension=0, tiled=True
        ).astype(jnp.float32),
        lax.psum_scatter(
            grad_attn_weight.astype(jnp.bfloat16), "wa", scatter_dimension=0, tiled=True
        ).astype(jnp.float32),
        lax.psum_scatter(
            grad_gain_two.astype(jnp.bfloat16), "wa", scatter_dimension=0, tiled=True
        ).astype(jnp.float32),
        lax.psum_scatter(
            grad_router.astype(jnp.bfloat16), "wa", scatter_dimension=0, tiled=True
        ).astype(jnp.float32),
        lax.psum_scatter(
            grad_w_in.astype(jnp.bfloat16), "wa", scatter_dimension=3, tiled=True
        ).astype(jnp.float32),
        lax.psum_scatter(
            grad_w_out.astype(jnp.bfloat16), "wa", scatter_dimension=1, tiled=True
        ).astype(jnp.float32),
    )
    summed = lax.psum((shares[0], shares[1], shares[2], shares[3], shares[4], shares[5]), "ctx")
    return (
        output[None],
        grad_input[None],
        summed[0],
        summed[1],
        summed[2],
        summed[3],
        summed[4],
        summed[5],
        shares[6],
        shares[7],
    )

MESH = pl.DeviceIdType.MESH
VMEM_LIMIT = 60 * 1024 * 1024


def chip_place():
    count = lax.axis_size("ctx")
    me = lax.axis_index("ctx")
    return me // 4, lax.rem(me // 2, 2), lax.rem(me, 2), count // 4


def ctx_of(z, y, c):
    return (z * 2 + y) * 2 + c


def greet(across_x=False):
    z, y, c, depth = chip_place()
    barrier = pltpu.get_barrier_semaphore()

    def signal(device):
        pl.semaphore_signal(barrier, 1, device_id=device, device_id_type=MESH)

    signal({"ctx": ctx_of(z, y, 1 - c)})
    signal({"ctx": ctx_of(z, 1 - y, c)})
    if across_x:
        signal({"wa": 1 - lax.axis_index("wa")})
    pl.when(z > 0)(lambda: signal({"ctx": ctx_of(z - 1, y, c)}))
    pl.when(z < depth - 1)(lambda: signal({"ctx": ctx_of(z + 1, y, c)}))
    ends = (z > 0).astype(jnp.int32) + (z < depth - 1).astype(jnp.int32)
    pl.semaphore_wait(barrier, (3 if across_x else 2) + ends)


def remote(source, target_ref, sems, at, device):
    return pltpu.make_async_remote_copy(
        src_ref=source,
        dst_ref=target_ref,
        send_sem=sems.at[(0,) + at],
        recv_sem=sems.at[(1,) + at],
        device_id=device,
        device_id_type=MESH,
    )


def each(step, act):
    z, _, _, depth = chip_place()
    if step == 0:
        act(z)
    else:
        pl.when(z + step < depth)(lambda: act(z + step))
        pl.when(z - step >= 0)(lambda: act(z - step))


def nearest(k):
    z, _, _, depth = chip_place()
    low = jnp.minimum(z, depth - 1 - z)
    step = (k + 1) // 2
    place = jnp.where(k > 2 * low, k, jnp.where(lax.rem(k, 2) == 1, low - step, low + step))
    return jnp.where(z == low, place, depth - 1 - place)


class Gather:
    def __init__(self, out, rows, sems, part=0, parts=1):
        self.out, self.block, self.rows = out, rows, rows // parts
        self.first = part * self.rows
        self.z_sems, self.y_sems, self.c_sems = sems
        self.z, self.y, self.c, self.depth = chip_place()

    @staticmethod
    def sems(depth):
        return [
            pltpu.SemaphoreType.DMA((2, 2, depth)),
            pltpu.SemaphoreType.DMA((2, depth)),
            pltpu.SemaphoreType.DMA((2, 2 * depth)),
        ]

    def slot(self, z, y, c):
        start = ctx_of(z, y, c) * self.block + self.first
        return self.out.at[pl.ds(pl.multiple_of(start, 16), self.rows)]

    def own(self):
        return self.slot(self.z, self.y, self.c)

    def on_z(self, way, of_z, source=None):
        goal = jnp.minimum(self.z + 1, self.depth - 1) if way == 0 else jnp.maximum(self.z - 1, 0)
        block = self.slot(of_z, self.y, self.c)
        target = {"ctx": ctx_of(goal, self.y, self.c)}
        return remote(block if source is None else source, block, self.z_sems, (way, of_z), target)

    def on_y(self, of_z, mine=True, source=None):
        block = self.slot(of_z, self.y if mine else 1 - self.y, self.c)
        target = {"ctx": ctx_of(self.z, 1 - self.y, self.c)}
        return remote(block if source is None else source, block, self.y_sems, (of_z,), target)

    def on_core(self, of_z, of_y, mine=True, source=None):
        block = self.slot(of_z, of_y, self.c if mine else 1 - self.c)
        target = {"ctx": ctx_of(self.z, self.y, 1 - self.c)}
        at = (of_z * 2 + of_y,)
        return remote(block if source is None else source, block, self.c_sems, at, target)

    def start(self, source=None):
        z, depth = self.z, self.depth
        if source is not None:
            source = source.at[pl.ds(self.first, self.rows)]
        pl.when(z < depth - 1)(lambda: self.on_z(0, z, source).start())
        pl.when(z > 0)(lambda: self.on_z(1, z, source).start())
        self.on_y(z, source=source).start()
        self.on_core(z, self.y, source=source).start()

    def along_z(self, step):
        z, depth = self.z, self.depth

        def from_side(way, of_z, more):
            self.on_z(way, of_z).wait_recv()
            pl.when(more)(lambda: self.on_z(way, of_z).start())
            self.on_y(of_z).start()
            self.on_core(of_z, self.y).start()

        pl.when(z - step >= 0)(lambda: from_side(0, z - step, z < depth - 1))
        pl.when(z + step < depth)(lambda: from_side(1, z + step, z > 0))

    def along_y(self, step):
        def across(of_z):
            self.on_y(of_z, mine=False).wait_recv()
            self.on_core(of_z, 1 - self.y).start()

        each(step, across)

    def take_core(self, of_z):
        for of_y in range(2):
            self.on_core(of_z, of_y, mine=False).wait_recv()

    def finish(self, *taken):
        z, depth = self.z, self.depth
        for of_z in range(depth):
            pl.when((z < depth - 1) & (of_z <= z))(lambda: self.on_z(0, of_z).wait_send())
            pl.when((z > 0) & (of_z >= z))(lambda: self.on_z(1, of_z).wait_send())
            self.on_y(of_z).wait_send()
            for of_y in range(2):
                self.on_core(of_z, of_y).wait_send()
            open_still = of_z >= 0
            for one in taken:
                open_still = (of_z != one) & open_still
            pl.when(open_still)(lambda: self.take_core(of_z))


class Several:
    def __init__(self, members):
        self.members = members

    def __getattr__(self, name):
        def every(*given, **named):
            for member in self.members:
                getattr(member, name)(*given, **named)

        return every


def gather_parts(out, rows, sems, parts):
    return Several(
        [Gather(out, rows, sems[3 * i : 3 * i + 3], i, parts) for i in range(parts)]
    )


def follow(gather):
    depth = chip_place()[3]
    gather.along_z(1)
    for step in range(depth):
        if step >= 1 and step + 1 < depth:
            gather.along_z(step + 1)
        gather.along_y(step)
    gather.finish()


def add_into(target, terms, rows):
    some = 32 if rows % 32 == 0 else 48 if rows % 48 == 0 else 16

    @pl.loop(0, rows // some)
    def _(turn):
        at = pl.ds(pl.multiple_of(turn * some, 16), some)
        total = terms[0][at, :].astype(jnp.float32)
        for term in terms[1:]:
            total = total + term[at, :].astype(jnp.float32)
        target[at, :] = total.astype(target.dtype)


class Scatter:
    def __init__(self, part, scratch, sums=None, piece=0, pieces=1):
        self.part = part
        self.from_core, self.totals, self.from_y, self.from_z = scratch[:4]
        self.sums = self.totals if sums is None else sums
        self.c_sems, self.y_sems, self.z_sems = scratch[4:]
        self.block = self.totals.shape[1]
        self.rows = self.block // pieces
        self.first = piece * self.rows
        self.z, self.y, self.c, self.depth = chip_place()

    @staticmethod
    def sems(depth):
        return [
            pltpu.SemaphoreType.DMA((2, 2 * depth)),
            pltpu.SemaphoreType.DMA((2, depth)),
            pltpu.SemaphoreType.DMA((2, 2, depth)),
        ]

    @staticmethod
    def scratch(depth, rows, columns, pieces=1):
        return [
            pltpu.VMEM((2 * depth, rows, columns), jnp.bfloat16),
            pltpu.VMEM((2 * depth, rows, columns), jnp.bfloat16),
            pltpu.VMEM((depth, rows, columns), jnp.bfloat16),
            pltpu.VMEM((depth + 1, rows, columns), jnp.bfloat16),
        ] + Scatter.sems(depth) * pieces

    def of(self, ref, place):
        return ref.at[place, pl.ds(self.first, self.rows)]

    def split(self):
        return len(self.part.shape) == 3

    def share(self, chip, c):
        start = (chip * 2 + c) * self.block + self.first
        return self.part.at[pl.ds(pl.multiple_of(start, 16), self.rows)]

    def on_core(self, chip):
        target = {"ctx": ctx_of(self.z, self.y, 1 - self.c)}
        source = self.of(self.part, chip) if self.split() else self.share(chip, 1 - self.c)
        return remote(source, self.of(self.from_core, chip), self.c_sems, (chip,), target)

    def send_core(self, chip):
        self.on_core(chip).start()

    def send_y(self, of_z):
        self.on_y(of_z).start()

    def on_y(self, of_z):
        target = {"ctx": ctx_of(self.z, 1 - self.y, self.c)}
        source = self.of(self.sums, of_z * 2 + 1 - self.y)
        return remote(source, self.of(self.from_y, of_z), self.y_sems, (of_z,), target)

    def on_z(self, way, of_z):
        goal = jnp.minimum(self.z + 1, self.depth - 1) if way == 0 else jnp.maximum(self.z - 1, 0)
        place = of_z if way == 0 else jnp.where(of_z == goal, self.depth, of_z)
        source = self.of(self.totals, of_z * 2 + self.y)
        target = {"ctx": ctx_of(goal, self.y, self.c)}
        return remote(source, self.of(self.from_z, place), self.z_sems, (way, of_z), target)

    def start(self):
        def send(of_z):
            self.on_core(of_z * 2 + 1 - self.y).start()
            self.on_core(of_z * 2 + self.y).start()

        for step in range(self.depth - 1, -1, -1):
            each(step, send)

    def add_chip(self, of_z, other, send=True):
        chip = of_z * 2 + (1 - self.y if other else self.y)
        self.on_core(chip).wait_recv()
        total = self.of(self.sums, chip)
        own = total if self.split() else self.share(chip, self.c)
        add_into(total, (own, self.of(self.from_core, chip)), self.rows)
        if other and send:
            self.on_y(of_z).start()

    def add_cores(self, step):
        def add(of_z):
            self.add_chip(of_z, True)
            self.add_chip(of_z, False)

        each(step, add)

    def add_y_of(self, of_z):
        z, depth = self.z, self.depth
        self.on_y(of_z).wait_recv()
        place = of_z * 2 + self.y
        total, own = self.of(self.totals, place), self.of(self.sums, place)
        other = self.of(self.from_y, of_z)
        upward, downward = (of_z > z) & (z > 0), (of_z < z) & (z < depth - 1)
        pl.when(upward)(lambda: self.on_z(0, of_z).wait_recv())
        pl.when(downward)(lambda: self.on_z(1, of_z).wait_recv())

        @pl.when(upward | downward)
        def _():
            add_into(total, (own, other, self.of(self.from_z, of_z)), self.rows)

        @pl.when(jnp.logical_not(upward | downward))
        def _():
            add_into(total, (own, other), self.rows)

        pl.when(of_z > z)(lambda: self.on_z(0, of_z).start())
        pl.when(of_z < z)(lambda: self.on_z(1, of_z).start())

    def add_y(self, step):
        each(step, self.add_y_of)

    def last(self, result):
        z, depth = self.z, self.depth
        own = self.of(self.totals, z * 2 + self.y)
        low, high = self.of(self.from_z, z), self.of(self.from_z, depth)
        result = result.at[pl.ds(self.first, self.rows)]
        pl.when(z > 0)(lambda: self.on_z(0, z).wait_recv())
        pl.when(z < depth - 1)(lambda: self.on_z(1, z).wait_recv())
        inside = (z > 0) & (z < depth - 1)
        pl.when(inside)(lambda: add_into(result, (own, low, high), self.rows))
        pl.when(z == 0)(lambda: add_into(result, (own, high), self.rows))
        pl.when(z == depth - 1)(lambda: add_into(result, (own, low), self.rows))

    def finish(self, cores=True):
        for of_z in range(self.depth):
            self.on_y(of_z).wait_send()
            if cores:
                self.on_core(of_z * 2).wait_send()
                self.on_core(of_z * 2 + 1).wait_send()
            pl.when(of_z > self.z)(lambda: self.on_z(0, of_z).wait_send())
            pl.when(of_z < self.z)(lambda: self.on_z(1, of_z).wait_send())


def scatter_parts(part, scratch, pieces, sums=None):
    arrays, sems = tuple(scratch[:4]), tuple(scratch[4:])
    return Several(
        [
            Scatter(part, arrays + sems[3 * i : 3 * i + 3], sums, i, pieces)
            for i in range(pieces)
        ]
    )


def call(
    kernel, out, scratch, number, name, *operands, outside=(), outside_out=(), late=(), early=()
):
    many = isinstance(out, (tuple, list))
    count, results = len(operands), len(out) if many else 1
    late, early = tuple(late), tuple(early)
    more = len(late) + len(early) + 1

    def spec(position, far):
        return pl.BlockSpec(memory_space=pl.ANY if position in far else pltpu.VMEM)

    def moving(*refs):
        near, sems = refs[-more:-1], refs[-1]
        loads = {
            i: pltpu.make_async_copy(refs[i], near[k], sems.at[k]) for k, i in enumerate(late)
        }
        stores = {
            i: pltpu.make_async_copy(near[k], refs[count + i], sems.at[k])
            for k, i in enumerate(early, len(late))
        }
        for copy in loads.values():
            copy.start()
        held = [near[late.index(i)] if i in late else refs[i] for i in range(count)]
        given = [
            near[len(late) + early.index(i)] if i in early else refs[count + i]
            for i in range(results)
        ]

        def arrive(*which):
            for i in which:
                loads[i].wait()

        def leave(*which):
            for i in which:
                stores[i].start()

        helpers = (arrive, leave) if early else (arrive,)
        kernel(*helpers, *held, *given, *refs[count + results : -more])
        for copy in stores.values():
            copy.wait()

    if late or early:
        scratch = list(scratch) + [pltpu.VMEM(operands[i].shape, operands[i].dtype) for i in late]
        scratch += [pltpu.VMEM(out[i].shape, out[i].dtype) for i in early]
        scratch.append(pltpu.SemaphoreType.DMA((more - 1,)))
    far, far_out = tuple(outside) + late, tuple(outside_out) + early
    out_specs = [spec(i, far_out) for i in range(results)]
    return pl.pallas_call(
        moving if late or early else kernel,
        out_shape=out,
        in_specs=[spec(i, far) for i in range(count)],
        out_specs=out_specs if many else out_specs[0],
        scratch_shapes=scratch,
        compiler_params=pltpu.CompilerParams(
            collective_id=number,
            has_side_effects=number is not None,
            vmem_limit_bytes=VMEM_LIMIT,
        ),
        name=name,
    )(*operands)


class Relay:
    def __init__(self, source, out, sems, parts=1, paired=False):
        self.source, self.out, self.sems, self.parts = source, out, sems, parts
        self.paired = paired
        self.z, self.y, self.c, _ = chip_place()
        self.odd = lax.rem(self.z, 2)
        self.rows = source.shape[0] // ((4 if paired else 2) * parts)

    @staticmethod
    def semaphores():
        return pltpu.SemaphoreType.DMA((2, 8))

    def block(self, ref, part, c, odd):
        place = (c * 2 + odd if self.paired else c) * self.parts + part
        return ref.at[pl.ds(pl.multiple_of(place * self.rows, 16), self.rows)]

    def on_x(self, part):
        source = self.block(self.source, part, self.c, self.odd)
        target = self.block(self.out, part, self.c, self.odd)
        return remote(source, target, self.sems, (part,), {"wa": 1 - lax.axis_index("wa")})

    def on_core(self, part, c, other_z=False):
        block = self.block(self.out, part, c, 1 - self.odd if other_z else self.odd)
        at = ((4 if other_z else 2) + part,)
        return remote(block, block, self.sems, at, {"ctx": ctx_of(self.z, self.y, 1 - self.c)})

    def on_pair(self, part, mine=True):
        block = self.block(self.out, part, self.c, self.odd if mine else 1 - self.odd)
        target = {"ctx": ctx_of(self.z + 1 - 2 * self.odd, self.y, self.c)}
        return remote(block, block, self.sems, (6 + part,), target)

    def start(self):
        for part in range(self.parts):
            self.on_x(part).start()

    def pass_on(self, part=0):
        self.on_x(part).wait_recv()
        if self.paired:
            self.on_pair(part).start()
        self.on_core(part, self.c).start()

    def pass_on_pair(self, part):
        self.on_pair(part, mine=False).wait_recv()
        self.on_core(part, self.c, other_z=True).start()

    def finish(self):
        for part in range(self.parts):
            self.on_x(part).wait_send()
            self.on_core(part, self.c).wait_send()
            self.on_core(part, 1 - self.c).wait_recv()
            if self.paired:
                self.on_pair(part).wait_send()
                self.on_core(part, self.c, other_z=True).wait_send()
                self.on_core(part, 1 - self.c, other_z=True).wait_recv()


def rows_by_rows(left, right):
    return lax.dot_general(
        left, right, (((1,), (1,)), ((), ())), preferred_element_type=jnp.float32
    )


def columns_by_columns(left, right):
    return lax.dot_general(
        left, right, (((0,), (0,)), ((), ())), preferred_element_type=jnp.float32
    )


def down(row):
    return jnp.transpose(jnp.broadcast_to(row.astype(jnp.float32), (128, 128)))


def allowed_bias(doc_row, tokens):
    keys, me = doc_row.shape[1], lax.axis_index("ctx")
    own = down(doc_row[:, pl.ds(pl.multiple_of(me * tokens, 128), tokens)])[:, :1]
    key_block = lax.broadcasted_iota(jnp.int32, (tokens, keys), 1) // BLOCK
    same = doc_row[...].astype(jnp.float32) == own
    return jnp.where(same & (key_block <= me * tokens // BLOCK), 0.0, NEGATIVE)


def chosen_by(routes, lanes, experts):
    numbers = lax.rem(lanes, experts).astype(jnp.float32)
    found = down(routes[:1]) == numbers
    for k in range(1, routes.shape[0]):
        found = found | (down(routes[k : k + 1]) == numbers)
    return found & (lanes < 2 * experts)


def side_columns(own):
    side = lax.axis_index("wa")
    return pl.ds(pl.multiple_of((side if own else 1 - side) * (D // 2), 128), D // 2)


def turned(values, cosine, sine):
    heads = []
    for head in range(values.shape[1] // HEAD_DIM):
        one = values[:, head * HEAD_DIM : (head + 1) * HEAD_DIM]
        heads.append(one * cosine + pltpu.roll(one, HEAD_DIM // 2, axis=1) * sine)
    return jnp.concatenate(heads, axis=1)


def normed(values, gain_vec):
    return values * lax.rsqrt(jnp.mean(values * values, axis=-1, keepdims=True) + EPSILON) * gain_vec


def fill_small(full, small, small_there):
    full[:, side_columns(True)] = small[...].astype(jnp.float32)
    full[:, side_columns(False)] = small_there[...].astype(jnp.float32)


def router_block(full, experts):
    rows = full[:experts]
    spare = jnp.zeros((128 - 2 * experts, rows.shape[1]), jnp.float32)
    return jnp.concatenate([rows, rows, spare], axis=0).astype(jnp.bfloat16)


def attend(
    x, d_out, router, gains, w_query, w_keyval, w_out_attn, w_out, angles, doc_row, routes
):
    count, tokens, features = lax.axis_size("ctx"), x.shape[0], x.shape[1]
    depth, length = count // 4, count * tokens
    kv_columns, experts = w_keyval.shape[1], router.shape[0]
    small_shape = (2 * experts, router.shape[1])

    def kernel(
        arrive, leave, x_ref, router_ref, query_own, keyval_own, attn_own, d_out_far, query_far,
        keyval_far, attn_far, out_far, cosine_ref, sine_ref, doc_row_ref, routes_ref, gain_one, gain_two,
        query, keyval, level, mixed, hidden, mixed_low, middle, send, gates_out, query_other,
        keyval_other, attn_other, small_there, d_out_all, out_other,
        small_ref,
        filled, full, stacked, bias, query_sems, keyval_sems, attn_sems, small_sems, own_sem, *sems,
    ):
        gather = gather_parts(keyval, tokens, sems[:6], 2)
        spread = gather_parts(d_out_all, tokens, sems[6:], 2)
        query_relay = Relay(query_far, query_other, query_sems, parts=2)
        keyval_relay = Relay(keyval_far, keyval_other, keyval_sems)
        attn = Relay(attn_far, attn_other, attn_sems, parts=2, paired=True)
        partner = {"wa": 1 - lax.axis_index("wa")}
        swap = remote(small_ref, small_there, small_sems, (0,), partner)
        swap_out = remote(out_far, out_other, small_sems, (1,), partner)
        keep = pltpu.make_async_copy(
            d_out_far, Gather(d_out_all, tokens, sems[6:9]).own(), own_sem.at[0]
        )
        keep.start()
        filled[...] = jnp.zeros_like(filled)
        filled[:experts] = router_ref[...].astype(jnp.float32)
        filled[experts : experts + 1] = gain_one[...].astype(jnp.float32)
        filled[experts + 1 : experts + 2] = gain_two[...].astype(jnp.float32)
        small_ref[...] = filled[...].astype(jnp.bfloat16)
        greet(across_x=True)
        swap.start()
        keyval_relay.start()
        query_relay.start()
        attn.start()
        swap_out.start()
        spread.start(d_out_far)
        swap.wait()
        fill_small(full, small_ref, small_there)
        residual = x_ref[...].astype(jnp.float32)
        hidden[...] = normed(residual, full[experts : experts + 1]).astype(jnp.bfloat16)
        own, other = hidden[:, side_columns(True)], hidden[:, side_columns(False)]
        cosine, sine = cosine_ref[...], sine_ref[...]

        def onto(matrix, matrix_other):
            return jnp.dot(own, matrix[...], preferred_element_type=jnp.float32) + jnp.dot(
                other, matrix_other[...], preferred_element_type=jnp.float32
            )

        bias[...] = allowed_bias(doc_row_ref, tokens)
        spread.along_z(1)
        spread.along_y(0)
        keyval_relay.pass_on()
        keyval_relay.finish()
        arrive(3)
        pre = onto(keyval_own, keyval_other)
        keys = turned(pre[:, : kv_columns // 2], cosine, sine)
        block = jnp.concatenate([keys, pre[:, kv_columns // 2 :]], axis=1)
        Gather(keyval, tokens, sems[:3]).own()[...] = block.astype(jnp.bfloat16)
        leave(4, 10)
        spread.along_z(2)
        spread.along_y(1)
        query_relay.pass_on(0)
        spread.along_z(3)
        gather.start()
        gather.along_z(1)
        spread.along_y(2)
        gather.along_y(0)
        gather.along_z(2)
        query_relay.pass_on(1)
        spread.along_y(3)
        gather.along_y(1)
        gather.along_z(3)
        query_relay.finish()
        arrive(2)
        query[...] = turned(onto(query_own, query_other), cosine, sine).astype(jnp.bfloat16)
        for head in range(HEADS):
            rows = slice(head * tokens, (head + 1) * tokens)
            stacked[rows, :] = query[:, head * 128 : (head + 1) * 128]
        leave(0, 9)
        attn.pass_on(0)
        gather.along_y(2)
        gather.along_y(3)
        gather.finish()
        leave(1)

        @pl.loop(0, HEADS // 2)
        def _(pair):
            rows = pl.ds(pl.multiple_of(pair * 2 * tokens, 128), 2 * tokens)
            kind = pair // (HEADS // KV_HEADS // 2)
            key_part = keyval[:, pl.ds(pl.multiple_of(kind * 128, 128), 128)]
            val_part = keyval[:, pl.ds(pl.multiple_of(kind * 128 + 256, 128), 128)]
            scores = rows_by_rows(stacked[rows, :], key_part) * HEAD_DIM**-0.5
            scores = (scores.reshape(2, tokens, -1) + bias[...][None]).reshape(scores.shape)
            top = jnp.max(scores, axis=-1, keepdims=True)
            weights = jnp.exp(scores - top)
            total = jnp.sum(weights, axis=-1, keepdims=True)
            probs = (weights * (1 / total)).astype(jnp.bfloat16)
            mixture = jnp.dot(probs, val_part, preferred_element_type=jnp.float32)
            for part in range(2):
                columns = pl.ds(pl.multiple_of((pair * 2 + part) * 128, 128), 128)
                mixed[:, columns] = mixture[part * tokens : (part + 1) * tokens]
            column = jnp.broadcast_to(top + jnp.log(total), (2 * tokens, 128))
            level[pl.ds(pair, 1), :] = jnp.transpose(column)[:1]
            pl.when(pair == 1)(lambda: attn.pass_on(1))
            pl.when(pair == 4)(lambda: attn.pass_on_pair(0))

        mixed_low[...] = mixed[...].astype(jnp.bfloat16)
        leave(3, 5)
        attn.pass_on_pair(1)
        own, other = mixed_low[:, side_columns(True)], mixed_low[:, side_columns(False)]
        arrive(4)
        attn.finish()
        leave(11)
        middle[...] = residual + onto(attn_own, attn_other)
        hidden_two = normed(middle[...], full[experts + 1 : experts + 2]).astype(jnp.bfloat16)
        send[:, :features] = hidden_two
        logits = rows_by_rows(hidden_two, router_block(full, experts))
        lane = lax.broadcasted_iota(jnp.int32, logits.shape, 1)
        masked = jnp.where(chosen_by(routes_ref[...], lane, experts), logits, NEGATIVE)
        weights = jnp.exp(masked - jnp.max(masked, axis=1, keepdims=True))
        total = jnp.sum(jnp.where(lane < experts, weights, 0.0), axis=1, keepdims=True)
        gates = weights / total
        high = gates.astype(jnp.bfloat16).astype(jnp.float32)
        carried = jnp.where(lane < experts, high, jnp.where(lane < 2 * experts, gates - high, 0.0))
        send[:, features:] = carried.astype(jnp.bfloat16)
        gates_out[...] = jnp.where(lane < experts, gates, 0.0)
        spread.finish()
        keep.wait()
        swap_out.wait()

    def shape(rows, columns, kind=jnp.bfloat16):
        return jax.ShapeDtypeStruct((rows, columns), kind)

    wide = features + 128
    out = [
        shape(tokens, features), shape(length, kv_columns), shape(8, 2 * tokens, jnp.float32),
        shape(tokens, features, jnp.float32), shape(tokens, features), shape(tokens, features),
        shape(tokens, features, jnp.float32), shape(tokens, wide), shape(tokens, 128, jnp.float32),
        shape(*w_query.shape), shape(*w_keyval.shape), shape(*w_out_attn.shape),
        shape(*small_shape), shape(length, features), shape(*w_out.shape), shape(*small_shape),
    ]
    scratch = [
        pltpu.VMEM(small_shape, jnp.float32),
        pltpu.VMEM((small_shape[0], features), jnp.float32),
        pltpu.VMEM((HEADS * tokens, HEAD_DIM), jnp.bfloat16),
        pltpu.VMEM((tokens, length), jnp.float32),
        Relay.semaphores(),
        Relay.semaphores(),
        Relay.semaphores(),
        pltpu.SemaphoreType.DMA((2, 2)),
        pltpu.SemaphoreType.DMA((1,)),
    ] + Gather.sems(depth) * 4
    return call(
        kernel, out, scratch, 2, "attend",
        x, router, w_query, w_keyval, w_out_attn, d_out, w_query, w_keyval, w_out_attn, w_out,
        *angles, doc_row, routes, *gains, outside=(5, 6, 7, 8, 9), outside_out=(13, 14), late=(3, 2, 4),
        early=(0, 1, 3, 4, 5, 9, 10, 11),
    )


def norm_back(values, gain_vec, grad):
    scale = lax.rsqrt(jnp.mean(values * values, axis=-1, keepdims=True) + EPSILON)
    through = jnp.mean(gain_vec * grad * values, axis=-1, keepdims=True)
    back = scale * gain_vec * grad - values * (scale * scale * scale * through)
    return back, jnp.sum(grad * values * scale, axis=0, keepdims=True)


def attend_back(
    returned, gates, small, small_there, middle, d_out, send, attn_own, attn_other, query, keyval,
    angles, doc_row, level, mixed, hidden, mixed_low, results, experts,
):
    count, tokens, features = lax.axis_size("ctx"), query.shape[0], query.shape[1]
    depth, length, kv_columns = count // 4, keyval.shape[0], keyval.shape[1]

    def kernel(
        arrive, leave, returned_ref, gates_ref, small_ref, small_there_ref, middle_ref, d_out_ref, send_ref,
        attn_own_ref, attn_other_ref, query_ref, keyval_ref, cosine_ref, sine_ref, doc_row_ref,
        level_ref, mixed_ref, hidden_ref, mixed_low_ref, results_ref,
        output, grad_middle, grad_middle_low, grad_middle_there, grad_query, grad_query_there,
        grad_keyval, grad_keyval_there, small_grads, hidden_own, hidden_there, mixed_own,
        mixed_there,
        full, grad_mixed, turned_query, own_keyval, result_sum, stacked, grads, bias, delta, total,
        part, x_sems, *scratch,
    ):
        result = scatter_parts(
            None, (None,) + tuple(scratch[:3]) + tuple(scratch[3:9]), 2, results_ref
        )
        keyval_sum = scatter_parts(part, scratch[9:], 2)
        partner = {"wa": 1 - lax.axis_index("wa")}
        swaps = [
            remote(source, target, x_sems, (i,), partner)
            for i, (source, target) in enumerate(
                [(grad_middle_low, grad_middle_there), (grad_query, grad_query_there),
                 (grad_keyval, grad_keyval_there),
                 (hidden_ref.at[:, side_columns(False)], hidden_there),
                 (mixed_low_ref.at[:, side_columns(False)], mixed_there)]
            )
        ]
        greet(across_x=True)
        arrive(18)
        for k in range(depth - 1, 0, -1):
            result.send_y(nearest(k))
        swaps[3].start()
        swaps[4].start()
        hidden_own[...] = hidden_ref[:, side_columns(True)]
        mixed_own[...] = mixed_low_ref[:, side_columns(True)]
        leave(9, 11)
        fill_small(full, small_ref, small_there_ref)
        arrive(0, 4, 5, 6)
        lane = lax.broadcasted_iota(jnp.int32, (tokens, 128), 1)
        gates = gates_ref[...]
        grad_gates = jnp.where(lane < experts, returned_ref[:, features:], 0.0)
        inner = jnp.sum(gates * grad_gates, axis=1, keepdims=True)
        grad_logits = (gates * (grad_gates - inner)).astype(jnp.bfloat16)
        z = chip_place()[0]
        at_end = (z == 0) | (z == depth - 1)
        within = jnp.logical_not(at_end)
        grad_two = returned_ref[:, :features] + jnp.dot(
            grad_logits, router_block(full, experts), preferred_element_type=jnp.float32
        )
        grad_router = columns_by_columns(grad_logits, send_ref[:, :features])
        back, grad_gain = norm_back(middle_ref[...], full[experts + 1 : experts + 2], grad_two)
        grad_middle[...] = d_out_ref[...].astype(jnp.float32) + back
        grad_middle_low[...] = grad_middle[...].astype(jnp.bfloat16)
        swaps[0].start()
        leave(1, 2)
        small_grads[:experts] = grad_router[:experts]
        row = lax.broadcasted_iota(jnp.int32, (small_grads.shape[0] - experts, 1), 0)
        small_grads[experts:] = jnp.where(row == 1, grad_gain, 0.0)
        arrive(7, 8)
        grad_mixed[:, side_columns(True)] = rows_by_rows(
            grad_middle_low[...], attn_own_ref[...]
        ).astype(jnp.bfloat16)
        grad_mixed[:, side_columns(False)] = rows_by_rows(
            grad_middle_low[...], attn_other_ref[...]
        ).astype(jnp.bfloat16)
        allowed = jnp.transpose(allowed_bias(doc_row_ref, tokens))
        bias[:, :tokens] = allowed
        bias[:, tokens:] = allowed
        total[...] = jnp.zeros_like(total)
        arrive(9, 10, 15)
        for head in range(HEADS):
            rows = slice(head * tokens, (head + 1) * tokens)
            columns = slice(head * 128, head * 128 + 128)
            stacked[rows, :] = query_ref[:, columns]
            grads[rows, :] = grad_mixed[:, columns]
            product = grad_mixed[:, columns].astype(jnp.float32) * mixed_ref[:, columns]
            delta[head // 2 : head // 2 + 1, (head % 2) * tokens : (head % 2 + 1) * tokens] = (
                jnp.sum(jnp.transpose(product), axis=0, keepdims=True)
            )

        @pl.loop(0, HEADS // 2)
        def _(pair):
            rows = pl.ds(pl.multiple_of(pair * 2 * tokens, 128), 2 * tokens)
            kind = pair // (HEADS // KV_HEADS // 2)
            key_columns = pl.ds(pl.multiple_of(kind * 128, 128), 128)
            val_columns = pl.ds(pl.multiple_of(kind * 128 + 256, 128), 128)
            key_part, val_part = keyval_ref[:, key_columns], keyval_ref[:, val_columns]
            own, grad = stacked[rows, :], grads[rows, :]
            pair_row = pl.ds(pair, 1)
            scores = rows_by_rows(key_part, own) * HEAD_DIM**-0.5 + bias[...]
            probs = jnp.exp(scores - level_ref[pair_row, :])
            grad_probs = rows_by_rows(val_part, grad)
            grad_scores = (probs * (grad_probs - delta[pair_row, :])).astype(jnp.bfloat16)
            own_grad = jnp.transpose(columns_by_columns(key_part, grad_scores))
            for half in range(2):
                columns = pl.ds(pl.multiple_of((pair * 2 + half) * 128, 128), 128)
                turned_query[:, columns] = (
                    own_grad[half * tokens : (half + 1) * tokens] * HEAD_DIM**-0.5
                )
            total[:, key_columns] += (
                jnp.dot(grad_scores, own, preferred_element_type=jnp.float32) * HEAD_DIM**-0.5
            )
            total[:, val_columns] += jnp.dot(
                probs.astype(jnp.bfloat16), grad, preferred_element_type=jnp.float32
            )
            pl.when((pair == HEADS // 4) & at_end)(lambda: result.add_y_of(nearest(depth - 1)))

        part[...] = total[...].astype(jnp.bfloat16)
        keyval_sum.start()
        cosine, sine = cosine_ref[...], -sine_ref[...]
        grad_query[...] = turned(turned_query[...], cosine, sine).astype(jnp.bfloat16)
        swaps[1].start()
        leave(4)
        steps = range(depth - 1, -1, -1)
        for step in steps:
            keyval_sum.add_cores(step)
        result.send_y(nearest(0))
        pl.when(within)(lambda: result.add_y_of(nearest(depth - 1)))
        for k in range(depth - 2, 0, -1):
            result.add_y_of(nearest(k))
            keyval_sum.add_y(k + 1)
        for step in (1, 0):
            keyval_sum.add_y(step)
        keyval_sum.last(own_keyval)
        keys = turned(own_keyval[:, : kv_columns // 2], cosine, sine)
        grad_keyval[...] = jnp.concatenate(
            [keys, own_keyval[:, kv_columns // 2 :]], axis=1
        ).astype(jnp.bfloat16)
        swaps[2].start()
        result.add_y_of(nearest(0))
        result.last(result_sum)
        output[...] = (middle_ref[...] + result_sum[...]).astype(jnp.bfloat16)
        keyval_sum.finish()
        result.finish(cores=False)
        for swap in swaps:
            swap.wait()

    def shape(like, kind=jnp.bfloat16):
        return jax.ShapeDtypeStruct(like, kind)

    rows, narrow = (tokens, features), (tokens, kv_columns)
    small_shape = (small.shape[0], features)
    out = [
        shape(rows), shape(rows, jnp.float32), shape(rows), shape(rows), shape(rows), shape(rows),
        shape(narrow), shape(narrow), shape(small_shape, jnp.float32),
    ] + [shape((tokens, features // 2))] * 4
    scratch = [
        pltpu.VMEM(small_shape, jnp.float32),
        pltpu.VMEM(rows, jnp.bfloat16),
        pltpu.VMEM(rows, jnp.float32),
        pltpu.VMEM(narrow, jnp.float32),
        pltpu.VMEM(rows, jnp.float32),
        pltpu.VMEM((HEADS * tokens, HEAD_DIM), jnp.bfloat16),
        pltpu.VMEM((HEADS * tokens, HEAD_DIM), jnp.bfloat16),
        pltpu.VMEM((length, 2 * tokens), jnp.float32),
        pltpu.VMEM((8, 2 * tokens), jnp.float32),
        pltpu.VMEM(keyval.shape, jnp.float32),
        pltpu.VMEM(keyval.shape, jnp.bfloat16),
        pltpu.SemaphoreType.DMA((2, 5)),
    ]
    wide = Scatter.scratch(depth, tokens, features)
    scratch += wide[1:4] + Scatter.sems(depth) * 2 + Scatter.scratch(depth, tokens, kv_columns, 2)
    return call(
        kernel, out, scratch, 4, "attend_back",
        returned, gates, small, small_there, middle, d_out, send, attn_own, attn_other, query,
        keyval, *angles, doc_row, level, mixed, hidden, mixed_low, results,
        late=(18, 0, 4, 5, 6, 7, 8, 9, 10, 15), early=(1, 2, 4, 9, 11),
    )


def gate_unit(first, second):
    root, cube = math.sqrt(2 / math.pi), 0.044715
    square = first * first
    bend = jnp.tanh(root * first * (1 + cube * square))
    lift = 0.5 * (1 + bend)
    slope = lift + 0.5 * first * (1 - bend * bend) * root * (1 + 3 * cube * square)
    gelu = first * lift
    return gelu * second, slope * second, gelu


def run_experts(send, d_out_all, in_own, out_own, out_other, experts):
    count, tokens = lax.axis_size("ctx"), send.shape[0]
    depth, chips, length = count // 4, count // 2, count * tokens
    wide, features = send.shape[1], d_out_all.shape[1]
    quarter = out_own.shape[0]
    width = 2 * quarter

    def kernel(
        send_ref, d_out_far, in_own_ref, out_own_ref, out_other_ref,
        returned, results_far, grad_in_far, grad_in_other_far, grad_out_far, grad_out_other_far,
        hidden_all, grad_both, gated_hidden, other_part, other_result, result_from, result_sems,
        in_ref, out_ref, d_out_ref, x_sems, near_sem, results, grad_in, grad_in_other, grad_out,
        grad_out_other, far_sems, *scratch,
    ):
        gather = gather_parts(hidden_all, tokens, scratch[:6], 2)
        scatter = scatter_parts(other_part, scratch[6:], 2)
        chip_sums = scratch[7]
        z, y, c, _ = chip_place()
        expert = lax.axis_index("ctx") // 2
        lane = lax.broadcasted_iota(jnp.int32, (1, 128), 1)
        Gather(hidden_all, tokens, scratch[:3]).own()[...] = send_ref[...]
        partner = {"wa": 1 - lax.axis_index("wa")}
        stores = [
            pltpu.make_async_copy(source, target, far_sems.at[i])
            for i, (source, target) in enumerate(
                [(results, results_far), (grad_in, grad_in_far),
                 (grad_in_other, grad_in_other_far), (grad_out, grad_out_far),
                 (grad_out_other, grad_out_other_far)]
            )
        ]
        near = pltpu.make_async_copy(d_out_far, d_out_ref, near_sem.at[0])
        near.start()
        swaps = [
            remote(
                in_own_ref.at[pl.ds(part * quarter, quarter)],
                in_ref.at[pl.ds((2 * part + 1) * quarter, quarter)],
                x_sems,
                (part,),
                partner,
            )
            for part in range(2)
        ]
        greet(across_x=True)
        gather.start()
        for swap in swaps:
            swap.start()
        out_ref[:quarter] = out_own_ref[...]
        out_ref[quarter:] = out_other_ref[...]
        in_ref[:quarter] = in_own_ref[:quarter]
        in_ref[width : width + quarter] = in_own_ref[quarter:]
        def chip_rows(chip):
            return pl.ds(pl.multiple_of(chip * 2 * tokens, 16), 2 * tokens)

        def parted(values):
            low, high = values[:tokens], values[tokens:]
            return jnp.where(c == 0, low, high), jnp.where(c == 0, high, low)

        def backward(chip):
            rows = chip_rows(chip)
            carried = hidden_all[rows, features:].astype(jnp.float32)
            mine = (lane == expert) | (lane == expert + experts)
            gate = jnp.sum(jnp.where(mine, carried, 0.0), axis=1, keepdims=True)
            both = rows_by_rows(hidden_all[rows, :features], in_ref[...])
            hidden, by_first, by_second = gate_unit(both[:, :width], both[:, width:])
            gated_hidden[rows, :] = (hidden * gate).astype(jnp.bfloat16)
            grad_hidden = rows_by_rows(d_out_ref[rows, :], out_ref[...])
            grad_gate = jnp.sum(grad_hidden * hidden, axis=1, keepdims=True)
            grad_hidden = grad_hidden * gate
            grad_both[rows, :width] = (grad_hidden * by_first).astype(jnp.bfloat16)
            grad_both[rows, width:] = (grad_hidden * by_second).astype(jnp.bfloat16)
            own, other = parted(
                jnp.dot(grad_both[rows, :], in_ref[...], preferred_element_type=jnp.float32)
            )
            chip_sums[chip, :, :features] = own.astype(jnp.bfloat16)
            other_part[chip, :, :features] = other.astype(jnp.bfloat16)
            own, other = parted(jnp.where(lane == expert, grad_gate, 0.0))
            chip_sums[chip, :, features:] = own.astype(jnp.bfloat16)
            other_part[chip, :, features:] = other.astype(jnp.bfloat16)
            scatter.send_core(chip)

        gather.along_z(1)
        for step in range(2, depth):
            gather.along_y(step - 2)
            gather.along_z(step)
        near.wait()
        for swap in swaps:
            swap.wait()
        for of_z in (nearest(1), z):
            gather.take_core(of_z)
        backward(nearest(1) * 2 + 1 - y)
        backward(nearest(1) * 2 + y)
        scatter.add_chip(nearest(1), True)
        gather.along_y(depth - 2)
        backward(z * 2 + 1 - y)
        gather.along_y(depth - 1)
        backward(z * 2 + y)
        gather.finish(nearest(1), z)
        scatter.add_chip(nearest(1), False)

        @pl.loop(0, depth - 2)
        def _(turn):
            of_z = nearest(depth - 1 - turn)
            backward(of_z * 2 + 1 - y)
            pl.when(turn > 0)(lambda: scatter.add_chip(nearest(depth - turn), False))
            backward(of_z * 2 + y)
            scatter.add_chip(of_z, True)

        scatter.add_chip(nearest(2), False)
        scatter.add_chip(z, True)
        scatter.add_chip(nearest(0), False)
        scatter.add_y_of(nearest(depth - 1))

        def result_copy(chip):
            target = {"ctx": ctx_of(z, y, 1 - c)}
            return remote(
                other_result.at[chip], result_from.at[chip], result_sems, (chip,), target
            )

        @pl.loop(0, chips)
        def _(chip):
            result = jnp.dot(
                gated_hidden[chip_rows(chip), :], out_ref[...], preferred_element_type=jnp.float32
            )
            own, other = parted(result)
            results[chip] = own.astype(jnp.bfloat16)
            other_result[chip] = other.astype(jnp.bfloat16)
            result_copy(chip).start()

        scatter.add_y_of(nearest(depth - 2))

        for k in range(depth - 3, 0, -1):
            scatter.add_y_of(nearest(k))

        @pl.loop(0, features // 512)
        def _(turn):
            at = pl.ds(pl.multiple_of(turn * 512, 512), 512)
            grad = columns_by_columns(gated_hidden[...], d_out_ref[:, at])
            grad_out[:, at] = grad[:quarter]
            grad_out_other[:, at] = grad[quarter:].astype(jnp.bfloat16)

        stores[3].start()
        stores[4].start()

        @pl.loop(0, features // 512)
        def _(turn):
            at = pl.ds(pl.multiple_of(turn * 512, 512), 512)
            grad = columns_by_columns(grad_both[...], hidden_all[:, at])
            for part in range(2):
                rows = slice(part * quarter, (part + 1) * quarter)
                first = part * width
                grad_in[rows, at] = grad[first : first + quarter]
                grad_in_other[rows, at] = grad[first + quarter : first + width].astype(jnp.bfloat16)

        stores[1].start()
        stores[2].start()

        @pl.loop(0, chips)
        def _(chip):
            result_copy(chip).wait_recv()
            add_into(results.at[chip], (results.at[chip], result_from.at[chip]), tokens)

        stores[0].start()
        scatter.add_y_of(nearest(0))
        scatter.last(returned)
        scatter.finish()
        for chip in range(chips):
            result_copy(chip).wait_send()
        for store in stores:
            store.wait()

    block = (chips, tokens, features)
    out = [
        jax.ShapeDtypeStruct((tokens, wide), jnp.float32),
        jax.ShapeDtypeStruct(block, jnp.bfloat16),
        jax.ShapeDtypeStruct(in_own.shape, jnp.float32),
        jax.ShapeDtypeStruct(in_own.shape, jnp.bfloat16),
        jax.ShapeDtypeStruct(out_own.shape, jnp.float32),
        jax.ShapeDtypeStruct(out_own.shape, jnp.bfloat16),
    ]
    scratch = [
        pltpu.VMEM((length, wide), jnp.bfloat16),
        pltpu.VMEM((length, 2 * width), jnp.bfloat16),
        pltpu.VMEM((length, width), jnp.bfloat16),
        pltpu.VMEM((chips, tokens, wide), jnp.bfloat16),
        pltpu.VMEM(block, jnp.bfloat16),
        pltpu.VMEM(block, jnp.bfloat16),
        pltpu.SemaphoreType.DMA((2, chips)),
        pltpu.VMEM((2 * width, features), jnp.bfloat16),
        pltpu.VMEM((width, features), jnp.bfloat16),
        pltpu.VMEM(d_out_all.shape, jnp.bfloat16),
        pltpu.SemaphoreType.DMA((2, 2)),
        pltpu.SemaphoreType.DMA((1,)),
    ]
    scratch += [pltpu.VMEM(one.shape, one.dtype) for one in out[1:]]
    scratch.append(pltpu.SemaphoreType.DMA((5,)))
    scratch += Gather.sems(depth) * 2 + Scatter.scratch(depth, tokens, wide, 2)
    return call(
        kernel, out, scratch, 3, "experts", send, d_out_all, in_own, out_own, out_other, outside=(1,),
        outside_out=range(1, 6),
    )


def finish(
    x, grad_middle, small, small_there, small_grads, matrices, hidden, mixed, middle, query, keyval,
    expert_in, expert_out,
):
    count, tokens, half = lax.axis_size("ctx"), x.shape[0], x.shape[1] // 2
    depth, rows = count // 4, half // count
    widths = (middle[0].shape[1], query[0].shape[1], keyval[0].shape[1])
    experts = small.shape[0] // 2

    def kernel(
        arrive, leave, x_ref, grad_middle_ref, small_ref, small_there_ref, small_grads_ref,
        query_own, query_other, keyval_own, keyval_other,
        hidden_ref, hidden_there, mixed_ref, mixed_there, middle_ref, middle_there,
        query_ref, query_there, keyval_ref, keyval_there, in_ref, out_ref,
        attn_sum, query_sum, keyval_sum, small_sum, grad_input, in_there, out_there,
        attn_part, query_part, keyval_part, pair, full, grad_one, small_mine, small_came, small_all,
        x_sems, *scratch,
    ):
        scatters, gathers = [], []
        parts, sums = (attn_part, query_part, keyval_part), (attn_sum, query_sum, keyval_sum)
        for part, total in zip(parts, sums):
            scatters.append(Scatter(part, scratch[:7]))
            gathers.append(Gather(total, rows, scratch[7:10]))
            scratch = scratch[10:]
        small_out = Gather(small_all, small_came.shape[0], scratch)
        (attn, query_, keyval_), (attn_out, query_out, keyval_out) = scatters, gathers
        partner = {"wa": 1 - lax.axis_index("wa")}
        swaps = [
            remote(source, target, x_sems, (i,), partner)
            for i, (source, target) in enumerate(
                [(small_mine.at[:, side_columns(False)], small_came), (in_ref, in_there),
                 (out_ref, out_there)]
            )
        ]
        steps = range(depth - 1, -1, -1)

        def products(left, left_there, right, right_there, part):
            pair[:tokens] = left[...]
            pair[tokens:] = left_there[...]

            @pl.loop(0, part.shape[1] // 512)
            def _(turn):
                at = pl.ds(pl.multiple_of(turn * 512, 512), 512)
                both = jnp.concatenate([right[:, at], right_there[:, at]], axis=0)
                part[:, at] = columns_by_columns(pair[...], both).astype(jnp.bfloat16)

        products(mixed_ref, mixed_there, middle_ref, middle_there, attn_part)
        greet(across_x=True)
        attn.start()
        arrive(9, 10, 15, 16)
        products(hidden_ref, hidden_there, query_ref, query_there, query_part)
        for step in steps:
            attn.add_cores(step)
        query_.start()
        arrive(17, 18)
        products(hidden_ref, hidden_there, keyval_ref, keyval_there, keyval_part)
        keyval_.start()
        for step in steps:
            query_.add_cores(step)
        attn.add_y(depth - 1)
        fill_small(full, small_ref, small_there_ref)
        arrive(0, 1, 5, 6, 7, 8)
        grad_one[:, side_columns(True)] = rows_by_rows(
            query_ref[...], query_own[...]
        ) + rows_by_rows(keyval_ref[...], keyval_own[...])
        attn.add_y(depth - 2)
        grad_one[:, side_columns(False)] = rows_by_rows(
            query_ref[...], query_other[...]
        ) + rows_by_rows(keyval_ref[...], keyval_other[...])
        back, grad_gain = norm_back(
            x_ref[...].astype(jnp.float32), full[experts : experts + 1], grad_one[...]
        )
        grad_input[...] = (grad_middle_ref[...] + back).astype(jnp.bfloat16)
        leave(4)
        row = lax.broadcasted_iota(jnp.int32, (small_mine.shape[0], 1), 0)
        small_mine[...] = jnp.where(row == experts, grad_gain, small_grads_ref[...])
        swaps[0].start()
        for step in range(depth - 3, -1, -1):
            attn.add_y(step)
        for step in steps:
            keyval_.add_cores(step)
        attn.last(attn_out.own())
        attn_out.start()
        swaps[1].start()
        swaps[2].start()
        swaps[0].wait()
        small_out.own()[...] = (small_mine[:, side_columns(True)] + small_came[...]).astype(
            jnp.bfloat16
        )
        small_out.start()
        for step in steps:
            query_.add_y(step)
        attn_out.along_z(1)
        query_.last(query_out.own())
        query_out.start()
        attn_out.along_z(2)
        attn_out.along_y(0)
        small_out.along_z(1)
        for step in steps:
            keyval_.add_y(step)
        attn_out.along_z(3)
        attn_out.along_y(1)
        keyval_.last(keyval_out.own())
        keyval_out.start()
        query_out.along_z(1)
        small_out.along_z(2)
        attn_out.along_y(2)
        query_out.along_z(2)
        small_out.along_z(3)
        query_out.along_y(0)
        keyval_out.along_z(1)
        query_out.along_z(3)
        attn_out.along_y(3)
        keyval_out.along_z(2)
        query_out.along_y(1)
        keyval_out.along_z(3)
        query_out.along_y(2)
        attn_out.finish()
        leave(0)
        small_out.along_y(0)
        keyval_out.along_y(0)
        small_out.along_y(1)
        query_out.along_y(3)
        keyval_out.along_y(1)
        small_out.along_y(2)
        keyval_out.along_y(2)
        small_out.along_y(3)
        keyval_out.along_y(3)
        query_out.finish()
        leave(1)
        keyval_out.finish()
        leave(2)
        for one in [small_out] + scatters:
            one.finish()
        small_rows = small_came.shape[0]
        total = small_all[:small_rows].astype(jnp.float32)
        for device in range(1, count):
            rows_of = slice(device * small_rows, (device + 1) * small_rows)
            total = total + small_all[rows_of].astype(jnp.float32)
        small_sum[...] = total
        swaps[1].wait()
        swaps[2].wait()

    small_shape = (small.shape[0], half)
    out = [jax.ShapeDtypeStruct((half, width), jnp.bfloat16) for width in widths]
    out += [
        jax.ShapeDtypeStruct(small_shape, jnp.float32),
        jax.ShapeDtypeStruct(x.shape, jnp.bfloat16),
        jax.ShapeDtypeStruct(expert_in.shape, expert_in.dtype),
        jax.ShapeDtypeStruct(expert_out.shape, expert_out.dtype),
    ]
    scratch = [pltpu.VMEM((half, width), jnp.bfloat16) for width in widths]
    scratch += [
        pltpu.VMEM((2 * tokens, half), jnp.bfloat16),
        pltpu.VMEM(small_grads.shape, jnp.float32),
        pltpu.VMEM(x.shape, jnp.float32),
        pltpu.VMEM(small_grads.shape, jnp.float32),
        pltpu.VMEM(small_shape, jnp.float32),
        pltpu.VMEM((count * small.shape[0], half), jnp.bfloat16),
        pltpu.SemaphoreType.DMA((2, 3)),
    ]
    for width in widths:
        scratch += Scatter.scratch(depth, rows, width) + Gather.sems(depth)
    scratch += Gather.sems(depth)
    return call(
        kernel, out, scratch, 1, "finish",
        x, grad_middle, small, small_there, small_grads, *matrices, *hidden, *mixed, *middle,
        *query, *keyval, expert_in, expert_out, outside=(19, 20), outside_out=(5, 6),
        late=(9, 10, 15, 16, 17, 18, 5, 6, 7, 8, 0, 1), early=(0, 1, 2, 4),
    )


def widen(query, keyval, attn, grad_in, in_there, grad_out, out_there, small):
    quarter, features = grad_out.shape
    steps, experts = 4, small.shape[0] // 2

    def kernel(*refs):
        query_ref, keyval_ref, attn_ref, in_ref, in_there_ref, out_ref, out_there_ref = refs[:7]
        small_ref, query_out, keyval_out, attn_out, in_out, out_out, router_out = refs[7:]
        router_out[...] = small_ref[:experts]
        query_out[...] = query_ref[...].astype(jnp.float32)
        keyval_out[...] = keyval_ref[...].astype(jnp.float32)
        attn_out[...] = attn_ref[...].astype(jnp.float32)
        both = in_ref[...] + in_there_ref[...].astype(jnp.float32)
        in_out[...] = both
        out_out[0] = out_ref[...] + out_there_ref[...].astype(jnp.float32)

    def rows(values):
        return pl.BlockSpec((values.shape[0] // steps, values.shape[1]), lambda i: (i, 0))

    operands = (query, keyval, attn, grad_in, in_there, grad_out, out_there)
    return pl.pallas_call(
        kernel,
        grid=(steps,),
        out_shape=[
            jax.ShapeDtypeStruct(query.shape, jnp.float32),
            jax.ShapeDtypeStruct(keyval.shape, jnp.float32),
            jax.ShapeDtypeStruct(attn.shape, jnp.float32),
            jax.ShapeDtypeStruct(grad_in.shape, jnp.float32),
            jax.ShapeDtypeStruct((1, quarter, features), jnp.float32),
            jax.ShapeDtypeStruct((experts, small.shape[1]), jnp.float32),
        ],
        in_specs=[rows(values) for values in operands]
        + [pl.BlockSpec(small.shape, lambda i: (0, 0))],
        out_specs=[
            rows(query), rows(keyval), rows(attn),
            rows(grad_in),
            pl.BlockSpec((1, quarter // steps, features), lambda i: (0, i, 0)),
            pl.BlockSpec((experts, small.shape[1]), lambda i: (0, 0)),
        ],
        compiler_params=pltpu.CompilerParams(vmem_limit_bytes=VMEM_LIMIT),
        name="widen",
    )(*operands, small)


def gathered_body(
    layer_input, seq_ids, routes, gain_attn, w_query, w_keyval, w_out_attn, gain_ffn, router,
    w_in, w_out, d_out,
):
    me = lax.axis_index("ctx")
    tokens, experts = layer_input.shape[1], router.shape[1]
    x, grad_out = layer_input[0], d_out[0]
    turns = angle_table(me * tokens + jnp.arange(tokens, dtype=jnp.int32))[:, 0]
    cosine, sine = jnp.cos(turns), jnp.sin(turns)
    angles = (
        jnp.concatenate([cosine, cosine], axis=1), jnp.concatenate([-sine, sine], axis=1)
    )
    in_own = jnp.swapaxes(w_in[0], 1, 2).reshape(-1, D)

    (
        query, keyval, level, mixed, hidden, mixed_low, middle, send, gates, w_query_there,
        w_keyval_there, w_out_attn_there, small_there, d_out_all, w_out_there, small,
    ) = attend(
        x, grad_out, router.T, (gain_attn[None], gain_ffn[None]), w_query, w_keyval, w_out_attn,
        w_out[0], angles, seq_ids, routes[0].T,
    )
    projections = (w_query, w_query_there, w_keyval, w_keyval_there)
    returned, results, grad_in, grad_in_other, grad_out_matrix, grad_out_other = run_experts(
        send, d_out_all, in_own, w_out[0], w_out_there, experts
    )
    (
        output, grad_middle, middle_low, middle_there, grad_query, query_there, grad_keyval,
        keyval_there, small_grads, *halves,
    ) = attend_back(
        returned, gates, small, small_there, middle, grad_out, send, w_out_attn, w_out_attn_there,
        query, keyval, angles, seq_ids, level, mixed, hidden, mixed_low, results, experts,
    )
    attn_sum, query_sum, keyval_sum, small_sum, grad_input, in_there, out_there = finish(
        x, grad_middle, small, small_there, small_grads, projections, halves[:2], halves[2:],
        (middle_low, middle_there), (grad_query, query_there),
        (grad_keyval, keyval_there), grad_in_other, grad_out_other,
    )
    query_sum, keyval_sum, attn_sum, grad_w_in, grad_w_out, grad_router = widen(
        query_sum, keyval_sum, attn_sum, grad_in, in_there, grad_out_matrix, out_there, small_sum
    )
    return (
        output[None],
        grad_input[None],
        small_sum[experts],
        query_sum,
        keyval_sum,
        attn_sum,
        small_sum[experts + 1],
        grad_router.T,
        jnp.swapaxes(grad_w_in.reshape(2, -1, D), 1, 2)[None],
        grad_w_out,
    )


def solution(mesh):
    in_specs = (
        P("wa", "ctx", None),
        P("wa", None),
        P("wa", "ctx", None),
        P("wa"),
        P("wa", None),
        P("wa", None),
        P("wa", None),
        P("wa"),
        P("wa", None),
        P("ctx", None, None, "wa"),
        P("ctx", "wa", None),
        P("wa", "ctx", None),
    )
    out_specs = (
        P("wa", "ctx", None),
        P("wa", "ctx", None),
        P("wa"),
        P("wa", None),
        P("wa", None),
        P("wa", None),
        P("wa"),
        P("wa", None),
        P("ctx", None, None, "wa"),
        P("ctx", "wa", None),
    )
    depth = mesh.shape["ctx"]
    body = gathered_body if depth == 16 else routed_body
    return jax.shard_map(body, mesh=mesh, in_specs=in_specs, out_specs=out_specs, check_vma=False)
```

```python
import functools
import math

import jax
import jax.numpy as jnp
from jax import lax
from jax.experimental import pallas as pl
from jax.experimental.pallas import tpu as pltpu
from jax.sharding import PartitionSpec as P

D = 1536
HEADS = 12
KV_HEADS = 2
HEAD_DIM = 128
TOP = 4
BLOCK = 256


EPSILON = 1e-06
THETA = 1000000.0
NEGATIVE = -1e30


def rms_scale(values, gain_vec):
    return (
        values * lax.rsqrt(jnp.mean(values * values, axis=-1, keepdims=True) + EPSILON) * gain_vec
    )


def rotate(values, angles):
    half_dim = values.shape[-1] // 2
    cosine = jnp.cos(angles)
    sine_part = jnp.sin(angles)
    first_half = values[..., :half_dim]
    second = values[..., half_dim:]
    return jnp.concatenate(
        [first_half * cosine - second * sine_part, second * cosine + first_half * sine_part],
        axis=-1,
    )


def angle_table(positions):
    half_dim = HEAD_DIM // 2
    frequency = THETA ** (-2.0 * jnp.arange(half_dim, dtype=jnp.float32) / HEAD_DIM)
    return (positions.astype(jnp.float32)[:, None] * frequency[None, :])[:, None, :]


def gated(stacked):
    return jax.nn.gelu(stacked[..., 0, :], approximate=True) * stacked[..., 1, :]


def over_keys(key_rows, running, advance):
    key_count = key_rows.shape[0]
    key_width = math.gcd(key_count, 512)

    def one_turn(state_now, block_index):
        key_offset = block_index * key_width
        key_part = lax.dynamic_slice_in_dim(key_rows, key_offset, key_width, 0)
        return (advance(state_now, key_part, key_offset), None)

    running, unused = lax.scan(
        one_turn, running, jnp.arange(key_count // key_width, dtype=jnp.int32)
    )
    return running


def routed_body(
    layer_input,
    seq_ids,
    routes,
    gain_attn,
    w_query,
    w_keyval,
    w_out_attn,
    gain_ffn,
    router,
    w_in,
    w_out,
    d_out,
):
    ctx_count = lax.axis_size("ctx")
    ctx_index = lax.axis_index("ctx")
    tokens = layer_input.shape[1]
    length = tokens * ctx_count
    experts_all = ctx_count // 2
    capacity = 2 * tokens * TOP // experts_all
    group = HEADS // KV_HEADS
    kv_width = KV_HEADS * HEAD_DIM
    row_count = group * tokens
    scale = HEAD_DIM ** (-0.5)
    gain_one, query_matrix, keyvalue_matrix, attention_matrix = (
        lax.all_gather(gain_attn, "wa", axis=0, tiled=True),
        lax.all_gather(w_query, "wa", axis=0, tiled=True),
        lax.all_gather(w_keyval, "wa", axis=0, tiled=True),
        lax.all_gather(w_out_attn, "wa", axis=0, tiled=True),
    )
    residual = layer_input[0].astype(jnp.float32)
    normed_one, norm_one_back = jax.vjp(rms_scale, residual, gain_one.astype(jnp.float32))
    hidden_first_norm = normed_one.astype(jnp.bfloat16)
    positions = ctx_index * tokens + jnp.arange(tokens, dtype=jnp.int32)
    angles = angle_table(positions)
    query_projected = jnp.dot(
        hidden_first_norm, query_matrix, preferred_element_type=jnp.float32
    ).reshape(tokens, HEADS, HEAD_DIM)
    keyvalue_projected = jnp.dot(
        hidden_first_norm, keyvalue_matrix, preferred_element_type=jnp.float32
    )
    key_pre = keyvalue_projected[:, :kv_width].reshape(tokens, KV_HEADS, HEAD_DIM)
    query_low = rotate(query_projected, angles).astype(jnp.bfloat16)
    key_low = rotate(key_pre, angles).astype(jnp.bfloat16)
    value_low = keyvalue_projected[:, kv_width:].astype(jnp.bfloat16)
    keyval_send = jnp.concatenate([key_low.reshape(tokens, kv_width), value_low], axis=1)
    query_rows = (
        query_low.reshape(tokens, KV_HEADS, group, HEAD_DIM)
        .transpose(1, 2, 0, 3)
        .reshape(KV_HEADS, row_count, HEAD_DIM)
    )
    doc_row = seq_ids[0]
    query_docs = lax.dynamic_slice_in_dim(doc_row, ctx_index * tokens, tokens, 0)
    query_blocks = positions // BLOCK

    def block_scores(key_part, first_key):
        key_count = key_part.shape[0]
        split_part = key_part.reshape(key_count, 2, KV_HEADS, HEAD_DIM)
        keys_here = split_part[:, 0]
        values_here = split_part[:, 1]
        scores = (
            jnp.einsum("hrd,nhd->hrn", query_rows, keys_here, preferred_element_type=jnp.float32)
            * scale
        )
        key_docs = lax.dynamic_slice_in_dim(doc_row, first_key, key_count, 0)
        key_blocks = (first_key + jnp.arange(key_count, dtype=jnp.int32)) // BLOCK
        allowed = (query_docs[:, None] == key_docs[None, :]) & (
            key_blocks[None, :] <= query_blocks[:, None]
        )
        allowed = jnp.broadcast_to(allowed[None], (group, tokens, key_count)).reshape(
            1, row_count, key_count
        )
        return (jnp.where(allowed, scores, NEGATIVE), allowed, keys_here, values_here)

    def probs_of(masked, allowed, largest, totals):
        return jnp.where(allowed, jnp.exp(masked - largest[..., None]) / totals[..., None], 0.0)

    def stats_step(running, key_part, first_key):
        largest, totals = running
        masked, allowed, keys_here, values_here = block_scores(key_part, first_key)
        new_largest = jnp.maximum(largest, jnp.max(masked, axis=-1))
        weights = jnp.where(allowed, jnp.exp(masked - new_largest[..., None]), 0.0)
        return (new_largest, totals * jnp.exp(largest - new_largest) + jnp.sum(weights, axis=-1))

    start_stats = (
        jnp.full((KV_HEADS, row_count), NEGATIVE, jnp.float32),
        jnp.zeros((KV_HEADS, row_count), jnp.float32),
    )
    largest, totals = over_keys(
        lax.all_gather(keyval_send, "ctx", axis=0, tiled=True), start_stats, stats_step
    )

    def values_step(running, key_part, first_key):
        masked, allowed, keys_here, values_here = block_scores(key_part, first_key)
        probs_low = probs_of(masked, allowed, largest, totals).astype(jnp.bfloat16)
        return running + jnp.einsum(
            "hrn,nhd->hrd", probs_low, values_here, preferred_element_type=jnp.float32
        )

    start_values = jnp.zeros((KV_HEADS, row_count, HEAD_DIM), jnp.float32)
    mixed_rows = over_keys(
        lax.all_gather(keyval_send, "ctx", axis=0, tiled=True), start_values, values_step
    )
    mixed_low = (
        mixed_rows.reshape(KV_HEADS, group, tokens, HEAD_DIM)
        .transpose(2, 0, 1, 3)
        .reshape(tokens, HEADS * HEAD_DIM)
        .astype(jnp.bfloat16)
    )
    middle_activation = residual + jnp.dot(
        mixed_low, attention_matrix, preferred_element_type=jnp.float32
    )
    gain_two, router_full, w_in_full, w_out_full = (
        lax.all_gather(gain_ffn, "wa", axis=0, tiled=True),
        lax.all_gather(router, "wa", axis=0, tiled=True),
        lax.all_gather(w_in, "wa", axis=3, tiled=True),
        lax.all_gather(w_out, "wa", axis=1, tiled=True),
    )
    in_half = w_in_full[0]
    out_half = w_out_full[0]
    normed_two, norm_two_back = jax.vjp(rms_scale, middle_activation, gain_two.astype(jnp.float32))
    hidden_second_norm = normed_two.astype(jnp.bfloat16)
    router_logits = jnp.dot(hidden_second_norm, router_full, preferred_element_type=jnp.float32)
    route_ids = routes[0]

    def gate_values(logit_rows):
        return jax.nn.softmax(jnp.take_along_axis(logit_rows, route_ids, axis=-1), axis=-1)

    gates, gate_back = jax.vjp(gate_values, router_logits)
    flat_ids = route_ids.reshape(tokens * TOP)
    expert_hits = (flat_ids[:, None] == jnp.arange(experts_all, dtype=jnp.int32)[None, :]).astype(
        jnp.int32
    )
    ranks = jnp.sum(expert_hits * (jnp.cumsum(expert_hits, axis=0) - expert_hits), axis=1)
    slot_first = 2 * flat_ids * capacity + ranks
    slot_second = slot_first + capacity
    slot_total = ctx_count * capacity
    slot_numbers = jnp.arange(slot_total, dtype=jnp.int32)[:, None]
    placed = (
        (slot_first[None, :] == slot_numbers) | (slot_second[None, :] == slot_numbers)
    ).astype(jnp.bfloat16)
    dispatch = jnp.sum(placed.reshape(slot_total, tokens, TOP), axis=2)
    send_rows = (
        jnp.dot(dispatch, hidden_second_norm, preferred_element_type=jnp.float32)
        .astype(jnp.bfloat16)
        .reshape(ctx_count, capacity, D)
    )
    arrived = lax.all_to_all(send_rows, "ctx", split_axis=0, concat_axis=0, tiled=True)
    stacked = jnp.einsum("ncd,gdf->ncgf", arrived, in_half, preferred_element_type=jnp.float32)
    hidden_low = gated(stacked).astype(jnp.bfloat16)
    result = jnp.einsum(
        "ncf,fd->ncd", hidden_low, out_half, preferred_element_type=jnp.float32
    ).astype(jnp.bfloat16)
    returned_rows = lax.all_to_all(result, "ctx", split_axis=0, concat_axis=0, tiled=True)
    returned_flat = returned_rows.reshape(slot_total, D)
    pair_rows = (
        returned_flat[slot_first].astype(jnp.float32)
        + returned_flat[slot_second].astype(jnp.float32)
    ).reshape(tokens, TOP, D)
    output = (middle_activation + jnp.sum(gates[:, :, None] * pair_rows, axis=1)).astype(
        jnp.bfloat16
    )
    grad_out = d_out[0].astype(jnp.float32)
    grad_gates = jnp.sum(pair_rows * grad_out[:, None, :], axis=-1)
    (grad_logits,) = gate_back(grad_gates)
    grad_logits_low = grad_logits.astype(jnp.bfloat16)
    gate_slots = jnp.dot(
        placed.astype(jnp.float32), gates.reshape(tokens * TOP), precision=lax.Precision.HIGHEST
    )
    routed_grad = jnp.dot(dispatch, d_out[0], preferred_element_type=jnp.float32)
    grad_send_rows = (
        (gate_slots[:, None] * routed_grad).astype(jnp.bfloat16).reshape(ctx_count, capacity, D)
    )
    grad_arrived = lax.all_to_all(grad_send_rows, "ctx", split_axis=0, concat_axis=0, tiled=True)
    grad_hidden = jnp.einsum(
        "ncd,fd->ncf", grad_arrived, out_half, preferred_element_type=jnp.float32
    )
    hidden_again, gated_back = jax.vjp(gated, stacked)
    (grad_stacked,) = gated_back(grad_hidden)
    grad_stacked_low = grad_stacked.astype(jnp.bfloat16)
    grad_rows = jnp.einsum(
        "ncgf,gdf->ncd", grad_stacked_low, in_half, preferred_element_type=jnp.float32
    ).astype(jnp.bfloat16)
    grad_returned = lax.all_to_all(grad_rows, "ctx", split_axis=0, concat_axis=0, tiled=True)
    grad_w_in = jnp.einsum(
        "ncd,ncgf->gdf", arrived, grad_stacked_low, preferred_element_type=jnp.float32
    )[None]
    grad_w_out = jnp.einsum(
        "ncf,ncd->fd",
        hidden_again.astype(jnp.bfloat16),
        grad_arrived,
        preferred_element_type=jnp.float32,
    )[None]
    grad_hidden_two = jnp.einsum(
        "st,sd->td",
        dispatch,
        grad_returned.reshape(slot_total, D),
        preferred_element_type=jnp.float32,
    )
    grad_hidden_two = grad_hidden_two + jnp.dot(
        grad_logits_low, router_full.T, preferred_element_type=jnp.float32
    )
    grad_router = jnp.dot(hidden_second_norm.T, grad_logits_low, preferred_element_type=jnp.float32)
    grad_middle_norm, grad_gain_two = norm_two_back(grad_hidden_two)
    grad_middle = grad_out + grad_middle_norm
    grad_middle_low = grad_middle.astype(jnp.bfloat16)
    grad_attn_weight = jnp.dot(mixed_low.T, grad_middle_low, preferred_element_type=jnp.float32)
    grad_mixed = jnp.dot(
        grad_middle_low, attention_matrix.T, preferred_element_type=jnp.float32
    ).astype(jnp.bfloat16)
    grad_rows_out = (
        grad_mixed.reshape(tokens, KV_HEADS, group, HEAD_DIM)
        .transpose(1, 2, 0, 3)
        .reshape(KV_HEADS, row_count, HEAD_DIM)
    )
    delta = jnp.sum(grad_rows_out.astype(jnp.float32) * mixed_rows, axis=-1)

    def score_grads(key_part, first_key):
        masked, allowed, keys_here, values_here = block_scores(key_part, first_key)
        probs = probs_of(masked, allowed, largest, totals)
        grad_probs = jnp.einsum(
            "hrd,nhd->hrn", grad_rows_out, values_here, preferred_element_type=jnp.float32
        )
        grad_scores = (probs * (grad_probs - delta[..., None])).astype(jnp.bfloat16)
        return (grad_scores, probs.astype(jnp.bfloat16), keys_here)

    def key_terms(grad_scores, probs_low, key_count):
        grad_keys = (
            jnp.einsum("hrn,hrd->nhd", grad_scores, query_rows, preferred_element_type=jnp.float32)
            * scale
        )
        grad_values = jnp.einsum(
            "hrn,hrd->nhd", probs_low, grad_rows_out, preferred_element_type=jnp.float32
        )
        return jnp.concatenate(
            [grad_keys.reshape(key_count, kv_width), grad_values.reshape(key_count, kv_width)],
            axis=1,
        )

    start_query = jnp.zeros((KV_HEADS, row_count, HEAD_DIM), jnp.float32)

    def back_step(running, key_part, first_key):
        grad_query_rows, grad_keyvals = running
        grad_scores, probs_low, keys_here = score_grads(key_part, first_key)
        grad_query_rows = (
            grad_query_rows
            + jnp.einsum("hrn,nhd->hrd", grad_scores, keys_here, preferred_element_type=jnp.float32)
            * scale
        )
        fresh = key_terms(grad_scores, probs_low, key_part.shape[0])
        return (grad_query_rows, lax.dynamic_update_slice_in_dim(grad_keyvals, fresh, first_key, 0))

    start_back = (start_query, jnp.zeros((length, 2 * kv_width), jnp.float32))
    grad_query_rows, grad_keyvals = over_keys(
        lax.all_gather(keyval_send, "ctx", axis=0, tiled=True), start_back, back_step
    )
    grad_keyval_mine = lax.psum_scatter(grad_keyvals, "ctx", scatter_dimension=0, tiled=True)
    grad_query = grad_query_rows.reshape(KV_HEADS, group, tokens, HEAD_DIM).transpose(2, 0, 1, 3)
    grad_query_pre = (
        rotate(grad_query.reshape(tokens, HEADS, HEAD_DIM), -angles)
        .reshape(tokens, HEADS * HEAD_DIM)
        .astype(jnp.bfloat16)
    )
    grad_key_pre = rotate(
        grad_keyval_mine[:, :kv_width].reshape(tokens, KV_HEADS, HEAD_DIM), -angles
    ).reshape(tokens, kv_width)
    grad_keyval_pre = jnp.concatenate(
        [grad_key_pre, grad_keyval_mine[:, kv_width:]], axis=1
    ).astype(jnp.bfloat16)
    grad_hidden_one = jnp.dot(
        grad_query_pre, query_matrix.T, preferred_element_type=jnp.float32
    ) + jnp.dot(grad_keyval_pre, keyvalue_matrix.T, preferred_element_type=jnp.float32)
    grad_query_weight = jnp.dot(
        hidden_first_norm.T, grad_query_pre, preferred_element_type=jnp.float32
    )
    grad_keyval_weight = jnp.dot(
        hidden_first_norm.T, grad_keyval_pre, preferred_element_type=jnp.float32
    )
    grad_residual_norm, grad_gain_one = norm_one_back(grad_hidden_one)
    grad_input = (grad_middle + grad_residual_norm).astype(jnp.bfloat16)
    shares = (
        lax.psum_scatter(
            grad_gain_one.astype(jnp.bfloat16), "wa", scatter_dimension=0, tiled=True
        ).astype(jnp.float32),
        lax.psum_scatter(
            grad_query_weight.astype(jnp.bfloat16), "wa", scatter_dimension=0, tiled=True
        ).astype(jnp.float32),
        lax.psum_scatter(
            grad_keyval_weight.astype(jnp.bfloat16), "wa", scatter_dimension=0, tiled=True
        ).astype(jnp.float32),
        lax.psum_scatter(
            grad_attn_weight.astype(jnp.bfloat16), "wa", scatter_dimension=0, tiled=True
        ).astype(jnp.float32),
        lax.psum_scatter(
            grad_gain_two.astype(jnp.bfloat16), "wa", scatter_dimension=0, tiled=True
        ).astype(jnp.float32),
        lax.psum_scatter(
            grad_router.astype(jnp.bfloat16), "wa", scatter_dimension=0, tiled=True
        ).astype(jnp.float32),
        lax.psum_scatter(
            grad_w_in.astype(jnp.bfloat16), "wa", scatter_dimension=3, tiled=True
        ).astype(jnp.float32),
        lax.psum_scatter(
            grad_w_out.astype(jnp.bfloat16), "wa", scatter_dimension=1, tiled=True
        ).astype(jnp.float32),
    )
    summed = lax.psum((shares[0], shares[1], shares[2], shares[3], shares[4], shares[5]), "ctx")
    return (
        output[None],
        grad_input[None],
        summed[0],
        summed[1],
        summed[2],
        summed[3],
        summed[4],
        summed[5],
        shares[6],
        shares[7],
    )

MESH = pl.DeviceIdType.MESH
VMEM_LIMIT = 60 * 1024 * 1024


def chip_place():
    count = lax.axis_size("ctx")
    me = lax.axis_index("ctx")
    return me // 4, lax.rem(me // 2, 2), lax.rem(me, 2), count // 4


def ctx_of(z, y, c):
    return (z * 2 + y) * 2 + c


def greet(across_x=False):
    z, y, c, depth = chip_place()
    barrier = pltpu.get_barrier_semaphore()

    def signal(device):
        pl.semaphore_signal(barrier, 1, device_id=device, device_id_type=MESH)

    signal({"ctx": ctx_of(z, y, 1 - c)})
    signal({"ctx": ctx_of(z, 1 - y, c)})
    if across_x:
        signal({"wa": 1 - lax.axis_index("wa")})
    pl.when(z > 0)(lambda: signal({"ctx": ctx_of(z - 1, y, c)}))
    pl.when(z < depth - 1)(lambda: signal({"ctx": ctx_of(z + 1, y, c)}))
    ends = (z > 0).astype(jnp.int32) + (z < depth - 1).astype(jnp.int32)
    pl.semaphore_wait(barrier, (3 if across_x else 2) + ends)


def remote(source, target_ref, sems, at, device):
    return pltpu.make_async_remote_copy(
        src_ref=source,
        dst_ref=target_ref,
        send_sem=sems.at[(0,) + at],
        recv_sem=sems.at[(1,) + at],
        device_id=device,
        device_id_type=MESH,
    )


def each(step, act):
    z, _, _, depth = chip_place()
    if step == 0:
        act(z)
    else:
        pl.when(z + step < depth)(lambda: act(z + step))
        pl.when(z - step >= 0)(lambda: act(z - step))


def nearest(k):
    z, _, _, depth = chip_place()
    low = jnp.minimum(z, depth - 1 - z)
    step = (k + 1) // 2
    place = jnp.where(k > 2 * low, k, jnp.where(lax.rem(k, 2) == 1, low - step, low + step))
    return jnp.where(z == low, place, depth - 1 - place)


class Gather:
    def __init__(self, out, rows, sems, part=0, parts=1):
        self.out, self.block, self.rows = out, rows, rows // parts
        self.first = part * self.rows
        self.z_sems, self.y_sems, self.c_sems = sems
        self.z, self.y, self.c, self.depth = chip_place()

    @staticmethod
    def sems(depth):
        return [
            pltpu.SemaphoreType.DMA((2, 2, depth)),
            pltpu.SemaphoreType.DMA((2, depth)),
            pltpu.SemaphoreType.DMA((2, 2 * depth)),
        ]

    def slot(self, z, y, c):
        start = ctx_of(z, y, c) * self.block + self.first
        return self.out.at[pl.ds(pl.multiple_of(start, 16), self.rows)]

    def own(self):
        return self.slot(self.z, self.y, self.c)

    def on_z(self, way, of_z, source=None):
        goal = jnp.minimum(self.z + 1, self.depth - 1) if way == 0 else jnp.maximum(self.z - 1, 0)
        block = self.slot(of_z, self.y, self.c)
        target = {"ctx": ctx_of(goal, self.y, self.c)}
        return remote(block if source is None else source, block, self.z_sems, (way, of_z), target)

    def on_y(self, of_z, mine=True, source=None):
        block = self.slot(of_z, self.y if mine else 1 - self.y, self.c)
        target = {"ctx": ctx_of(self.z, 1 - self.y, self.c)}
        return remote(block if source is None else source, block, self.y_sems, (of_z,), target)

    def on_core(self, of_z, of_y, mine=True, source=None):
        block = self.slot(of_z, of_y, self.c if mine else 1 - self.c)
        target = {"ctx": ctx_of(self.z, self.y, 1 - self.c)}
        at = (of_z * 2 + of_y,)
        return remote(block if source is None else source, block, self.c_sems, at, target)

    def start(self, source=None):
        z, depth = self.z, self.depth
        if source is not None:
            source = source.at[pl.ds(self.first, self.rows)]
        pl.when(z < depth - 1)(lambda: self.on_z(0, z, source).start())
        pl.when(z > 0)(lambda: self.on_z(1, z, source).start())
        self.on_y(z, source=source).start()
        self.on_core(z, self.y, source=source).start()

    def along_z(self, step):
        z, depth = self.z, self.depth

        def from_side(way, of_z, more):
            self.on_z(way, of_z).wait_recv()
            pl.when(more)(lambda: self.on_z(way, of_z).start())
            self.on_y(of_z).start()
            self.on_core(of_z, self.y).start()

        pl.when(z - step >= 0)(lambda: from_side(0, z - step, z < depth - 1))
        pl.when(z + step < depth)(lambda: from_side(1, z + step, z > 0))

    def along_y(self, step):
        def across(of_z):
            self.on_y(of_z, mine=False).wait_recv()
            self.on_core(of_z, 1 - self.y).start()

        each(step, across)

    def take_core(self, of_z):
        for of_y in range(2):
            self.on_core(of_z, of_y, mine=False).wait_recv()

    def finish(self, *taken):
        z, depth = self.z, self.depth
        for of_z in range(depth):
            pl.when((z < depth - 1) & (of_z <= z))(lambda: self.on_z(0, of_z).wait_send())
            pl.when((z > 0) & (of_z >= z))(lambda: self.on_z(1, of_z).wait_send())
            self.on_y(of_z).wait_send()
            for of_y in range(2):
                self.on_core(of_z, of_y).wait_send()
            open_still = of_z >= 0
            for one in taken:
                open_still = (of_z != one) & open_still
            pl.when(open_still)(lambda: self.take_core(of_z))


class Several:
    def __init__(self, members):
        self.members = members

    def __getattr__(self, name):
        def every(*given, **named):
            for member in self.members:
                getattr(member, name)(*given, **named)

        return every


def gather_parts(out, rows, sems, parts):
    return Several(
        [Gather(out, rows, sems[3 * i : 3 * i + 3], i, parts) for i in range(parts)]
    )


def follow(gather):
    depth = chip_place()[3]
    gather.along_z(1)
    for step in range(depth):
        if step >= 1 and step + 1 < depth:
            gather.along_z(step + 1)
        gather.along_y(step)
    gather.finish()


def add_into(target, terms, rows):
    some = 32 if rows % 32 == 0 else 48 if rows % 48 == 0 else 16

    @pl.loop(0, rows // some)
    def _(turn):
        at = pl.ds(pl.multiple_of(turn * some, 16), some)
        total = terms[0][at, :].astype(jnp.float32)
        for term in terms[1:]:
            total = total + term[at, :].astype(jnp.float32)
        target[at, :] = total.astype(target.dtype)


class Scatter:
    def __init__(self, part, scratch, sums=None, piece=0, pieces=1):
        self.part = part
        self.from_core, self.totals, self.from_y, self.from_z = scratch[:4]
        self.sums = self.totals if sums is None else sums
        self.c_sems, self.y_sems, self.z_sems = scratch[4:]
        self.block = self.totals.shape[1]
        self.rows = self.block // pieces
        self.first = piece * self.rows
        self.z, self.y, self.c, self.depth = chip_place()

    @staticmethod
    def sems(depth):
        return [
            pltpu.SemaphoreType.DMA((2, 2 * depth)),
            pltpu.SemaphoreType.DMA((2, depth)),
            pltpu.SemaphoreType.DMA((2, 2, depth)),
        ]

    @staticmethod
    def scratch(depth, rows, columns, pieces=1):
        return [
            pltpu.VMEM((2 * depth, rows, columns), jnp.bfloat16),
            pltpu.VMEM((2 * depth, rows, columns), jnp.bfloat16),
            pltpu.VMEM((depth, rows, columns), jnp.bfloat16),
            pltpu.VMEM((depth + 1, rows, columns), jnp.bfloat16),
        ] + Scatter.sems(depth) * pieces

    def of(self, ref, place):
        return ref.at[place, pl.ds(self.first, self.rows)]

    def split(self):
        return len(self.part.shape) == 3

    def share(self, chip, c):
        start = (chip * 2 + c) * self.block + self.first
        return self.part.at[pl.ds(pl.multiple_of(start, 16), self.rows)]

    def on_core(self, chip):
        target = {"ctx": ctx_of(self.z, self.y, 1 - self.c)}
        source = self.of(self.part, chip) if self.split() else self.share(chip, 1 - self.c)
        return remote(source, self.of(self.from_core, chip), self.c_sems, (chip,), target)

    def send_core(self, chip):
        self.on_core(chip).start()

    def send_y(self, of_z):
        self.on_y(of_z).start()

    def on_y(self, of_z):
        target = {"ctx": ctx_of(self.z, 1 - self.y, self.c)}
        source = self.of(self.sums, of_z * 2 + 1 - self.y)
        return remote(source, self.of(self.from_y, of_z), self.y_sems, (of_z,), target)

    def on_z(self, way, of_z):
        goal = jnp.minimum(self.z + 1, self.depth - 1) if way == 0 else jnp.maximum(self.z - 1, 0)
        place = of_z if way == 0 else jnp.where(of_z == goal, self.depth, of_z)
        source = self.of(self.totals, of_z * 2 + self.y)
        target = {"ctx": ctx_of(goal, self.y, self.c)}
        return remote(source, self.of(self.from_z, place), self.z_sems, (way, of_z), target)

    def start(self):
        def send(of_z):
            self.on_core(of_z * 2 + 1 - self.y).start()
            self.on_core(of_z * 2 + self.y).start()

        for step in range(self.depth - 1, -1, -1):
            each(step, send)

    def add_chip(self, of_z, other, send=True):
        chip = of_z * 2 + (1 - self.y if other else self.y)
        self.on_core(chip).wait_recv()
        total = self.of(self.sums, chip)
        own = total if self.split() else self.share(chip, self.c)
        add_into(total, (own, self.of(self.from_core, chip)), self.rows)
        if other and send:
            self.on_y(of_z).start()

    def add_cores(self, step):
        def add(of_z):
            self.add_chip(of_z, True)
            self.add_chip(of_z, False)

        each(step, add)

    def add_y_of(self, of_z):
        z, depth = self.z, self.depth
        self.on_y(of_z).wait_recv()
        place = of_z * 2 + self.y
        total, own = self.of(self.totals, place), self.of(self.sums, place)
        other = self.of(self.from_y, of_z)
        upward, downward = (of_z > z) & (z > 0), (of_z < z) & (z < depth - 1)
        pl.when(upward)(lambda: self.on_z(0, of_z).wait_recv())
        pl.when(downward)(lambda: self.on_z(1, of_z).wait_recv())

        @pl.when(upward | downward)
        def _():
            add_into(total, (own, other, self.of(self.from_z, of_z)), self.rows)

        @pl.when(jnp.logical_not(upward | downward))
        def _():
            add_into(total, (own, other), self.rows)

        pl.when(of_z > z)(lambda: self.on_z(0, of_z).start())
        pl.when(of_z < z)(lambda: self.on_z(1, of_z).start())

    def add_y(self, step):
        each(step, self.add_y_of)

    def last(self, result):
        z, depth = self.z, self.depth
        own = self.of(self.totals, z * 2 + self.y)
        low, high = self.of(self.from_z, z), self.of(self.from_z, depth)
        result = result.at[pl.ds(self.first, self.rows)]
        pl.when(z > 0)(lambda: self.on_z(0, z).wait_recv())
        pl.when(z < depth - 1)(lambda: self.on_z(1, z).wait_recv())
        inside = (z > 0) & (z < depth - 1)
        pl.when(inside)(lambda: add_into(result, (own, low, high), self.rows))
        pl.when(z == 0)(lambda: add_into(result, (own, high), self.rows))
        pl.when(z == depth - 1)(lambda: add_into(result, (own, low), self.rows))

    def finish(self, cores=True):
        for of_z in range(self.depth):
            self.on_y(of_z).wait_send()
            if cores:
                self.on_core(of_z * 2).wait_send()
                self.on_core(of_z * 2 + 1).wait_send()
            pl.when(of_z > self.z)(lambda: self.on_z(0, of_z).wait_send())
            pl.when(of_z < self.z)(lambda: self.on_z(1, of_z).wait_send())


def scatter_parts(part, scratch, pieces, sums=None):
    arrays, sems = tuple(scratch[:4]), tuple(scratch[4:])
    return Several(
        [
            Scatter(part, arrays + sems[3 * i : 3 * i + 3], sums, i, pieces)
            for i in range(pieces)
        ]
    )


def call(
    kernel, out, scratch, number, name, *operands, outside=(), outside_out=(), late=(), early=()
):
    many = isinstance(out, (tuple, list))
    count, results = len(operands), len(out) if many else 1
    late, early = tuple(late), tuple(early)
    more = len(late) + len(early) + 1

    def spec(position, far):
        return pl.BlockSpec(memory_space=pl.ANY if position in far else pltpu.VMEM)

    def moving(*refs):
        near, sems = refs[-more:-1], refs[-1]
        loads = {
            i: pltpu.make_async_copy(refs[i], near[k], sems.at[k]) for k, i in enumerate(late)
        }
        stores = {
            i: pltpu.make_async_copy(near[k], refs[count + i], sems.at[k])
            for k, i in enumerate(early, len(late))
        }
        for copy in loads.values():
            copy.start()
        held = [near[late.index(i)] if i in late else refs[i] for i in range(count)]
        given = [
            near[len(late) + early.index(i)] if i in early else refs[count + i]
            for i in range(results)
        ]

        def arrive(*which):
            for i in which:
                loads[i].wait()

        def leave(*which):
            for i in which:
                stores[i].start()

        helpers = (arrive, leave) if early else (arrive,)
        kernel(*helpers, *held, *given, *refs[count + results : -more])
        for copy in stores.values():
            copy.wait()

    if late or early:
        scratch = list(scratch) + [pltpu.VMEM(operands[i].shape, operands[i].dtype) for i in late]
        scratch += [pltpu.VMEM(out[i].shape, out[i].dtype) for i in early]
        scratch.append(pltpu.SemaphoreType.DMA((more - 1,)))
    far, far_out = tuple(outside) + late, tuple(outside_out) + early
    out_specs = [spec(i, far_out) for i in range(results)]
    return pl.pallas_call(
        moving if late or early else kernel,
        out_shape=out,
        in_specs=[spec(i, far) for i in range(count)],
        out_specs=out_specs if many else out_specs[0],
        scratch_shapes=scratch,
        compiler_params=pltpu.CompilerParams(
            collective_id=number,
            has_side_effects=number is not None,
            vmem_limit_bytes=VMEM_LIMIT,
        ),
        name=name,
    )(*operands)


class Relay:
    def __init__(self, source, out, sems, parts=1, paired=False):
        self.source, self.out, self.sems, self.parts = source, out, sems, parts
        self.paired = paired
        self.z, self.y, self.c, _ = chip_place()
        self.odd = lax.rem(self.z, 2)
        self.rows = source.shape[0] // ((4 if paired else 2) * parts)

    @staticmethod
    def semaphores():
        return pltpu.SemaphoreType.DMA((2, 8))

    def block(self, ref, part, c, odd):
        place = (c * 2 + odd if self.paired else c) * self.parts + part
        return ref.at[pl.ds(pl.multiple_of(place * self.rows, 16), self.rows)]

    def on_x(self, part):
        source = self.block(self.source, part, self.c, self.odd)
        target = self.block(self.out, part, self.c, self.odd)
        return remote(source, target, self.sems, (part,), {"wa": 1 - lax.axis_index("wa")})

    def on_core(self, part, c, other_z=False):
        block = self.block(self.out, part, c, 1 - self.odd if other_z else self.odd)
        at = ((4 if other_z else 2) + part,)
        return remote(block, block, self.sems, at, {"ctx": ctx_of(self.z, self.y, 1 - self.c)})

    def on_pair(self, part, mine=True):
        block = self.block(self.out, part, self.c, self.odd if mine else 1 - self.odd)
        target = {"ctx": ctx_of(self.z + 1 - 2 * self.odd, self.y, self.c)}
        return remote(block, block, self.sems, (6 + part,), target)

    def start(self):
        for part in range(self.parts):
            self.on_x(part).start()

    def pass_on(self, part=0):
        self.on_x(part).wait_recv()
        if self.paired:
            self.on_pair(part).start()
        self.on_core(part, self.c).start()

    def pass_on_pair(self, part):
        self.on_pair(part, mine=False).wait_recv()
        self.on_core(part, self.c, other_z=True).start()

    def finish(self):
        for part in range(self.parts):
            self.on_x(part).wait_send()
            self.on_core(part, self.c).wait_send()
            self.on_core(part, 1 - self.c).wait_recv()
            if self.paired:
                self.on_pair(part).wait_send()
                self.on_core(part, self.c, other_z=True).wait_send()
                self.on_core(part, 1 - self.c, other_z=True).wait_recv()


def rows_by_rows(left, right):
    return lax.dot_general(
        left, right, (((1,), (1,)), ((), ())), preferred_element_type=jnp.float32
    )


def columns_by_columns(left, right):
    return lax.dot_general(
        left, right, (((0,), (0,)), ((), ())), preferred_element_type=jnp.float32
    )


def down(row):
    return jnp.transpose(jnp.broadcast_to(row.astype(jnp.float32), (128, 128)))


def allowed_bias(doc_row, tokens):
    keys, me = doc_row.shape[1], lax.axis_index("ctx")
    own = down(doc_row[:, pl.ds(pl.multiple_of(me * tokens, 128), tokens)])[:, :1]
    key_block = lax.broadcasted_iota(jnp.int32, (tokens, keys), 1) // BLOCK
    same = doc_row[...].astype(jnp.float32) == own
    return jnp.where(same & (key_block <= me * tokens // BLOCK), 0.0, NEGATIVE)


def chosen_by(routes, lanes, experts):
    numbers = lax.rem(lanes, experts).astype(jnp.float32)
    found = down(routes[:1]) == numbers
    for k in range(1, routes.shape[0]):
        found = found | (down(routes[k : k + 1]) == numbers)
    return found & (lanes < 2 * experts)


def side_columns(own):
    side = lax.axis_index("wa")
    return pl.ds(pl.multiple_of((side if own else 1 - side) * (D // 2), 128), D // 2)


def turned(values, cosine, sine):
    heads = []
    for head in range(values.shape[1] // HEAD_DIM):
        one = values[:, head * HEAD_DIM : (head + 1) * HEAD_DIM]
        heads.append(one * cosine + pltpu.roll(one, HEAD_DIM // 2, axis=1) * sine)
    return jnp.concatenate(heads, axis=1)


def normed(values, gain_vec):
    return values * lax.rsqrt(jnp.mean(values * values, axis=-1, keepdims=True) + EPSILON) * gain_vec


def fill_small(full, small, small_there):
    full[:, side_columns(True)] = small[...].astype(jnp.float32)
    full[:, side_columns(False)] = small_there[...].astype(jnp.float32)


def router_block(full, experts):
    rows = full[:experts]
    spare = jnp.zeros((128 - 2 * experts, rows.shape[1]), jnp.float32)
    return jnp.concatenate([rows, rows, spare], axis=0).astype(jnp.bfloat16)


def attend(
    x, d_out, router, gains, w_query, w_keyval, w_out_attn, w_out, angles, doc_row, routes
):
    count, tokens, features = lax.axis_size("ctx"), x.shape[0], x.shape[1]
    depth, length = count // 4, count * tokens
    kv_columns, experts = w_keyval.shape[1], router.shape[0]
    small_shape = (2 * experts, router.shape[1])

    def kernel(
        arrive, leave, x_ref, router_ref, query_own, keyval_own, attn_own, d_out_far, query_far,
        keyval_far, attn_far, out_far, cosine_ref, sine_ref, doc_row_ref, routes_ref, gain_one, gain_two,
        query, keyval, level, mixed, hidden, mixed_low, middle, send, gates_out, query_other,
        keyval_other, attn_other, small_there, d_out_all, out_other,
        small_ref,
        filled, full, stacked, bias, query_sems, keyval_sems, attn_sems, small_sems, own_sem, *sems,
    ):
        gather = gather_parts(keyval, tokens, sems[:6], 2)
        spread = gather_parts(d_out_all, tokens, sems[6:], 2)
        query_relay = Relay(query_far, query_other, query_sems, parts=2)
        keyval_relay = Relay(keyval_far, keyval_other, keyval_sems)
        attn = Relay(attn_far, attn_other, attn_sems, parts=2, paired=True)
        partner = {"wa": 1 - lax.axis_index("wa")}
        swap = remote(small_ref, small_there, small_sems, (0,), partner)
        swap_out = remote(out_far, out_other, small_sems, (1,), partner)
        keep = pltpu.make_async_copy(
            d_out_far, Gather(d_out_all, tokens, sems[6:9]).own(), own_sem.at[0]
        )
        keep.start()
        filled[...] = jnp.zeros_like(filled)
        filled[:experts] = router_ref[...].astype(jnp.float32)
        filled[experts : experts + 1] = gain_one[...].astype(jnp.float32)
        filled[experts + 1 : experts + 2] = gain_two[...].astype(jnp.float32)
        small_ref[...] = filled[...].astype(jnp.bfloat16)
        greet(across_x=True)
        swap.start()
        keyval_relay.start()
        query_relay.start()
        attn.start()
        swap_out.start()
        spread.start(d_out_far)
        swap.wait()
        fill_small(full, small_ref, small_there)
        residual = x_ref[...].astype(jnp.float32)
        hidden[...] = normed(residual, full[experts : experts + 1]).astype(jnp.bfloat16)
        own, other = hidden[:, side_columns(True)], hidden[:, side_columns(False)]
        cosine, sine = cosine_ref[...], sine_ref[...]

        def onto(matrix, matrix_other):
            return jnp.dot(own, matrix[...], preferred_element_type=jnp.float32) + jnp.dot(
                other, matrix_other[...], preferred_element_type=jnp.float32
            )

        bias[...] = allowed_bias(doc_row_ref, tokens)
        spread.along_z(1)
        spread.along_y(0)
        keyval_relay.pass_on()
        keyval_relay.finish()
        arrive(3)
        pre = onto(keyval_own, keyval_other)
        keys = turned(pre[:, : kv_columns // 2], cosine, sine)
        block = jnp.concatenate([keys, pre[:, kv_columns // 2 :]], axis=1)
        Gather(keyval, tokens, sems[:3]).own()[...] = block.astype(jnp.bfloat16)
        leave(4, 10)
        spread.along_z(2)
        spread.along_y(1)
        query_relay.pass_on(0)
        spread.along_z(3)
        gather.start()
        gather.along_z(1)
        spread.along_y(2)
        gather.along_y(0)
        gather.along_z(2)
        query_relay.pass_on(1)
        spread.along_y(3)
        gather.along_y(1)
        gather.along_z(3)
        query_relay.finish()
        arrive(2)
        query[...] = turned(onto(query_own, query_other), cosine, sine).astype(jnp.bfloat16)
        for head in range(HEADS):
            rows = slice(head * tokens, (head + 1) * tokens)
            stacked[rows, :] = query[:, head * 128 : (head + 1) * 128]
        leave(0, 9)
        attn.pass_on(0)
        gather.along_y(2)
        gather.along_y(3)
        gather.finish()
        leave(1)

        @pl.loop(0, HEADS // 2)
        def _(pair):
            rows = pl.ds(pl.multiple_of(pair * 2 * tokens, 128), 2 * tokens)
            kind = pair // (HEADS // KV_HEADS // 2)
            key_part = keyval[:, pl.ds(pl.multiple_of(kind * 128, 128), 128)]
            val_part = keyval[:, pl.ds(pl.multiple_of(kind * 128 + 256, 128), 128)]
            scores = rows_by_rows(stacked[rows, :], key_part) * HEAD_DIM**-0.5
            scores = (scores.reshape(2, tokens, -1) + bias[...][None]).reshape(scores.shape)
            top = jnp.max(scores, axis=-1, keepdims=True)
            weights = jnp.exp(scores - top)
            total = jnp.sum(weights, axis=-1, keepdims=True)
            probs = (weights * (1 / total)).astype(jnp.bfloat16)
            mixture = jnp.dot(probs, val_part, preferred_element_type=jnp.float32)
            for part in range(2):
                columns = pl.ds(pl.multiple_of((pair * 2 + part) * 128, 128), 128)
                mixed[:, columns] = mixture[part * tokens : (part + 1) * tokens]
            column = jnp.broadcast_to(top + jnp.log(total), (2 * tokens, 128))
            level[pl.ds(pair, 1), :] = jnp.transpose(column)[:1]
            pl.when(pair == 1)(lambda: attn.pass_on(1))
            pl.when(pair == 4)(lambda: attn.pass_on_pair(0))

        mixed_low[...] = mixed[...].astype(jnp.bfloat16)
        leave(3, 5)
        attn.pass_on_pair(1)
        own, other = mixed_low[:, side_columns(True)], mixed_low[:, side_columns(False)]
        arrive(4)
        attn.finish()
        leave(11)
        middle[...] = residual + onto(attn_own, attn_other)
        hidden_two = normed(middle[...], full[experts + 1 : experts + 2]).astype(jnp.bfloat16)
        send[:, :features] = hidden_two
        logits = rows_by_rows(hidden_two, router_block(full, experts))
        lane = lax.broadcasted_iota(jnp.int32, logits.shape, 1)
        masked = jnp.where(chosen_by(routes_ref[...], lane, experts), logits, NEGATIVE)
        weights = jnp.exp(masked - jnp.max(masked, axis=1, keepdims=True))
        total = jnp.sum(jnp.where(lane < experts, weights, 0.0), axis=1, keepdims=True)
        gates = weights / total
        high = gates.astype(jnp.bfloat16).astype(jnp.float32)
        carried = jnp.where(lane < experts, high, jnp.where(lane < 2 * experts, gates - high, 0.0))
        send[:, features:] = carried.astype(jnp.bfloat16)
        gates_out[...] = jnp.where(lane < experts, gates, 0.0)
        spread.finish()
        keep.wait()
        swap_out.wait()

    def shape(rows, columns, kind=jnp.bfloat16):
        return jax.ShapeDtypeStruct((rows, columns), kind)

    wide = features + 128
    out = [
        shape(tokens, features), shape(length, kv_columns), shape(8, 2 * tokens, jnp.float32),
        shape(tokens, features, jnp.float32), shape(tokens, features), shape(tokens, features),
        shape(tokens, features, jnp.float32), shape(tokens, wide), shape(tokens, 128, jnp.float32),
        shape(*w_query.shape), shape(*w_keyval.shape), shape(*w_out_attn.shape),
        shape(*small_shape), shape(length, features), shape(*w_out.shape), shape(*small_shape),
    ]
    scratch = [
        pltpu.VMEM(small_shape, jnp.float32),
        pltpu.VMEM((small_shape[0], features), jnp.float32),
        pltpu.VMEM((HEADS * tokens, HEAD_DIM), jnp.bfloat16),
        pltpu.VMEM((tokens, length), jnp.float32),
        Relay.semaphores(),
        Relay.semaphores(),
        Relay.semaphores(),
        pltpu.SemaphoreType.DMA((2, 2)),
        pltpu.SemaphoreType.DMA((1,)),
    ] + Gather.sems(depth) * 4
    return call(
        kernel, out, scratch, 2, "attend",
        x, router, w_query, w_keyval, w_out_attn, d_out, w_query, w_keyval, w_out_attn, w_out,
        *angles, doc_row, routes, *gains, outside=(5, 6, 7, 8, 9), outside_out=(13, 14), late=(3, 2, 4),
        early=(0, 1, 3, 4, 5, 9, 10, 11),
    )


def norm_back(values, gain_vec, grad):
    scale = lax.rsqrt(jnp.mean(values * values, axis=-1, keepdims=True) + EPSILON)
    through = jnp.mean(gain_vec * grad * values, axis=-1, keepdims=True)
    back = scale * gain_vec * grad - values * (scale * scale * scale * through)
    return back, jnp.sum(grad * values * scale, axis=0, keepdims=True)


def attend_back(
    returned, gates, small, small_there, middle, d_out, send, attn_own, attn_other, query, keyval,
    angles, doc_row, level, mixed, hidden, mixed_low, results, experts,
):
    count, tokens, features = lax.axis_size("ctx"), query.shape[0], query.shape[1]
    depth, length, kv_columns = count // 4, keyval.shape[0], keyval.shape[1]

    def kernel(
        arrive, leave, returned_ref, gates_ref, small_ref, small_there_ref, middle_ref, d_out_ref, send_ref,
        attn_own_ref, attn_other_ref, query_ref, keyval_ref, cosine_ref, sine_ref, doc_row_ref,
        level_ref, mixed_ref, hidden_ref, mixed_low_ref, results_ref,
        output, grad_middle, grad_middle_low, grad_middle_there, grad_query, grad_query_there,
        grad_keyval, grad_keyval_there, small_grads, hidden_own, hidden_there, mixed_own,
        mixed_there,
        full, grad_mixed, turned_query, own_keyval, result_sum, stacked, grads, bias, delta, total,
        part, x_sems, *scratch,
    ):
        result = scatter_parts(
            None, (None,) + tuple(scratch[:3]) + tuple(scratch[3:9]), 2, results_ref
        )
        keyval_sum = scatter_parts(part, scratch[9:], 2)
        partner = {"wa": 1 - lax.axis_index("wa")}
        swaps = [
            remote(source, target, x_sems, (i,), partner)
            for i, (source, target) in enumerate(
                [(grad_middle_low, grad_middle_there), (grad_query, grad_query_there),
                 (grad_keyval, grad_keyval_there),
                 (hidden_ref.at[:, side_columns(False)], hidden_there),
                 (mixed_low_ref.at[:, side_columns(False)], mixed_there)]
            )
        ]
        greet(across_x=True)
        arrive(18)
        for k in range(depth - 1, 0, -1):
            result.send_y(nearest(k))
        arrive(16, 17)
        swaps[3].start()
        swaps[4].start()
        hidden_own[...] = hidden_ref[:, side_columns(True)]
        mixed_own[...] = mixed_low_ref[:, side_columns(True)]
        leave(9, 11)
        fill_small(full, small_ref, small_there_ref)
        arrive(0, 4, 5, 6)
        lane = lax.broadcasted_iota(jnp.int32, (tokens, 128), 1)
        gates = gates_ref[...]
        grad_gates = jnp.where(lane < experts, returned_ref[:, features:], 0.0)
        inner = jnp.sum(gates * grad_gates, axis=1, keepdims=True)
        grad_logits = (gates * (grad_gates - inner)).astype(jnp.bfloat16)
        z = chip_place()[0]
        at_end = (z == 0) | (z == depth - 1)
        within = jnp.logical_not(at_end)
        grad_two = returned_ref[:, :features] + jnp.dot(
            grad_logits, router_block(full, experts), preferred_element_type=jnp.float32
        )
        grad_router = columns_by_columns(grad_logits, send_ref[:, :features])
        back, grad_gain = norm_back(middle_ref[...], full[experts + 1 : experts + 2], grad_two)
        grad_middle[...] = d_out_ref[...].astype(jnp.float32) + back
        grad_middle_low[...] = grad_middle[...].astype(jnp.bfloat16)
        swaps[0].start()
        leave(1, 2)
        small_grads[:experts] = grad_router[:experts]
        row = lax.broadcasted_iota(jnp.int32, (small_grads.shape[0] - experts, 1), 0)
        small_grads[experts:] = jnp.where(row == 1, grad_gain, 0.0)
        arrive(7, 8)
        grad_mixed[:, side_columns(True)] = rows_by_rows(
            grad_middle_low[...], attn_own_ref[...]
        ).astype(jnp.bfloat16)
        grad_mixed[:, side_columns(False)] = rows_by_rows(
            grad_middle_low[...], attn_other_ref[...]
        ).astype(jnp.bfloat16)
        allowed = jnp.transpose(allowed_bias(doc_row_ref, tokens))
        bias[:, :tokens] = allowed
        bias[:, tokens:] = allowed
        total[...] = jnp.zeros_like(total)
        arrive(9, 10, 15)
        for head in range(HEADS):
            rows = slice(head * tokens, (head + 1) * tokens)
            columns = slice(head * 128, head * 128 + 128)
            stacked[rows, :] = query_ref[:, columns]
            grads[rows, :] = grad_mixed[:, columns]
            product = grad_mixed[:, columns].astype(jnp.float32) * mixed_ref[:, columns]
            delta[head // 2 : head // 2 + 1, (head % 2) * tokens : (head % 2 + 1) * tokens] = (
                jnp.sum(jnp.transpose(product), axis=0, keepdims=True)
            )

        @pl.loop(0, HEADS // 2)
        def _(pair):
            rows = pl.ds(pl.multiple_of(pair * 2 * tokens, 128), 2 * tokens)
            kind = pair // (HEADS // KV_HEADS // 2)
            key_columns = pl.ds(pl.multiple_of(kind * 128, 128), 128)
            val_columns = pl.ds(pl.multiple_of(kind * 128 + 256, 128), 128)
            key_part, val_part = keyval_ref[:, key_columns], keyval_ref[:, val_columns]
            own, grad = stacked[rows, :], grads[rows, :]
            pair_row = pl.ds(pair, 1)
            scores = rows_by_rows(key_part, own) * HEAD_DIM**-0.5 + bias[...]
            probs = jnp.exp(scores - level_ref[pair_row, :])
            grad_probs = rows_by_rows(val_part, grad)
            grad_scores = (probs * (grad_probs - delta[pair_row, :])).astype(jnp.bfloat16)
            own_grad = jnp.transpose(columns_by_columns(key_part, grad_scores))
            for half in range(2):
                columns = pl.ds(pl.multiple_of((pair * 2 + half) * 128, 128), 128)
                turned_query[:, columns] = (
                    own_grad[half * tokens : (half + 1) * tokens] * HEAD_DIM**-0.5
                )
            total[:, key_columns] += (
                jnp.dot(grad_scores, own, preferred_element_type=jnp.float32) * HEAD_DIM**-0.5
            )
            total[:, val_columns] += jnp.dot(
                probs.astype(jnp.bfloat16), grad, preferred_element_type=jnp.float32
            )
            pl.when((pair == HEADS // 4) & at_end)(lambda: result.add_y_of(nearest(depth - 1)))

        part[...] = total[...].astype(jnp.bfloat16)
        keyval_sum.start()
        cosine, sine = cosine_ref[...], -sine_ref[...]
        grad_query[...] = turned(turned_query[...], cosine, sine).astype(jnp.bfloat16)
        swaps[1].start()
        leave(4)
        steps = range(depth - 1, -1, -1)
        for step in steps:
            keyval_sum.add_cores(step)
        result.send_y(nearest(0))
        pl.when(within)(lambda: result.add_y_of(nearest(depth - 1)))
        for k in range(depth - 2, 0, -1):
            result.add_y_of(nearest(k))
            keyval_sum.add_y(k + 1)
        for step in (1, 0):
            keyval_sum.add_y(step)
        keyval_sum.last(own_keyval)
        keys = turned(own_keyval[:, : kv_columns // 2], cosine, sine)
        grad_keyval[...] = jnp.concatenate(
            [keys, own_keyval[:, kv_columns // 2 :]], axis=1
        ).astype(jnp.bfloat16)
        swaps[2].start()
        result.add_y_of(nearest(0))
        result.last(result_sum)
        output[...] = (middle_ref[...] + result_sum[...]).astype(jnp.bfloat16)
        keyval_sum.finish()
        result.finish(cores=False)
        for swap in swaps:
            swap.wait()

    def shape(like, kind=jnp.bfloat16):
        return jax.ShapeDtypeStruct(like, kind)

    rows, narrow = (tokens, features), (tokens, kv_columns)
    small_shape = (small.shape[0], features)
    out = [
        shape(rows), shape(rows, jnp.float32), shape(rows), shape(rows), shape(rows), shape(rows),
        shape(narrow), shape(narrow), shape(small_shape, jnp.float32),
    ] + [shape((tokens, features // 2))] * 4
    scratch = [
        pltpu.VMEM(small_shape, jnp.float32),
        pltpu.VMEM(rows, jnp.bfloat16),
        pltpu.VMEM(rows, jnp.float32),
        pltpu.VMEM(narrow, jnp.float32),
        pltpu.VMEM(rows, jnp.float32),
        pltpu.VMEM((HEADS * tokens, HEAD_DIM), jnp.bfloat16),
        pltpu.VMEM((HEADS * tokens, HEAD_DIM), jnp.bfloat16),
        pltpu.VMEM((length, 2 * tokens), jnp.float32),
        pltpu.VMEM((8, 2 * tokens), jnp.float32),
        pltpu.VMEM(keyval.shape, jnp.float32),
        pltpu.VMEM(keyval.shape, jnp.bfloat16),
        pltpu.SemaphoreType.DMA((2, 5)),
    ]
    wide = Scatter.scratch(depth, tokens, features)
    scratch += wide[1:4] + Scatter.sems(depth) * 2 + Scatter.scratch(depth, tokens, kv_columns, 2)
    return call(
        kernel, out, scratch, 4, "attend_back",
        returned, gates, small, small_there, middle, d_out, send, attn_own, attn_other, query,
        keyval, *angles, doc_row, level, mixed, hidden, mixed_low, results,
        late=(18, 16, 17, 0, 4, 5, 6, 7, 8, 9, 10, 15), early=(1, 2, 4, 9, 11),
    )


def gate_unit(first, second):
    root, cube = math.sqrt(2 / math.pi), 0.044715
    square = first * first
    bend = jnp.tanh(root * first * (1 + cube * square))
    lift = 0.5 * (1 + bend)
    slope = lift + 0.5 * first * (1 - bend * bend) * root * (1 + 3 * cube * square)
    gelu = first * lift
    return gelu * second, slope * second, gelu


def run_experts(send, d_out_all, in_own, out_own, out_other, experts):
    count, tokens = lax.axis_size("ctx"), send.shape[0]
    depth, chips, length = count // 4, count // 2, count * tokens
    wide, features = send.shape[1], d_out_all.shape[1]
    quarter = out_own.shape[0]
    width = 2 * quarter

    def kernel(
        arrive, send_ref, d_out_far, in_own_ref, out_own_ref, out_other_ref,
        returned, results_far, grad_in_far, grad_in_other_far, grad_out_far, grad_out_other_far,
        hidden_all, grad_both, gated_hidden, other_part, other_result, result_from, result_sems,
        in_ref, out_ref, d_out_ref, x_sems, near_sem, results, grad_in, grad_in_other, grad_out,
        grad_out_other, far_sems, *scratch,
    ):
        gather = gather_parts(hidden_all, tokens, scratch[:6], 2)
        scatter = scatter_parts(other_part, scratch[6:], 2)
        chip_sums = scratch[7]
        z, y, c, _ = chip_place()
        expert = lax.axis_index("ctx") // 2
        lane = lax.broadcasted_iota(jnp.int32, (1, 128), 1)
        Gather(hidden_all, tokens, scratch[:3]).own()[...] = send_ref[...]
        partner = {"wa": 1 - lax.axis_index("wa")}
        stores = [
            pltpu.make_async_copy(source, target, far_sems.at[i])
            for i, (source, target) in enumerate(
                [(results, results_far), (grad_in, grad_in_far),
                 (grad_in_other, grad_in_other_far), (grad_out, grad_out_far),
                 (grad_out_other, grad_out_other_far)]
            )
        ]
        near = pltpu.make_async_copy(d_out_far, d_out_ref, near_sem.at[0])
        near.start()
        swaps = [
            remote(
                in_own_ref.at[pl.ds(part * quarter, quarter)],
                in_ref.at[pl.ds((2 * part + 1) * quarter, quarter)],
                x_sems,
                (part,),
                partner,
            )
            for part in range(2)
        ]
        greet(across_x=True)
        gather.start()
        arrive(2)
        for swap in swaps:
            swap.start()
        arrive(3, 4)
        out_ref[:quarter] = out_own_ref[...]
        out_ref[quarter:] = out_other_ref[...]
        in_ref[:quarter] = in_own_ref[:quarter]
        in_ref[width : width + quarter] = in_own_ref[quarter:]
        def chip_rows(chip):
            return pl.ds(pl.multiple_of(chip * 2 * tokens, 16), 2 * tokens)

        def parted(values):
            low, high = values[:tokens], values[tokens:]
            return jnp.where(c == 0, low, high), jnp.where(c == 0, high, low)

        def backward(chip):
            rows = chip_rows(chip)
            carried = hidden_all[rows, features:].astype(jnp.float32)
            mine = (lane == expert) | (lane == expert + experts)
            gate = jnp.sum(jnp.where(mine, carried, 0.0), axis=1, keepdims=True)
            both = rows_by_rows(hidden_all[rows, :features], in_ref[...])
            hidden, by_first, by_second = gate_unit(both[:, :width], both[:, width:])
            gated_hidden[rows, :] = (hidden * gate).astype(jnp.bfloat16)
            grad_hidden = rows_by_rows(d_out_ref[rows, :], out_ref[...])
            grad_gate = jnp.sum(grad_hidden * hidden, axis=1, keepdims=True)
            grad_hidden = grad_hidden * gate
            grad_both[rows, :width] = (grad_hidden * by_first).astype(jnp.bfloat16)
            grad_both[rows, width:] = (grad_hidden * by_second).astype(jnp.bfloat16)
            own, other = parted(
                jnp.dot(grad_both[rows, :], in_ref[...], preferred_element_type=jnp.float32)
            )
            chip_sums[chip, :, :features] = own.astype(jnp.bfloat16)
            other_part[chip, :, :features] = other.astype(jnp.bfloat16)
            own, other = parted(jnp.where(lane == expert, grad_gate, 0.0))
            chip_sums[chip, :, features:] = own.astype(jnp.bfloat16)
            other_part[chip, :, features:] = other.astype(jnp.bfloat16)
            scatter.send_core(chip)

        gather.along_z(1)
        for step in range(2, depth):
            gather.along_y(step - 2)
            gather.along_z(step)
        near.wait()
        for swap in swaps:
            swap.wait()
        for of_z in (nearest(1), z):
            gather.take_core(of_z)
        backward(nearest(1) * 2 + 1 - y)
        backward(nearest(1) * 2 + y)
        scatter.add_chip(nearest(1), True)
        gather.along_y(depth - 2)
        backward(z * 2 + 1 - y)
        gather.along_y(depth - 1)
        backward(z * 2 + y)
        gather.finish(nearest(1), z)
        scatter.add_chip(nearest(1), False)

        @pl.loop(0, depth - 2)
        def _(turn):
            of_z = nearest(depth - 1 - turn)
            backward(of_z * 2 + 1 - y)
            pl.when(turn > 0)(lambda: scatter.add_chip(nearest(depth - turn), False))
            backward(of_z * 2 + y)
            scatter.add_chip(of_z, True)

        scatter.add_chip(nearest(2), False)
        scatter.add_chip(z, True)
        scatter.add_chip(nearest(0), False)
        scatter.add_y_of(nearest(depth - 1))

        def result_copy(chip):
            target = {"ctx": ctx_of(z, y, 1 - c)}
            return remote(
                other_result.at[chip], result_from.at[chip], result_sems, (chip,), target
            )

        @pl.loop(0, chips)
        def _(chip):
            result = jnp.dot(
                gated_hidden[chip_rows(chip), :], out_ref[...], preferred_element_type=jnp.float32
            )
            own, other = parted(result)
            results[chip] = own.astype(jnp.bfloat16)
            other_result[chip] = other.astype(jnp.bfloat16)
            result_copy(chip).start()

        scatter.add_y_of(nearest(depth - 2))

        for k in range(depth - 3, 0, -1):
            scatter.add_y_of(nearest(k))

        @pl.loop(0, features // 512)
        def _(turn):
            at = pl.ds(pl.multiple_of(turn * 512, 512), 512)
            grad = columns_by_columns(gated_hidden[...], d_out_ref[:, at])
            grad_out[:, at] = grad[:quarter]
            grad_out_other[:, at] = grad[quarter:].astype(jnp.bfloat16)

        stores[3].start()
        stores[4].start()

        @pl.loop(0, features // 512)
        def _(turn):
            at = pl.ds(pl.multiple_of(turn * 512, 512), 512)
            grad = columns_by_columns(grad_both[...], hidden_all[:, at])
            for part in range(2):
                rows = slice(part * quarter, (part + 1) * quarter)
                first = part * width
                grad_in[rows, at] = grad[first : first + quarter]
                grad_in_other[rows, at] = grad[first + quarter : first + width].astype(jnp.bfloat16)

        stores[1].start()
        stores[2].start()

        @pl.loop(0, chips)
        def _(chip):
            result_copy(chip).wait_recv()
            add_into(results.at[chip], (results.at[chip], result_from.at[chip]), tokens)

        stores[0].start()
        scatter.add_y_of(nearest(0))
        scatter.last(returned)
        scatter.finish()
        for chip in range(chips):
            result_copy(chip).wait_send()
        for store in stores:
            store.wait()

    block = (chips, tokens, features)
    out = [
        jax.ShapeDtypeStruct((tokens, wide), jnp.float32),
        jax.ShapeDtypeStruct(block, jnp.bfloat16),
        jax.ShapeDtypeStruct(in_own.shape, jnp.float32),
        jax.ShapeDtypeStruct(in_own.shape, jnp.bfloat16),
        jax.ShapeDtypeStruct(out_own.shape, jnp.float32),
        jax.ShapeDtypeStruct(out_own.shape, jnp.bfloat16),
    ]
    scratch = [
        pltpu.VMEM((length, wide), jnp.bfloat16),
        pltpu.VMEM((length, 2 * width), jnp.bfloat16),
        pltpu.VMEM((length, width), jnp.bfloat16),
        pltpu.VMEM((chips, tokens, wide), jnp.bfloat16),
        pltpu.VMEM(block, jnp.bfloat16),
        pltpu.VMEM(block, jnp.bfloat16),
        pltpu.SemaphoreType.DMA((2, chips)),
        pltpu.VMEM((2 * width, features), jnp.bfloat16),
        pltpu.VMEM((width, features), jnp.bfloat16),
        pltpu.VMEM(d_out_all.shape, jnp.bfloat16),
        pltpu.SemaphoreType.DMA((2, 2)),
        pltpu.SemaphoreType.DMA((1,)),
    ]
    scratch += [pltpu.VMEM(one.shape, one.dtype) for one in out[1:]]
    scratch.append(pltpu.SemaphoreType.DMA((5,)))
    scratch += Gather.sems(depth) * 2 + Scatter.scratch(depth, tokens, wide, 2)
    return call(
        kernel, out, scratch, 3, "experts", send, d_out_all, in_own, out_own, out_other, outside=(1,),
        outside_out=range(1, 6), late=(2, 3, 4),
    )


def finish(
    x, grad_middle, small, small_there, small_grads, matrices, hidden, mixed, middle, query, keyval,
    expert_in, expert_out,
):
    count, tokens, half = lax.axis_size("ctx"), x.shape[0], x.shape[1] // 2
    depth, rows = count // 4, half // count
    widths = (middle[0].shape[1], query[0].shape[1], keyval[0].shape[1])
    experts = small.shape[0] // 2

    def kernel(
        arrive, leave, x_ref, grad_middle_ref, small_ref, small_there_ref, small_grads_ref,
        query_own, query_other, keyval_own, keyval_other,
        hidden_ref, hidden_there, mixed_ref, mixed_there, middle_ref, middle_there,
        query_ref, query_there, keyval_ref, keyval_there, in_ref, out_ref,
        attn_sum, query_sum, keyval_sum, small_sum, grad_input, in_there, out_there,
        attn_part, query_part, keyval_part, pair, full, grad_one, small_mine, small_came, small_all,
        x_sems, *scratch,
    ):
        scatters, gathers = [], []
        parts, sums = (attn_part, query_part, keyval_part), (attn_sum, query_sum, keyval_sum)
        for part, total in zip(parts, sums):
            scatters.append(Scatter(part, scratch[:7]))
            gathers.append(Gather(total, rows, scratch[7:10]))
            scratch = scratch[10:]
        small_out = Gather(small_all, small_came.shape[0], scratch)
        (attn, query_, keyval_), (attn_out, query_out, keyval_out) = scatters, gathers
        partner = {"wa": 1 - lax.axis_index("wa")}
        swaps = [
            remote(source, target, x_sems, (i,), partner)
            for i, (source, target) in enumerate(
                [(small_mine.at[:, side_columns(False)], small_came), (in_ref, in_there),
                 (out_ref, out_there)]
            )
        ]
        steps = range(depth - 1, -1, -1)

        def products(left, left_there, right, right_there, part):
            pair[:tokens] = left[...]
            pair[tokens:] = left_there[...]

            @pl.loop(0, part.shape[1] // 512)
            def _(turn):
                at = pl.ds(pl.multiple_of(turn * 512, 512), 512)
                both = jnp.concatenate([right[:, at], right_there[:, at]], axis=0)
                part[:, at] = columns_by_columns(pair[...], both).astype(jnp.bfloat16)

        products(mixed_ref, mixed_there, middle_ref, middle_there, attn_part)
        greet(across_x=True)
        attn.start()
        arrive(9, 10, 15, 16)
        products(hidden_ref, hidden_there, query_ref, query_there, query_part)
        for step in steps:
            attn.add_cores(step)
        query_.start()
        arrive(17, 18)
        products(hidden_ref, hidden_there, keyval_ref, keyval_there, keyval_part)
        keyval_.start()
        for step in steps:
            query_.add_cores(step)
        attn.add_y(depth - 1)
        fill_small(full, small_ref, small_there_ref)
        arrive(0, 1, 5, 6, 7, 8)
        grad_one[:, side_columns(True)] = rows_by_rows(
            query_ref[...], query_own[...]
        ) + rows_by_rows(keyval_ref[...], keyval_own[...])
        attn.add_y(depth - 2)
        grad_one[:, side_columns(False)] = rows_by_rows(
            query_ref[...], query_other[...]
        ) + rows_by_rows(keyval_ref[...], keyval_other[...])
        back, grad_gain = norm_back(
            x_ref[...].astype(jnp.float32), full[experts : experts + 1], grad_one[...]
        )
        grad_input[...] = (grad_middle_ref[...] + back).astype(jnp.bfloat16)
        leave(4)
        row = lax.broadcasted_iota(jnp.int32, (small_mine.shape[0], 1), 0)
        small_mine[...] = jnp.where(row == experts, grad_gain, small_grads_ref[...])
        swaps[0].start()
        for step in range(depth - 3, -1, -1):
            attn.add_y(step)
        for step in steps:
            keyval_.add_cores(step)
        attn.last(attn_out.own())
        attn_out.start()
        swaps[1].start()
        swaps[2].start()
        swaps[0].wait()
        small_out.own()[...] = (small_mine[:, side_columns(True)] + small_came[...]).astype(
            jnp.bfloat16
        )
        small_out.start()
        for step in steps:
            query_.add_y(step)
        attn_out.along_z(1)
        query_.last(query_out.own())
        query_out.start()
        attn_out.along_z(2)
        attn_out.along_y(0)
        small_out.along_z(1)
        for step in steps:
            keyval_.add_y(step)
        attn_out.along_z(3)
        attn_out.along_y(1)
        keyval_.last(keyval_out.own())
        keyval_out.start()
        query_out.along_z(1)
        small_out.along_z(2)
        attn_out.along_y(2)
        query_out.along_z(2)
        small_out.along_z(3)
        query_out.along_y(0)
        keyval_out.along_z(1)
        query_out.along_z(3)
        attn_out.along_y(3)
        keyval_out.along_z(2)
        query_out.along_y(1)
        keyval_out.along_z(3)
        query_out.along_y(2)
        attn_out.finish()
        leave(0)
        small_out.along_y(0)
        keyval_out.along_y(0)
        small_out.along_y(1)
        query_out.along_y(3)
        keyval_out.along_y(1)
        small_out.along_y(2)
        keyval_out.along_y(2)
        small_out.along_y(3)
        keyval_out.along_y(3)
        query_out.finish()
        leave(1)
        keyval_out.finish()
        leave(2)
        for one in [small_out] + scatters:
            one.finish()
        small_rows = small_came.shape[0]
        total = small_all[:small_rows].astype(jnp.float32)
        for device in range(1, count):
            rows_of = slice(device * small_rows, (device + 1) * small_rows)
            total = total + small_all[rows_of].astype(jnp.float32)
        small_sum[...] = total
        swaps[1].wait()
        swaps[2].wait()

    small_shape = (small.shape[0], half)
    out = [jax.ShapeDtypeStruct((half, width), jnp.bfloat16) for width in widths]
    out += [
        jax.ShapeDtypeStruct(small_shape, jnp.float32),
        jax.ShapeDtypeStruct(x.shape, jnp.bfloat16),
        jax.ShapeDtypeStruct(expert_in.shape, expert_in.dtype),
        jax.ShapeDtypeStruct(expert_out.shape, expert_out.dtype),
    ]
    scratch = [pltpu.VMEM((half, width), jnp.bfloat16) for width in widths]
    scratch += [
        pltpu.VMEM((2 * tokens, half), jnp.bfloat16),
        pltpu.VMEM(small_grads.shape, jnp.float32),
        pltpu.VMEM(x.shape, jnp.float32),
        pltpu.VMEM(small_grads.shape, jnp.float32),
        pltpu.VMEM(small_shape, jnp.float32),
        pltpu.VMEM((count * small.shape[0], half), jnp.bfloat16),
        pltpu.SemaphoreType.DMA((2, 3)),
    ]
    for width in widths:
        scratch += Scatter.scratch(depth, rows, width) + Gather.sems(depth)
    scratch += Gather.sems(depth)
    return call(
        kernel, out, scratch, 1, "finish",
        x, grad_middle, small, small_there, small_grads, *matrices, *hidden, *mixed, *middle,
        *query, *keyval, expert_in, expert_out, outside=(19, 20), outside_out=(5, 6),
        late=(9, 10, 15, 16, 17, 18, 5, 6, 7, 8, 0, 1), early=(0, 1, 2, 4),
    )


def widen(query, keyval, attn, grad_in, in_there, grad_out, out_there, small):
    quarter, features = grad_out.shape
    steps, experts = 4, small.shape[0] // 2

    def kernel(*refs):
        query_ref, keyval_ref, attn_ref, in_ref, in_there_ref, out_ref, out_there_ref = refs[:7]
        small_ref, query_out, keyval_out, attn_out, in_out, out_out, router_out = refs[7:]
        router_out[...] = small_ref[:experts]
        query_out[...] = query_ref[...].astype(jnp.float32)
        keyval_out[...] = keyval_ref[...].astype(jnp.float32)
        attn_out[...] = attn_ref[...].astype(jnp.float32)
        both = in_ref[...] + in_there_ref[...].astype(jnp.float32)
        in_out[...] = both
        out_out[0] = out_ref[...] + out_there_ref[...].astype(jnp.float32)

    def rows(values):
        return pl.BlockSpec((values.shape[0] // steps, values.shape[1]), lambda i: (i, 0))

    operands = (query, keyval, attn, grad_in, in_there, grad_out, out_there)
    return pl.pallas_call(
        kernel,
        grid=(steps,),
        out_shape=[
            jax.ShapeDtypeStruct(query.shape, jnp.float32),
            jax.ShapeDtypeStruct(keyval.shape, jnp.float32),
            jax.ShapeDtypeStruct(attn.shape, jnp.float32),
            jax.ShapeDtypeStruct(grad_in.shape, jnp.float32),
            jax.ShapeDtypeStruct((1, quarter, features), jnp.float32),
            jax.ShapeDtypeStruct((experts, small.shape[1]), jnp.float32),
        ],
        in_specs=[rows(values) for values in operands]
        + [pl.BlockSpec(small.shape, lambda i: (0, 0))],
        out_specs=[
            rows(query), rows(keyval), rows(attn),
            rows(grad_in),
            pl.BlockSpec((1, quarter // steps, features), lambda i: (0, i, 0)),
            pl.BlockSpec((experts, small.shape[1]), lambda i: (0, 0)),
        ],
        compiler_params=pltpu.CompilerParams(vmem_limit_bytes=VMEM_LIMIT),
        name="widen",
    )(*operands, small)


def gathered_body(
    layer_input, seq_ids, routes, gain_attn, w_query, w_keyval, w_out_attn, gain_ffn, router,
    w_in, w_out, d_out,
):
    me = lax.axis_index("ctx")
    tokens, experts = layer_input.shape[1], router.shape[1]
    x, grad_out = layer_input[0], d_out[0]
    turns = angle_table(me * tokens + jnp.arange(tokens, dtype=jnp.int32))[:, 0]
    cosine, sine = jnp.cos(turns), jnp.sin(turns)
    angles = (
        jnp.concatenate([cosine, cosine], axis=1), jnp.concatenate([-sine, sine], axis=1)
    )
    in_own = jnp.swapaxes(w_in[0], 1, 2).reshape(-1, D)

    (
        query, keyval, level, mixed, hidden, mixed_low, middle, send, gates, w_query_there,
        w_keyval_there, w_out_attn_there, small_there, d_out_all, w_out_there, small,
    ) = attend(
        x, grad_out, router.T, (gain_attn[None], gain_ffn[None]), w_query, w_keyval, w_out_attn,
        w_out[0], angles, seq_ids, routes[0].T,
    )
    projections = (w_query, w_query_there, w_keyval, w_keyval_there)
    returned, results, grad_in, grad_in_other, grad_out_matrix, grad_out_other = run_experts(
        send, d_out_all, in_own, w_out[0], w_out_there, experts
    )
    (
        output, grad_middle, middle_low, middle_there, grad_query, query_there, grad_keyval,
        keyval_there, small_grads, *halves,
    ) = attend_back(
        returned, gates, small, small_there, middle, grad_out, send, w_out_attn, w_out_attn_there,
        query, keyval, angles, seq_ids, level, mixed, hidden, mixed_low, results, experts,
    )
    attn_sum, query_sum, keyval_sum, small_sum, grad_input, in_there, out_there = finish(
        x, grad_middle, small, small_there, small_grads, projections, halves[:2], halves[2:],
        (middle_low, middle_there), (grad_query, query_there),
        (grad_keyval, keyval_there), grad_in_other, grad_out_other,
    )
    query_sum, keyval_sum, attn_sum, grad_w_in, grad_w_out, grad_router = widen(
        query_sum, keyval_sum, attn_sum, grad_in, in_there, grad_out_matrix, out_there, small_sum
    )
    return (
        output[None],
        grad_input[None],
        small_sum[experts],
        query_sum,
        keyval_sum,
        attn_sum,
        small_sum[experts + 1],
        grad_router.T,
        jnp.swapaxes(grad_w_in.reshape(2, -1, D), 1, 2)[None],
        grad_w_out,
    )


def solution(mesh):
    in_specs = (
        P("wa", "ctx", None),
        P("wa", None),
        P("wa", "ctx", None),
        P("wa"),
        P("wa", None),
        P("wa", None),
        P("wa", None),
        P("wa"),
        P("wa", None),
        P("ctx", None, None, "wa"),
        P("ctx", "wa", None),
        P("wa", "ctx", None),
    )
    out_specs = (
        P("wa", "ctx", None),
        P("wa", "ctx", None),
        P("wa"),
        P("wa", None),
        P("wa", None),
        P("wa", None),
        P("wa"),
        P("wa", None),
        P("ctx", None, None, "wa"),
        P("ctx", "wa", None),
    )
    depth = mesh.shape["ctx"]
    body = gathered_body if depth == 16 else routed_body
    return jax.shard_map(body, mesh=mesh, in_specs=in_specs, out_specs=out_specs, check_vma=False)
```
